32 devices in a mesh: batch: 16 (over z, y, core), heads: 2 (over x).
Axes of the slice: x: 2, y: 2, z: 4, core: 2. Of those that a mesh axis runs over, the one named last changes fastest.
Arguments:
- residual_in: bfloat16 [16, 1024, 768], P('batch', 'heads'), may hold values from -6 to 6
- norm_gain: bfloat16 [768], replicated, may hold values from 0.5 to 1.5
- gate_proj: bfloat16 [768, 1536], P(None, 'heads'), may hold values from -0.21875 to 0.21875
- value_proj: bfloat16 [768, 1536], P(None, 'heads'), may hold values from -0.21875 to 0.21875
- state_proj: bfloat16 [768, 256], replicated, may hold values from -0.21875 to 0.21875
- step_proj: bfloat16 [768, 24], P(None, 'heads'), may hold values from -0.21875 to 0.21875
- value_conv: bfloat16 [4, 1536], P(None, 'heads'), may hold values from -3 to 3
- value_shift: bfloat16 [1536], P('heads'), may hold values from -0.5 to 0.5
- state_conv: bfloat16 [4, 256], replicated, may hold values from -3 to 3
- state_shift: bfloat16 [256], replicated, may hold values from -0.5 to 0.5
- step_bias: float32 [24], P('heads'), may hold values from -4 to 1
- log_rate: float32 [24], P('heads'), may hold values from -2 to 1.5
- skip_gain: float32 [24], P('heads'), may hold values from 0.5 to 1.5
- gated_gain: bfloat16 [1536], P('heads'), may hold values from 0.5 to 1.5
- out_proj: bfloat16 [1536, 768], P('heads'), may hold values from -0.15625 to 0.15625
- grad_out: bfloat16 [16, 1024, 768], P('batch', 'heads'), may hold values from -6 to 6
Outputs:
- mixed: float32 [16, 1024, 768], P('batch', 'heads')
- grad_input: float32 [16, 1024, 768], P('batch', 'heads')
- grad_norm_gain: float32 [768], replicated
- grad_gate_proj: float32 [768, 1536], P(None, 'heads')
- grad_value_proj: float32 [768, 1536], P(None, 'heads')
- grad_state_proj: float32 [768, 256], replicated
- grad_step_proj: float32 [768, 24], P(None, 'heads')
- grad_value_conv: float32 [4, 1536], P(None, 'heads')
- grad_value_shift: float32 [1536], P('heads')
- grad_state_conv: float32 [4, 256], replicated
- grad_state_shift: float32 [256], replicated
- grad_step_bias: float32 [24], P('heads')
- grad_log_rate: float32 [24], P('heads')
- grad_skip_gain: float32 [24], P('heads')
- grad_gated_gain: float32 [1536], P('heads')
- grad_out_proj: float32 [1536, 768], P('heads')
The draws below stay inside these ranges and needn't reach their ends.
All inputs are finite; a program needn't handle non-finite values.
Results may differ from the reference program's by a relative error of at most 0.0083.
Values may be sent and summed in bfloat16 or wider, within the bound.
No kernel may reach another device: no remote copies, remote signals or barrier semaphores. Data moves between devices by JAX's collectives and lax.ppermute only.
A program may use at most 128 MiB of HBM per device.

```python
import jax
import jax.numpy as jnp
from jax import lax

D = 768
NHEADS = 24
DSTATE = 128
DCONV = 4
GROUP = 256
D_INNER = 1536
SEQ_LEN = 1024
NSEQ = 16


def block_levels(rng, shape, split, low, top_value):
    level = 1.0
    for axis_at, blocks in split:
        heights = jax.random.uniform(jax.random.fold_in(jax.random.fold_in(rng, 6), axis_at), (blocks,), jnp.float32, low / len(split), top_value / len(split))
        level = level * jnp.repeat(jnp.exp(heights), shape[axis_at] // blocks).reshape((-1,) + (1,) * (len(shape) - 1 - axis_at))
    return level


def noise(rng, shape, scale, reach, cuts=(), dtype=jnp.bfloat16):
    level = block_levels(rng, shape, cuts, -0.22, 0.18) if cuts else 1.0
    drawn = jax.random.normal(rng, shape, jnp.float32) * scale * level
    return jnp.minimum(jnp.maximum(drawn, -reach), reach).astype(dtype)


def setup_inputs(seed: int = 0) -> dict:
    streams_of = jax.random.split(jax.random.key(seed), 17)
    residual_in = noise(streams_of[0], (NSEQ, SEQ_LEN, D), 1.0, 6.0, ((0, 16), (1, 2)))
    norm_gain = jnp.clip(1.0 + 0.1 * jax.random.normal(streams_of[1], (D,), jnp.float32), 0.5, 1.5).astype(jnp.bfloat16)
    gate_proj = noise(streams_of[2], (D, D_INNER), D ** -0.5, 0.21875, ((1, 2),))
    value_proj = noise(streams_of[3], (D, D_INNER), D ** -0.5, 0.21875, ((1, 2),))
    state_proj = noise(streams_of[4], (D, 2 * DSTATE), D ** -0.5, 0.21875)
    step_proj = noise(streams_of[5], (D, NHEADS), D ** -0.5, 0.21875, ((1, 2),))
    value_conv = noise(streams_of[6], (DCONV, D_INNER), DCONV ** -0.5, 3.0, ((1, 2),))
    value_shift = jnp.clip(jax.random.uniform(streams_of[7], (D_INNER,), jnp.float32, -0.5, 0.5) * block_levels(streams_of[7], (D_INNER,), ((0, 2),), -0.4, 0.0), -0.5, 0.5).astype(jnp.bfloat16)
    state_conv = noise(streams_of[8], (DCONV, 2 * DSTATE), DCONV ** -0.5, 3.0)
    state_shift = jnp.clip(jax.random.uniform(streams_of[9], (2 * DSTATE,), jnp.float32, -0.5, 0.5), -0.5, 0.5).astype(jnp.bfloat16)
    step_bias = jnp.clip(-4.0 + 5.0 * jax.random.uniform(streams_of[10], (NHEADS,), jnp.float32) ** block_levels(streams_of[10], (NHEADS,), ((0, 2),), -0.2, 0.2), -4.0, 1.0)
    log_rate = jnp.clip(-2.0 + 3.5 * jax.random.uniform(streams_of[11], (NHEADS,), jnp.float32) ** block_levels(streams_of[11], (NHEADS,), ((0, 2),), -0.2, 0.2), -2.0, 1.5)
    skip_gain = jnp.clip(0.5 + 1.0 * jax.random.uniform(streams_of[12], (NHEADS,), jnp.float32) ** block_levels(streams_of[12], (NHEADS,), ((0, 2),), -0.2, 0.2), 0.5, 1.5)
    gated_gain = jnp.clip(1.0 + 0.1 * jax.random.normal(streams_of[13], (D_INNER,), jnp.float32), 0.5, 1.5).astype(jnp.bfloat16)
    out_proj = noise(streams_of[14], (D_INNER, D), D_INNER ** -0.5, 0.15625, ((0, 2),))
    grad_out = noise(streams_of[15], (NSEQ, SEQ_LEN, D), 1.0, 6.0, ((0, 16), (1, 2)))
    return dict(residual_in=residual_in, norm_gain=norm_gain, gate_proj=gate_proj, value_proj=value_proj, state_proj=state_proj, step_proj=step_proj, value_conv=value_conv, value_shift=value_shift, state_conv=state_conv, state_shift=state_shift, step_bias=step_bias, log_rate=log_rate, skip_gain=skip_gain, gated_gain=gated_gain, out_proj=out_proj, grad_out=grad_out)


EPSILON = 1e-05
HIGHEST = lax.Precision.HIGHEST

@jax.custom_vjp
def low(v):
    return lax.optimization_barrier(v.astype(jnp.bfloat16)).astype(jnp.float32)

@jax.custom_vjp
def low_back(v):
    return v

def low_keep(v):
    return (low(v), None)

def low_pass(kept, grad):
    return (grad,)

def back_keep(v):
    return (v, None)

def back_low(kept, grad):
    return (low(grad),)
low.defvjp(low_keep, low_pass)
low_back.defvjp(back_keep, back_low)

def causal_conv(signal, kernel, offset):
    taps = kernel.shape[0]
    length = signal.shape[0]
    padded = jnp.pad(signal, ((taps - 1, 0), (0, 0)))
    summed = jnp.zeros_like(signal) + offset[None, :]
    for lag_index in range(taps):
        summed = summed + kernel[lag_index][None, :] * padded[lag_index:lag_index + length]
    return summed

def scan_heads(values, step_sizes, decays, b_rows, c_rows, skip_gain, span_rows):
    length, head_count, head_width = values.shape
    number = length // span_rows
    state_width = b_rows.shape[1]

    def advance(carry_state, pieces):
        value_blk, step_blk, decay_blk, b_blk, c_blk = pieces
        running = jnp.cumsum(decay_blk, axis=0)
        scores = jnp.dot(c_blk, b_blk.T, precision=HIGHEST)
        causal = lax.broadcasted_iota(jnp.int32, (span_rows, span_rows), 0) >= lax.broadcasted_iota(jnp.int32, (span_rows, span_rows), 1)
        spread = running[:, None, :] - running[None, :, :]
        factor = jnp.where(causal[:, :, None], jnp.exp(jnp.where(causal[:, :, None], spread, 0.0)), 0.0)
        mixing = scores[:, :, None] * factor * step_blk[None, :, :]
        output = jnp.einsum('tsh,shp->thp', mixing, value_blk, precision=HIGHEST)
        carried = jnp.einsum('tn,nhp->thp', c_blk, carry_state, precision=HIGHEST)
        output = output + jnp.exp(running)[:, :, None] * carried + skip_gain[None, :, None] * value_blk
        tail_weight = jnp.exp(running[-1][None, :] - running) * step_blk
        update = jnp.einsum('sn,shp->nhp', b_blk, value_blk * tail_weight[:, :, None], precision=HIGHEST)
        carry_state = jnp.exp(running[-1])[None, :, None] * carry_state + update
        return (carry_state, output)
    pieces = (values.reshape(number, span_rows, head_count, head_width), step_sizes.reshape(number, span_rows, head_count), decays.reshape(number, span_rows, head_count), b_rows.reshape(number, span_rows, state_width), c_rows.reshape(number, span_rows, state_width))
    initial = jnp.zeros((state_width, head_count, head_width), jnp.float32)
    final_state, outputs = lax.scan(jax.checkpoint(advance), initial, pieces)
    return outputs.reshape(length, head_count * head_width)

def mixer_core(projected, value_conv, value_shift, state_conv, state_shift, step_bias, log_rate, skip_gain, span_rows):
    inner_width = value_conv.shape[1]
    state_width = state_conv.shape[1] // 2
    head_count = step_bias.shape[0]
    length = projected.shape[0]
    gate_part = projected[:, :inner_width]
    value_pre = projected[:, inner_width:2 * inner_width]
    state_pre = projected[:, 2 * inner_width:2 * inner_width + 2 * state_width]
    step_raw = projected[:, 2 * inner_width + 2 * state_width:]
    values = jax.nn.silu(causal_conv(value_pre, value_conv, value_shift))
    states = jax.nn.silu(causal_conv(state_pre, state_conv, state_shift))
    step_sizes = jax.nn.softplus(step_raw + step_bias[None, :])
    decays = -jnp.exp(log_rate)[None, :] * step_sizes
    scanned = scan_heads(values.reshape(length, head_count, inner_width // head_count), step_sizes, decays, states[:, :state_width], states[:, state_width:], skip_gain, span_rows)
    return scanned * jax.nn.silu(gate_part)

def forward(residual_rows, norm_gain, gate_proj, value_proj, state_proj, step_proj, value_conv, value_shift, state_conv, state_shift, step_bias, log_rate, skip_gain, gated_gain, out_proj):
    scale_in = lax.rsqrt(lax.optimization_barrier(jnp.mean(residual_rows * residual_rows, axis=-1, keepdims=True)) + EPSILON)
    normed = low(residual_rows * scale_in * norm_gain[None, :])
    weights = jnp.concatenate([gate_proj, value_proj, state_proj, step_proj], axis=1)
    projected = low_back(jnp.dot(normed, weights, precision=HIGHEST))
    gated = mixer_core(projected, value_conv, value_shift, state_conv, state_shift, step_bias, log_rate, skip_gain, GROUP)
    scale_out = lax.rsqrt(lax.optimization_barrier(jnp.mean(gated * gated, axis=-1, keepdims=True)) + EPSILON)
    normed_out = low(gated * scale_out * gated_gain[None, :])
    return residual_rows + jnp.dot(normed_out, out_proj, precision=HIGHEST)

def reference(residual_in, norm_gain, gate_proj, value_proj, state_proj, step_proj, value_conv, value_shift, state_conv, state_shift, step_bias, log_rate, skip_gain, gated_gain, out_proj, grad_out):
    params = tuple((arg.astype(jnp.float32) for arg in (norm_gain, gate_proj, value_proj, state_proj, step_proj, value_conv, value_shift, state_conv, state_shift, step_bias, log_rate, skip_gain, gated_gain, out_proj)))

    def one_sequence(totals, inputs_pair):
        seq_rows, cotangent = inputs_pair
        result, pull_back = jax.vjp(forward, seq_rows, *params)
        gradients = pull_back(cotangent)
        totals = jax.tree.map(lambda left, right: left + right, totals, tuple(gradients[1:]))
        return (totals, (result, gradients[0]))
    zero_totals = jax.tree.map(jnp.zeros_like, params)
    totals, outputs = lax.scan(one_sequence, zero_totals, (residual_in.astype(jnp.float32), grad_out.astype(jnp.float32)))
    mixed, grad_input = outputs
    g_norm, g_gate, g_value, g_state, g_step, g_vconv, g_vshift, g_sconv, g_sshift, g_sbias, g_rate, g_skip, g_ggain, g_out = totals
    return (mixed, grad_input, g_norm, g_gate, g_value, g_state, g_step, g_vconv, g_vshift, g_sconv, g_sshift, g_sbias, g_rate, g_skip, g_ggain, g_out)
```

```python
import functools

import jax
import jax.numpy as jnp
from jax import lax
from jax.experimental import pallas as pl
from jax.experimental.pallas import tpu as pltpu
from jax.sharding import PartitionSpec as P

EPSILON = 1e-05
HIGHEST = lax.Precision.HIGHEST
BLOCK = 256
CHUNK = 128
LANES = 128
LOG2E = 1.4426950408889634
f32 = jnp.float32
bf16 = jnp.bfloat16


def dot(left, right, over=((1,), (0,)), precision=None):
    return lax.dot_general(
        left, right, (over, ((), ())), preferred_element_type=f32, precision=precision
    )


TN = ((0,), (0,))
NT = ((1,), (1,))


def sigmoid(v):
    return 0.5 * jnp.tanh(0.5 * v) + 0.5


def split(v):
    high = v.astype(bf16)
    return jnp.concatenate([high, (v - high.astype(f32)).astype(bf16)], axis=1)


def lower_mask(rows):
    return lax.broadcasted_iota(jnp.int32, (rows, rows), 0) >= lax.broadcasted_iota(
        jnp.int32, (rows, rows), 1
    )


def chunk_scalars(z, log_rate):
    step = jnp.maximum(z, 0.0) + jnp.log1p(jnp.exp(-jnp.abs(z)))
    rate = -jnp.exp(log_rate)
    decay = step * (rate * LOG2E)
    ones = lower_mask(CHUNK).astype(f32)
    running = dot(ones, decay, precision=HIGHEST)
    grown = jnp.exp2(running)
    tail = jnp.exp2(running[CHUNK - 1 : CHUNK, :] - running)
    return step, rate, running, grown, tail


def pair_decay(running, running_t, pair, mask):
    out = []
    for head in (2 * pair, 2 * pair + 1):
        spread = running[:, head : head + 1] - running_t[head : head + 1, :]
        out.append(jnp.exp2(jnp.where(mask, spread, -1e30)))
    return out


def half_masks():
    lane = lax.broadcasted_iota(jnp.int32, (1, LANES), 1)
    first = (lane < LANES // 2).astype(bf16)
    return first, 1 - first


def stacked(rows, masks):
    return jnp.concatenate([rows * masks[0], rows * masks[1]], axis=0)


def forward_kernel(
    half_blocks,
    at_ref,
    own_ref,
    other_ref,
    gain_ref,
    gate_w,
    value_w,
    state_w,
    step_w,
    vconv_ref,
    vshift_ref,
    sconv_ref,
    sshift_ref,
    sbias_ref,
    rate_ref,
    skip_ref,
    ggain_ref,
    out_w,
    spread_ref,
    normed_ref,
    g_ref,
    y_ref,
    gg_ref,
    av_ref,
    vp_ref,
    as_ref,
    sp_ref,
    z_ref,
    sin_ref,
    sq_ref,
    branch_ref,
    gbuf,
    vbuf,
    sbuf,
    state,
    stepx,
    grownx,
    tailx,
    carried,
    vtail,
):
    step_at = pl.program_id(0)
    pairs = vbuf.shape[1] // LANES
    nstate = state.shape[0]

    @pl.when(step_at == 0)
    def _():
        state[...] = jnp.zeros_like(state)
        vbuf[0:8, :] = jnp.zeros((8, vbuf.shape[1]), f32)
        sbuf[0:8, :] = jnp.zeros((8, sbuf.shape[1]), f32)

    mine = (step_at // half_blocks) == at_ref[0]
    rows = jnp.where(mine, own_ref[...].astype(f32), other_ref[...].astype(f32))
    scale = lax.rsqrt(jnp.mean(rows * rows, axis=1, keepdims=True) + EPSILON)
    normed = (rows * scale * gain_ref[...]).astype(bf16)
    normed_ref[...] = normed
    gbuf[...] = dot(normed, gate_w[...])
    g_ref[...] = gbuf[...]
    vbuf[8:, :] = dot(normed, value_w[...])
    vp_ref[...] = vbuf[8:, :]
    sbuf[8:, :] = dot(normed, state_w[...])
    sp_ref[...] = sbuf[8:, :]
    z_ref[...] = dot(normed, step_w[...]) + sbias_ref[...]

    mask = lower_mask(CHUNK)
    masks = half_masks()
    for chunk in range(BLOCK // CHUNK):
        r0 = chunk * CHUNK
        here = pl.ds(r0, CHUNK)
        step, _, running, grown, tail = chunk_scalars(z_ref[here, :], rate_ref[...])
        running_t = running.T
        stepx[...] = dot(split(step), spread_ref[...])
        grownx[...] = dot(split(grown), spread_ref[...])
        tailx[...] = dot(split(tail), spread_ref[...])
        conv = sshift_ref[...]
        for tap in range(4):
            conv = conv + sconv_ref[tap : tap + 1, :] * sbuf[pl.ds(r0 + 5 + tap, CHUNK), :]
        as_ref[here, :] = conv
        states_f = conv * sigmoid(conv)
        states = states_f.astype(bf16)
        b_rows, c_rows = states[:, :nstate], states[:, nstate:]
        bb, cc = split(states_f[:, :nstate]), split(states_f[:, nstate:])
        scores = dot(jnp.concatenate([cc, cc[:, :nstate]], axis=1), jnp.concatenate([bb[:, :nstate], bb[:, :nstate], bb[:, nstate:]], axis=1), NT)
        before = state[...].astype(bf16)
        sin_ref[chunk, :, :] = before
        carried[...] = dot(c_rows, before)
        squares = jnp.zeros((CHUNK, LANES), f32)
        for pair in range(pairs):
            lanes = slice(pair * LANES, (pair + 1) * LANES)
            conv = vshift_ref[:, lanes]
            for tap in range(4):
                conv = conv + vconv_ref[tap : tap + 1, lanes] * vbuf[pl.ds(r0 + 5 + tap, CHUNK), lanes]
            av_ref[here, lanes] = conv
            values = conv * sigmoid(conv)
            stepped = values * stepx[:, lanes]
            vtail[:, lanes] = (stepped * tailx[:, lanes]).astype(bf16)
            first, second = pair_decay(running, running_t, pair, mask)
            mixing = jnp.concatenate(
                [(scores * first).astype(bf16), (scores * second).astype(bf16)], axis=1
            )
            scanned = dot(mixing, stacked(stepped.astype(bf16), masks))
            scanned = scanned + grownx[:, lanes] * carried[:, lanes] + skip_ref[:, lanes] * values
            y_ref[here, lanes] = scanned
            g = gbuf[here, lanes]
            gated = scanned * (g * sigmoid(g))
            gg_ref[here, lanes] = (gated * ggain_ref[:, lanes]).astype(bf16)
            squares = squares + gated * gated
        sq_ref[:, here] = dot(jnp.ones((8, LANES), f32), squares, NT, HIGHEST)
        state[...] = grownx[CHUNK - 1 : CHUNK, :] * state[...] + dot(b_rows, vtail[...], TN)
    branch_ref[...] = dot(gg_ref[...], out_w[...]).astype(bf16)
    vbuf[0:8, :] = vbuf[BLOCK : BLOCK + 8, :]
    sbuf[0:8, :] = sbuf[BLOCK : BLOCK + 8, :]


def stats_kernel(half_blocks, at_ref, own_ref, other_ref, gg_ref, sq_ref, out_w, og_ref, stats_ref):
    mine = (pl.program_id(0) // half_blocks) == at_ref[0]
    cot = jnp.where(mine, own_ref[...], other_ref[...])
    og = dot(cot, out_w[...], NT)
    og_ref[...] = og
    prod = (og * gg_ref[...].astype(f32)).astype(bf16)
    dots = dot(jnp.ones((8, prod.shape[1]), bf16), prod, NT)
    row = lax.broadcasted_iota(jnp.int32, dots.shape, 0)
    stats_ref[...] = jnp.where(row == 0, sq_ref[...], dots)


def gate_kernel(
    half_blocks,
    inner_all,
    at_ref,
    own_ref,
    other_ref,
    here_ref,
    there_ref,
    normed_ref,
    og_ref,
    y_ref,
    g_ref,
    gg_ref,
    ggain_ref,
    dg_ref,
    dy_ref,
    grad_out_ref,
    grad_gate_ref,
    grad_gain_ref,
):
    step_at = pl.program_id(0)
    pairs = og_ref.shape[1] // LANES

    @pl.when(step_at == 0)
    def _():
        grad_out_ref[...] = jnp.zeros_like(grad_out_ref)
        grad_gate_ref[...] = jnp.zeros_like(grad_gate_ref)
        grad_gain_ref[...] = jnp.zeros_like(grad_gain_ref)

    sums = here_ref[...] + there_ref[...]
    scale_row = lax.rsqrt(sums[0:1, :] / inner_all + EPSILON)
    pull_row = scale_row * scale_row * scale_row * sums[1:2, :] / inner_all
    columns = jnp.concatenate(
        [scale_row, pull_row, jnp.zeros((LANES - 2, BLOCK), f32)], axis=0
    ).T
    scale, pull = columns[:, 0:1], columns[:, 1:2]
    mine = (step_at // half_blocks) == at_ref[0]
    cot = jnp.where(mine, own_ref[...], other_ref[...]).astype(f32)
    scaled = (cot * scale).astype(bf16)
    for pair in range(pairs):
        lanes = slice(pair * LANES, (pair + 1) * LANES)
        og = og_ref[:, lanes].astype(f32) * scale
        y = y_ref[:, lanes].astype(f32)
        g = g_ref[:, lanes].astype(f32)
        sig = sigmoid(g)
        silu = g * sig
        gated = y * silu
        grad_gain_ref[0:1, lanes] += jnp.sum(og * gated, axis=0, keepdims=True)
        gated_grad = ggain_ref[:, lanes] * og - gated * pull
        dy_ref[:, lanes] = (gated_grad * silu).astype(bf16)
        dg_ref[:, lanes] = (gated_grad * y * (sig + silu * (1.0 - sig))).astype(bf16)
    grad_out_ref[...] += dot(gg_ref[...], scaled, TN)
    grad_gate_ref[...] += dot(normed_ref[...], dg_ref[...], TN)


def backward_kernel(
    at_ref,
    normed_ref,
    dg_ref,
    dy_ref,
    av_ref,
    vp_ref,
    as_ref,
    sp_ref,
    z_ref,
    sin_ref,
    gate_w,
    value_w,
    state_w,
    step_w,
    vconv_ref,
    sconv_ref,
    rate_ref,
    skip_ref,
    spread_ref,
    gather_ref,
    ng_ref,
    grad_value_ref,
    grad_state_ref,
    grad_step_ref,
    grad_vconv_ref,
    grad_sconv_ref,
    grad_head_ref,
    dabuf,
    dsbuf,
    dstate,
    stepx,
    grownx,
    tailx,
    carried,
    pulled,
    ubuf,
    vtail,
    dvalue,
    dstates,
    dstep,
):
    step_at = pl.program_id(0)
    width = dabuf.shape[1]
    pairs = width // LANES
    nstate = dstate.shape[0]

    @pl.when(step_at == 0)
    def _():
        dstate[...] = jnp.zeros_like(dstate)
        dabuf[BLOCK:, :] = jnp.zeros((8, width), f32)
        dsbuf[BLOCK:, :] = jnp.zeros((8, dsbuf.shape[1]), f32)
        for ref in (
            grad_value_ref,
            grad_state_ref,
            grad_step_ref,
            grad_vconv_ref,
            grad_sconv_ref,
            grad_head_ref,
        ):
            ref[...] = jnp.zeros_like(ref)

    @pl.when(step_at > 0)
    def _():
        dabuf[BLOCK:, :] = dabuf[0:8, :]
        dsbuf[BLOCK:, :] = dsbuf[0:8, :]

    mask = lower_mask(CHUNK)
    later = jnp.logical_not(mask).astype(f32)
    masks = half_masks()
    for chunk in reversed(range(BLOCK // CHUNK)):
        r0 = chunk * CHUNK
        here = pl.ds(r0, CHUNK)
        z = z_ref[here, :]
        step, rate, running, grown, tail = chunk_scalars(z, rate_ref[...])
        running_t = running.T
        stepx[...] = dot(split(step), spread_ref[...])
        grownx[...] = dot(split(grown), spread_ref[...])
        tailx[...] = dot(split(tail), spread_ref[...])
        conv_s = as_ref[here, :]
        sig_s = sigmoid(conv_s)
        states_f = conv_s * sig_s
        states = states_f.astype(bf16)
        b_rows, c_rows = states[:, :nstate], states[:, nstate:]
        bb, cc = split(states_f[:, :nstate]), split(states_f[:, nstate:])
        scores = dot(jnp.concatenate([cc, cc[:, :nstate]], axis=1), jnp.concatenate([bb[:, :nstate], bb[:, :nstate], bb[:, nstate:]], axis=1), NT)
        before = sin_ref[chunk, :, :]
        after = dstate[...].astype(bf16)
        carried[...] = dot(c_rows, before)
        pulled[...] = dot(b_rows, after)
        dscores = jnp.zeros((CHUNK, CHUNK), f32)
        inner = jnp.zeros((CHUNK, LANES), f32)
        outer = jnp.zeros((CHUNK, LANES), f32)
        sides = jnp.zeros((CHUNK, LANES), f32)
        for pair in range(pairs):
            lanes = slice(pair * LANES, (pair + 1) * LANES)
            conv = av_ref[here, lanes].astype(f32)
            sig = sigmoid(conv)
            values = conv * sig
            steps = stepx[:, lanes]
            stepped = values * steps
            low = stepped.astype(bf16)
            dy_low = dy_ref[here, lanes]
            dy = dy_low.astype(f32)
            first, second = pair_decay(running, running_t, pair, mask)
            mixing = jnp.concatenate(
                [(scores * first).astype(bf16), (scores * second).astype(bf16)], axis=1
            )
            dy_two = stacked(dy_low, masks)
            scanned = dot(mixing, stacked(low, masks))
            both = jnp.concatenate([mixing[:, :CHUNK], mixing[:, CHUNK:]], axis=0)
            dstepped = dot(both, dy_two, TN)
            dmixing = dot(dy_two, low, NT)
            dscores = dscores + dmixing[:CHUNK] * first + dmixing[CHUNK:] * second
            inside = dy * scanned - low.astype(f32) * dstepped
            u = (dy * grownx[:, lanes]).astype(bf16)
            ubuf[:, lanes] = u
            tails = tailx[:, lanes]
            v = (stepped * tails).astype(bf16)
            vtail[:, lanes] = v
            pull = pulled[:, lanes]
            dstepped = dstepped + tails * pull
            sums = gather_ref[pair * 2 * LANES : (pair + 1) * 2 * LANES, :]
            inner = inner + dot(split(inside), sums[:, :LANES])
            outer = outer + dot(
                jnp.concatenate(
                    [
                        (u.astype(f32) * carried[:, lanes]).astype(bf16),
                        (v.astype(f32) * pull).astype(bf16),
                    ],
                    axis=1,
                ),
                sums[:, LANES:],
            )
            sides = sides + dot(
                jnp.concatenate(
                    [(values * dstepped).astype(bf16), (values * dy).astype(bf16)], axis=1
                ),
                sums[:, LANES:],
            )
            dvalues = steps * dstepped + skip_ref[:, lanes] * dy
            da = dvalues * (sig + values * (1.0 - sig))
            dabuf[here, lanes] = da
            vp = vp_ref[here, lanes].astype(f32)
            dv = jnp.zeros((CHUNK, LANES), f32)
            rows = []
            for tap in range(4):
                moved = da if tap == 3 else dabuf[pl.ds(r0 + 3 - tap, CHUNK), lanes]
                dv = dv + vconv_ref[tap : tap + 1, lanes] * moved
                rows.append(jnp.sum(vp * moved, axis=0, keepdims=True))
            rows.append(jnp.sum(da, axis=0, keepdims=True))
            rows.append(jnp.zeros((3, LANES), f32))
            grad_vconv_ref[:, lanes] += jnp.concatenate(rows, axis=0)
            dvalue[here, lanes] = dv.astype(bf16)
        dlow = dscores.astype(bf16)
        drest = (dscores - dlow.astype(f32)).astype(bf16)
        db = dot(dlow, cc[:, :nstate], TN) + dot(dlow, cc[:, nstate:], TN)+ dot(drest, c_rows, TN) + dot(vtail[...], after, NT)
        dc = dot(dlow, b_rows) + dot(drest, b_rows) + dot(dlow, bb[:, nstate:]) + dot(ubuf[...], before, NT)
        ds = jnp.concatenate([db, dc], axis=1) * (sig_s + conv_s * sig_s * (1.0 - sig_s))
        dsbuf[here, :] = ds
        sp = sp_ref[here, :]
        dpre = jnp.zeros(ds.shape, f32)
        rows = []
        for tap in range(4):
            moved = ds if tap == 3 else dsbuf[pl.ds(r0 + 3 - tap, CHUNK), :]
            dpre = dpre + sconv_ref[tap : tap + 1, :] * moved
            rows.append(jnp.sum(sp * moved, axis=0, keepdims=True))
        rows.append(jnp.sum(ds, axis=0, keepdims=True))
        rows.append(jnp.zeros((3, ds.shape[1]), f32))
        grad_sconv_ref[...] += jnp.concatenate(rows, axis=0)
        dstates[here, :] = dpre.astype(bf16)

        overlap = jnp.sum(before.astype(f32) * dstate[...], axis=0, keepdims=True)
        overlap = jnp.broadcast_to(overlap * grownx[CHUNK - 1 : CHUNK, :], (8, width))
        held = jnp.zeros((8, LANES), f32)
        for pair in range(pairs):
            lanes = slice(pair * LANES, (pair + 1) * LANES)
            sums = gather_ref[pair * 2 * LANES : (pair + 1) * 2 * LANES, :]
            held = held + dot(split(overlap[:, lanes]), sums[:, :LANES])
        half = LANES // 2
        spare = jnp.zeros((CHUNK, half), f32)
        ddecay = (
            dot(mask.astype(f32), inner + jnp.concatenate([outer[:, :half], spare], axis=1), TN, HIGHEST)
            + dot(1.0 - mask.astype(f32).T, jnp.concatenate([outer[:, half:], spare], axis=1), precision=HIGHEST)
            + held[0:1, :]
        )
        dstep_all = jnp.concatenate([sides[:, :half], spare], axis=1) + ddecay * rate
        dz = dstep_all * sigmoid(z)
        dstep[here, :] = dz.astype(bf16)
        skips = jnp.concatenate([sides[:, half:], spare], axis=1)
        grad_head_ref[...] += jnp.concatenate(
            [
                jnp.sum(dz, axis=0, keepdims=True),
                jnp.sum(ddecay * step, axis=0, keepdims=True) * rate,
                jnp.sum(skips, axis=0, keepdims=True),
                jnp.zeros((5, LANES), f32),
            ],
            axis=0,
        )
        dstate[...] = grownx[CHUNK - 1 : CHUNK, :] * dstate[...] + dot(c_rows, ubuf[...], TN)

    normed = normed_ref[...]
    grad_value_ref[...] += dot(normed, dvalue[...], TN)
    grad_state_ref[...] += dot(normed, dstates[...], TN)
    grad_step_ref[...] += dot(normed, dstep[...], TN)
    ng_ref[...] = (
        dot(dg_ref[...], gate_w[...], NT)
        + dot(dvalue[...], value_w[...], NT)
        + dot(dstates[...], state_w[...], NT)
        + dot(dstep[...], step_w[...], NT)
    ).astype(ng_ref.dtype)


def whole(array):
    return pl.BlockSpec(array.shape, lambda i, at: (0,) * array.ndim)


def call(kernel, blocks, at, ins, outs, scratch):
    return pl.pallas_call(
        kernel,
        grid_spec=pltpu.PrefetchScalarGridSpec(
            num_scalar_prefetch=1,
            grid=(blocks,),
            in_specs=[whole(a) if s is None else s for a, s in ins],
            out_specs=[s for _, _, s in outs],
            scratch_shapes=scratch,
        ),
        out_shape=[jax.ShapeDtypeStruct(shape, dtype) for shape, dtype, _ in outs],
        compiler_params=pltpu.CompilerParams(
            dimension_semantics=("arbitrary",), vmem_limit_bytes=56 * 2**20
        ),
    )(at, *[a for a, _ in ins])


def per_device(
    residual_in,
    norm_gain,
    gate_proj,
    value_proj,
    state_proj,
    step_proj,
    value_conv,
    value_shift,
    state_conv,
    state_shift,
    step_bias,
    log_rate,
    skip_gain,
    gated_gain,
    out_proj,
    grad_out,
):
    parts = lax.axis_size("heads")
    two = parts == 2
    rows_here, model = residual_in.shape[1:]
    length = rows_here * parts
    inner = value_conv.shape[1]
    inner_all = inner * parts
    heads = step_bias.shape[0]
    head_width = inner // heads
    pad_heads = heads % 2
    nheads = heads + pad_heads
    width = nheads * head_width
    nstate2 = state_conv.shape[1]
    blocks = length // BLOCK
    chunks = BLOCK // CHUNK
    half_blocks = rows_here // BLOCK if two else blocks

    def wide(a, axis):
        pads = [(0, 0)] * a.ndim
        pads[axis] = (0, width - inner)
        return jnp.pad(a, pads) if width > inner else a

    def lanes_of(a):
        return jnp.pad(a, [(0, 0)] * (a.ndim - 1) + [(0, LANES - a.shape[-1])])

    residual = residual_in[0]
    cot = grad_out[0]
    if two:
        swap = [(0, 1), (1, 0)]
        at = lax.axis_index("heads").astype(jnp.int32).reshape(1)
        pair_of = lambda a: (a, lax.ppermute(a, "heads", swap))
        add_other = lambda a: lax.ppermute(a, "heads", swap)
    else:
        at = jnp.zeros((1,), jnp.int32)

        def pair_of(a):
            full = lax.all_gather(a, "heads", axis=0, tiled=True)
            return (full, full)

        add_other = lambda a: lax.psum(a, "heads") - a

    own_rows, other_rows = pair_of(residual)
    own_cot, other_cot = pair_of(cot)

    gate_w, value_w = wide(gate_proj, 1), wide(value_proj, 1)
    out_w = wide(out_proj, 0)
    step_w = lanes_of(step_proj)
    gain_in = norm_gain.astype(f32)[None, :]
    vconv = wide(value_conv.astype(f32), 1)
    vshift = wide(value_shift.astype(f32)[None, :], 1)
    sconv = state_conv.astype(f32)
    sshift = state_shift.astype(f32)[None, :]
    sbias, rate = lanes_of(step_bias[None, :]), lanes_of(log_rate[None, :])
    skipx = wide(jnp.repeat(skip_gain, head_width)[None, :], 1)
    ggain = wide(gated_gain.astype(f32)[None, :], 1)
    head_of = jnp.arange(width) // head_width
    spread = (jnp.arange(LANES)[:, None] == head_of[None, :]).astype(bf16)
    spread = jnp.concatenate([spread, spread], axis=0)
    half = LANES // 2
    first = head_of.reshape(-1, 1, LANES, 1)
    column = jnp.arange(2 * LANES)
    top = (column == first) | (column == first + LANES)
    bottom = (column == first) | (column == first + LANES + half)
    gather = jnp.concatenate([top, bottom], axis=1).reshape(-1, 2 * LANES).astype(bf16)

    if two:

        def own_block(i, a):
            return (jnp.clip(i - a[0] * half_blocks, 0, half_blocks - 1), 0)

        def other_block(i, a):
            return (jnp.clip(i - (1 - a[0]) * half_blocks, 0, half_blocks - 1), 0)

        def turned(i, a):
            return (lax.rem(i + a[0] * half_blocks, blocks), 0)

    else:
        own_block = other_block = turned = lambda i, a: (i, 0)

    def rows(n, index=lambda i, a: (i, 0)):
        return pl.BlockSpec((BLOCK, n), index)

    def back(index):
        return lambda i, a: index(blocks - 1 - i, a)

    along = pl.BlockSpec((8, BLOCK), lambda i, a: (0, i))
    fixed = lambda *shape: pl.BlockSpec(shape, lambda i, a: (0,) * len(shape))
    states_spec = lambda index: pl.BlockSpec((chunks, nstate2 // 2, width), index)
    big = lambda *shape: pltpu.VMEM(shape, f32)
    low = lambda *shape: pltpu.VMEM(shape, bf16)

    normed, g, y, gg, av, vp, conv_s, sp, z, sin, sq, branch = call(
        functools.partial(forward_kernel, half_blocks),
        blocks,
        at,
        [
            (own_rows, rows(model, own_block)),
            (other_rows, rows(model, other_block)),
            (gain_in, None),
            (gate_w, None),
            (value_w, None),
            (state_proj, None),
            (step_w, None),
            (vconv, None),
            (vshift, None),
            (sconv, None),
            (sshift, None),
            (sbias, None),
            (rate, None),
            (skipx, None),
            (ggain, None),
            (out_w, None),
            (spread, None),
        ],
        [
            ((length, model), bf16, rows(model)),
            ((length, width), f32, rows(width)),
            ((length, width), f32, rows(width)),
            ((length, width), bf16, rows(width)),
            ((length, width), f32, rows(width)),
            ((length, width), f32, rows(width)),
            ((length, nstate2), f32, rows(nstate2)),
            ((length, nstate2), f32, rows(nstate2)),
            ((length, LANES), f32, rows(LANES)),
            ((blocks * chunks, nstate2 // 2, width), bf16, states_spec(lambda i, a: (i, 0, 0))),
            ((8, length), f32, along),
            ((length, model), bf16, rows(model, turned)),
        ],
        [
            big(BLOCK, width),
            big(BLOCK + 8, width),
            big(BLOCK + 8, nstate2),
            big(nstate2 // 2, width),
            big(CHUNK, width),
            big(CHUNK, width),
            big(CHUNK, width),
            big(CHUNK, width),
            low(CHUNK, width),
        ],
    )
    og, stats = call(
        functools.partial(stats_kernel, half_blocks),
        blocks,
        at,
        [
            (own_cot, rows(model, own_block)),
            (other_cot, rows(model, other_block)),
            (gg, rows(width)),
            (sq, along),
            (out_w, None),
        ],
        [((length, width), f32, rows(width)), ((8, length), f32, along)],
        [],
    )
    other_stats = add_other(stats)
    dg, dy, grad_out_proj, grad_gate, grad_gain = call(
        functools.partial(gate_kernel, half_blocks, inner_all),
        blocks,
        at,
        [
            (own_cot, rows(model, own_block)),
            (other_cot, rows(model, other_block)),
            (stats, along),
            (other_stats, along),
            (normed, rows(model)),
            (og, rows(width)),
            (y, rows(width)),
            (g, rows(width)),
            (gg, rows(width)),
            (ggain, None),
        ],
        [
            ((length, width), bf16, rows(width)),
            ((length, width), bf16, rows(width)),
            ((width, model), f32, fixed(width, model)),
            ((model, width), f32, fixed(model, width)),
            ((8, width), f32, fixed(8, width)),
        ],
        [],
    )
    plain = lambda i, a: (i, 0)
    ng, grad_value, grad_state, grad_step, grad_vconv, grad_sconv, grad_head = call(
        backward_kernel,
        blocks,
        at,
        [
            (normed, rows(model, back(plain))),
            (dg, rows(width, back(plain))),
            (dy, rows(width, back(plain))),
            (av, rows(width, back(plain))),
            (vp, rows(width, back(plain))),
            (conv_s, rows(nstate2, back(plain))),
            (sp, rows(nstate2, back(plain))),
            (z, rows(LANES, back(plain))),
            (sin, states_spec(lambda i, a: (blocks - 1 - i, 0, 0))),
            (gate_w, None),
            (value_w, None),
            (state_proj, None),
            (step_w, None),
            (vconv, None),
            (sconv, None),
            (rate, None),
            (skipx, None),
            (spread, None),
            (gather, None),
        ],
        [
            ((length, model), bf16, rows(model, back(turned))),
            ((model, width), f32, fixed(model, width)),
            ((model, nstate2), f32, fixed(model, nstate2)),
            ((model, LANES), f32, fixed(model, LANES)),
            ((8, width), f32, fixed(8, width)),
            ((8, nstate2), f32, fixed(8, nstate2)),
            ((8, LANES), f32, fixed(8, LANES)),
        ],
        [
            big(BLOCK + 8, width),
            big(BLOCK + 8, nstate2),
            big(nstate2 // 2, width),
            big(CHUNK, width),
            big(CHUNK, width),
            big(CHUNK, width),
            big(CHUNK, width),
            big(CHUNK, width),
            low(CHUNK, width),
            low(CHUNK, width),
            low(BLOCK, width),
            low(BLOCK, nstate2),
            low(BLOCK, LANES),
        ],
    )

    def scattered(a):
        if two:
            return a[:rows_here].astype(f32) + lax.ppermute(a[rows_here:], "heads", swap).astype(f32)
        return lax.psum_scatter(a.astype(f32), "heads", scatter_dimension=0, tiled=True)

    sums = stats[0] + other_stats[0]
    own_sums = lax.dynamic_slice_in_dim(sums, lax.axis_index("heads") * rows_here, rows_here, 0)
    scale_out = lax.rsqrt(own_sums / inner_all + EPSILON)[:, None]
    residual_rows = residual.astype(f32)
    mixed = residual_rows + scale_out * scattered(branch)

    normed_grad = scattered(ng)
    scale_in = lax.rsqrt(jnp.mean(residual_rows * residual_rows, axis=-1, keepdims=True) + EPSILON)
    inner_dot = jnp.sum(normed_grad * gain_in * residual_rows, axis=1, keepdims=True)
    grad_input = (
        cot.astype(f32)
        + gain_in * scale_in * normed_grad
        - residual_rows * (scale_in * scale_in * scale_in) * inner_dot / model
    )

    grad_norm = (
        jnp.sum(grad_gate * gate_w.astype(f32), axis=1)
        + jnp.sum(grad_value * value_w.astype(f32), axis=1)
        + jnp.sum(grad_state * state_proj.astype(f32), axis=1)
        + jnp.sum(grad_step * step_w.astype(f32), axis=1)
    ) / gain_in[0]

    big_sums = lax.psum(
        tuple(a.astype(bf16) for a in (grad_gate, grad_value, grad_out_proj, grad_step)), "batch"
    )
    grad_gate, grad_value, grad_out_proj, grad_step = (a.astype(f32) for a in big_sums)
    grad_state = lax.psum(grad_state.astype(bf16), ("batch", "heads")).astype(f32)
    grad_vconv, grad_head, grad_gain = lax.psum((grad_vconv, grad_head, grad_gain), "batch")
    grad_sconv, grad_norm = lax.psum((grad_sconv, grad_norm), ("batch", "heads"))
    return (
        mixed[None],
        grad_input[None],
        grad_norm,
        grad_gate[:, :inner],
        grad_value[:, :inner],
        grad_state,
        grad_step[:, :heads],
        grad_vconv[:4, :inner],
        grad_vconv[4, :inner],
        grad_sconv[:4],
        grad_sconv[4],
        grad_head[0, :heads],
        grad_head[1, :heads],
        grad_head[2, :heads],
        grad_gain[0, :inner],
        grad_out_proj[:inner],
    )


def solution(mesh):
    return jax.shard_map(
        per_device,
        mesh=mesh,
        in_specs=(
            P("batch", "heads", None),
            P(),
            P(None, "heads"),
            P(None, "heads"),
            P(),
            P(None, "heads"),
            P(None, "heads"),
            P("heads"),
            P(),
            P(),
            P("heads"),
            P("heads"),
            P("heads"),
            P("heads"),
            P("heads", None),
            P("batch", "heads", None),
        ),
        out_specs=(
            P("batch", "heads", None),
            P("batch", "heads", None),
            P(),
            P(None, "heads"),
            P(None, "heads"),
            P(),
            P(None, "heads"),
            P(None, "heads"),
            P("heads"),
            P(),
            P(),
            P("heads"),
            P("heads"),
            P("heads"),
            P("heads"),
            P("heads", None),
        ),
        check_vma=False,
    )
```

```python
import functools

import jax
import jax.numpy as jnp
from jax import lax
from jax.experimental import pallas as pl
from jax.experimental.pallas import tpu as pltpu
from jax.sharding import PartitionSpec as P

EPSILON = 1e-05
HIGHEST = lax.Precision.HIGHEST
BLOCK = 256
CHUNK = 128
LANES = 128
LOG2E = 1.4426950408889634
f32 = jnp.float32
bf16 = jnp.bfloat16


def dot(left, right, over=((1,), (0,)), precision=None):
    return lax.dot_general(
        left, right, (over, ((), ())), preferred_element_type=f32, precision=precision
    )


TN = ((0,), (0,))
NT = ((1,), (1,))


def sigmoid(v):
    return 0.5 * jnp.tanh(0.5 * v) + 0.5


def split(v):
    high = v.astype(bf16)
    return jnp.concatenate([high, (v - high.astype(f32)).astype(bf16)], axis=1)


def lower_mask(rows):
    return lax.broadcasted_iota(jnp.int32, (rows, rows), 0) >= lax.broadcasted_iota(
        jnp.int32, (rows, rows), 1
    )


def chunk_scalars(z, log_rate):
    step = jnp.maximum(z, 0.0) + jnp.log1p(jnp.exp(-jnp.abs(z)))
    rate = -jnp.exp(log_rate)
    decay = step * (rate * LOG2E)
    ones = lower_mask(CHUNK).astype(f32)
    running = dot(ones, decay, precision=HIGHEST)
    grown = jnp.exp2(running)
    tail = jnp.exp2(running[CHUNK - 1 : CHUNK, :] - running)
    return step, rate, running, grown, tail


def chunk_scores(states):
    n = states.shape[1] // 2
    b, c = split(states[:, :n]), split(states[:, n:])
    left = jnp.concatenate([c, c[:, :n]], axis=1)
    right = jnp.concatenate([b[:, :n], b[:, :n], b[:, n:]], axis=1)
    return b, c, dot(left, right, NT)


def pair_decay(running, running_t, pair, mask):
    out = []
    for head in (2 * pair, 2 * pair + 1):
        spread = running[:, head : head + 1] - running_t[head : head + 1, :]
        out.append(jnp.exp2(jnp.where(mask, spread, -1e30)))
    return out


def half_masks():
    lane = lax.broadcasted_iota(jnp.int32, (1, LANES), 1)
    first = (lane < LANES // 2).astype(bf16)
    return first, 1 - first


def stacked(rows, masks):
    return jnp.concatenate([rows * masks[0], rows * masks[1]], axis=0)


def forward_kernel(
    half_blocks,
    at_ref,
    own_ref,
    other_ref,
    gain_ref,
    gate_w,
    value_w,
    state_w,
    step_w,
    vconv_ref,
    vshift_ref,
    sconv_ref,
    sshift_ref,
    sbias_ref,
    rate_ref,
    skip_ref,
    ggain_ref,
    spread_ref,
    normed_ref,
    g_ref,
    y_ref,
    gg_ref,
    av_ref,
    vp_ref,
    as_ref,
    sp_ref,
    z_ref,
    sin_ref,
    sq_ref,
    gbuf,
    vbuf,
    sbuf,
    state,
    stepx,
    grownx,
    tailx,
    carried,
    vtail,
):
    step_at = pl.program_id(0)
    pairs = vbuf.shape[1] // LANES
    nstate = state.shape[0]

    @pl.when(step_at == 0)
    def _():
        state[...] = jnp.zeros_like(state)
        vbuf[0:8, :] = jnp.zeros((8, vbuf.shape[1]), f32)
        sbuf[0:8, :] = jnp.zeros((8, sbuf.shape[1]), f32)

    mine = (step_at // half_blocks) == at_ref[0]
    rows = jnp.where(mine, own_ref[...].astype(f32), other_ref[...].astype(f32))
    scale = lax.rsqrt(jnp.mean(rows * rows, axis=1, keepdims=True) + EPSILON)
    normed = (rows * scale * gain_ref[...].astype(f32)).astype(bf16)
    normed_ref[...] = normed
    gbuf[...] = dot(normed, gate_w[...])
    g_ref[...] = gbuf[...]
    vbuf[8:, :] = dot(normed, value_w[...])
    vp_ref[...] = vbuf[8:, :]
    sbuf[8:, :] = dot(normed, state_w[...])
    sp_ref[...] = sbuf[8:, :]
    z_ref[...] = dot(normed, step_w[...]) + sbias_ref[...]

    mask = lower_mask(CHUNK)
    masks = half_masks()
    for chunk in range(BLOCK // CHUNK):
        r0 = chunk * CHUNK
        here = pl.ds(r0, CHUNK)
        step, _, running, grown, tail = chunk_scalars(z_ref[here, :], rate_ref[...])
        running_t = running.T
        stepx[...] = dot(split(step), spread_ref[...])
        grownx[...] = dot(split(grown), spread_ref[...])
        tailx[...] = dot(split(tail), spread_ref[...])
        conv = sshift_ref[...].astype(f32)
        for tap in range(4):
            conv = conv + sconv_ref[tap : tap + 1, :].astype(f32) * sbuf[pl.ds(r0 + 5 + tap, CHUNK), :]
        as_ref[here, :] = conv
        b_two, c_two, scores = chunk_scores(conv * sigmoid(conv))
        b_rows, c_rows = b_two[:, :nstate], c_two[:, :nstate]
        before = state[...].astype(bf16)
        sin_ref[chunk, :, :] = before
        carried[...] = dot(c_rows, before)
        squares = jnp.zeros((CHUNK, LANES), f32)
        for pair in range(pairs):
            lanes = slice(pair * LANES, (pair + 1) * LANES)
            conv = vshift_ref[:, lanes].astype(f32)
            for tap in range(4):
                moved = vbuf[pl.ds(r0 + 5 + tap, CHUNK), lanes]
                conv = conv + vconv_ref[tap : tap + 1, lanes].astype(f32) * moved
            av_ref[here, lanes] = conv
            values = conv * sigmoid(conv)
            stepped = values * stepx[:, lanes]
            vtail[:, lanes] = (stepped * tailx[:, lanes]).astype(bf16)
            first, second = pair_decay(running, running_t, pair, mask)
            mixing = jnp.concatenate(
                [(scores * first).astype(bf16), (scores * second).astype(bf16)], axis=1
            )
            scanned = dot(mixing, stacked(stepped.astype(bf16), masks))
            scanned = scanned + grownx[:, lanes] * carried[:, lanes] + skip_ref[:, lanes] * values
            y_ref[here, lanes] = scanned
            g = gbuf[here, lanes]
            gated = scanned * (g * sigmoid(g))
            gg_ref[here, lanes] = (gated * ggain_ref[:, lanes].astype(f32)).astype(bf16)
            squares = squares + gated * gated
        sq_ref[:, here] = dot(jnp.ones((8, LANES), f32), squares, NT, HIGHEST)
        state[...] = grownx[CHUNK - 1 : CHUNK, :] * state[...] + dot(b_rows, vtail[...], TN)
    vbuf[0:8, :] = vbuf[BLOCK : BLOCK + 8, :]
    sbuf[0:8, :] = sbuf[BLOCK : BLOCK + 8, :]


def stats_kernel(half_blocks, at_ref, own_ref, other_ref, gg_ref, sq_ref, out_w, og_ref, stats_ref):
    mine = (pl.program_id(0) // half_blocks) == at_ref[0]
    cot = jnp.where(mine, own_ref[...], other_ref[...])
    og = dot(cot, out_w[...], NT)
    og_ref[...] = og
    prod = (og * gg_ref[...].astype(f32)).astype(bf16)
    dots = dot(jnp.ones((8, prod.shape[1]), bf16), prod, NT)
    row = lax.broadcasted_iota(jnp.int32, dots.shape, 0)
    stats_ref[...] = jnp.where(row == 0, sq_ref[...], dots)


def branch_kernel(half_blocks, at_ref, gg_ref, out_w, own_ref, other_ref):
    mine = (pl.program_id(0) // half_blocks) == at_ref[0]
    rows = dot(gg_ref[...], out_w[...]).astype(bf16)

    @pl.when(mine)
    def _():
        own_ref[...] = rows

    @pl.when(jnp.logical_not(mine))
    def _():
        other_ref[...] = rows


def picked(cut, early, late):
    return jnp.where(pl.program_id(0) < cut, early[...], late[...])


def normed_grad_kernel(half_blocks, cut, at_ref, dg_ref, *refs):
    lows, (gate_w, value_w, state_w, step_w, own_ref, other_ref) = refs[:6], refs[6:]
    dv, ds, dz = (picked(cut, a, b) for a, b in zip(lows[:3], lows[3:]))
    mine = (pl.program_id(0) // half_blocks) == at_ref[0]
    rows = (
        dot(dg_ref[...], gate_w[...], NT)
        + dot(dv, value_w[...], NT)
        + dot(ds, state_w[...], NT)
        + dot(dz, step_w[...], NT)
    ).astype(bf16)

    @pl.when(mine)
    def _():
        own_ref[...] = rows

    @pl.when(jnp.logical_not(mine))
    def _():
        other_ref[...] = rows


def row_sums(grads, weights):
    prod = (grads * weights.astype(f32)).astype(bf16)
    return dot(jnp.ones((8, prod.shape[1]), bf16), prod, NT)


def emit(at_ref, parts, outs):
    half = outs[0].shape[0]
    for j, out in enumerate(outs):
        rows = pl.ds(pl.multiple_of((at_ref[1] ^ j) * half, LANES), half)
        left = 0
        for part in parts:
            out[:, left : left + part.shape[1]] = part[rows, :].astype(out.dtype)
            left += part.shape[1]


def row_column(rows):
    return jnp.concatenate([rows, jnp.zeros((LANES - rows.shape[0], BLOCK), f32)], axis=0).T


def mixed_kernel(inner_all, at_ref, rows_ref, own_ref, other_ref, here_ref, there_ref, out_ref, token_ref):
    token_ref[...] = jnp.zeros_like(token_ref)
    sums = here_ref[...] + there_ref[...]
    scale = row_column(lax.rsqrt(sums / inner_all + EPSILON))[:, 0:1]
    branch = own_ref[...].astype(f32) + other_ref[...].astype(f32)
    out_ref[...] = rows_ref[...].astype(f32) + scale * branch


def input_kernel(at_ref, rows_ref, cot_ref, own_ref, other_ref, gain_ref, out_ref, token_ref):
    token_ref[...] = jnp.zeros_like(token_ref)
    rows = rows_ref[...].astype(f32)
    scale = lax.rsqrt(jnp.mean(rows * rows, axis=1, keepdims=True) + EPSILON)
    pulled = (own_ref[...].astype(f32) + other_ref[...].astype(f32)) * gain_ref[...].astype(f32)
    inner = jnp.mean(pulled * rows, axis=1, keepdims=True) * (scale * scale * scale)
    out_ref[...] = cot_ref[...].astype(f32) + scale * pulled - rows * inner


def gate_kernel(
    half_blocks,
    inner_all,
    fast,
    at_ref,
    own_ref,
    other_ref,
    here_ref,
    there_ref,
    normed_ref,
    og_ref,
    y_ref,
    g_ref,
    gg_ref,
    ggain_ref,
    gate_w,
    _,
    dg_ref,
    dy_ref,
    first_ref,
    second_ref,
    grad_gain_ref,
    norm_ref,
    *scratch,
):
    step_at = pl.program_id(0)
    pairs = og_ref.shape[1] // LANES
    grad_gate, grad_out = scratch if fast else (first_ref, second_ref)

    @pl.when(step_at == 0)
    def _():
        grad_out[...] = jnp.zeros_like(grad_out)
        grad_gate[...] = jnp.zeros_like(grad_gate)
        grad_gain_ref[...] = jnp.zeros_like(grad_gain_ref)

    sums = here_ref[...] + there_ref[...]
    scale_row = lax.rsqrt(sums[0:1, :] / inner_all + EPSILON)
    pull_row = scale_row * scale_row * scale_row * sums[1:2, :] / inner_all
    columns = row_column(jnp.concatenate([scale_row, pull_row], axis=0))
    scale, pull = columns[:, 0:1], columns[:, 1:2]
    mine = (step_at // half_blocks) == at_ref[0]
    cot = jnp.where(mine, own_ref[...], other_ref[...]).astype(f32)
    scaled = (cot * scale).astype(bf16)
    for pair in range(pairs):
        lanes = slice(pair * LANES, (pair + 1) * LANES)
        og = og_ref[:, lanes] * scale
        y = y_ref[:, lanes]
        g = g_ref[:, lanes]
        sig = sigmoid(g)
        silu = g * sig
        gated = y * silu
        grad_gain_ref[0:1, lanes] += jnp.sum(og * gated, axis=0, keepdims=True)
        gated_grad = ggain_ref[:, lanes].astype(f32) * og - gated * pull
        dy_ref[:, lanes] = (gated_grad * silu).astype(bf16)
        dg_ref[:, lanes] = (gated_grad * y * (sig + silu * (1.0 - sig))).astype(bf16)
    grad_out[...] += dot(gg_ref[...], scaled, TN)
    grad_gate[...] += dot(normed_ref[...], dg_ref[...], TN)

    @pl.when(step_at == pl.num_programs(0) - 1)
    def _():
        norm_ref[...] = row_sums(grad_gate[...], gate_w[...])
        if fast:
            emit(at_ref, (grad_gate, grad_out), (first_ref, second_ref))


def weights_kernel(fast, extra, cut, at_ref, normed_ref, *refs):
    step_at = pl.program_id(0)
    lows, refs = refs[:6], refs[6:]
    value_w, state_w, step_w, gain_ref, vec_ref, svec_ref, head_ref, ggain_ref, norm_ref = refs[:9]
    outs, acc = refs[9 + extra : -3], refs[-3:]

    @pl.when(step_at == 0)
    def _():
        for a in acc:
            a[...] = jnp.zeros_like(a)

    normed = normed_ref[...]
    for a, early, late in zip(acc, lows[:3], lows[3:]):
        a[...] += dot(normed, picked(cut, early, late), TN)

    @pl.when(step_at == pl.num_programs(0) - 1)
    def _():
        norm = norm_ref[...]
        for a, w in zip(acc, (value_w, state_w, step_w)):
            norm = norm + row_sums(a[...], w[...])
        norm = norm / gain_ref[...].astype(f32)
        if not fast:
            for o, a in zip(outs, acc):
                o[...] = a[...]
            outs[3][...] = norm
            return
        pack_vectors(acc[2], vec_ref, svec_ref, head_ref, ggain_ref, norm)
        emit(at_ref, acc, outs)


VEC_AT = 16
SVEC_AT = 24
HEAD_AT = 32
HALF = LANES // 2


def pack_vectors(block, vec_ref, svec_ref, head_ref, ggain_ref, norm):
    model = block.shape[0]
    row = lax.broadcasted_iota(jnp.int32, (8, model), 0)
    vec = jnp.where(row == 5, ggain_ref[0:1, :], jnp.where(row == 6, norm[0:1, :], vec_ref[...]))

    def tall(v):
        return jnp.concatenate([v, jnp.zeros((8, model - v.shape[1]), f32)], axis=1)

    rows = jnp.concatenate(
        [
            jnp.zeros((VEC_AT, model), f32),
            vec,
            tall(svec_ref[...]),
            tall(head_ref[...]),
            jnp.zeros((LANES - HEAD_AT - 8, model), f32),
        ],
        axis=0,
    )
    lane = lax.broadcasted_iota(jnp.int32, (1, LANES), 1)
    full = jnp.where(lane < VEC_AT, block[...], rows.T)
    block[...] = carry_rest(jnp.where(lane < HALF, full, 0.0))


def carry_rest(full):
    high = full.astype(bf16).astype(f32)
    return high + pltpu.roll(full - high, HALF, 1)


def join_rest(block):
    lane = lax.broadcasted_iota(jnp.int32, (1, LANES), 1)
    return jnp.where(lane < HALF, block + pltpu.roll(block, HALF, 1), 0.0)


def fold_step(me, ins, outs, buf, vectors):
    width = buf.shape[1] - (LANES if vectors else 0)
    total = ins[0][:, :width].astype(f32)
    for r in ins[1:]:
        total = total + r[:, :width].astype(f32)
    buf[:, :width] = total.astype(bf16)
    if vectors:
        last = ins[0][:, width:].astype(f32)
        for r in ins[1:]:
            last = last + r[:, width:].astype(f32)
        buf[:, width:] = carry_rest(join_rest(last)).astype(bf16)
    rows = outs[0].shape[0]
    if len(outs) == 1:
        outs[0][...] = buf[...]
        return
    for j, o in enumerate(outs):
        o[...] = buf[pl.ds(pl.multiple_of((me ^ j) * rows, 16), rows), :]


def join_step(me, ins, out):
    rows = ins[0].shape[0]
    for j, r in enumerate(ins):
        out[pl.ds(pl.multiple_of((me ^ j) * rows, 16), rows), :] = r[...]


def stage_kernel(plan, extra, at_ref, *refs):
    n_in = sum(count for _, _, count, _, _ in plan)
    ins, refs = refs[:n_in], refs[n_in + extra :]
    n_out = sum(count for _, _, _, count, _ in plan)
    outs, bufs = refs[:n_out], list(refs[n_out:])
    for kind, axis, take, give, vectors in plan:
        if kind == "fold":
            fold_step(at_ref[axis], ins[:take], outs[:give], bufs.pop(0), vectors)
        else:
            join_step(at_ref[axis], ins[:take], outs[0])
        ins, outs = ins[take:], outs[give:]


def stage(at, steps, after=()):
    plan, arrays, shapes, scratch = [], [], [], []
    for kind, axis, ins, *rest in steps:
        rows, width = ins[0].shape
        count, vectors = rest if rest else (1, False)
        if kind == "fold":
            shapes += [(rows // count, width)] * count
            scratch.append(pltpu.VMEM((rows, width), bf16))
        else:
            shapes.append((rows * len(ins), width))
        plan.append((kind, axis, len(ins), count, vectors))
        arrays += ins
    out = call(
        functools.partial(stage_kernel, tuple(plan), len(after)),
        1,
        at,
        [(a, None) for a in arrays] + [(a, pl.BlockSpec(memory_space=pl.ANY)) for a in after],
        [(shape, bf16, pl.BlockSpec(shape, lambda i, a: (0, 0))) for shape in shapes],
        scratch,
        24,
    )
    out, results = list(out), []
    for _, _, _, give, _ in plan:
        results.append(out[:give])
        out = out[give:]
    return results


def heads_kernel(at_ref, own_ref, other_ref, out_ref):
    split_at = out_ref.shape[1] - other_ref.shape[1]
    state = other_ref.shape[1] - LANES
    out_ref[:, :split_at] = own_ref[:, :split_at]
    out_ref[:, split_at : split_at + state] = (
        own_ref[:, split_at : split_at + state].astype(f32) + other_ref[:, :state].astype(f32)
    ).astype(bf16)
    lane = lax.broadcasted_iota(jnp.int32, (1, LANES), 1)
    shared = (lane == VEC_AT + 6) | ((lane >= SVEC_AT) & (lane < HEAD_AT))
    mine = join_rest(own_ref[:, split_at + state :].astype(f32))
    theirs = join_rest(other_ref[:, state:].astype(f32))
    out_ref[:, split_at + state :] = carry_rest(
        mine + jnp.where(shared, theirs, 0.0)
    ).astype(bf16)


def halves_of(at_ref, own_ref, other_ref, left, right):
    rows = own_ref.shape[0]
    for j, ref in enumerate((own_ref, other_ref)):
        yield pl.ds(pl.multiple_of((at_ref[1] ^ j) * rows, LANES), rows), ref[:, left:right].astype(f32)


def early_kernel(at_ref, own_ref, other_ref, *outs):
    outs[-1][...] = jnp.zeros_like(outs[-1])
    left = 0
    for o in outs[:-1]:
        right = left + o.shape[1]
        for at, v in halves_of(at_ref, own_ref, other_ref, left, right):
            o[at, :] = v
        left = right


def late_kernel(at_ref, own_ref, other_ref, *refs):
    outs, block = refs[:-1], refs[-1]
    left = 0
    for o in (outs[0], outs[1], block):
        right = left + o.shape[1]
        for at, v in halves_of(at_ref, own_ref, other_ref, left, right):
            o[at, :] = v
        left = right
    full = join_rest(block[...])
    heads = outs[2].shape[1]
    outs[2][...] = full[:, :heads]
    rows = full.T
    vec, svec = rows[VEC_AT : VEC_AT + 8], rows[SVEC_AT : SVEC_AT + 8]
    head = rows[HEAD_AT : HEAD_AT + 8]
    vconv, vshift, ggain, norm, sconv, sshift, bias, rate, skip = outs[3:]
    vconv[...] = vec[:4]
    for o, row in ((vshift, vec[4:5]), (ggain, vec[5:6]), (norm, vec[6:7]), (sshift, svec[4:5])):
        o[...] = row[:, : o.shape[0]].reshape(o.shape)
    sconv[...] = svec[:4, : sconv.shape[1]]
    for j, o in enumerate((bias, rate, skip)):
        o[...] = head[j : j + 1, : o.shape[0]].reshape(o.shape)


def backward_kernel(
    carried_in,
    extra,
    at_ref,
    dy_ref,
    av_ref,
    vp_ref,
    as_ref,
    sp_ref,
    z_ref,
    sin_ref,
    vconv_ref,
    sconv_ref,
    rate_ref,
    skip_ref,
    spread_ref,
    gather_ref,
    *refs,
):
    carries, refs = (refs[:6], refs[6:]) if carried_in else ((), refs)
    refs = refs[extra:]
    dvalue, dstates, dstep, dstate_out, dahalo, dshalo, grad_vconv_ref, grad_sconv_ref, grad_head_ref = refs[:9]
    dabuf, dsbuf, dstate, stepx, grownx, tailx, carried, pulled, ubuf, vtail = refs[9:]
    step_at = pl.program_id(0)
    width = dabuf.shape[1]
    pairs = width // LANES
    nstate = dstate.shape[0]

    @pl.when(step_at == 0)
    def _():
        if carried_in:
            dstate[...] = carries[0][...]
            dabuf[BLOCK:, :] = carries[1][...]
            dsbuf[BLOCK:, :] = carries[2][...]
            grad_vconv_ref[...] = carries[3][...]
            grad_sconv_ref[...] = carries[4][...]
            grad_head_ref[...] = carries[5][...]
        else:
            dstate[...] = jnp.zeros_like(dstate)
            dabuf[BLOCK:, :] = jnp.zeros((8, width), f32)
            dsbuf[BLOCK:, :] = jnp.zeros((8, dsbuf.shape[1]), f32)
            for ref in (grad_vconv_ref, grad_sconv_ref, grad_head_ref):
                ref[...] = jnp.zeros_like(ref)

    @pl.when(step_at > 0)
    def _():
        dabuf[BLOCK:, :] = dabuf[0:8, :]
        dsbuf[BLOCK:, :] = dsbuf[0:8, :]

    mask = lower_mask(CHUNK)
    masks = half_masks()
    for chunk in reversed(range(BLOCK // CHUNK)):
        r0 = chunk * CHUNK
        here = pl.ds(r0, CHUNK)
        z = z_ref[here, :]
        step, rate, running, grown, tail = chunk_scalars(z, rate_ref[...])
        running_t = running.T
        stepx[...] = dot(split(step), spread_ref[...])
        grownx[...] = dot(split(grown), spread_ref[...])
        tailx[...] = dot(split(tail), spread_ref[...])
        conv_s = as_ref[here, :]
        sig_s = sigmoid(conv_s)
        b_two, c_two, scores = chunk_scores(conv_s * sig_s)
        b_rows, c_rows = b_two[:, :nstate], c_two[:, :nstate]
        before = sin_ref[chunk, :, :]
        after = dstate[...].astype(bf16)
        carried[...] = dot(c_rows, before)
        pulled[...] = dot(b_rows, after)
        dscores = jnp.zeros((CHUNK, CHUNK), f32)
        inner = jnp.zeros((CHUNK, LANES), f32)
        outer = jnp.zeros((CHUNK, LANES), f32)
        sides = jnp.zeros((CHUNK, LANES), f32)
        for pair in range(pairs):
            lanes = slice(pair * LANES, (pair + 1) * LANES)
            conv = av_ref[here, lanes]
            sig = sigmoid(conv)
            values = conv * sig
            steps = stepx[:, lanes]
            stepped = values * steps
            low = stepped.astype(bf16)
            dy_low = dy_ref[here, lanes]
            dy = dy_low.astype(f32)
            first, second = pair_decay(running, running_t, pair, mask)
            mixing = jnp.concatenate(
                [(scores * first).astype(bf16), (scores * second).astype(bf16)], axis=1
            )
            dy_two = stacked(dy_low, masks)
            scanned = dot(mixing, stacked(low, masks))
            both = jnp.concatenate([mixing[:, :CHUNK], mixing[:, CHUNK:]], axis=0)
            dstepped = dot(both, dy_two, TN)
            dmixing = dot(dy_two, low, NT)
            dscores = dscores + dmixing[:CHUNK] * first + dmixing[CHUNK:] * second
            inside = dy * scanned - low.astype(f32) * dstepped
            u = (dy * grownx[:, lanes]).astype(bf16)
            ubuf[:, lanes] = u
            tails = tailx[:, lanes]
            v = (stepped * tails).astype(bf16)
            vtail[:, lanes] = v
            pull = pulled[:, lanes]
            dstepped = dstepped + tails * pull
            sums = gather_ref[pair * 2 * LANES : (pair + 1) * 2 * LANES, :]
            inner = inner + dot(split(inside), sums[:, :LANES])
            outer = outer + dot(
                jnp.concatenate(
                    [
                        (u.astype(f32) * carried[:, lanes]).astype(bf16),
                        (v.astype(f32) * pull).astype(bf16),
                    ],
                    axis=1,
                ),
                sums[:, LANES:],
            )
            sides = sides + dot(
                jnp.concatenate(
                    [(values * dstepped).astype(bf16), (values * dy).astype(bf16)], axis=1
                ),
                sums[:, LANES:],
            )
            dvalues = steps * dstepped + skip_ref[:, lanes] * dy
            da = dvalues * (sig + values * (1.0 - sig))
            dabuf[here, lanes] = da
            vp = vp_ref[here, lanes]
            dv = jnp.zeros((CHUNK, LANES), f32)
            rows = []
            for tap in range(4):
                moved = da if tap == 3 else dabuf[pl.ds(r0 + 3 - tap, CHUNK), lanes]
                dv = dv + vconv_ref[tap : tap + 1, lanes].astype(f32) * moved
                rows.append(jnp.sum(vp * moved, axis=0, keepdims=True))
            rows.append(jnp.sum(da, axis=0, keepdims=True))
            rows.append(jnp.zeros((3, LANES), f32))
            grad_vconv_ref[:, lanes] += jnp.concatenate(rows, axis=0)
            dvalue[here, lanes] = dv.astype(bf16)
        dlow = dscores.astype(bf16)
        drest = (dscores - dlow.astype(f32)).astype(bf16)
        db = (
            dot(jnp.concatenate([dlow, dlow, drest], axis=0), jnp.concatenate([c_rows, c_two[:, nstate:], c_rows], axis=0), TN)
            + dot(vtail[...], after, NT)
        )
        dc = (
            dot(jnp.concatenate([dlow, dlow, drest], axis=1), jnp.concatenate([b_rows, b_two[:, nstate:], b_rows], axis=0))
            + dot(ubuf[...], before, NT)
        )
        ds = jnp.concatenate([db, dc], axis=1) * (sig_s + conv_s * sig_s * (1.0 - sig_s))
        dsbuf[here, :] = ds
        sp = sp_ref[here, :]
        dpre = jnp.zeros(ds.shape, f32)
        rows = []
        for tap in range(4):
            moved = ds if tap == 3 else dsbuf[pl.ds(r0 + 3 - tap, CHUNK), :]
            dpre = dpre + sconv_ref[tap : tap + 1, :].astype(f32) * moved
            rows.append(jnp.sum(sp * moved, axis=0, keepdims=True))
        rows.append(jnp.sum(ds, axis=0, keepdims=True))
        rows.append(jnp.zeros((3, ds.shape[1]), f32))
        grad_sconv_ref[...] += jnp.concatenate(rows, axis=0)
        dstates[here, :] = dpre.astype(bf16)

        overlap = jnp.sum(before.astype(f32) * dstate[...], axis=0, keepdims=True)
        overlap = jnp.broadcast_to(overlap * grownx[CHUNK - 1 : CHUNK, :], (8, width))
        held = jnp.zeros((8, LANES), f32)
        for pair in range(pairs):
            lanes = slice(pair * LANES, (pair + 1) * LANES)
            sums = gather_ref[pair * 2 * LANES : (pair + 1) * 2 * LANES, :]
            held = held + dot(split(overlap[:, lanes]), sums[:, :LANES])
        spare = jnp.zeros((CHUNK, HALF), f32)
        lower = mask.astype(f32)
        ddecay = (
            dot(lower, inner + jnp.concatenate([outer[:, :HALF], spare], axis=1), TN, HIGHEST)
            + dot(1.0 - lower.T, jnp.concatenate([outer[:, HALF:], spare], axis=1), precision=HIGHEST)
            + held[0:1, :]
        )
        dstep_all = jnp.concatenate([sides[:, :HALF], spare], axis=1) + ddecay * rate
        dz = dstep_all * sigmoid(z)
        dstep[here, :] = dz.astype(bf16)
        skips = jnp.concatenate([sides[:, HALF:], spare], axis=1)
        grad_head_ref[...] += jnp.concatenate(
            [
                jnp.sum(dz, axis=0, keepdims=True),
                jnp.sum(ddecay * step, axis=0, keepdims=True) * rate,
                jnp.sum(skips, axis=0, keepdims=True),
                jnp.zeros((5, LANES), f32),
            ],
            axis=0,
        )
        dstate[...] = grownx[CHUNK - 1 : CHUNK, :] * dstate[...] + dot(c_rows, ubuf[...], TN)

    @pl.when(step_at == pl.num_programs(0) - 1)
    def _():
        dstate_out[...] = dstate[...]
        dahalo[...] = dabuf[0:8, :]
        dshalo[...] = dsbuf[0:8, :]


COST = dict(forward_kernel=4.5, backward_kernel=7, stats_kernel=1, branch_kernel=.6, gate_kernel=2.4, weights_kernel=1.2, normed_grad_kernel=1.2, mixed_kernel=1, input_kernel=1, early_kernel=3, late_kernel=3)


def whole(array):
    return pl.BlockSpec(array.shape, lambda i, at: (0,) * array.ndim)


def call(kernel, blocks, at, ins, outs, scratch, mib=40):
    return pl.pallas_call(
        kernel,
        name=getattr(kernel, "func", kernel).__name__,
        grid_spec=pltpu.PrefetchScalarGridSpec(
            num_scalar_prefetch=1,
            grid=(blocks,),
            in_specs=[whole(a) if s is None else s for a, s in ins],
            out_specs=[s for _, _, s in outs],
            scratch_shapes=scratch,
        ),
        out_shape=[jax.ShapeDtypeStruct(shape, dtype) for shape, dtype, _ in outs],
        cost_estimate=pl.CostEstimate(flops=int(COST.get(getattr(kernel, "func", kernel).__name__, 1)*blocks * 10**9), bytes_accessed=0, transcendentals=0),
        compiler_params=pltpu.CompilerParams(
            dimension_semantics=("arbitrary",), vmem_limit_bytes=mib * 2**20
        ),
    )(at, *[a for a, _ in ins])


def per_device(
    residual_in,
    norm_gain,
    gate_proj,
    value_proj,
    state_proj,
    step_proj,
    value_conv,
    value_shift,
    state_conv,
    state_shift,
    step_bias,
    log_rate,
    skip_gain,
    gated_gain,
    out_proj,
    grad_out,
):
    parts = lax.axis_size("heads")
    two = parts == 2
    rows_here, model = residual_in.shape[1:]
    length = rows_here * parts
    inner = value_conv.shape[1]
    inner_all = inner * parts
    heads = step_bias.shape[0]
    head_width = inner // heads
    pad_heads = heads % 2
    nheads = heads + pad_heads
    width = nheads * head_width
    nstate2 = state_conv.shape[1]
    blocks = length // BLOCK
    chunks = BLOCK // CHUNK
    half_blocks = rows_here // BLOCK if two else blocks

    def wide(a, axis):
        pads = [(0, 0)] * a.ndim
        pads[axis] = (0, width - inner)
        return jnp.pad(a, pads) if width > inner else a

    def lanes_of(a):
        return jnp.pad(a, [(0, 0)] * (a.ndim - 1) + [(0, LANES - a.shape[-1])])

    residual = residual_in[0]
    cot = grad_out[0]
    batch = lax.axis_size("batch")
    fast = two and batch == 16 and width == model and model % BLOCK == 0
    nstate = nstate2 // 2
    place = lax.axis_index("batch").astype(jnp.int32)
    across = lax.axis_index("heads").astype(jnp.int32) if two else jnp.int32(0)
    own_from = lax.axis_index("heads").astype(jnp.int32) * rows_here
    at = jnp.stack([across, place & 1, (place >> 1) & 1, place >> 2, own_from])
    if two:
        swap = [(0, 1), (1, 0)]
        pair_of = lambda a: (a, lax.ppermute(a, "heads", swap))
        add_other = lambda a: lax.ppermute(a, "heads", swap)
    else:

        def pair_of(a):
            full = lax.all_gather(a, "heads", axis=0, tiled=True)
            return (full, full)

        add_other = lambda a: lax.psum(a, "heads") - a

    def hop(a, way):
        mask = {"core": 1, "line": 2}.get(way) or 4 * way
        return lax.ppermute(a, "batch", [(i, i ^ mask) for i in range(batch)])

    own_rows, other_rows = pair_of(residual)
    own_cot, other_cot = pair_of(cot)

    gate_w, value_w = wide(gate_proj, 1), wide(value_proj, 1)
    out_w = wide(out_proj, 0)
    step_w = lanes_of(step_proj)
    gain_in = norm_gain[None, :]
    vconv, vshift = wide(value_conv, 1), wide(value_shift[None, :], 1)
    sshift = state_shift[None, :]
    sbias, rate = lanes_of(step_bias[None, :]), lanes_of(log_rate[None, :])
    skipx = wide(jnp.repeat(skip_gain, head_width)[None, :], 1)
    ggain = wide(gated_gain[None, :], 1)
    head_of = jnp.arange(width) // head_width
    spread = (jnp.arange(LANES)[:, None] == head_of[None, :]).astype(bf16)
    spread = jnp.concatenate([spread, spread], axis=0)
    first = head_of.reshape(-1, 1, LANES, 1)
    column = jnp.arange(2 * LANES)
    top = (column == first) | (column == first + LANES)
    bottom = (column == first) | (column == first + LANES + HALF)
    gather = jnp.concatenate([top, bottom], axis=1).reshape(-1, 2 * LANES).astype(bf16)

    def own_block(i, a):
        return (jnp.clip(i - a[0] * half_blocks, 0, half_blocks - 1), 0)

    def other_block(i, a):
        return (jnp.clip(i - (1 - a[0]) * half_blocks, 0, half_blocks - 1), 0) if two else (0, 0)

    other_read = other_block if two else own_block

    def rows(n, index=lambda i, a: (i, 0)):
        return pl.BlockSpec((BLOCK, n), index)

    along = pl.BlockSpec((8, BLOCK), lambda i, a: (0, i))
    fixed = lambda *shape: pl.BlockSpec(shape, lambda i, a: (0,) * len(shape))
    states_spec = lambda index: pl.BlockSpec((chunks, nstate, width), index)
    big = lambda *shape: pltpu.VMEM(shape, f32)
    low = lambda *shape: pltpu.VMEM(shape, bf16)
    halves = [
        ((rows_here if two else length, model), bf16, rows(model, own_block)),
        ((rows_here if two else BLOCK, model), bf16, rows(model, other_block)),
    ]

    normed, g, y, gg, av, vp, conv_s, sp, z, sin, sq = call(
        functools.partial(forward_kernel, half_blocks),
        blocks,
        at,
        [
            (own_rows, rows(model, own_block)),
            (other_rows, rows(model, other_read)),
            (gain_in, None),
            (gate_w, None),
            (value_w, None),
            (state_proj, None),
            (step_w, None),
            (vconv, None),
            (vshift, None),
            (state_conv, None),
            (sshift, None),
            (sbias, None),
            (rate, None),
            (skipx, None),
            (ggain, None),
            (spread, None),
        ],
        [
            ((length, model), bf16, rows(model)),
            ((length, width), f32, rows(width)),
            ((length, width), f32, rows(width)),
            ((length, width), bf16, rows(width)),
            ((length, width), f32, rows(width)),
            ((length, width), f32, rows(width)),
            ((length, nstate2), f32, rows(nstate2)),
            ((length, nstate2), f32, rows(nstate2)),
            ((length, LANES), f32, rows(LANES)),
            ((blocks * chunks, nstate, width), bf16, states_spec(lambda i, a: (i, 0, 0))),
            ((8, length), f32, along),
        ],
        [
            big(BLOCK, width),
            big(BLOCK + 8, width),
            big(BLOCK + 8, nstate2),
            big(nstate, width),
            big(CHUNK, width),
            big(CHUNK, width),
            big(CHUNK, width),
            big(CHUNK, width),
            low(CHUNK, width),
        ],
    )
    og, stats = call(
        functools.partial(stats_kernel, half_blocks),
        blocks,
        at,
        [
            (own_cot, rows(model, own_block)),
            (other_cot, rows(model, other_read)),
            (gg, rows(width)),
            (sq, along),
            (out_w, None),
        ],
        [((length, width), f32, rows(width)), ((8, length), f32, along)],
        [],
    )
    other_stats = add_other(stats)
    own_along = pl.BlockSpec((8, BLOCK), lambda i, a: (0, i + a[4] // BLOCK))
    branch, branch_sent = call(
        functools.partial(branch_kernel, half_blocks),
        blocks,
        at,
        [(gg, rows(width)), (out_w, None)],
        halves,
        [],
    )

    def other_half(own, sent):
        if two:
            return lax.ppermute(sent, "heads", swap)
        total = lax.psum_scatter(own.astype(f32), "heads", scatter_dimension=0, tiled=True)
        mine = lax.dynamic_slice_in_dim(own, own_from, rows_here, 0).astype(f32)
        return total - mine

    branch_got = other_half(branch, branch_sent)
    if not two:
        branch = lax.dynamic_slice_in_dim(branch, own_from, rows_here, 0)
    if fast:
        pieces = [((model // 2, 2 * model), bf16, fixed(model // 2, 2 * model))] * 2
    else:
        pieces = [
            ((model, width), f32, fixed(model, width)),
            ((width, model), f32, fixed(width, model)),
        ]
    dg, dy, early_a, early_b, grad_gain, norm = call(
        functools.partial(gate_kernel, half_blocks, inner_all, fast),
        blocks,
        at,
        [
            (own_cot, rows(model, own_block)),
            (other_cot, rows(model, other_read)),
            (stats, along),
            (other_stats, along),
            (normed, rows(model)),
            (og, rows(width)),
            (y, rows(width)),
            (g, rows(width)),
            (gg, rows(width)),
            (ggain, None),
            (gate_w, None),
            (branch, pl.BlockSpec(memory_space=pl.ANY)),
        ],
        [
            ((length, width), bf16, rows(width)),
            ((length, width), bf16, rows(width)),
            *pieces,
            ((8, width), f32, fixed(8, width)),
            ((8, model), f32, fixed(8, model)),
        ],
        [big(model, width), big(width, model)] if fast else [],
    )

    def backward(start, count, carry, after=()):
        def behind(n):
            return rows(n, lambda i, a: (start + count - 1 - i, 0))

        def local(n):
            return rows(n, lambda i, a: (count - 1 - i, 0))

        states = states_spec(lambda i, a: (start + count - 1 - i, 0, 0))
        vectors = [(nstate, width), (8, width), (8, nstate2), (8, width), (8, nstate2), (8, LANES)]
        out = call(
            functools.partial(backward_kernel, bool(carry), len(after)),
            count,
            at,
            [
                (dy, behind(width)),
                (av, behind(width)),
                (vp, behind(width)),
                (conv_s, behind(nstate2)),
                (sp, behind(nstate2)),
                (z, behind(LANES)),
                (sin, states),
                (vconv, None),
                (state_conv, None),
                (rate, None),
                (skipx, None),
                (spread, None),
                (gather, None),
                *[(c, None) for c in carry],
                *[(a, pl.BlockSpec(memory_space=pl.ANY)) for a in after],
            ],
            [
                ((count * BLOCK, width), bf16, local(width)),
                ((count * BLOCK, nstate2), bf16, local(nstate2)),
                ((count * BLOCK, LANES), bf16, local(LANES)),
                *[(shape, f32, fixed(*shape)) for shape in vectors],
            ],
            [
                big(BLOCK + 8, width),
                big(BLOCK + 8, nstate2),
                big(nstate, width),
                big(CHUNK, width),
                big(CHUNK, width),
                big(CHUNK, width),
                big(CHUNK, width),
                big(CHUNK, width),
                low(CHUNK, width),
                low(CHUNK, width),
            ],
        )
        return out[:3], out[3:]

    cut = blocks // 2
    behind = ()
    if fast:
        ((kept, sent),) = stage(at, [("fold", 2, [early_a, hop(early_b, "core")], 2, False)])
        early = [kept, hop(sent, "line")]
        behind = (kept,)
    low_b, carry = backward(cut, blocks - cut, (), behind)
    if fast:
        ((kept, *sent),) = stage(at, [("fold", 3, early, 4, False)])
        early = [kept] + [hop(a, k + 1) for k, a in enumerate(sent)]
        behind = (kept, branch_got)
    low_a, carry = backward(0, cut, carry, behind)
    vec, svec, head = carry[3:]
    lows = [(a, rows(a.shape[1], lambda i, at: (jnp.minimum(i, cut - 1), 0))) for a in low_a]
    lows += [(a, rows(a.shape[1], lambda i, at: (jnp.maximum(i - cut, 0), 0))) for a in low_b]
    behind = early[1:] if fast else ()

    if fast:
        shape = (model // 2, width + nstate2 + LANES)
        pieces = [(shape, bf16, fixed(*shape))] * 2
    else:
        shapes = [(model, width), (model, nstate2), (model, LANES), (8, model)]
        pieces = [(shape, f32, fixed(*shape)) for shape in shapes]
    late = call(
        functools.partial(weights_kernel, fast, len(behind), cut),
        blocks,
        at,
        [
            (normed, rows(model)),
            *lows,
            (value_w, None),
            (state_proj, None),
            (step_w, None),
            (gain_in, None),
            (vec, None),
            (svec, None),
            (head, None),
            (grad_gain, None),
            (norm, None),
            *[(a, pl.BlockSpec(memory_space=pl.ANY)) for a in behind],
        ],
        pieces,
        [big(model, width), big(model, nstate2), big(model, LANES)],
    )
    ng, ng_sent = call(
        functools.partial(normed_grad_kernel, half_blocks, cut),
        blocks,
        at,
        [
            (dg, rows(width)),
            *lows,
            (gate_w, None),
            (value_w, None),
            (state_proj, None),
            (step_w, None),
        ],
        halves,
        [],
    )

    mixed, token = call(
        functools.partial(mixed_kernel, inner_all),
        rows_here // BLOCK,
        at,
        [
            (residual, rows(model)),
            (branch, rows(model)),
            (branch_got, rows(model)),
            (stats, own_along),
            (other_stats, own_along),
        ],
        [((rows_here, model), f32, rows(model)), ((8, LANES), f32, fixed(8, LANES))],
        [],
    )
    ng_got = other_half(ng, ng_sent)
    if not two:
        ng = lax.dynamic_slice_in_dim(ng, own_from, rows_here, 0)
    grad_input, token_b = call(
        input_kernel,
        rows_here // BLOCK,
        at,
        [
            (residual, rows(model)),
            (cot, rows(model)),
            (ng, rows(model)),
            (ng_got, rows(model)),
            (gain_in, None),
        ],
        [((rows_here, model), f32, rows(model)), ((8, LANES), f32, fixed(8, LANES))],
        [],
    )

    if fast:
        kept, sent = late
        steps = [("fold", 2, [kept, hop(sent, "core")], 2, True), ("fold", 3, early, 1, False)]
        (kept, sent), (early,) = stage(at, steps)
        got = hop(sent, "line")
        early = [early] + [hop(early, k) for k in (1, 2, 3)]
        steps = [("fold", 3, [kept, got], 4, True), ("join", 3, early)]
        (kept, *sent), (early,) = stage(at, steps, (ng, token))
        got = [hop(a, k + 1) for k, a in enumerate(sent)]
        early = [early, hop(early, "line")]
        steps = [("fold", 3, [kept, *got], 1, True), ("join", 2, early)]
        (done,), (early,) = stage(at, steps, (ng_got,))
        theirs = lax.ppermute(done[:, width:], "heads", swap)
        done = call(
            heads_kernel,
            1,
            at,
            [(done, None), (theirs, None)],
            [(done.shape, bf16, fixed(*done.shape))],
            [],
            16,
        )[0]
        grad_gate, grad_out_proj, token_c = call(
            early_kernel,
            1,
            at,
            [(early, None), (hop(early, "core"), None)],
            [((model, model), f32, fixed(model, model))] * 2
            + [((8, LANES), f32, fixed(8, LANES))],
            [],
        )
        ((done,),) = stage(at, [("join", 3, [done] + [hop(done, k) for k in (1, 2, 3)])])
        steps = [("join", 2, [done, hop(done, "line")])]
        ((done,),) = stage(at, steps, (token_b, token_c))
        shapes = [
            (model, width),
            (model, nstate2),
            (model, heads),
            (4, width),
            (width,),
            (width,),
            (model,),
            (4, nstate2),
            (nstate2,),
            (heads,),
            (heads,),
            (heads,),
        ]
        (
            grad_value,
            grad_state,
            grad_step,
            grad_vconv,
            grad_vshift,
            grad_ggain,
            grad_norm,
            grad_sconv,
            grad_sshift,
            grad_bias,
            grad_rate,
            grad_skip,
        ) = call(
            late_kernel,
            1,
            at,
            [(done, None), (hop(done, "core"), None)],
            [(shape, f32, fixed(*shape)) for shape in shapes],
            [big(model, LANES)],
        )
        return (
            mixed[None],
            grad_input[None],
            grad_norm,
            grad_gate,
            grad_value,
            grad_state,
            grad_step,
            grad_vconv,
            grad_vshift,
            grad_sconv,
            grad_sshift,
            grad_bias,
            grad_rate,
            grad_skip,
            grad_ggain,
            grad_out_proj,
        )
    grad_value, grad_state, grad_step, norm = late
    grad_gate, grad_value, grad_out_proj, grad_step, vec, head, grad_gain = lax.psum(
        (early_a, grad_value, early_b, grad_step, vec, head, grad_gain), "batch"
    )
    grad_state, svec, norm = lax.psum((grad_state, svec, norm), ("batch", "heads"))
    norm, ggrad = norm[0], grad_gain[0]
    return (
        mixed[None],
        grad_input[None],
        norm,
        grad_gate[:, :inner],
        grad_value[:, :inner],
        grad_state,
        grad_step[:, :heads],
        vec[:4, :inner],
        vec[4, :inner],
        svec[:4],
        svec[4],
        head[0, :heads],
        head[1, :heads],
        head[2, :heads],
        ggrad[:inner],
        grad_out_proj[:inner],
    )


def solution(mesh):
    return jax.shard_map(
        per_device,
        mesh=mesh,
        in_specs=(
            P("batch", "heads", None),
            P(),
            P(None, "heads"),
            P(None, "heads"),
            P(),
            P(None, "heads"),
            P(None, "heads"),
            P("heads"),
            P(),
            P(),
            P("heads"),
            P("heads"),
            P("heads"),
            P("heads"),
            P("heads", None),
            P("batch", "heads", None),
        ),
        out_specs=(
            P("batch", "heads", None),
            P("batch", "heads", None),
            P(),
            P(None, "heads"),
            P(None, "heads"),
            P(),
            P(None, "heads"),
            P(None, "heads"),
            P("heads"),
            P(),
            P(),
            P("heads"),
            P("heads"),
            P("heads"),
            P("heads"),
            P("heads", None),
        ),
        check_vma=False,
    )
```

```python
import functools

import jax
import jax.numpy as jnp
from jax import lax
from jax.experimental import pallas as pl
from jax.experimental.pallas import tpu as pltpu
from jax.sharding import PartitionSpec as P

EPSILON = 1e-05
HIGHEST = lax.Precision.HIGHEST
BLOCK = 256
CHUNK = 128
LANES = 128
HALF = LANES // 2
QUAD = 2 * LANES
LOG2E = 1.4426950408889634
f32 = jnp.float32
bf16 = jnp.bfloat16


def dot(left, right, over=((1,), (0,)), precision=None):
    return lax.dot_general(
        left, right, (over, ((), ())), preferred_element_type=f32, precision=precision
    )


TN = ((0,), (0,))
NT = ((1,), (1,))


def sigmoid(v):
    return 0.5 * jnp.tanh(0.5 * v) + 0.5


def silu(v):
    half = 0.5 * v
    return half + half * jnp.tanh(half)


def silu_slope(v):
    half = 0.5 * v
    t = jnp.tanh(half)
    out = half + half * t
    sig = 0.5 + 0.5 * t
    return out, sig + out * (1.0 - sig)


def causal_back(buf, slab, r0, grad, pre, taps, extra):
    buf[slab, pl.ds(r0, CHUNK), :] = grad
    lanes = slice(slab * LANES, (slab + 1) * LANES)
    out, rows = 0.0, []
    for tap in range(4):
        moved = grad if tap == 3 else buf[slab, pl.ds(r0 + 3 - tap, CHUNK), :]
        out = out + taps[tap : tap + 1, lanes].astype(f32) * moved
        rows.append(jnp.sum(pre * moved, axis=0, keepdims=True))
    rows.append(jnp.sum(grad, axis=0, keepdims=True))
    rows += [extra, jnp.zeros((2, LANES), f32)]
    return out, jnp.concatenate(rows, axis=0)


def split(v):
    high = v.astype(bf16)
    return jnp.concatenate([high, (v - high.astype(f32)).astype(bf16)], axis=1)


def lower_mask(rows):
    return lax.broadcasted_iota(jnp.int32, (rows, rows), 0) >= lax.broadcasted_iota(
        jnp.int32, (rows, rows), 1
    )


def chunk_mask(strict=False):
    row = lax.broadcasted_iota(jnp.int32, (BLOCK, BLOCK), 0)
    column = lax.broadcasted_iota(jnp.int32, (BLOCK, BLOCK), 1)
    ordered = row > column if strict else row >= column
    return (ordered & (row // CHUNK == column // CHUNK)).astype(bf16)


def block_scalars(z, log_rate, spread):
    step = jnp.maximum(z, 0.0) + jnp.log1p(jnp.exp(-jnp.abs(z)))
    rate = -jnp.exp(log_rate)
    decay = jnp.where(lax.broadcasted_iota(jnp.int32, (1, LANES), 1) < 32, step * (rate * LOG2E), 0.0)
    high = decay.astype(bf16).astype(f32)
    middle = (decay - high).astype(bf16).astype(f32)
    packed = high + pltpu.roll(middle, 32, 1) + pltpu.roll(decay - high - middle, 64, 1)
    sums = dot(chunk_mask(), packed.astype(bf16))
    running = sums + pltpu.roll(sums, LANES - 32, 1) + pltpu.roll(sums, LANES - 64, 1)
    last = [running[r + CHUNK - 1 : r + CHUNK, :] for r in range(0, BLOCK, CHUNK)]
    tail = [jnp.exp2(v - running[k * CHUNK : (k + 1) * CHUNK, :]) for k, v in enumerate(last)]
    tail = step * jnp.concatenate(tail, axis=0)
    wide = dot(jnp.concatenate([split(jnp.exp2(running)), split(tail)], axis=0), spread)
    return step, running, running - jnp.log2(step), wide[:BLOCK], wide[BLOCK:]


def causal(buf, slab, taps, shift):
    lanes = slice(slab * LANES, (slab + 1) * LANES)
    conv = shift[:, lanes].astype(f32)
    for tap in range(4):
        conv = conv + taps[tap : tap + 1, lanes].astype(f32) * buf[slab, pl.ds(5 + tap, BLOCK), :]
    return conv


def chunk_scores(b_rows, c_rows):
    n = b_rows.shape[1]
    b, c = split(b_rows), split(c_rows)
    left = jnp.concatenate([c, c[:, :n]], axis=1)
    right = jnp.concatenate([b[:, :n], b[:, :n], b[:, n:]], axis=1)
    return b, c, dot(left, right, NT)


def quad_mixing(scores, running, shifted_t, quad, mask):
    factors, mixes = [], []
    for head in range(4 * quad, 4 * quad + 4):
        spread = running[:, head : head + 1] - shifted_t[head : head + 1, :]
        factors.append(jnp.exp2(jnp.where(mask, spread, -1e30)))
        mixes.append((scores * factors[-1]).astype(bf16))
    return factors, mixes


def heads_apart(left, right):
    lane = lax.broadcasted_iota(jnp.int32, (1, LANES), 1)
    first = (lane < HALF).astype(bf16)
    zero = jnp.zeros(left.shape, bf16)
    rows = [jnp.concatenate([left * m, zero], axis=1) for m in (first, 1 - first)]
    rows += [jnp.concatenate([zero, right * m], axis=1) for m in (first, 1 - first)]
    return jnp.concatenate(rows, axis=0)


def forward_kernel(
    half_blocks,
    at_ref,
    own_ref,
    other_ref,
    gain_ref,
    gate_w,
    value_w,
    state_w,
    step_w,
    vconv_ref,
    vshift_ref,
    sconv_ref,
    sshift_ref,
    sbias_ref,
    rate_ref,
    skip_ref,
    ggain_ref,
    spread_ref,
    normed_ref,
    g_ref,
    y_ref,
    gg_ref,
    av_ref,
    vp_ref,
    as_ref,
    sp_ref,
    z_ref,
    sin_ref,
    sq_ref,
    step_ref,
    running_ref,
    shifted_ref,
    grownx,
    tailx,
    vbuf,
    sbuf,
    state,
    carried,
    values,
    low,
    vtail,
):
    step_at = pl.program_id(0)
    pairs = vbuf.shape[0]
    nstate = state.shape[0]

    @pl.when(step_at == 0)
    def _():
        state[...] = jnp.zeros_like(state)
        for buf in (vbuf, sbuf):
            buf[:, 0:8, :] = jnp.zeros((buf.shape[0], 8, LANES), f32)

    mine = (step_at // half_blocks) == at_ref[0]
    rows = jnp.where(mine, own_ref[...], other_ref[...]).astype(f32)
    scale = lax.rsqrt(jnp.mean(rows * rows, axis=1, keepdims=True) + EPSILON)
    normed = (rows * scale * gain_ref[...].astype(f32)).astype(bf16)
    normed_ref[...] = normed
    z = dot(normed, step_w[...]) + sbias_ref[...]
    z_ref[...] = z
    for out, buf, w in ((sp_ref, sbuf, state_w), (vp_ref, vbuf, value_w)):
        pre = dot(normed, w[...])
        out[...] = pre
        for slab in range(buf.shape[0]):
            buf[slab, 8:, :] = pre[:, slab * LANES : (slab + 1) * LANES]
    g_ref[...] = dot(normed, gate_w[...])

    step, running, shifted, grownx[...], tailx[...] = block_scalars(z, rate_ref[...], spread_ref[...])
    step_ref[...] = step
    running_ref[...] = running
    shifted_ref[...] = shifted
    chunks = range(BLOCK // CHUNK)
    states = []
    for slab in range(sbuf.shape[0]):
        conv = causal(sbuf, slab, sconv_ref, sshift_ref)
        as_ref[:, slab * LANES : (slab + 1) * LANES] = conv
        states.append(silu(conv))
    for pair in range(pairs):
        lanes = slice(pair * LANES, (pair + 1) * LANES)
        conv = causal(vbuf, pair, vconv_ref, vshift_ref)
        av_ref[:, lanes] = conv
        out = silu(conv)
        values[:, lanes] = out
        low[:, lanes] = out.astype(bf16)
        vtail[:, lanes] = (out * tailx[:, lanes]).astype(bf16)
    parts = []
    for chunk in chunks:
        here = slice(chunk * CHUNK, (chunk + 1) * CHUNK)
        b_two, c_two, scores = chunk_scores(*(v[here] for v in states))
        parts.append(scores)
        before = state[...].astype(bf16)
        sin_ref[chunk, :, :] = before
        carried[here, :] = dot(c_two[:, :nstate], before)
        last = grownx[(chunk + 1) * CHUNK - 1 : (chunk + 1) * CHUNK, :]
        state[...] = last * state[...] + dot(b_two[:, :nstate], vtail[here, :], TN)
    mask = lower_mask(CHUNK)
    for chunk in chunks:
        here = slice(chunk * CHUNK, (chunk + 1) * CHUNK)
        run = running[here]
        run_t = shifted[here].T
        squares = jnp.zeros((CHUNK, LANES), f32)
        for quad in range(pairs // 2):
            _, mixes = quad_mixing(parts[chunk], run, run_t, quad, mask)
            sides = [slice((2 * quad + k) * LANES, (2 * quad + k + 1) * LANES) for k in range(2)]
            both = dot(
                jnp.concatenate(mixes, axis=1), heads_apart(*(low[here, lanes] for lanes in sides))
            )
            for k, lanes in enumerate(sides):
                scanned = both[:, k * LANES : (k + 1) * LANES]
                scanned = scanned + grownx[here, lanes] * carried[here, lanes]
                scanned = scanned + skip_ref[:, lanes] * values[here, lanes]
                y_ref[here, lanes] = scanned
                gated = scanned * silu(g_ref[here, lanes])
                gg_ref[here, lanes] = (gated * ggain_ref[:, lanes].astype(f32)).astype(bf16)
                squares = squares + gated * gated
        sq_ref[:, here] = dot(jnp.ones((8, LANES), f32), squares, NT, HIGHEST)
    for buf in (vbuf, sbuf):
        buf[:, 0:8, :] = buf[:, BLOCK : BLOCK + 8, :]


def stats_kernel(half_blocks, at_ref, own_ref, other_ref, gg_ref, sq_ref, out_w, og_ref, stats_ref):
    mine = (pl.program_id(0) // half_blocks) == at_ref[0]
    cot = jnp.where(mine, own_ref[...], other_ref[...])
    og = dot(cot, out_w[...], NT)
    og_ref[...] = og
    prod = (og * gg_ref[...].astype(f32)).astype(bf16)
    dots = dot(jnp.ones((8, prod.shape[1]), bf16), prod, NT)
    row = lax.broadcasted_iota(jnp.int32, dots.shape, 0)
    stats_ref[...] = jnp.where(row == 0, sq_ref[...], dots)


def bring_kernel(at_ref, *refs):
    count = len(refs) // 2
    for src, dst in zip(refs[:count], refs[count:]):
        dst[...] = src[...]


def branch_kernel(half_blocks, at_ref, gg_ref, out_w, own_ref, other_ref):
    mine = (pl.program_id(0) // half_blocks) == at_ref[0]
    rows = dot(gg_ref[...], out_w[...]).astype(bf16)

    @pl.when(mine)
    def _():
        own_ref[...] = rows

    @pl.when(jnp.logical_not(mine))
    def _():
        other_ref[...] = rows


def picked(cut, early, late):
    return jnp.where(pl.program_id(0) < cut, early[...], late[...])


def normed_grad_kernel(half_blocks, cut, at_ref, dg_ref, *refs):
    lows, (gate_w, value_w, state_w, step_w, own_ref, other_ref) = refs[:6], refs[6:]
    dv, ds, dz = (picked(cut, a, b) for a, b in zip(lows[:3], lows[3:]))
    mine = (pl.program_id(0) // half_blocks) == at_ref[0]
    rows = (
        dot(dg_ref[...], gate_w[...], NT)
        + dot(dv, value_w[...], NT)
        + dot(ds, state_w[...], NT)
        + dot(dz, step_w[...], NT)
    ).astype(bf16)

    @pl.when(mine)
    def _():
        own_ref[...] = rows

    @pl.when(jnp.logical_not(mine))
    def _():
        other_ref[...] = rows


def row_sums(grads, weights):
    prod = (grads * weights.astype(f32)).astype(bf16)
    return dot(jnp.ones((8, prod.shape[1]), bf16), prod, NT)


def emit(at_ref, parts, outs):
    half = outs[0].shape[0]
    for j, out in enumerate(outs):
        rows = pl.ds(pl.multiple_of((at_ref[1] ^ j) * half, LANES), half)
        left = 0
        for part in parts:
            out[:, left : left + part.shape[1]] = part[rows, :].astype(out.dtype)
            left += part.shape[1]


def row_column(rows):
    return jnp.concatenate([rows, jnp.zeros((LANES - rows.shape[0], BLOCK), f32)], axis=0).T


def mixed_kernel(inner_all, at_ref, rows_ref, own_ref, other_ref, here_ref, there_ref, out_ref, token_ref):
    token_ref[...] = jnp.zeros_like(token_ref)
    sums = here_ref[...] + there_ref[...]
    scale = row_column(lax.rsqrt(sums / inner_all + EPSILON))[:, 0:1]
    branch = own_ref[...].astype(f32) + other_ref[...].astype(f32)
    out_ref[...] = rows_ref[...].astype(f32) + scale * branch


def input_kernel(at_ref, rows_ref, cot_ref, own_ref, other_ref, gain_ref, out_ref, token_ref):
    token_ref[...] = jnp.zeros_like(token_ref)
    rows = rows_ref[...].astype(f32)
    scale = lax.rsqrt(jnp.mean(rows * rows, axis=1, keepdims=True) + EPSILON)
    pulled = (own_ref[...].astype(f32) + other_ref[...].astype(f32)) * gain_ref[...].astype(f32)
    inner = jnp.mean(pulled * rows, axis=1, keepdims=True) * (scale * scale * scale)
    out_ref[...] = cot_ref[...].astype(f32) + scale * pulled - rows * inner


def gate_kernel(
    half_blocks,
    inner_all,
    fast,
    at_ref,
    own_ref,
    other_ref,
    here_ref,
    there_ref,
    normed_ref,
    og_ref,
    y_ref,
    g_ref,
    gg_ref,
    ggain_ref,
    gate_w,
    _,
    dg_ref,
    dy_ref,
    first_ref,
    second_ref,
    grad_gain_ref,
    norm_ref,
    scaled_ref,
    *scratch,
):
    step_at = pl.program_id(0)
    here = pl.ds(pl.multiple_of(step_at * BLOCK, BLOCK), BLOCK)
    pairs = og_ref.shape[1] // LANES
    grad_gate, grad_out = scratch if fast else (first_ref, second_ref)

    @pl.when(step_at == 0)
    def _():
        grad_gain_ref[...] = jnp.zeros_like(grad_gain_ref)

    sums = here_ref[...] + there_ref[...]
    scale_row = lax.rsqrt(sums[0:1, :] / inner_all + EPSILON)
    pull_row = scale_row * scale_row * scale_row * sums[1:2, :] / inner_all
    columns = row_column(jnp.concatenate([scale_row, pull_row], axis=0))
    scale, pull = columns[:, 0:1], columns[:, 1:2]
    mine = (step_at // half_blocks) == at_ref[0]
    cot = jnp.where(mine, own_ref[...], other_ref[...]).astype(f32)
    scaled_ref[here, :] = (cot * scale).astype(bf16)
    for pair in range(pairs):
        lanes = slice(pair * LANES, (pair + 1) * LANES)
        og = og_ref[:, lanes] * scale
        y = y_ref[:, lanes]
        g = g_ref[:, lanes]
        gate, slope = silu_slope(g)
        gated = y * gate
        grad_gain_ref[0:1, lanes] += jnp.sum(og * gated, axis=0, keepdims=True)
        gated_grad = ggain_ref[:, lanes].astype(f32) * og - gated * pull
        dy_ref[:, lanes] = (gated_grad * gate).astype(bf16)
        dg_ref[here, lanes] = (gated_grad * y * slope).astype(bf16)

    @pl.when(step_at == pl.num_programs(0) - 1)
    def _():
        grad_out[...] = dot(gg_ref[...], scaled_ref[...], TN)
        grad_gate[...] = dot(normed_ref[...], dg_ref[...], TN)
        norm_ref[...] = row_sums(grad_gate[...], gate_w[...])
        if fast:
            emit(at_ref, (grad_gate, grad_out), (first_ref, second_ref))


def weights_kernel(fast, extra, at_ref, normed_ref, *refs):
    lows, refs = refs[:6], refs[6:]
    value_w, state_w, step_w, gain_ref, vec_ref, svec_ref, head_ref, ggain_ref, norm_ref = refs[:9]
    outs, acc = refs[9 + extra : -3], refs[-3:]
    for a, early, late in zip(acc, lows[:3], lows[3:]):
        a[...] = dot(normed_ref[...], jnp.concatenate([early[...], late[...]], axis=0), TN)
    norm = norm_ref[...]
    for a, w in zip(acc, (value_w, state_w, step_w)):
        norm = norm + row_sums(a[...], w[...])
    norm = norm / gain_ref[...].astype(f32)
    if fast:
        pack_vectors(acc[2], vec_ref, svec_ref, head_ref, ggain_ref, norm)
        emit(at_ref, acc, outs)
        return
    for o, a in zip(outs, acc):
        o[...] = a[...]
    outs[3][...] = norm


VEC_AT = 16
SVEC_AT = 24
HEAD_AT = 32


def pack_vectors(block, vec_ref, svec_ref, head_ref, ggain_ref, norm):
    model = block.shape[0]
    row = lax.broadcasted_iota(jnp.int32, (8, model), 0)
    vec = jnp.where(row == 5, ggain_ref[0:1, :], jnp.where(row == 6, norm[0:1, :], vec_ref[...]))

    def tall(v):
        return jnp.concatenate([v, jnp.zeros((8, model - v.shape[1]), f32)], axis=1)

    rows = jnp.concatenate(
        [
            jnp.zeros((VEC_AT, model), f32),
            vec,
            tall(svec_ref[...]),
            tall(head_ref[...]),
            jnp.zeros((LANES - HEAD_AT - 8, model), f32),
        ],
        axis=0,
    )
    lane = lax.broadcasted_iota(jnp.int32, (1, LANES), 1)
    full = jnp.where(lane < VEC_AT, block[...], rows.T)
    block[...] = carry_rest(jnp.where(lane < HALF, full, 0.0))


def carry_rest(full):
    high = full.astype(bf16).astype(f32)
    return high + pltpu.roll(full - high, HALF, 1)


def join_rest(block):
    lane = lax.broadcasted_iota(jnp.int32, (1, LANES), 1)
    return jnp.where(lane < HALF, block + pltpu.roll(block, HALF, 1), 0.0)


def fold_step(me, ins, outs, buf, vectors):
    width = buf.shape[1] - (LANES if vectors else 0)
    total = ins[0][:, :width].astype(f32)
    for r in ins[1:]:
        total = total + r[:, :width].astype(f32)
    buf[:, :width] = total.astype(bf16)
    if vectors:
        last = ins[0][:, width:].astype(f32)
        for r in ins[1:]:
            last = last + r[:, width:].astype(f32)
        buf[:, width:] = carry_rest(join_rest(last)).astype(bf16)
    rows = outs[0].shape[0]
    if len(outs) == 1:
        outs[0][...] = buf[...]
        return
    for j, o in enumerate(outs):
        o[...] = buf[pl.ds(pl.multiple_of((me ^ j) * rows, 16), rows), :]


def join_step(me, ins, out):
    rows = ins[0].shape[0]
    for j, r in enumerate(ins):
        out[pl.ds(pl.multiple_of((me ^ j) * rows, 16), rows), :] = r[...]


def stage_kernel(plan, extra, at_ref, *refs):
    n_in = sum(count for _, _, count, _, _ in plan)
    ins, refs = refs[:n_in], refs[n_in + extra :]
    n_out = sum(count for _, _, _, count, _ in plan)
    outs, bufs = refs[:n_out], list(refs[n_out:])
    for kind, axis, take, give, vectors in plan:
        if kind == "fold":
            fold_step(at_ref[axis], ins[:take], outs[:give], bufs.pop(0), vectors)
        else:
            join_step(at_ref[axis], ins[:take], outs[0])
        ins, outs = ins[take:], outs[give:]


def stage(at, steps, after=()):
    plan, arrays, shapes, scratch = [], [], [], []
    for kind, axis, ins, *rest in steps:
        rows, width = ins[0].shape
        count, vectors = rest if rest else (1, False)
        if kind == "fold":
            shapes += [(rows // count, width)] * count
            scratch.append(pltpu.VMEM((rows, width), bf16))
        else:
            shapes.append((rows * len(ins), width))
        plan.append((kind, axis, len(ins), count, vectors))
        arrays += ins
    out = call(
        functools.partial(stage_kernel, tuple(plan), len(after)),
        1,
        at,
        [(a, None) for a in arrays] + [(a, pl.BlockSpec(memory_space=pl.ANY)) for a in after],
        [(shape, bf16, pl.BlockSpec(shape, lambda i, a: (0, 0))) for shape in shapes],
        scratch,
    )
    out, results = list(out), []
    for _, _, _, give, _ in plan:
        results.append(out[:give])
        out = out[give:]
    return results


def heads_kernel(at_ref, own_ref, other_ref, out_ref):
    split_at = out_ref.shape[1] - other_ref.shape[1]
    state = other_ref.shape[1] - LANES
    out_ref[:, :split_at] = own_ref[:, :split_at]
    out_ref[:, split_at : split_at + state] = (
        own_ref[:, split_at : split_at + state].astype(f32) + other_ref[:, :state].astype(f32)
    ).astype(bf16)
    lane = lax.broadcasted_iota(jnp.int32, (1, LANES), 1)
    shared = (lane == VEC_AT + 6) | ((lane >= SVEC_AT) & (lane < HEAD_AT))
    mine = join_rest(own_ref[:, split_at + state :].astype(f32))
    theirs = join_rest(other_ref[:, state:].astype(f32))
    out_ref[:, split_at + state :] = carry_rest(
        mine + jnp.where(shared, theirs, 0.0)
    ).astype(bf16)


def halves_of(at_ref, own_ref, other_ref, left, right):
    rows = own_ref.shape[0]
    for j, ref in enumerate((own_ref, other_ref)):
        yield pl.ds(pl.multiple_of((at_ref[1] ^ j) * rows, LANES), rows), ref[:, left:right].astype(f32)


def early_kernel(at_ref, own_ref, other_ref, *outs):
    outs[-1][...] = jnp.zeros_like(outs[-1])
    left = 0
    for o in outs[:-1]:
        right = left + o.shape[1]
        for at, v in halves_of(at_ref, own_ref, other_ref, left, right):
            o[at, :] = v
        left = right


def late_kernel(at_ref, own_ref, other_ref, *refs):
    outs, block = refs[:-1], refs[-1]
    left = 0
    for o in (outs[0], outs[1], block):
        right = left + o.shape[1]
        for at, v in halves_of(at_ref, own_ref, other_ref, left, right):
            o[at, :] = v
        left = right
    full = join_rest(block[...])
    heads = outs[2].shape[1]
    outs[2][...] = full[:, :heads]
    rows = full.T
    vec, svec = rows[VEC_AT : VEC_AT + 8], rows[SVEC_AT : SVEC_AT + 8]
    head = rows[HEAD_AT : HEAD_AT + 8]
    vconv, vshift, ggain, norm, sconv, sshift, bias, rate, skip = outs[3:]
    vconv[...] = vec[:4]
    for o, row in ((vshift, vec[4:5]), (ggain, vec[5:6]), (norm, vec[6:7]), (sshift, svec[4:5])):
        o[...] = row[:, : o.shape[0]].reshape(o.shape)
    sconv[...] = svec[:4, : sconv.shape[1]]
    for j, o in enumerate((bias, rate, skip)):
        o[...] = head[j : j + 1, : o.shape[0]].reshape(o.shape)


def backward_kernel(
    carried_in,
    extra,
    at_ref,
    dy_ref,
    av_ref,
    vp_ref,
    as_ref,
    sp_ref,
    z_ref,
    step_ref,
    running_ref,
    shifted_ref,
    grownx,
    tailx,
    sin_ref,
    vconv_ref,
    sconv_ref,
    rate_ref,
    skip_ref,
    gather_ref,
    *refs,
):
    carries, refs = (refs[:6], refs[6:]) if carried_in else ((), refs)
    refs = refs[extra:]
    dvalue, dstates, dstep, dstate_out, dahalo, dshalo, grad_vconv_ref, grad_sconv_ref, grad_head_ref = refs[:9]
    dabuf, dsbuf, dstate, carried, pulled, ubuf, vtail, inner, outer = refs[9:]
    step_at = pl.program_id(0)
    nstate, width = dstate.shape
    size = dy_ref.shape[0]
    pairs = width // LANES

    @pl.when(step_at == 0)
    def _():
        if carried_in:
            dstate[...] = carries[0][...]
            dabuf[:, size:, :] = carries[1][...]
            dsbuf[:, size:, :] = carries[2][...]
            grad_vconv_ref[...] = carries[3][...]
            grad_sconv_ref[...] = carries[4][...]
            grad_head_ref[...] = carries[5][...]
        else:
            dstate[...] = jnp.zeros_like(dstate)
            for buf in (dabuf, dsbuf):
                buf[:, size:, :] = jnp.zeros((buf.shape[0], 8, LANES), f32)
            for ref in (grad_vconv_ref, grad_sconv_ref, grad_head_ref):
                ref[...] = jnp.zeros_like(ref)

    @pl.when(step_at > 0)
    def _():
        for buf in (dabuf, dsbuf):
            buf[:, size:, :] = buf[:, 0:8, :]

    chunks = [slice(r, r + CHUNK) for r in range(0, size, CHUNK)]
    zero_row = jnp.zeros((1, LANES), f32)
    rate = -jnp.exp(rate_ref[...])
    states, slopes = [], []
    for slab in range(2):
        out, slope = silu_slope(as_ref[:, slab * LANES : (slab + 1) * LANES])
        states.append(out)
        slopes.append(slope)
    for pair in range(pairs):
        lanes = slice(pair * LANES, (pair + 1) * LANES)
        ubuf[:, lanes] = (dy_ref[:, lanes].astype(f32) * grownx[:, lanes]).astype(bf16)
    two = [chunk_scores(*(v[here] for v in states)) for here in chunks]
    helds, afters = [None] * len(chunks), [None] * len(chunks)
    for chunk in reversed(range(len(chunks))):
        here = chunks[chunk]
        b_two, c_two, _ = two[chunk]
        before = sin_ref[chunk, :, :]
        last = grownx[here.stop - 1 : here.stop, :]
        grad = dstate[...]
        afters[chunk] = grad.astype(bf16)
        carried[here, :] = dot(c_two[:, :nstate], before)
        pulled[here, :] = dot(b_two[:, :nstate], afters[chunk])
        overlap = jnp.sum(before.astype(f32) * grad, axis=0, keepdims=True) * last
        overlap = jnp.broadcast_to(overlap, (8, width))
        tall = [split(overlap[:, p * LANES : (p + 1) * LANES]) for p in range(pairs)]
        held = dot(jnp.concatenate(tall, axis=1), gather_ref[...])[0:1]
        helds[chunk] = held[:, :LANES] + held[:, LANES:]
        dstate[...] = last * grad + dot(c_two[:, :nstate], ubuf[here, :], TN)

    mask = lower_mask(CHUNK)
    for chunk in reversed(range(len(chunks))):
        here = chunks[chunk]
        b_two, c_two, scores = two[chunk]
        run = running_ref[here, :]
        run_t = shifted_ref[here, :].T
        dscores = jnp.zeros((CHUNK, CHUNK), f32)
        for quad in range(pairs // 2):
            factors, mixes = quad_mixing(scores, run, run_t, quad, mask)
            both = [slice((2 * quad + k) * LANES, (2 * quad + k + 1) * LANES) for k in range(2)]
            values, slope = zip(*(silu_slope(av_ref[here, lanes]) for lanes in both))
            low = [v.astype(bf16) for v in values]
            dy_low = [dy_ref[here, lanes] for lanes in both]
            apart = heads_apart(*low)
            scanned = dot(jnp.concatenate(mixes, axis=1), apart)
            dsteps = dot(jnp.concatenate(mixes, axis=0), heads_apart(*dy_low), TN)
            for k, lanes in enumerate(both):
                pair = 2 * quad + k
                own = slice(k * LANES, (k + 1) * LANES)
                dmixing = dot(dy_low[k], apart[2 * k * CHUNK : 2 * (k + 1) * CHUNK, own], NT)
                dscores = dscores + dmixing[:, :CHUNK] * factors[2 * k]
                dscores = dscores + dmixing[:, CHUNK:] * factors[2 * k + 1]
                wide = slice(2 * pair * LANES, (2 * pair + 1) * LANES)
                wide_b = slice((2 * pair + 1) * LANES, (2 * pair + 2) * LANES)
                dy = dy_low[k].astype(f32)
                dvalues = dsteps[:, own]
                pulls = low[k].astype(f32) * dvalues
                inside = dy * scanned[:, own] - pulls + ubuf[here, lanes].astype(f32) * carried[here, lanes]
                high = inside.astype(bf16)
                inner[here, wide] = high
                inner[here, wide_b] = (inside - high.astype(f32)).astype(bf16)
                tails, pull = tailx[here, lanes], pulled[here, lanes]
                v = (values[k] * tails).astype(bf16)
                vtail[here, lanes] = v
                outer[here, wide] = pulls.astype(bf16)
                outer[here, wide_b] = (v.astype(f32) * pull).astype(bf16)
                da = (dvalues + tails * pull + skip_ref[:, lanes] * dy) * slope[k]
                skips = jnp.sum(values[k] * dy, axis=0, keepdims=True)
                dv, rows = causal_back(dabuf, pair, here.start, da, vp_ref[here, lanes], vconv_ref, skips)
                grad_vconv_ref[:, lanes] += rows
                dvalue[here, lanes] = dv.astype(bf16)
        dlow = dscores.astype(bf16)
        drest = (dscores - dlow.astype(f32)).astype(bf16)
        b_rows, c_rows = b_two[:, :nstate], c_two[:, :nstate]
        cross = dot(
            jnp.concatenate([vtail[here, :], ubuf[here, :]], axis=0),
            jnp.concatenate([afters[chunk], sin_ref[chunk, :, :]], axis=0),
            NT,
        )
        db = cross[:CHUNK, :nstate] + dot(
            jnp.concatenate([dlow, dlow, drest], axis=0),
            jnp.concatenate([c_rows, c_two[:, nstate:], c_rows], axis=0),
            TN,
        )
        dc = cross[CHUNK:, nstate:] + dot(
            jnp.concatenate([dlow, dlow, drest], axis=1),
            jnp.concatenate([b_rows, b_two[:, nstate:], b_rows], axis=0),
        )
        for slab, d in enumerate((db, dc)):
            lanes = slice(slab * LANES, (slab + 1) * LANES)
            d = d * slopes[slab][here]
            dpre, rows = causal_back(dsbuf, slab, here.start, d, sp_ref[here, lanes], sconv_ref, zero_row)
            grad_sconv_ref[:, lanes] += rows
            dstates[here, lanes] = dpre.astype(bf16)

    gathered = dot(jnp.concatenate([inner[...], outer[...]], axis=0), gather_ref[...])
    heads = [jnp.zeros((1, LANES), f32)] * 2
    for r in range(0, size, BLOCK):
        here = slice(r, r + BLOCK)
        sums, outs = gathered[here], gathered[size + r : size + r + BLOCK]
        ddecay = dot(chunk_mask(), split(sums[:, :LANES] + sums[:, LANES:]), TN)
        ddecay = ddecay[:, :LANES] + ddecay[:, LANES:]
        ddecay = ddecay + dot(chunk_mask(True), outs[:, LANES:].astype(bf16))
        held = [jnp.broadcast_to(helds[k // CHUNK], (CHUNK, LANES)) for k in range(r, r + BLOCK, CHUNK)]
        ddecay = ddecay + jnp.concatenate(held, axis=0)
        step = step_ref[here, :]
        direct = (outs[:, :LANES] + outs[:, LANES:]) / jnp.maximum(step, 1e-37)
        dz = (direct + ddecay * rate) * sigmoid(z_ref[here, :])
        dstep[here, :] = dz.astype(bf16)
        heads[0] = heads[0] + jnp.sum(dz, axis=0, keepdims=True)
        heads[1] = heads[1] + jnp.sum(ddecay * step, axis=0, keepdims=True) * rate
    grad_head_ref[...] += jnp.concatenate([*heads, jnp.zeros((6, LANES), f32)], axis=0)

    @pl.when(step_at == pl.num_programs(0) - 1)
    def _():
        dstate_out[...] = dstate[...]
        vectors = grad_vconv_ref[...]
        tall = [split(vectors[:, p * LANES : (p + 1) * LANES]) for p in range(pairs)]
        skips = dot(jnp.concatenate(tall, axis=1), gather_ref[...])
        grad_head_ref[2:3, :] = skips[5:6, :LANES] + skips[5:6, LANES:]
        dahalo[...] = dabuf[:, 0:8, :]
        dshalo[...] = dsbuf[:, 0:8, :]


MIB = dict(
    forward_kernel=14,
    stats_kernel=8,
    branch_kernel=8,
    gate_kernel=16,
    backward_kernel=22,
    weights_kernel=14,
    normed_grad_kernel=12,
    mixed_kernel=8,
    input_kernel=8,
    early_kernel=10,
    late_kernel=10,
)
COST = dict(forward_kernel=4.5, backward_kernel=7, stats_kernel=1, branch_kernel=.6, gate_kernel=2.4, weights_kernel=1.2, normed_grad_kernel=1.2, mixed_kernel=1, input_kernel=1, early_kernel=3, late_kernel=3)


def whole(array):
    return pl.BlockSpec(array.shape, lambda i, at: (0,) * array.ndim)


def call(kernel, blocks, at, ins, outs, scratch, small=True):
    title = getattr(kernel, "func", kernel).__name__
    return pl.pallas_call(
        kernel,
        name=title,
        grid_spec=pltpu.PrefetchScalarGridSpec(
            num_scalar_prefetch=1,
            grid=(blocks,),
            in_specs=[whole(a) if s is None else s for a, s in ins],
            out_specs=[out[2] for out in outs],
            scratch_shapes=scratch,
        ),
        out_shape=[
            pltpu.VMEM(shape, dtype) if rest and rest[0] else jax.ShapeDtypeStruct(shape, dtype)
            for shape, dtype, _, *rest in outs
        ],
        cost_estimate=pl.CostEstimate(flops=int(COST.get(title, 1)*blocks * 10**9), bytes_accessed=0, transcendentals=0),
        compiler_params=pltpu.CompilerParams(
            dimension_semantics=("arbitrary",), vmem_limit_bytes=(MIB.get(title, 16) if small else 48) * 2**20
        ),
    )(at, *[a for a, _ in ins])


def per_device(
    residual_in,
    norm_gain,
    gate_proj,
    value_proj,
    state_proj,
    step_proj,
    value_conv,
    value_shift,
    state_conv,
    state_shift,
    step_bias,
    log_rate,
    skip_gain,
    gated_gain,
    out_proj,
    grad_out,
):
    parts = lax.axis_size("heads")
    two = parts == 2
    rows_here, model = residual_in.shape[1:]
    length = rows_here * parts
    inner = value_conv.shape[1]
    inner_all = inner * parts
    heads = step_bias.shape[0]
    head_width = inner // heads
    pad_heads = -heads % 4
    nheads = heads + pad_heads
    width = nheads * head_width
    nstate2 = state_conv.shape[1]
    blocks = length // BLOCK
    chunks = BLOCK // CHUNK
    half_blocks = rows_here // BLOCK if two else blocks

    def wide(a, axis):
        pads = [(0, 0)] * a.ndim
        pads[axis] = (0, width - inner)
        return jnp.pad(a, pads) if width > inner else a

    def lanes_of(a):
        return jnp.pad(a, [(0, 0)] * (a.ndim - 1) + [(0, LANES - a.shape[-1])])

    residual = residual_in[0]
    cot = grad_out[0]
    batch = lax.axis_size("batch")
    fast = two and batch == 16 and width == model and model % BLOCK == 0
    nstate = nstate2 // 2
    run = functools.partial(call, small=fast)
    place = lax.axis_index("batch").astype(jnp.int32)
    across = lax.axis_index("heads").astype(jnp.int32) if two else jnp.int32(0)
    own_from = lax.axis_index("heads").astype(jnp.int32) * rows_here
    at = jnp.stack([across, place & 1, (place >> 1) & 1, place >> 2, own_from])
    if two:
        swap = [(0, 1), (1, 0)]
        pair_of = lambda a: (a, lax.ppermute(a, "heads", swap))
        add_other = lambda a: lax.ppermute(a, "heads", swap)
    else:

        def pair_of(a):
            full = lax.all_gather(a, "heads", axis=0, tiled=True)
            return (full, full)

        add_other = lambda a: lax.psum(a, "heads") - a

    def hop(a, way):
        mask = {"core": 1, "line": 2}.get(way) or 4 * way
        return lax.ppermute(a, "batch", [(i, i ^ mask) for i in range(batch)])

    def bring(*arrays):
        if not fast:
            return arrays
        return run(
            bring_kernel,
            1,
            at,
            [(a, None) for a in arrays],
            [(a.shape, a.dtype, pl.BlockSpec(a.shape, lambda i, at: (0, 0)), True) for a in arrays],
            [],
        )

    own_rows, other_rows = pair_of(residual)
    own_cot, other_cot = pair_of(cot)

    gate_w, value_w = wide(gate_proj, 1), wide(value_proj, 1)
    out_w = wide(out_proj, 0)
    step_w = lanes_of(step_proj)
    gain_in = norm_gain[None, :]
    vconv, vshift = wide(value_conv, 1), wide(value_shift[None, :], 1)
    sshift = state_shift[None, :]
    sbias, rate = lanes_of(step_bias[None, :]), lanes_of(log_rate[None, :])
    skipx = wide(jnp.repeat(skip_gain, head_width)[None, :], 1)
    ggain = wide(gated_gain[None, :], 1)
    head_of = jnp.arange(width) // head_width
    spread = (jnp.arange(LANES)[:, None] == head_of[None, :]).astype(bf16)
    spread = jnp.concatenate([spread, spread], axis=0)
    first = head_of.reshape(-1, 1, LANES, 1) + jnp.arange(2).reshape(1, 2, 1, 1) * LANES
    gather = (jnp.arange(2 * LANES) == first).reshape(-1, 2 * LANES).astype(bf16)

    gate_w, value_w, state_proj, step_w, out_w, spread, gather = bring(
        gate_w, value_w, state_proj, step_w, out_w, spread, gather
    )
    gain_in, vconv, vshift, state_conv, sshift, sbias, rate, skipx, ggain = bring(
        gain_in, vconv, vshift, state_conv, sshift, sbias, rate, skipx, ggain
    )

    def own_block(i, a):
        return (jnp.clip(i - a[0] * half_blocks, 0, half_blocks - 1), 0)

    def other_block(i, a):
        return (jnp.clip(i - (1 - a[0]) * half_blocks, 0, half_blocks - 1), 0) if two else (0, 0)

    other_read = other_block if two else own_block

    def rows(n, index=lambda i, a: (i, 0)):
        return pl.BlockSpec((BLOCK, n), index)

    along = pl.BlockSpec((8, BLOCK), lambda i, a: (0, i))
    fixed = lambda *shape: pl.BlockSpec(shape, lambda i, a: (0,) * len(shape))
    states_spec = lambda index: pl.BlockSpec((chunks, nstate, width), index)
    big = lambda *shape: pltpu.VMEM(shape, f32)
    low = lambda *shape: pltpu.VMEM(shape, bf16)
    halves = [
        ((rows_here if two else length, model), bf16, rows(model, own_block)),
        ((rows_here if two else BLOCK, model), bf16, rows(model, other_block)),
    ]

    normed, g, y, gg, av, vp, conv_s, sp, z, sin, sq, step, running, shifted, grownx, tailx = run(
        functools.partial(forward_kernel, half_blocks),
        blocks,
        at,
        [
            (own_rows, rows(model, own_block)),
            (other_rows, rows(model, other_read)),
            (gain_in, None),
            (gate_w, None),
            (value_w, None),
            (state_proj, None),
            (step_w, None),
            (vconv, None),
            (vshift, None),
            (state_conv, None),
            (sshift, None),
            (sbias, None),
            (rate, None),
            (skipx, None),
            (ggain, None),
            (spread, None),
        ],
        [
            *[
                (shape, dtype, spec, fast)
                for shape, dtype, spec in (
                    ((length, model), bf16, rows(model)),
                    ((length, width), f32, rows(width)),
                    ((length, width), f32, rows(width)),
                    ((length, width), bf16, rows(width)),
                    ((length, width), f32, rows(width)),
                    ((length, width), f32, rows(width)),
                    ((length, nstate2), f32, rows(nstate2)),
                    ((length, nstate2), f32, rows(nstate2)),
                    ((length, LANES), f32, rows(LANES)),
                    ((blocks * chunks, nstate, width), bf16, states_spec(lambda i, a: (i, 0, 0))),
                    ((8, length), f32, along),
                    ((length, LANES), f32, rows(LANES)),
                    ((length, LANES), f32, rows(LANES)),
                    ((length, LANES), f32, rows(LANES)),
                    ((length, width), f32, rows(width)),
                    ((length, width), f32, rows(width)),
                )
            ]
        ],
        [
            big(width // LANES, BLOCK + 8, LANES),
            big(nstate2 // LANES, BLOCK + 8, LANES),
            big(nstate, width),
            big(BLOCK, width),
            big(BLOCK, width),
            low(BLOCK, width),
            low(BLOCK, width),
        ],
    )
    og, stats = run(
        functools.partial(stats_kernel, half_blocks),
        blocks,
        at,
        [
            (own_cot, rows(model, own_block)),
            (other_cot, rows(model, other_read)),
            (gg, rows(width)),
            (sq, along),
            (out_w, None),
        ],
        [((length, width), f32, rows(width), fast), ((8, length), f32, along)],
        [],
    )
    other_stats = add_other(stats)
    own_along = pl.BlockSpec((8, BLOCK), lambda i, a: (0, i + a[4] // BLOCK))
    branch, branch_sent = run(
        functools.partial(branch_kernel, half_blocks),
        blocks,
        at,
        [(gg, rows(width)), (out_w, None)],
        halves,
        [],
    )

    def other_half(own, sent):
        if two:
            return lax.ppermute(sent, "heads", swap)
        total = lax.psum_scatter(own.astype(f32), "heads", scatter_dimension=0, tiled=True)
        mine = lax.dynamic_slice_in_dim(own, own_from, rows_here, 0).astype(f32)
        return total - mine

    branch_got = other_half(branch, branch_sent)
    if not two:
        branch = lax.dynamic_slice_in_dim(branch, own_from, rows_here, 0)
    if fast:
        pieces = [((model // 2, 2 * model), bf16, fixed(model // 2, 2 * model))] * 2
    else:
        pieces = [
            ((model, width), f32, fixed(model, width)),
            ((width, model), f32, fixed(width, model)),
        ]
    dg, dy, early_a, early_b, grad_gain, norm = run(
        functools.partial(gate_kernel, half_blocks, inner_all, fast),
        blocks,
        at,
        [
            (own_cot, rows(model, own_block)),
            (other_cot, rows(model, other_read)),
            (stats, along),
            (other_stats, along),
            (normed, None),
            (og, rows(width)),
            (y, rows(width)),
            (g, rows(width)),
            (gg, None),
            (ggain, None),
            (gate_w, None),
            (branch, pl.BlockSpec(memory_space=pl.ANY)),
        ],
        [
            ((length, width), bf16, fixed(length, width), fast),
            ((length, width), bf16, rows(width), fast),
            *pieces,
            ((8, width), f32, fixed(8, width)),
            ((8, model), f32, fixed(8, model)),
        ],
        [low(length, model)] + ([big(model, width), big(width, model)] if fast else []),
    )

    def backward(start, count, carry, after=()):
        size = 2 * BLOCK if start % 2 == 0 and count % 2 == 0 else BLOCK
        steps, base = count * BLOCK // size, start * BLOCK // size

        def behind(n):
            return pl.BlockSpec((size, n), lambda i, a: (base + steps - 1 - i, 0))

        def local(n):
            return pl.BlockSpec((size, n), lambda i, a: (steps - 1 - i, 0))

        states = pl.BlockSpec(
            (size // CHUNK, nstate, width), lambda i, a: (base + steps - 1 - i, 0, 0)
        )
        slabs = [(width // LANES, 8, LANES), (nstate2 // LANES, 8, LANES)]
        vectors = [(nstate, width), *slabs, (8, width), (8, nstate2), (8, LANES)]
        out = run(
            functools.partial(backward_kernel, bool(carry), len(after)),
            steps,
            at,
            [
                (dy, behind(width)),
                (av, behind(width)),
                (vp, behind(width)),
                (conv_s, behind(nstate2)),
                (sp, behind(nstate2)),
                (z, behind(LANES)),
                (step, behind(LANES)),
                (running, behind(LANES)),
                (shifted, behind(LANES)),
                (grownx, behind(width)),
                (tailx, behind(width)),
                (sin, states),
                (vconv, None),
                (state_conv, None),
                (rate, None),
                (skipx, None),
                (gather, None),
                *[(c, None) for c in carry],
                *[(a, pl.BlockSpec(memory_space=pl.ANY)) for a in after],
            ],
            [
                ((count * BLOCK, width), bf16, local(width)),
                ((count * BLOCK, nstate2), bf16, local(nstate2)),
                ((count * BLOCK, LANES), bf16, local(LANES)),
                *[(shape, f32, fixed(*shape)) for shape in vectors],
            ],
            [
                big(width // LANES, size + 8, LANES),
                big(nstate2 // LANES, size + 8, LANES),
                big(nstate, width),
                big(size, width),
                big(size, width),
                low(size, width),
                low(size, width),
                low(size, 2 * width),
                low(size, 2 * width),
            ],
        )
        return out[:3], out[3:]

    cut = blocks // 2
    behind = ()
    if fast:
        ((kept, sent),) = stage(at, [("fold", 2, [early_a, hop(early_b, "core")], 2, False)])
        early = [kept, hop(sent, "line")]
        behind = (kept,)
    low_b, carry = backward(cut, blocks - cut, (), behind)
    if fast:
        ((kept, *sent),) = stage(at, [("fold", 3, early, 4, False)])
        early = [kept] + [hop(a, k + 1) for k, a in enumerate(sent)]
        behind = (kept, branch_got)
    low_a, carry = backward(0, cut, carry, behind)
    vec, svec, head = carry[3:]
    lows = [(a, rows(a.shape[1], lambda i, at: (jnp.minimum(i, cut - 1), 0))) for a in low_a]
    lows += [(a, rows(a.shape[1], lambda i, at: (jnp.maximum(i - cut, 0), 0))) for a in low_b]
    behind = early[1:] if fast else ()

    if fast:
        shape = (model // 2, width + nstate2 + LANES)
        pieces = [(shape, bf16, fixed(*shape))] * 2
    else:
        shapes = [(model, width), (model, nstate2), (model, LANES), (8, model)]
        pieces = [(shape, f32, fixed(*shape)) for shape in shapes]
    late = run(
        functools.partial(weights_kernel, fast, len(behind)),
        1,
        at,
        [
            (normed, None),
            *[(a, None) for a, _ in lows],
            (value_w, None),
            (state_proj, None),
            (step_w, None),
            (gain_in, None),
            (vec, None),
            (svec, None),
            (head, None),
            (grad_gain, None),
            (norm, None),
            *[(a, pl.BlockSpec(memory_space=pl.ANY)) for a in behind],
        ],
        pieces,
        [big(model, width), big(model, nstate2), big(model, LANES)],
    )
    ng, ng_sent = run(
        functools.partial(normed_grad_kernel, half_blocks, cut),
        blocks,
        at,
        [
            (dg, rows(width)),
            *lows,
            (gate_w, None),
            (value_w, None),
            (state_proj, None),
            (step_w, None),
        ],
        halves,
        [],
    )

    mixed, token = run(
        functools.partial(mixed_kernel, inner_all),
        rows_here // BLOCK,
        at,
        [
            (residual, rows(model)),
            (branch, rows(model)),
            (branch_got, rows(model)),
            (stats, own_along),
            (other_stats, own_along),
        ],
        [((rows_here, model), f32, rows(model)), ((8, LANES), f32, fixed(8, LANES))],
        [],
    )
    ng_got = other_half(ng, ng_sent)
    if not two:
        ng = lax.dynamic_slice_in_dim(ng, own_from, rows_here, 0)
    grad_input, token_b = run(
        input_kernel,
        rows_here // BLOCK,
        at,
        [
            (residual, rows(model)),
            (cot, rows(model)),
            (ng, rows(model)),
            (ng_got, rows(model)),
            (gain_in, None),
        ],
        [((rows_here, model), f32, rows(model)), ((8, LANES), f32, fixed(8, LANES))],
        [],
    )

    if fast:
        kept, sent = late
        steps = [("fold", 2, [kept, hop(sent, "core")], 2, True), ("fold", 3, early, 1, False)]
        (kept, sent), (early,) = stage(at, steps)
        got = hop(sent, "line")
        early = [early] + [hop(early, k) for k in (1, 2, 3)]
        ((kept, *sent),) = stage(at, [("fold", 3, [kept, got], 4, True)], (ng,))
        got = [hop(a, k + 1) for k, a in enumerate(sent)]
        steps = [("fold", 3, [kept, *got], 1, True), ("join", 3, early)]
        (done,), (early,) = stage(at, steps, (token,))
        early = [early, hop(early, "line")]
        theirs = lax.ppermute(done[:, width:], "heads", swap)
        done = run(
            heads_kernel,
            1,
            at,
            [(done, None), (theirs, None)],
            [(done.shape, bf16, fixed(*done.shape))],
            [],
        )[0]
        done = [done] + [hop(done, k) for k in (1, 2, 3)]
        (done,), (early,) = stage(at, [("join", 3, done), ("join", 2, early)], (token_b,))
        grad_gate, grad_out_proj, token_c = run(
            early_kernel,
            1,
            at,
            [(early, None), (hop(early, "core"), None)],
            [((model, model), f32, fixed(model, model))] * 2
            + [((8, LANES), f32, fixed(8, LANES))],
            [],
        )
        ((done,),) = stage(at, [("join", 2, [done, hop(done, "line")])], (token_c,))
        shapes = [
            (model, width),
            (model, nstate2),
            (model, heads),
            (4, width),
            (width,),
            (width,),
            (model,),
            (4, nstate2),
            (nstate2,),
            (heads,),
            (heads,),
            (heads,),
        ]
        (
            grad_value,
            grad_state,
            grad_step,
            grad_vconv,
            grad_vshift,
            grad_ggain,
            grad_norm,
            grad_sconv,
            grad_sshift,
            grad_bias,
            grad_rate,
            grad_skip,
        ) = run(
            late_kernel,
            1,
            at,
            [(done, None), (hop(done, "core"), None)],
            [(shape, f32, fixed(*shape)) for shape in shapes],
            [big(model, LANES)],
        )
        return (
            mixed[None],
            grad_input[None],
            grad_norm,
            grad_gate,
            grad_value,
            grad_state,
            grad_step,
            grad_vconv,
            grad_vshift,
            grad_sconv,
            grad_sshift,
            grad_bias,
            grad_rate,
            grad_skip,
            grad_ggain,
            grad_out_proj,
        )
    grad_value, grad_state, grad_step, norm = late
    grad_gate, grad_value, grad_out_proj, grad_step, vec, head, grad_gain = lax.psum(
        (early_a, grad_value, early_b, grad_step, vec, head, grad_gain), "batch"
    )
    grad_state, svec, norm = lax.psum((grad_state, svec, norm), ("batch", "heads"))
    norm, ggrad = norm[0], grad_gain[0]
    return (
        mixed[None],
        grad_input[None],
        norm,
        grad_gate[:, :inner],
        grad_value[:, :inner],
        grad_state,
        grad_step[:, :heads],
        vec[:4, :inner],
        vec[4, :inner],
        svec[:4],
        svec[4],
        head[0, :heads],
        head[1, :heads],
        head[2, :heads],
        ggrad[:inner],
        grad_out_proj[:inner],
    )


def solution(mesh):
    return jax.shard_map(
        per_device,
        mesh=mesh,
        in_specs=(
            P("batch", "heads", None),
            P(),
            P(None, "heads"),
            P(None, "heads"),
            P(),
            P(None, "heads"),
            P(None, "heads"),
            P("heads"),
            P(),
            P(),
            P("heads"),
            P("heads"),
            P("heads"),
            P("heads"),
            P("heads", None),
            P("batch", "heads", None),
        ),
        out_specs=(
            P("batch", "heads", None),
            P("batch", "heads", None),
            P(),
            P(None, "heads"),
            P(None, "heads"),
            P(),
            P(None, "heads"),
            P(None, "heads"),
            P("heads"),
            P(),
            P(),
            P("heads"),
            P("heads"),
            P("heads"),
            P("heads"),
            P("heads", None),
        ),
        check_vma=False,
    )
```

```python
import functools

import jax
import jax.numpy as jnp
from jax import lax
from jax.experimental import pallas as pl
from jax.experimental.pallas import tpu as pltpu
from jax.sharding import PartitionSpec as P

EPSILON = 1e-05
HIGHEST = lax.Precision.HIGHEST
BLOCK = 256
CHUNK = 128
LANES = 128
HALF = LANES // 2
QUAD = 2 * LANES
LOG2E = 1.4426950408889634
f32 = jnp.float32
bf16 = jnp.bfloat16


def dot(left, right, over=((1,), (0,)), precision=None):
    return lax.dot_general(
        left, right, (over, ((), ())), preferred_element_type=f32, precision=precision
    )


TN = ((0,), (0,))
NT = ((1,), (1,))


def sigmoid(v):
    return 0.5 * jnp.tanh(0.5 * v) + 0.5


def silu(v):
    half = 0.5 * v
    return half + half * jnp.tanh(half)


def silu_slope(v):
    half = 0.5 * v
    t = jnp.tanh(half)
    out = half + half * t
    sig = 0.5 + 0.5 * t
    return out, sig + out * (1.0 - sig)


def causal_back(buf, slab, r0, grad, pre, taps, extra):
    buf[slab, pl.ds(r0, CHUNK), :] = grad
    lanes = slice(slab * LANES, (slab + 1) * LANES)
    pre = pre.astype(f32)
    out, rows = 0.0, []
    for tap in range(4):
        moved = grad if tap == 3 else buf[slab, pl.ds(r0 + 3 - tap, CHUNK), :]
        out = out + taps[tap : tap + 1, lanes].astype(f32) * moved
        rows.append(jnp.sum(pre * moved, axis=0, keepdims=True))
    rows.append(jnp.sum(grad, axis=0, keepdims=True))
    rows += [extra, jnp.zeros((2, LANES), f32)]
    return out, jnp.concatenate(rows, axis=0)


def split(v):
    high = v.astype(bf16)
    return jnp.concatenate([high, (v - high.astype(f32)).astype(bf16)], axis=1)


def lower_mask(rows):
    return lax.broadcasted_iota(jnp.int32, (rows, rows), 0) >= lax.broadcasted_iota(
        jnp.int32, (rows, rows), 1
    )


def chunk_mask(strict=False):
    row = lax.broadcasted_iota(jnp.int32, (BLOCK, BLOCK), 0)
    column = lax.broadcasted_iota(jnp.int32, (BLOCK, BLOCK), 1)
    ordered = row > column if strict else row >= column
    return (ordered & (row // CHUNK == column // CHUNK)).astype(bf16)


def block_scalars(z, log_rate, spread):
    step = jnp.maximum(z, 0.0) + jnp.log1p(jnp.exp(-jnp.abs(z)))
    rate = -jnp.exp(log_rate)
    decay = jnp.where(lax.broadcasted_iota(jnp.int32, (1, LANES), 1) < 32, step * (rate * LOG2E), 0.0)
    high = decay.astype(bf16).astype(f32)
    middle = (decay - high).astype(bf16).astype(f32)
    packed = high + pltpu.roll(middle, 32, 1) + pltpu.roll(decay - high - middle, 64, 1)
    sums = dot(chunk_mask(), packed.astype(bf16))
    running = sums + pltpu.roll(sums, LANES - 32, 1) + pltpu.roll(sums, LANES - 64, 1)
    last = [running[r + CHUNK - 1 : r + CHUNK, :] for r in range(0, BLOCK, CHUNK)]
    tail = [jnp.exp2(v - running[k * CHUNK : (k + 1) * CHUNK, :]) for k, v in enumerate(last)]
    tail = step * jnp.concatenate(tail, axis=0)
    wide = dot(jnp.concatenate([split(jnp.exp2(running)), split(tail)], axis=0), spread)
    return step, running, running - jnp.log2(step), wide[:BLOCK], wide[BLOCK:]


def causal(buf, slab, taps, shift):
    lanes = slice(slab * LANES, (slab + 1) * LANES)
    conv = shift[:, lanes].astype(f32)
    for tap in range(4):
        conv = conv + taps[tap : tap + 1, lanes].astype(f32) * buf[slab, pl.ds(5 + tap, BLOCK), :]
    return conv


def chunk_scores(b_rows, c_rows):
    n = b_rows.shape[1]
    b, c = split(b_rows), split(c_rows)
    left = jnp.concatenate([c, c[:, :n]], axis=1)
    right = jnp.concatenate([b[:, :n], b[:, :n], b[:, n:]], axis=1)
    return b, c, dot(left, right, NT)


def quad_mixing(scores, running, shifted_t, quad, mask):
    factors, mixes = [], []
    for head in range(4 * quad, 4 * quad + 4):
        spread = running[:, head : head + 1] - shifted_t[head : head + 1, :]
        factors.append(jnp.exp2(jnp.where(mask, spread, -1e30)))
        mixes.append((scores * factors[-1]).astype(bf16))
    return factors, mixes


def heads_apart(left, right):
    lane = lax.broadcasted_iota(jnp.int32, (1, LANES), 1)
    first = (lane < HALF).astype(bf16)
    zero = jnp.zeros(left.shape, bf16)
    rows = [jnp.concatenate([left * m, zero], axis=1) for m in (first, 1 - first)]
    rows += [jnp.concatenate([zero, right * m], axis=1) for m in (first, 1 - first)]
    return jnp.concatenate(rows, axis=0)


def forward_kernel(
    half_blocks,
    at_ref,
    own_ref,
    other_ref,
    gain_ref,
    gate_w,
    value_w,
    state_w,
    step_w,
    vconv_ref,
    vshift_ref,
    sconv_ref,
    sshift_ref,
    sbias_ref,
    rate_ref,
    skip_ref,
    ggain_ref,
    spread_ref,
    normed_ref,
    g_ref,
    y_ref,
    gg_ref,
    low_ref,
    slope_ref,
    vp_ref,
    as_ref,
    sp_ref,
    z_ref,
    sin_ref,
    sq_ref,
    step_ref,
    running_ref,
    shifted_ref,
    grownx,
    tailx,
    vbuf,
    sbuf,
    state,
    carried,
    values,
    vtail,
):
    step_at = pl.program_id(0)
    pairs = vbuf.shape[0]
    nstate = state.shape[0]

    @pl.when(step_at == 0)
    def _():
        state[...] = jnp.zeros_like(state)
        for buf in (vbuf, sbuf):
            buf[:, 0:8, :] = jnp.zeros((buf.shape[0], 8, LANES), f32)

    mine = (step_at // half_blocks) == at_ref[0]
    rows = jnp.where(mine, own_ref[...], other_ref[...]).astype(f32)
    scale = lax.rsqrt(jnp.mean(rows * rows, axis=1, keepdims=True) + EPSILON)
    normed = (rows * scale * gain_ref[...].astype(f32)).astype(bf16)
    normed_ref[...] = normed
    z = dot(normed, step_w[...]) + sbias_ref[...]
    z_ref[...] = z
    for out, buf, w in ((sp_ref, sbuf, state_w), (vp_ref, vbuf, value_w)):
        pre = dot(normed, w[...])
        out[...] = pre.astype(bf16)
        for slab in range(buf.shape[0]):
            buf[slab, 8:, :] = pre[:, slab * LANES : (slab + 1) * LANES]
    g_ref[...] = dot(normed, gate_w[...])

    step, running, shifted, grownx[...], tailx[...] = block_scalars(z, rate_ref[...], spread_ref[...])
    step_ref[...] = step
    running_ref[...] = running
    shifted_ref[...] = shifted
    chunks = range(BLOCK // CHUNK)
    states = []
    for slab in range(sbuf.shape[0]):
        conv = causal(sbuf, slab, sconv_ref, sshift_ref)
        as_ref[:, slab * LANES : (slab + 1) * LANES] = conv
        states.append(silu(conv))
    for pair in range(pairs):
        lanes = slice(pair * LANES, (pair + 1) * LANES)
        out, slope = silu_slope(causal(vbuf, pair, vconv_ref, vshift_ref))
        slope_ref[:, lanes] = slope.astype(bf16)
        values[:, lanes] = out
        low_ref[:, lanes] = out.astype(bf16)
        vtail[:, lanes] = (out * tailx[:, lanes]).astype(bf16)
    parts = []
    for chunk in chunks:
        here = slice(chunk * CHUNK, (chunk + 1) * CHUNK)
        b_two, c_two, scores = chunk_scores(*(v[here] for v in states))
        parts.append(scores)
        before = state[...].astype(bf16)
        sin_ref[chunk, :, :] = before
        carried[here, :] = dot(c_two[:, :nstate], before)
        last = grownx[(chunk + 1) * CHUNK - 1 : (chunk + 1) * CHUNK, :]
        state[...] = last * state[...] + dot(b_two[:, :nstate], vtail[here, :], TN)
    mask = lower_mask(CHUNK)
    for chunk in chunks:
        here = slice(chunk * CHUNK, (chunk + 1) * CHUNK)
        run = running[here]
        run_t = shifted[here].T
        squares = jnp.zeros((CHUNK, LANES), f32)
        for quad in range(pairs // 2):
            _, mixes = quad_mixing(parts[chunk], run, run_t, quad, mask)
            sides = [slice((2 * quad + k) * LANES, (2 * quad + k + 1) * LANES) for k in range(2)]
            both = dot(
                jnp.concatenate(mixes, axis=1), heads_apart(*(low_ref[here, lanes] for lanes in sides))
            )
            for k, lanes in enumerate(sides):
                scanned = both[:, k * LANES : (k + 1) * LANES]
                scanned = scanned + grownx[here, lanes] * carried[here, lanes]
                scanned = scanned + skip_ref[:, lanes] * values[here, lanes]
                y_ref[here, lanes] = scanned
                gated = scanned * silu(g_ref[here, lanes])
                gg_ref[here, lanes] = (gated * ggain_ref[:, lanes].astype(f32)).astype(bf16)
                squares = squares + gated * gated
        sq_ref[:, here] = dot(jnp.ones((8, LANES), f32), squares, NT, HIGHEST)
    for buf in (vbuf, sbuf):
        buf[:, 0:8, :] = buf[:, BLOCK : BLOCK + 8, :]


def stats_kernel(at_ref, cot_ref, gg_ref, sq_ref, out_w, og_ref, stats_ref):
    og = dot(cot_ref[...], out_w[...], NT)
    og_ref[...] = og
    prod = (og * gg_ref[...].astype(f32)).astype(bf16)
    dots = dot(jnp.ones((8, prod.shape[1]), bf16), prod, NT)
    row = lax.broadcasted_iota(jnp.int32, dots.shape, 0)
    stats_ref[...] = jnp.where(row == 0, sq_ref[...], dots)


def bring_kernel(at_ref, *refs):
    count = len(refs) // 2
    for src, dst in zip(refs[:count], refs[count:]):
        dst[...] = src[...]


def branch_kernel(half_blocks, at_ref, gg_ref, out_w, own_ref, other_ref):
    mine = (pl.program_id(0) // half_blocks) == at_ref[0]
    rows = dot(gg_ref[...], out_w[...]).astype(bf16)

    @pl.when(mine)
    def _():
        own_ref[...] = rows

    @pl.when(jnp.logical_not(mine))
    def _():
        other_ref[...] = rows


def gate_back_kernel(at_ref, dg_ref, gate_w, out_ref):
    out_ref[...] = dot(dg_ref[...], gate_w[...], NT)


def picked(cut, early, late):
    return jnp.where(pl.program_id(0) < cut, early[...], late[...])


def normed_grad_kernel(half_blocks, cut, at_ref, from_gate, *refs):
    lows, (value_w, state_w, step_w, own_ref, other_ref) = refs[:6], refs[6:]
    dv, ds, dz = (picked(cut, a, b) for a, b in zip(lows[:3], lows[3:]))
    mine = (pl.program_id(0) // half_blocks) == at_ref[0]
    rows = (
        from_gate[...]
        + dot(dv, value_w[...], NT)
        + dot(ds, state_w[...], NT)
        + dot(dz, step_w[...], NT)
    ).astype(bf16)

    @pl.when(mine)
    def _():
        own_ref[...] = rows

    @pl.when(jnp.logical_not(mine))
    def _():
        other_ref[...] = rows


def row_sums(grads, weights):
    prod = (grads * weights.astype(f32)).astype(bf16)
    return dot(jnp.ones((8, prod.shape[1]), bf16), prod, NT)


def emit(at_ref, parts, outs):
    half = outs[0].shape[0]
    for j, out in enumerate(outs):
        rows = pl.ds(pl.multiple_of((at_ref[1] ^ j) * half, LANES), half)
        left = 0
        for part in parts:
            out[:, left : left + part.shape[1]] = part[rows, :].astype(out.dtype)
            left += part.shape[1]


def row_column(rows):
    return jnp.concatenate([rows, jnp.zeros((LANES - rows.shape[0], BLOCK), f32)], axis=0).T


def mixed_kernel(inner_all, at_ref, rows_ref, own_ref, other_ref, here_ref, there_ref, out_ref, token_ref):
    token_ref[...] = jnp.zeros_like(token_ref)
    sums = here_ref[...] + there_ref[...]
    scale = row_column(lax.rsqrt(sums / inner_all + EPSILON))[:, 0:1]
    branch = own_ref[...].astype(f32) + other_ref[...].astype(f32)
    out_ref[...] = rows_ref[...].astype(f32) + scale * branch


def input_kernel(at_ref, rows_ref, cot_ref, own_ref, other_ref, gain_ref, out_ref, token_ref):
    token_ref[...] = jnp.zeros_like(token_ref)
    rows = rows_ref[...].astype(f32)
    scale = lax.rsqrt(jnp.mean(rows * rows, axis=1, keepdims=True) + EPSILON)
    pulled = (own_ref[...].astype(f32) + other_ref[...].astype(f32)) * gain_ref[...].astype(f32)
    inner = jnp.mean(pulled * rows, axis=1, keepdims=True) * (scale * scale * scale)
    out_ref[...] = cot_ref[...].astype(f32) + scale * pulled - rows * inner


def gate_kernel(
    half_blocks,
    inner_all,
    fast,
    at_ref,
    own_ref,
    other_ref,
    here_a,
    there_a,
    here_b,
    there_b,
    normed_ref,
    og_a,
    og_b,
    y_ref,
    g_ref,
    gg_ref,
    ggain_ref,
    gate_w,
    _,
    dg_ref,
    dy_ref,
    first_ref,
    second_ref,
    grad_gain_ref,
    norm_ref,
    scaled_ref,
    *scratch,
):
    step_at = pl.program_id(0)
    here = pl.ds(pl.multiple_of(step_at * BLOCK, BLOCK), BLOCK)
    pairs = og_a.shape[1] // LANES
    grad_gate, grad_out = scratch if fast else (first_ref, second_ref)

    @pl.when(step_at == 0)
    def _():
        grad_gain_ref[...] = jnp.zeros_like(grad_gain_ref)

    mine = (step_at // half_blocks) == at_ref[0]
    sums = jnp.where(mine, here_a[...] + there_a[...], here_b[...] + there_b[...])
    scale_row = lax.rsqrt(sums[0:1, :] / inner_all + EPSILON)
    pull_row = scale_row * scale_row * scale_row * sums[1:2, :] / inner_all
    columns = row_column(jnp.concatenate([scale_row, pull_row], axis=0))
    scale, pull = columns[:, 0:1], columns[:, 1:2]
    cot = jnp.where(mine, own_ref[...], other_ref[...]).astype(f32)
    scaled_ref[here, :] = (cot * scale).astype(bf16)
    for pair in range(pairs):
        lanes = slice(pair * LANES, (pair + 1) * LANES)
        og = jnp.where(mine, og_a[:, lanes], og_b[:, lanes]) * scale
        y = y_ref[:, lanes]
        g = g_ref[:, lanes]
        gate, slope = silu_slope(g)
        gated = y * gate
        grad_gain_ref[0:1, lanes] += jnp.sum(og * gated, axis=0, keepdims=True)
        gated_grad = ggain_ref[:, lanes].astype(f32) * og - gated * pull
        dy_ref[:, lanes] = (gated_grad * gate).astype(bf16)
        dg_ref[here, lanes] = (gated_grad * y * slope).astype(bf16)

    @pl.when(step_at == pl.num_programs(0) - 1)
    def _():
        grad_out[...] = dot(gg_ref[...], scaled_ref[...], TN)
        grad_gate[...] = dot(normed_ref[...], dg_ref[...], TN)
        norm_ref[...] = row_sums(grad_gate[...], gate_w[...])
        if fast:
            emit(at_ref, (grad_gate, grad_out), (first_ref, second_ref))


def weights_kernel(fast, at_ref, normed_ref, *refs):
    lows, refs = refs[:6], refs[6:]
    value_w, state_w, step_w, gain_ref, vec_ref, svec_ref, head_ref, ggain_ref, norm_ref = refs[:9]
    outs, acc = refs[9:-3], refs[-3:]
    if fast:
        pieces, outs, done_ref = outs[:4], outs[4:6], outs[6]
        total = pieces[0][...].astype(f32)
        for r in pieces[1:]:
            total = total + r[...].astype(f32)
        done_ref[...] = total.astype(bf16)
    for a, early, late in zip(acc, lows[:3], lows[3:]):
        a[...] = dot(normed_ref[...], jnp.concatenate([early[...], late[...]], axis=0), TN)
    norm = norm_ref[...]
    for a, w in zip(acc, (value_w, state_w, step_w)):
        norm = norm + row_sums(a[...], w[...])
    norm = norm / gain_ref[...].astype(f32)
    if fast:
        pack_vectors(acc[2], vec_ref, svec_ref, head_ref, ggain_ref, norm)
        emit(at_ref, acc, outs)
        return
    for o, a in zip(outs, acc):
        o[...] = a[...]
    outs[3][...] = norm


VEC_AT = 16
SVEC_AT = 24
HEAD_AT = 32


def pack_vectors(block, vec_ref, svec_ref, head_ref, ggain_ref, norm):
    model = block.shape[0]
    row = lax.broadcasted_iota(jnp.int32, (8, model), 0)
    vec = jnp.where(row == 5, ggain_ref[0:1, :], jnp.where(row == 6, norm[0:1, :], vec_ref[...]))

    def tall(v):
        return jnp.concatenate([v, jnp.zeros((8, model - v.shape[1]), f32)], axis=1)

    rows = jnp.concatenate(
        [
            jnp.zeros((VEC_AT, model), f32),
            vec,
            tall(svec_ref[...]),
            tall(head_ref[...]),
            jnp.zeros((LANES - HEAD_AT - 8, model), f32),
        ],
        axis=0,
    )
    lane = lax.broadcasted_iota(jnp.int32, (1, LANES), 1)
    full = jnp.where(lane < VEC_AT, block[...], rows.T)
    block[...] = carry_rest(jnp.where(lane < HALF, full, 0.0))


def carry_rest(full):
    high = full.astype(bf16).astype(f32)
    return high + pltpu.roll(full - high, HALF, 1)


def join_rest(block):
    lane = lax.broadcasted_iota(jnp.int32, (1, LANES), 1)
    return jnp.where(lane < HALF, block + pltpu.roll(block, HALF, 1), 0.0)


def fold_step(me, ins, outs, buf, vectors):
    width = buf.shape[1] - (LANES if vectors else 0)
    total = ins[0][:, :width].astype(f32)
    for r in ins[1:]:
        total = total + r[:, :width].astype(f32)
    buf[:, :width] = total.astype(bf16)
    if vectors:
        last = ins[0][:, width:].astype(f32)
        for r in ins[1:]:
            last = last + r[:, width:].astype(f32)
        buf[:, width:] = carry_rest(join_rest(last)).astype(bf16)
    rows = outs[0].shape[0]
    if rows == buf.shape[0]:
        left = 0
        for o in outs:
            o[...] = buf[:, left : left + o.shape[1]]
            left += o.shape[1]
        return
    for j, o in enumerate(outs):
        o[...] = buf[pl.ds(pl.multiple_of((me ^ j) * rows, 16), rows), :]


def join_step(me, ins, out):
    rows = ins[0].shape[0]
    count = out.shape[0] // rows
    left = 0
    for first in range(0, len(ins), count):
        right = left + ins[first].shape[1]
        for j, r in enumerate(ins[first : first + count]):
            out[pl.ds(pl.multiple_of((me ^ j) * rows, 16), rows), left:right] = r[...]
        left = right


def stage_kernel(plan, extra, at_ref, *refs):
    n_in = sum(count for _, _, count, _, _ in plan)
    ins, refs = refs[:n_in], refs[n_in + extra :]
    n_out = sum(count for _, _, _, count, _ in plan)
    outs, bufs = refs[:n_out], list(refs[n_out:])
    for kind, axis, take, give, vectors in plan:
        if kind != "join":
            fold_step(at_ref[axis if kind == "fold" else 0], ins[:take], outs[:give], bufs.pop(0), vectors)
        else:
            join_step(at_ref[axis], ins[:take], outs[0])
        ins, outs = ins[take:], outs[give:]


def stage(at, steps, after=()):
    plan, arrays, shapes, scratch = [], [], [], []
    for kind, axis, ins, *rest in steps:
        rows, width = ins[0].shape
        count, vectors = rest if rest else (1, False)
        if kind == "fold":
            shapes += [(rows // count, width)] * count
        elif kind == "part":
            shapes += [(rows, axis), (rows, width - axis)]
        else:
            widths = {a.shape[1] for a in ins}
            shapes.append((rows * len(ins) // len(widths), sum(widths)))
        if kind != "join":
            scratch.append(pltpu.VMEM((rows, width), bf16))
        plan.append((kind, axis, len(ins), count, vectors))
        arrays += ins
    out = call(
        functools.partial(stage_kernel, tuple(plan), len(after)),
        1,
        at,
        [(a, None) for a in arrays] + [(a, pl.BlockSpec(memory_space=pl.ANY)) for a in after],
        [(shape, bf16, pl.BlockSpec(shape, lambda i, a: (0, 0))) for shape in shapes],
        scratch,
    )
    out, results = list(out), []
    for _, _, _, give, _ in plan:
        results.append(out[:give])
        out = out[give:]
    return results


def heads_kernel(at_ref, done_ref, own_ref, other_ref, out_ref):
    start = done_ref.shape[1]
    state = own_ref.shape[1] - LANES
    out_ref[:, :start] = done_ref[...]
    sums = own_ref[:, :state].astype(f32) + other_ref[:, :state].astype(f32)
    out_ref[:, start : start + state] = sums.astype(bf16)
    lane = lax.broadcasted_iota(jnp.int32, (1, LANES), 1)
    shared = (lane == VEC_AT + 6) | ((lane >= SVEC_AT) & (lane < HEAD_AT))
    mine = join_rest(own_ref[:, state:].astype(f32))
    theirs = join_rest(other_ref[:, state:].astype(f32))
    out_ref[:, start + state :] = carry_rest(mine + jnp.where(shared, theirs, 0.0)).astype(bf16)


def halves_of(at_ref, own_ref, other_ref, left, right):
    rows = own_ref.shape[0]
    for j, ref in enumerate((own_ref, other_ref)):
        yield pl.ds(pl.multiple_of((at_ref[1] ^ j) * rows, LANES), rows), ref[:, left:right].astype(f32)


def early_kernel(at_ref, own_ref, other_ref, *outs):
    outs[-1][...] = jnp.zeros_like(outs[-1])
    left = 0
    for o in outs[:-1]:
        right = left + o.shape[1]
        for at, v in halves_of(at_ref, own_ref, other_ref, left, right):
            o[at, :] = v
        left = right


def late_kernel(at_ref, own_ref, other_ref, *refs):
    outs, block = refs[:-1], refs[-1]
    left = 0
    for o in (outs[0], outs[1], block):
        right = left + o.shape[1]
        for at, v in halves_of(at_ref, own_ref, other_ref, left, right):
            o[at, :] = v
        left = right
    full = join_rest(block[...])
    rows = full.T
    outs[2][...] = rows[: outs[2].shape[0]]
    vec, svec = rows[VEC_AT : VEC_AT + 8], rows[SVEC_AT : SVEC_AT + 8]
    head = rows[HEAD_AT : HEAD_AT + 8]
    vconv, vshift, ggain, norm, sconv, sshift, bias, rate, skip = outs[3:]
    vconv[...] = vec[:4]
    for o, row in ((vshift, vec[4:5]), (ggain, vec[5:6]), (norm, vec[6:7]), (sshift, svec[4:5])):
        o[...] = row[:, : o.shape[0]].reshape(o.shape)
    sconv[...] = svec[:4, : sconv.shape[1]]
    for j, o in enumerate((bias, rate, skip)):
        o[...] = head[j : j + 1, : o.shape[0]].reshape(o.shape)


def backward_kernel(
    size,
    from_row,
    carried_in,
    extra,
    at_ref,
    dy_ref,
    low_ref,
    slope_ref,
    vp_ref,
    as_ref,
    sp_ref,
    z_ref,
    step_ref,
    running_ref,
    shifted_ref,
    grownx,
    tailx,
    sin_ref,
    vconv_ref,
    sconv_ref,
    rate_ref,
    skip_ref,
    gather_ref,
    *refs,
):
    carries, refs = (refs[:6], refs[6:]) if carried_in else ((), refs)
    refs = refs[extra:]
    dvalue, dstates, dstep, dstate_out, dahalo, dshalo, grad_vconv_ref, grad_sconv_ref, grad_head_ref = refs[:9]
    dabuf, dsbuf, dstate, carried, pulled, ubuf, vtail, inner, outer = refs[9:]
    step_at = pl.program_id(0)
    nstate, width = dstate.shape
    pairs = width // LANES

    def row_at(start, count=CHUNK):
        return slice(from_row + start, from_row + start + count)


    @pl.when(step_at == 0)
    def _():
        if carried_in:
            dstate[...] = carries[0][...]
            dabuf[:, size:, :] = carries[1][...]
            dsbuf[:, size:, :] = carries[2][...]
            grad_vconv_ref[...] = carries[3][...]
            grad_sconv_ref[...] = carries[4][...]
            grad_head_ref[...] = carries[5][...]
        else:
            dstate[...] = jnp.zeros_like(dstate)
            for buf in (dabuf, dsbuf):
                buf[:, size:, :] = jnp.zeros((buf.shape[0], 8, LANES), f32)
            for ref in (grad_vconv_ref, grad_sconv_ref, grad_head_ref):
                ref[...] = jnp.zeros_like(ref)

    @pl.when(step_at > 0)
    def _():
        for buf in (dabuf, dsbuf):
            buf[:, size:, :] = buf[:, 0:8, :]

    chunks = [slice(r, r + CHUNK) for r in range(0, size, CHUNK)]
    zero_row = jnp.zeros((1, LANES), f32)
    rate = -jnp.exp(rate_ref[...])
    states, slopes = [], []
    for slab in range(2):
        out, slope = silu_slope(as_ref[row_at(0, size), slab * LANES : (slab + 1) * LANES])
        states.append(out)
        slopes.append(slope)
    for pair in range(pairs):
        lanes = slice(pair * LANES, (pair + 1) * LANES)
        there = (row_at(0, size), lanes)
        ubuf[:, lanes] = (dy_ref[there].astype(f32) * grownx[there]).astype(bf16)
    two = [chunk_scores(*(v[here] for v in states)) for here in chunks]
    helds, afters = [None] * len(chunks), [None] * len(chunks)
    for chunk in reversed(range(len(chunks))):
        here = chunks[chunk]
        b_two, c_two, _ = two[chunk]
        before = sin_ref[from_row // CHUNK + chunk, :, :]
        last = grownx[row_at(here.stop - 1, 1), :]
        grad = dstate[...]
        afters[chunk] = grad.astype(bf16)
        carried[here, :] = dot(c_two[:, :nstate], before)
        pulled[here, :] = dot(b_two[:, :nstate], afters[chunk])
        overlap = jnp.sum(before.astype(f32) * grad, axis=0, keepdims=True) * last
        overlap = jnp.broadcast_to(overlap, (8, width))
        tall = [split(overlap[:, p * LANES : (p + 1) * LANES]) for p in range(pairs)]
        held = dot(jnp.concatenate(tall, axis=1), gather_ref[...])[0:1]
        helds[chunk] = held[:, :LANES] + held[:, LANES:]
        dstate[...] = last * grad + dot(c_two[:, :nstate], ubuf[here, :], TN)

    mask = lower_mask(CHUNK)
    for chunk in reversed(range(len(chunks))):
        here = chunks[chunk]
        b_two, c_two, scores = two[chunk]
        rows_in = row_at(here.start)
        run = running_ref[rows_in, :]
        run_t = shifted_ref[rows_in, :].T
        dscores = jnp.zeros((CHUNK, CHUNK), f32)
        for quad in range(pairs // 2):
            factors, mixes = quad_mixing(scores, run, run_t, quad, mask)
            both = [slice((2 * quad + k) * LANES, (2 * quad + k + 1) * LANES) for k in range(2)]
            low = [low_ref[rows_in, lanes] for lanes in both]
            dy_low = [dy_ref[rows_in, lanes] for lanes in both]
            apart = heads_apart(*low)
            scanned = dot(jnp.concatenate(mixes, axis=1), apart)
            dsteps = dot(jnp.concatenate(mixes, axis=0), heads_apart(*dy_low), TN)
            for k, lanes in enumerate(both):
                pair = 2 * quad + k
                own = slice(k * LANES, (k + 1) * LANES)
                dmixing = dot(dy_low[k], apart[2 * k * CHUNK : 2 * (k + 1) * CHUNK, own], NT)
                dscores = dscores + dmixing[:, :CHUNK] * factors[2 * k]
                dscores = dscores + dmixing[:, CHUNK:] * factors[2 * k + 1]
                wide = slice(2 * pair * LANES, (2 * pair + 1) * LANES)
                wide_b = slice((2 * pair + 1) * LANES, (2 * pair + 2) * LANES)
                dy, values = dy_low[k].astype(f32), low[k].astype(f32)
                dvalues = dsteps[:, own]
                pulls = values * dvalues
                inside = dy * scanned[:, own] - pulls + ubuf[here, lanes].astype(f32) * carried[here, lanes]
                high = inside.astype(bf16)
                inner[here, wide] = high
                inner[here, wide_b] = (inside - high.astype(f32)).astype(bf16)
                tails, pull = tailx[rows_in, lanes], pulled[here, lanes]
                v = (values * tails).astype(bf16)
                vtail[here, lanes] = v
                outer[here, wide] = pulls.astype(bf16)
                outer[here, wide_b] = (v.astype(f32) * pull).astype(bf16)
                da = (dvalues + tails * pull + skip_ref[:, lanes] * dy) * slope_ref[rows_in, lanes].astype(f32)
                skips = jnp.sum(values * dy, axis=0, keepdims=True)
                dv, rows = causal_back(dabuf, pair, here.start, da, vp_ref[rows_in, lanes], vconv_ref, skips)
                grad_vconv_ref[:, lanes] += rows
                dvalue[here, lanes] = dv.astype(bf16)
        dlow = dscores.astype(bf16)
        drest = (dscores - dlow.astype(f32)).astype(bf16)
        b_rows, c_rows = b_two[:, :nstate], c_two[:, :nstate]
        cross = dot(
            jnp.concatenate([vtail[here, :], ubuf[here, :]], axis=0),
            jnp.concatenate([afters[chunk], sin_ref[from_row // CHUNK + chunk, :, :]], axis=0),
            NT,
        )
        db = cross[:CHUNK, :nstate] + dot(
            jnp.concatenate([dlow, dlow, drest], axis=0),
            jnp.concatenate([c_rows, c_two[:, nstate:], c_rows], axis=0),
            TN,
        )
        dc = cross[CHUNK:, nstate:] + dot(
            jnp.concatenate([dlow, dlow, drest], axis=1),
            jnp.concatenate([b_rows, b_two[:, nstate:], b_rows], axis=0),
        )
        for slab, d in enumerate((db, dc)):
            lanes = slice(slab * LANES, (slab + 1) * LANES)
            d = d * slopes[slab][here]
            dpre, rows = causal_back(dsbuf, slab, here.start, d, sp_ref[rows_in, lanes], sconv_ref, zero_row)
            grad_sconv_ref[:, lanes] += rows
            dstates[here, lanes] = dpre.astype(bf16)

    gathered = dot(jnp.concatenate([inner[...], outer[...]], axis=0), gather_ref[...])
    heads = [jnp.zeros((1, LANES), f32)] * 2
    for r in range(0, size, BLOCK):
        here = slice(r, r + BLOCK)
        sums, outs = gathered[here], gathered[size + r : size + r + BLOCK]
        ddecay = dot(chunk_mask(), split(sums[:, :LANES] + sums[:, LANES:]), TN)
        ddecay = ddecay[:, :LANES] + ddecay[:, LANES:]
        ddecay = ddecay + dot(chunk_mask(True), outs[:, LANES:].astype(bf16))
        held = [jnp.broadcast_to(helds[k // CHUNK], (CHUNK, LANES)) for k in range(r, r + BLOCK, CHUNK)]
        ddecay = ddecay + jnp.concatenate(held, axis=0)
        rows_in = row_at(r, BLOCK)
        step = step_ref[rows_in, :]
        direct = (outs[:, :LANES] + outs[:, LANES:]) / jnp.maximum(step, 1e-37)
        dz = (direct + ddecay * rate) * sigmoid(z_ref[rows_in, :])
        dstep[here, :] = dz.astype(bf16)
        heads[0] = heads[0] + jnp.sum(dz, axis=0, keepdims=True)
        heads[1] = heads[1] + jnp.sum(ddecay * step, axis=0, keepdims=True) * rate
    grad_head_ref[...] += jnp.concatenate([*heads, jnp.zeros((6, LANES), f32)], axis=0)

    @pl.when(step_at == pl.num_programs(0) - 1)
    def _():
        dstate_out[...] = dstate[...]
        vectors = grad_vconv_ref[...]
        tall = [split(vectors[:, p * LANES : (p + 1) * LANES]) for p in range(pairs)]
        skips = dot(jnp.concatenate(tall, axis=1), gather_ref[...])
        grad_head_ref[2:3, :] = skips[5:6, :LANES] + skips[5:6, LANES:]
        dahalo[...] = dabuf[:, 0:8, :]
        dshalo[...] = dsbuf[:, 0:8, :]


MIB = dict(
    forward_kernel=14,
    stats_kernel=8,
    branch_kernel=8,
    gate_kernel=12,
    backward_kernel=24,
    weights_kernel=14,
    normed_grad_kernel=12,
    mixed_kernel=8,
    input_kernel=8,
    early_kernel=10,
    late_kernel=10,
)
COST = dict(forward_kernel=4.5, backward_kernel=7, stats_kernel=1, branch_kernel=.6, gate_kernel=2.4, weights_kernel=1.2, normed_grad_kernel=1.2, mixed_kernel=1, input_kernel=1, early_kernel=3, late_kernel=3)


def whole(array):
    return pl.BlockSpec(array.shape, lambda i, at: (0,) * array.ndim)


def call(kernel, blocks, at, ins, outs, scratch, small=True):
    title = getattr(kernel, "func", kernel).__name__
    return pl.pallas_call(
        kernel,
        name=title,
        grid_spec=pltpu.PrefetchScalarGridSpec(
            num_scalar_prefetch=1,
            grid=(blocks,),
            in_specs=[whole(a) if s is None else s for a, s in ins],
            out_specs=[out[2] for out in outs],
            scratch_shapes=scratch,
        ),
        out_shape=[
            pltpu.VMEM(shape, dtype) if rest and rest[0] else jax.ShapeDtypeStruct(shape, dtype)
            for shape, dtype, _, *rest in outs
        ],
        cost_estimate=pl.CostEstimate(flops=int(COST.get(title, 1)*blocks * 10**9), bytes_accessed=0, transcendentals=0),
        compiler_params=pltpu.CompilerParams(
            dimension_semantics=("arbitrary",), vmem_limit_bytes=(MIB.get(title, 16) if small else 48) * 2**20
        ),
    )(at, *[a for a, _ in ins])


def per_device(
    residual_in,
    norm_gain,
    gate_proj,
    value_proj,
    state_proj,
    step_proj,
    value_conv,
    value_shift,
    state_conv,
    state_shift,
    step_bias,
    log_rate,
    skip_gain,
    gated_gain,
    out_proj,
    grad_out,
):
    parts = lax.axis_size("heads")
    two = parts == 2
    rows_here, model = residual_in.shape[1:]
    length = rows_here * parts
    inner = value_conv.shape[1]
    inner_all = inner * parts
    heads = step_bias.shape[0]
    head_width = inner // heads
    pad_heads = -heads % 4
    nheads = heads + pad_heads
    width = nheads * head_width
    nstate2 = state_conv.shape[1]
    blocks = length // BLOCK
    chunks = BLOCK // CHUNK
    half_blocks = rows_here // BLOCK if two else blocks

    def wide(a, axis):
        pads = [(0, 0)] * a.ndim
        pads[axis] = (0, width - inner)
        return jnp.pad(a, pads) if width > inner else a

    def lanes_of(a):
        return jnp.pad(a, [(0, 0)] * (a.ndim - 1) + [(0, LANES - a.shape[-1])])

    residual = residual_in[0]
    cot = grad_out[0]
    batch = lax.axis_size("batch")
    fast = two and batch == 16 and width == model and model % BLOCK == 0
    nstate = nstate2 // 2
    run = functools.partial(call, small=fast)
    place = lax.axis_index("batch").astype(jnp.int32)
    across = lax.axis_index("heads").astype(jnp.int32) if two else jnp.int32(0)
    own_from = lax.axis_index("heads").astype(jnp.int32) * rows_here
    at = jnp.stack([across, place & 1, (place >> 1) & 1, place >> 2, own_from])
    if two:
        swap = [(0, 1), (1, 0)]
        pair_of = lambda a: (a, lax.ppermute(a, "heads", swap))
        add_other = lambda a: lax.ppermute(a, "heads", swap)
    else:

        def pair_of(a):
            full = lax.all_gather(a, "heads", axis=0, tiled=True)
            return (full, full)

        add_other = lambda a: lax.psum(a, "heads") - a

    def hop(a, way):
        mask = {"core": 1, "line": 2}.get(way) or 4 * way
        return lax.ppermute(a, "batch", [(i, i ^ mask) for i in range(batch)])

    def bring(*arrays):
        if not fast:
            return arrays
        return run(
            bring_kernel,
            1,
            at,
            [(a, None) for a in arrays],
            [(a.shape, a.dtype, pl.BlockSpec(a.shape, lambda i, at: (0, 0)), True) for a in arrays],
            [],
        )

    own_rows, other_rows = pair_of(residual)
    own_cot, other_cot = pair_of(cot)

    gate_w, value_w = wide(gate_proj, 1), wide(value_proj, 1)
    out_w = wide(out_proj, 0)
    step_w = lanes_of(step_proj)
    gain_in = norm_gain[None, :]
    vconv, vshift = wide(value_conv, 1), wide(value_shift[None, :], 1)
    sshift = state_shift[None, :]
    sbias, rate = lanes_of(step_bias[None, :]), lanes_of(log_rate[None, :])
    skipx = wide(jnp.repeat(skip_gain, head_width)[None, :], 1)
    ggain = wide(gated_gain[None, :], 1)
    head_of = jnp.arange(width) // head_width
    spread = (jnp.arange(LANES)[:, None] == head_of[None, :]).astype(bf16)
    spread = jnp.concatenate([spread, spread], axis=0)
    first = head_of.reshape(-1, 1, LANES, 1) + jnp.arange(2).reshape(1, 2, 1, 1) * LANES
    gather = (jnp.arange(2 * LANES) == first).reshape(-1, 2 * LANES).astype(bf16)

    gate_w, value_w, state_proj, step_w, out_w, spread, gather = bring(
        gate_w, value_w, state_proj, step_w, out_w, spread, gather
    )
    gain_in, vconv, vshift, state_conv, sshift, sbias, rate, skipx, ggain = bring(
        gain_in, vconv, vshift, state_conv, sshift, sbias, rate, skipx, ggain
    )

    def own_block(i, a):
        return (jnp.clip(i - a[0] * half_blocks, 0, half_blocks - 1), 0)

    def other_block(i, a):
        return (jnp.clip(i - (1 - a[0]) * half_blocks, 0, half_blocks - 1), 0) if two else (0, 0)

    other_read = other_block if two else own_block

    def rows(n, index=lambda i, a: (i, 0)):
        return pl.BlockSpec((BLOCK, n), index)

    along = pl.BlockSpec((8, BLOCK), lambda i, a: (0, i))
    fixed = lambda *shape: pl.BlockSpec(shape, lambda i, a: (0,) * len(shape))
    states_spec = lambda index: pl.BlockSpec((chunks, nstate, width), index)
    big = lambda *shape: pltpu.VMEM(shape, f32)
    low = lambda *shape: pltpu.VMEM(shape, bf16)
    halves = [
        ((rows_here if two else length, model), bf16, rows(model, own_block)),
        ((rows_here if two else BLOCK, model), bf16, rows(model, other_block)),
    ]

    normed, g, y, gg, values, slope, vp, conv_s, sp, z, sin, sq, step, running, shifted, grownx, tailx = run(
        functools.partial(forward_kernel, half_blocks),
        blocks,
        at,
        [
            (own_rows, rows(model, own_block)),
            (other_rows, rows(model, other_read)),
            (gain_in, None),
            (gate_w, None),
            (value_w, None),
            (state_proj, None),
            (step_w, None),
            (vconv, None),
            (vshift, None),
            (state_conv, None),
            (sshift, None),
            (sbias, None),
            (rate, None),
            (skipx, None),
            (ggain, None),
            (spread, None),
        ],
        [
            *[
                (shape, dtype, spec, fast)
                for shape, dtype, spec in (
                    ((length, model), bf16, rows(model)),
                    ((length, width), f32, rows(width)),
                    ((length, width), f32, rows(width)),
                    ((length, width), bf16, rows(width)),
                    ((length, width), bf16, rows(width)),
                    ((length, width), bf16, rows(width)),
                    ((length, width), bf16, rows(width)),
                    ((length, nstate2), f32, rows(nstate2)),
                    ((length, nstate2), bf16, rows(nstate2)),
                    ((length, LANES), f32, rows(LANES)),
                    ((blocks * chunks, nstate, width), bf16, states_spec(lambda i, a: (i, 0, 0))),
                    ((8, length), f32, along),
                    ((length, LANES), f32, rows(LANES)),
                    ((length, LANES), f32, rows(LANES)),
                    ((length, LANES), f32, rows(LANES)),
                    ((length, width), f32, rows(width)),
                    ((length, width), f32, rows(width)),
                )
            ]
        ],
        [
            big(width // LANES, BLOCK + 8, LANES),
            big(nstate2 // LANES, BLOCK + 8, LANES),
            big(nstate, width),
            big(BLOCK, width),
            big(BLOCK, width),
            low(BLOCK, width),
        ],
    )
    def stats_of(cot_rows, theirs):
        first = (lambda a: (1 - a[0]) * half_blocks) if theirs else (lambda a: a[0] * half_blocks)
        count = cot_rows.shape[0]
        return run(
            stats_kernel,
            count // BLOCK,
            at,
            [
                (cot_rows, rows(model)),
                (gg, rows(width, lambda i, a: (first(a) + i, 0))),
                (sq, pl.BlockSpec((8, BLOCK), lambda i, a: (0, first(a) + i))),
                (out_w, None),
            ],
            [((count, width), f32, rows(width), fast), ((8, count), f32, along)],
            [],
        )

    og, stats = stats_of(own_cot, False)
    if two:
        og_b, stats_b = stats_of(other_cot, True)
        got_b, got = add_other(stats), add_other(stats_b)
    else:
        og_b, stats_b, got = og, stats, add_other(stats)
        got_b = got

    def own_along(i, a):
        return own_block(i, a)[::-1]

    def other_along(i, a):
        return other_read(i, a)[::-1]

    branch, branch_sent = run(
        functools.partial(branch_kernel, half_blocks),
        blocks,
        at,
        [(gg, rows(width)), (out_w, None)],
        halves,
        [],
    )

    def other_half(own, sent):
        if two:
            return lax.ppermute(sent, "heads", swap)
        total = lax.psum_scatter(own.astype(f32), "heads", scatter_dimension=0, tiled=True)
        mine = lax.dynamic_slice_in_dim(own, own_from, rows_here, 0).astype(f32)
        return total - mine

    branch_got = other_half(branch, branch_sent)
    if not two:
        branch = lax.dynamic_slice_in_dim(branch, own_from, rows_here, 0)
    if fast:
        pieces = [((model // 2, 2 * model), bf16, fixed(model // 2, 2 * model))] * 2
    else:
        pieces = [
            ((model, width), f32, fixed(model, width)),
            ((width, model), f32, fixed(width, model)),
        ]
    dg, dy, early_a, early_b, grad_gain, norm = run(
        functools.partial(gate_kernel, half_blocks, inner_all, fast),
        blocks,
        at,
        [
            (own_cot, rows(model, own_block)),
            (other_cot, rows(model, other_read)),
            (stats, pl.BlockSpec((8, BLOCK), own_along)),
            (got, pl.BlockSpec((8, BLOCK), own_along)),
            (stats_b, pl.BlockSpec((8, BLOCK), other_along)),
            (got_b, pl.BlockSpec((8, BLOCK), other_along)),
            (normed, None),
            (og, rows(width, own_block)),
            (og_b, rows(width, other_read)),
            (y, rows(width)),
            (g, rows(width)),
            (gg, None),
            (ggain, None),
            (gate_w, None),
            (branch, pl.BlockSpec(memory_space=pl.ANY)),
        ],
        [
            ((length, width), bf16, fixed(length, width), fast),
            ((length, width), bf16, rows(width), fast),
            *pieces,
            ((8, width), f32, fixed(8, width)),
            ((8, model), f32, fixed(8, model)),
        ],
        [low(length, model)] + ([big(model, width), big(width, model)] if fast else []),
    )

    def backward(start, count, carry, after=()):
        size = 2 * BLOCK if start % 2 == 0 and count % 2 == 0 else BLOCK
        size = count * BLOCK if fast else size
        steps, base = count * BLOCK // size, start * BLOCK // size

        def local(n):
            return pl.BlockSpec((size, n), lambda i, a: (steps - 1 - i, 0))

        def taken(array):
            if fast:
                return (array, None)
            shape = (size // CHUNK if array.ndim == 3 else size, *array.shape[1:])
            rest = (0,) * (array.ndim - 1)
            return (array, pl.BlockSpec(shape, lambda i, a: (base + steps - 1 - i, *rest)))

        slabs = [(width // LANES, 8, LANES), (nstate2 // LANES, 8, LANES)]
        vectors = [(nstate, width), *slabs, (8, width), (8, nstate2), (8, LANES)]
        out = run(
            functools.partial(
                backward_kernel, size, start * BLOCK if fast else 0, bool(carry), len(after)
            ),
            steps,
            at,
            [
                *[
                    taken(a)
                    for a in (dy, values, slope, vp, conv_s, sp, z, step, running, shifted, grownx, tailx, sin)
                ],
                (vconv, None),
                (state_conv, None),
                (rate, None),
                (skipx, None),
                (gather, None),
                *[(c, None) for c in carry],
                *[(a, pl.BlockSpec(memory_space=pl.ANY)) for a in after],
            ],
            [
                ((count * BLOCK, width), bf16, local(width)),
                ((count * BLOCK, nstate2), bf16, local(nstate2)),
                ((count * BLOCK, LANES), bf16, local(LANES)),
                *[(shape, f32, fixed(*shape)) for shape in vectors],
            ],
            [
                big(width // LANES, size + 8, LANES),
                big(nstate2 // LANES, size + 8, LANES),
                big(nstate, width),
                big(size, width),
                big(size, width),
                low(size, width),
                low(size, width),
                low(size, 2 * width),
                low(size, 2 * width),
            ],
        )
        return out[:3], out[3:]

    own_stats = along if two else pl.BlockSpec((8, BLOCK), lambda i, a: (0, i + a[4] // BLOCK))
    mixed, token = run(
        functools.partial(mixed_kernel, inner_all),
        rows_here // BLOCK,
        at,
        [
            (residual, rows(model)),
            (branch, rows(model)),
            (branch_got, rows(model)),
            (stats, own_stats),
            (got, own_stats),
        ],
        [((rows_here, model), f32, rows(model)), ((8, LANES), f32, fixed(8, LANES))],
        [],
    )
    from_gate = run(
        gate_back_kernel,
        blocks,
        at,
        [(dg, rows(width)), (gate_w, None)],
        [((length, model), f32, rows(model), fast)],
        [],
    )[0]
    cut = blocks // 2
    behind = ()
    if fast:
        steps = [("fold", 2, [early_a, hop(early_b, "core")], 2, False)]
        ((kept, sent),) = stage(at, steps, (from_gate,))
        early = [kept, hop(sent, "line")]
        behind = (kept,)
    low_b, carry = backward(cut, blocks - cut, (), behind)
    if fast:
        ((kept, *sent),) = stage(at, [("fold", 3, early, 4, False)])
        early = [kept] + [hop(a, k + 1) for k, a in enumerate(sent)]
        behind = (kept, branch_got)
    low_a, carry = backward(0, cut, carry, behind)
    vec, svec, head = carry[3:]
    early = early if fast else ()
    lows = [(a, rows(a.shape[1], lambda i, at: (jnp.minimum(i, cut - 1), 0))) for a in low_a]
    lows += [(a, rows(a.shape[1], lambda i, at: (jnp.maximum(i - cut, 0), 0))) for a in low_b]

    if fast:
        shape = (model // 2, width + nstate2 + LANES)
        pieces = [(shape, bf16, fixed(*shape))] * 2
        pieces.append((early[0].shape, bf16, fixed(*early[0].shape)))
    else:
        shapes = [(model, width), (model, nstate2), (model, LANES), (8, model)]
        pieces = [(shape, f32, fixed(*shape)) for shape in shapes]
    late = run(
        functools.partial(weights_kernel, fast),
        1,
        at,
        [
            (normed, None),
            *[(a, None) for a, _ in lows],
            (value_w, None),
            (state_proj, None),
            (step_w, None),
            (gain_in, None),
            (vec, None),
            (svec, None),
            (head, None),
            (grad_gain, None),
            (norm, None),
            *[(a, None) for a in early],
        ],
        pieces,
        [big(model, width), big(model, nstate2), big(model, LANES)],
    )
    ng, ng_sent = run(
        functools.partial(normed_grad_kernel, half_blocks, cut),
        blocks,
        at,
        [
            (from_gate, rows(model)),
            *lows,
            (value_w, None),
            (state_proj, None),
            (step_w, None),
        ],
        halves,
        [],
    )

    ng_got = other_half(ng, ng_sent)
    if not two:
        ng = lax.dynamic_slice_in_dim(ng, own_from, rows_here, 0)
    grad_input, token_b = run(
        input_kernel,
        rows_here // BLOCK,
        at,
        [
            (residual, rows(model)),
            (cot, rows(model)),
            (ng, rows(model)),
            (ng_got, rows(model)),
            (gain_in, None),
        ],
        [((rows_here, model), f32, rows(model)), ((8, LANES), f32, fixed(8, LANES))],
        [],
    )

    if fast:
        kept, sent, early = late
        ((kept, sent),) = stage(at, [("fold", 2, [kept, hop(sent, "core")], 2, True)])
        got = hop(sent, "line")
        early = [early] + [hop(early, k) for k in (1, 2, 3)]
        ((kept, *sent),) = stage(at, [("fold", 3, [kept, got], 4, True)], (ng,))
        got = [hop(a, k + 1) for k, a in enumerate(sent)]
        steps = [("part", width, [kept, *got], 2, True), ("join", 3, early)]
        (done, rest), (early,) = stage(at, steps, (token,))
        early = [early, hop(early, "line")]
        theirs = lax.ppermute(rest, "heads", swap)
        done = run(
            heads_kernel,
            1,
            at,
            [(done, None), (rest, None), (theirs, None)],
            [((rest.shape[0], width + rest.shape[1]), bf16, fixed(rest.shape[0], width + rest.shape[1]))],
            [],
        )[0]
        done = [done] + [hop(done, k) for k in (1, 2, 3)]
        (done,), (early,) = stage(at, [("join", 3, done), ("join", 2, early)], (token_b,))
        grad_gate, grad_out_proj, token_c = run(
            early_kernel,
            1,
            at,
            [(early, None), (hop(early, "core"), None)],
            [((model, model), f32, fixed(model, model))] * 2
            + [((8, LANES), f32, fixed(8, LANES))],
            [],
        )
        ((done,),) = stage(at, [("join", 2, [done, hop(done, "line")])], (token_c,))
        shapes = [
            (model, width),
            (model, nstate2),
            (heads, model),
            (4, width),
            (width,),
            (width,),
            (model,),
            (4, nstate2),
            (nstate2,),
            (heads,),
            (heads,),
            (heads,),
        ]
        (
            grad_value,
            grad_state,
            grad_step,
            grad_vconv,
            grad_vshift,
            grad_ggain,
            grad_norm,
            grad_sconv,
            grad_sshift,
            grad_bias,
            grad_rate,
            grad_skip,
        ) = run(
            late_kernel,
            1,
            at,
            [(done, None), (hop(done, "core"), None)],
            [(shape, f32, fixed(*shape)) for shape in shapes],
            [big(model, LANES)],
        )
        return (
            mixed[None],
            grad_input[None],
            grad_norm,
            grad_gate,
            grad_value,
            grad_state,
            grad_step.T,
            grad_vconv,
            grad_vshift,
            grad_sconv,
            grad_sshift,
            grad_bias,
            grad_rate,
            grad_skip,
            grad_ggain,
            grad_out_proj,
        )
    grad_value, grad_state, grad_step, norm = late
    grad_gate, grad_value, grad_out_proj, grad_step, vec, head, grad_gain = lax.psum(
        (early_a, grad_value, early_b, grad_step, vec, head, grad_gain), "batch"
    )
    grad_state, svec, norm = lax.psum((grad_state, svec, norm), ("batch", "heads"))
    norm, ggrad = norm[0], grad_gain[0]
    return (
        mixed[None],
        grad_input[None],
        norm,
        grad_gate[:, :inner],
        grad_value[:, :inner],
        grad_state,
        grad_step[:, :heads],
        vec[:4, :inner],
        vec[4, :inner],
        svec[:4],
        svec[4],
        head[0, :heads],
        head[1, :heads],
        head[2, :heads],
        ggrad[:inner],
        grad_out_proj[:inner],
    )


def solution(mesh):
    return jax.shard_map(
        per_device,
        mesh=mesh,
        in_specs=(
            P("batch", "heads", None),
            P(),
            P(None, "heads"),
            P(None, "heads"),
            P(),
            P(None, "heads"),
            P(None, "heads"),
            P("heads"),
            P(),
            P(),
            P("heads"),
            P("heads"),
            P("heads"),
            P("heads"),
            P("heads", None),
            P("batch", "heads", None),
        ),
        out_specs=(
            P("batch", "heads", None),
            P("batch", "heads", None),
            P(),
            P(None, "heads"),
            P(None, "heads"),
            P(),
            P(None, "heads"),
            P(None, "heads"),
            P("heads"),
            P(),
            P(),
            P("heads"),
            P("heads"),
            P("heads"),
            P("heads"),
            P("heads", None),
        ),
        check_vma=False,
    )
```

```python
import functools

import jax
import jax.numpy as jnp
from jax import lax
from jax.experimental import pallas as pl
from jax.experimental.pallas import tpu as pltpu
from jax.sharding import PartitionSpec as P

EPSILON = 1e-05
HIGHEST = lax.Precision.HIGHEST
BLOCK = 256
CHUNK = 128
LANES = 128
HALF = LANES // 2
QUAD = 2 * LANES
LOG2E = 1.4426950408889634
f32 = jnp.float32
bf16 = jnp.bfloat16


def dot(left, right, over=((1,), (0,)), precision=None):
    return lax.dot_general(
        left, right, (over, ((), ())), preferred_element_type=f32, precision=precision
    )


TN = ((0,), (0,))
NT = ((1,), (1,))


def sigmoid(v):
    return 0.5 * jnp.tanh(0.5 * v) + 0.5


def silu(v):
    half = 0.5 * v
    return half + half * jnp.tanh(half)


def silu_slope(v):
    half = 0.5 * v
    t = jnp.tanh(half)
    out = half + half * t
    sig = 0.5 + 0.5 * t
    return out, sig + out * (1.0 - sig)


def causal_back(buf, slab, r0, grad, pre, taps, extra):
    buf[slab, pl.ds(r0, CHUNK), :] = grad
    lanes = slice(slab * LANES, (slab + 1) * LANES)
    pre = pre.astype(f32)
    out, rows = 0.0, []
    for tap in range(4):
        moved = grad if tap == 3 else buf[slab, pl.ds(r0 + 3 - tap, CHUNK), :]
        out = out + taps[tap : tap + 1, lanes].astype(f32) * moved
        rows.append(jnp.sum(pre * moved, axis=0, keepdims=True))
    rows.append(jnp.sum(grad, axis=0, keepdims=True))
    rows += [extra, jnp.zeros((2, LANES), f32)]
    return out, jnp.concatenate(rows, axis=0)


def split(v):
    high = v.astype(bf16)
    return jnp.concatenate([high, (v - high.astype(f32)).astype(bf16)], axis=1)


def lower_mask(rows):
    return lax.broadcasted_iota(jnp.int32, (rows, rows), 0) >= lax.broadcasted_iota(
        jnp.int32, (rows, rows), 1
    )


def chunk_mask(strict=False):
    row = lax.broadcasted_iota(jnp.int32, (BLOCK, BLOCK), 0)
    column = lax.broadcasted_iota(jnp.int32, (BLOCK, BLOCK), 1)
    ordered = row > column if strict else row >= column
    return (ordered & (row // CHUNK == column // CHUNK)).astype(bf16)


def block_scalars(z, log_rate, spread):
    step = jnp.maximum(z, 0.0) + jnp.log1p(jnp.exp(-jnp.abs(z)))
    rate = -jnp.exp(log_rate)
    decay = jnp.where(lax.broadcasted_iota(jnp.int32, (1, LANES), 1) < 32, step * (rate * LOG2E), 0.0)
    high = decay.astype(bf16).astype(f32)
    middle = (decay - high).astype(bf16).astype(f32)
    packed = high + pltpu.roll(middle, 32, 1) + pltpu.roll(decay - high - middle, 64, 1)
    sums = dot(chunk_mask(), packed.astype(bf16))
    running = sums + pltpu.roll(sums, LANES - 32, 1) + pltpu.roll(sums, LANES - 64, 1)
    last = [running[r + CHUNK - 1 : r + CHUNK, :] for r in range(0, BLOCK, CHUNK)]
    tail = [jnp.exp2(v - running[k * CHUNK : (k + 1) * CHUNK, :]) for k, v in enumerate(last)]
    tail = step * jnp.concatenate(tail, axis=0)
    wide = dot(jnp.concatenate([split(jnp.exp2(running)), split(tail)], axis=0), spread)
    return step, running, running - jnp.log2(step), wide[:BLOCK], wide[BLOCK:]


def causal(buf, slab, taps, shift):
    lanes = slice(slab * LANES, (slab + 1) * LANES)
    conv = shift[:, lanes].astype(f32)
    for tap in range(4):
        conv = conv + taps[tap : tap + 1, lanes].astype(f32) * buf[slab, pl.ds(5 + tap, BLOCK), :]
    return conv


def chunk_scores(b_rows, c_rows):
    n = b_rows.shape[1]
    b, c = split(b_rows), split(c_rows)
    left = jnp.concatenate([c, c[:, :n]], axis=1)
    right = jnp.concatenate([b[:, :n], b[:, :n], b[:, n:]], axis=1)
    return b, c, dot(left, right, NT)


def quad_mixing(scores, running, shifted_t, quad, mask):
    factors, mixes = [], []
    for head in range(4 * quad, 4 * quad + 4):
        spread = running[:, head : head + 1] - shifted_t[head : head + 1, :]
        factors.append(jnp.exp2(jnp.where(mask, spread, -1e30)))
        mixes.append((scores * factors[-1]).astype(bf16))
    return factors, mixes


def heads_apart(left, right):
    lane = lax.broadcasted_iota(jnp.int32, (1, LANES), 1)
    first = (lane < HALF).astype(bf16)
    zero = jnp.zeros(left.shape, bf16)
    rows = [jnp.concatenate([left * m, zero], axis=1) for m in (first, 1 - first)]
    rows += [jnp.concatenate([zero, right * m], axis=1) for m in (first, 1 - first)]
    return jnp.concatenate(rows, axis=0)


def forward_kernel(
    half_blocks,
    at_ref,
    own_ref,
    other_ref,
    gain_ref,
    gate_w,
    value_w,
    state_w,
    step_w,
    vconv_ref,
    vshift_ref,
    sconv_ref,
    sshift_ref,
    sbias_ref,
    rate_ref,
    skip_ref,
    ggain_ref,
    spread_ref,
    normed_ref,
    g_ref,
    y_ref,
    gg_ref,
    low_ref,
    slope_ref,
    vp_ref,
    as_ref,
    sp_ref,
    z_ref,
    sin_ref,
    sq_ref,
    step_ref,
    running_ref,
    shifted_ref,
    grownx,
    tailx,
    vbuf,
    sbuf,
    state,
    carried,
    values,
    vtail,
):
    step_at = pl.program_id(0)
    pairs = vbuf.shape[0]
    nstate = state.shape[0]

    @pl.when(step_at == 0)
    def _():
        state[...] = jnp.zeros_like(state)
        for buf in (vbuf, sbuf):
            buf[:, 0:8, :] = jnp.zeros((buf.shape[0], 8, LANES), f32)

    mine = (step_at // half_blocks) == at_ref[0]
    rows = jnp.where(mine, own_ref[...], other_ref[...]).astype(f32)
    scale = lax.rsqrt(jnp.mean(rows * rows, axis=1, keepdims=True) + EPSILON)
    normed = (rows * scale * gain_ref[...].astype(f32)).astype(bf16)
    normed_ref[...] = normed
    z = dot(normed, step_w[...]) + sbias_ref[...]
    z_ref[...] = z
    for out, buf, w in ((sp_ref, sbuf, state_w), (vp_ref, vbuf, value_w)):
        pre = dot(normed, w[...])
        out[...] = pre.astype(bf16)
        for slab in range(buf.shape[0]):
            buf[slab, 8:, :] = pre[:, slab * LANES : (slab + 1) * LANES]
    g_ref[...] = dot(normed, gate_w[...])

    step, running, shifted, grownx[...], tailx[...] = block_scalars(z, rate_ref[...], spread_ref[...])
    step_ref[...] = step
    running_ref[...] = running
    shifted_ref[...] = shifted
    chunks = range(BLOCK // CHUNK)
    states = []
    for slab in range(sbuf.shape[0]):
        conv = causal(sbuf, slab, sconv_ref, sshift_ref)
        as_ref[:, slab * LANES : (slab + 1) * LANES] = conv
        states.append(silu(conv))
    for pair in range(pairs):
        lanes = slice(pair * LANES, (pair + 1) * LANES)
        out, slope = silu_slope(causal(vbuf, pair, vconv_ref, vshift_ref))
        slope_ref[:, lanes] = slope.astype(bf16)
        values[:, lanes] = out
        low_ref[:, lanes] = out.astype(bf16)
        vtail[:, lanes] = (out * tailx[:, lanes]).astype(bf16)
    parts = []
    for chunk in chunks:
        here = slice(chunk * CHUNK, (chunk + 1) * CHUNK)
        b_two, c_two, scores = chunk_scores(*(v[here] for v in states))
        parts.append(scores)
        before = state[...].astype(bf16)
        sin_ref[chunk, :, :] = before
        carried[here, :] = dot(c_two[:, :nstate], before)
        last = grownx[(chunk + 1) * CHUNK - 1 : (chunk + 1) * CHUNK, :]
        state[...] = last * state[...] + dot(b_two[:, :nstate], vtail[here, :], TN)
    mask = lower_mask(CHUNK)
    for chunk in chunks:
        here = slice(chunk * CHUNK, (chunk + 1) * CHUNK)
        run = running[here]
        run_t = shifted[here].T
        squares = jnp.zeros((CHUNK, LANES), f32)
        for quad in range(pairs // 2):
            _, mixes = quad_mixing(parts[chunk], run, run_t, quad, mask)
            sides = [slice((2 * quad + k) * LANES, (2 * quad + k + 1) * LANES) for k in range(2)]
            both = dot(
                jnp.concatenate(mixes, axis=1), heads_apart(*(low_ref[here, lanes] for lanes in sides))
            )
            for k, lanes in enumerate(sides):
                scanned = both[:, k * LANES : (k + 1) * LANES]
                scanned = scanned + grownx[here, lanes] * carried[here, lanes]
                scanned = scanned + skip_ref[:, lanes] * values[here, lanes]
                y_ref[here, lanes] = scanned
                gated = scanned * silu(g_ref[here, lanes])
                gg_ref[here, lanes] = (gated * ggain_ref[:, lanes].astype(f32)).astype(bf16)
                squares = squares + gated * gated
        sq_ref[:, here] = dot(jnp.ones((8, LANES), f32), squares, NT, HIGHEST)
    for buf in (vbuf, sbuf):
        buf[:, 0:8, :] = buf[:, BLOCK : BLOCK + 8, :]


def stats_kernel(at_ref, cot_ref, gg_ref, sq_ref, out_w, *refs):
    og_ref, stats_ref = refs[-2:]
    if len(refs) > 2:
        stats_ref[8:, :] = refs[0][...]
    og = dot(cot_ref[...], out_w[...], NT)
    og_ref[...] = og
    prod = (og * gg_ref[...].astype(f32)).astype(bf16)
    dots = dot(jnp.ones((8, prod.shape[1]), bf16), prod, NT)
    row = lax.broadcasted_iota(jnp.int32, dots.shape, 0)
    stats_ref[:8, :] = jnp.where(row == 0, sq_ref[...], dots)


def bring_kernel(at_ref, *refs):
    count = len(refs) // 2
    for src, dst in zip(refs[:count], refs[count:]):
        dst[...] = src[...]


def branch_kernel(half_blocks, at_ref, gg_ref, out_w, own_ref, other_ref):
    mine = (pl.program_id(0) // half_blocks) == at_ref[0]
    rows = dot(gg_ref[...], out_w[...]).astype(bf16)

    @pl.when(mine)
    def _():
        own_ref[...] = rows

    @pl.when(jnp.logical_not(mine))
    def _():
        other_ref[...] = rows


def gate_back_kernel(at_ref, dg_ref, gate_w, out_ref):
    out_ref[...] = dot(dg_ref[...], gate_w[...], NT)


def picked(cut, early, late):
    return jnp.where(pl.program_id(0) < cut, early[...], late[...])


def normed_grad_kernel(half_blocks, cut, at_ref, from_gate, *refs):
    lows, (value_w, state_w, step_w, own_ref, other_ref) = refs[:6], refs[6:]
    dv, ds, dz = (picked(cut, a, b) for a, b in zip(lows[:3], lows[3:]))
    mine = (pl.program_id(0) // half_blocks) == at_ref[0]
    rows = (
        from_gate[...]
        + dot(dv, value_w[...], NT)
        + dot(ds, state_w[...], NT)
        + dot(dz, step_w[...], NT)
    ).astype(bf16)

    @pl.when(mine)
    def _():
        own_ref[...] = rows

    @pl.when(jnp.logical_not(mine))
    def _():
        other_ref[...] = rows


def row_sums(grads, weights):
    prod = (grads * weights.astype(f32)).astype(bf16)
    return dot(jnp.ones((8, prod.shape[1]), bf16), prod, NT)


def emit(at_ref, parts, outs):
    half = outs[0].shape[0]
    for j, out in enumerate(outs):
        rows = pl.ds(pl.multiple_of((at_ref[1] ^ j) * half, LANES), half)
        left = 0
        for part in parts:
            out[:, left : left + part.shape[1]] = part[rows, :].astype(out.dtype)
            left += part.shape[1]


def row_column(rows):
    return jnp.concatenate([rows, jnp.zeros((LANES - rows.shape[0], BLOCK), f32)], axis=0).T


def mixed_kernel(inner_all, at_ref, rows_ref, own_ref, other_ref, here_ref, there_ref, out_ref, token_ref):
    token_ref[...] = jnp.zeros_like(token_ref)
    sums = here_ref[...] + there_ref[...]
    scale = row_column(lax.rsqrt(sums / inner_all + EPSILON))[:, 0:1]
    branch = own_ref[...].astype(f32) + other_ref[...].astype(f32)
    out_ref[...] = rows_ref[...].astype(f32) + scale * branch


def input_kernel(at_ref, rows_ref, cot_ref, own_ref, other_ref, gain_ref, out_ref, token_ref):
    token_ref[...] = jnp.zeros_like(token_ref)
    rows = rows_ref[...].astype(f32)
    scale = lax.rsqrt(jnp.mean(rows * rows, axis=1, keepdims=True) + EPSILON)
    pulled = (own_ref[...].astype(f32) + other_ref[...].astype(f32)) * gain_ref[...].astype(f32)
    inner = jnp.mean(pulled * rows, axis=1, keepdims=True) * (scale * scale * scale)
    out_ref[...] = cot_ref[...].astype(f32) + scale * pulled - rows * inner


def gate_kernel(
    half_blocks,
    inner_all,
    fast,
    at_ref,
    own_ref,
    other_ref,
    here_a,
    there_a,
    here_b,
    there_b,
    normed_ref,
    og_a,
    og_b,
    y_ref,
    g_ref,
    gg_ref,
    ggain_ref,
    gate_w,
    _,
    dg_ref,
    dy_ref,
    first_ref,
    second_ref,
    grad_gain_ref,
    norm_ref,
    scaled_ref,
    *scratch,
):
    step_at = pl.program_id(0)
    here = pl.ds(pl.multiple_of(step_at * BLOCK, BLOCK), BLOCK)
    pairs = og_a.shape[1] // LANES
    grad_gate, grad_out = scratch if fast else (first_ref, second_ref)

    @pl.when(step_at == 0)
    def _():
        grad_gain_ref[...] = jnp.zeros_like(grad_gain_ref)

    mine = (step_at // half_blocks) == at_ref[0]
    sums = jnp.where(mine, here_a[...] + there_a[...], here_b[...] + there_b[...])
    scale_row = lax.rsqrt(sums[0:1, :] / inner_all + EPSILON)
    pull_row = scale_row * scale_row * scale_row * sums[1:2, :] / inner_all
    columns = row_column(jnp.concatenate([scale_row, pull_row], axis=0))
    scale, pull = columns[:, 0:1], columns[:, 1:2]
    cot = jnp.where(mine, own_ref[...], other_ref[...]).astype(f32)
    scaled_ref[here, :] = (cot * scale).astype(bf16)
    for pair in range(pairs):
        lanes = slice(pair * LANES, (pair + 1) * LANES)
        og = jnp.where(mine, og_a[:, lanes], og_b[:, lanes]) * scale
        y = y_ref[:, lanes]
        g = g_ref[:, lanes]
        gate, slope = silu_slope(g)
        gated = y * gate
        grad_gain_ref[0:1, lanes] += jnp.sum(og * gated, axis=0, keepdims=True)
        gated_grad = ggain_ref[:, lanes].astype(f32) * og - gated * pull
        dy_ref[:, lanes] = (gated_grad * gate).astype(bf16)
        dg_ref[here, lanes] = (gated_grad * y * slope).astype(bf16)

    @pl.when(step_at == pl.num_programs(0) - 1)
    def _():
        grad_out[...] = dot(gg_ref[...], scaled_ref[...], TN)
        grad_gate[...] = dot(normed_ref[...], dg_ref[...], TN)
        norm_ref[...] = row_sums(grad_gate[...], gate_w[...])
        if fast:
            emit(at_ref, (grad_gate, grad_out), (first_ref, second_ref))


def partial_kernel(from_row, at_ref, normed_ref, *refs):
    for low, out in zip(refs[:3], refs[3:]):
        out[...] = dot(normed_ref[from_row:, :], low[...], TN)


def weights_kernel(fast, at_ref, normed_ref, *refs):
    lows, refs = refs[:6], refs[6:]
    value_w, state_w, step_w, gain_ref, vec_ref, svec_ref, head_ref, ggain_ref, norm_ref = refs[:9]
    outs, acc = refs[9:-3], refs[-3:]
    if fast:
        pieces, outs, done_ref = outs[:4], outs[4:6], outs[6]
        total = pieces[0][...].astype(f32)
        for r in pieces[1:]:
            total = total + r[...].astype(f32)
        done_ref[...] = total.astype(bf16)
    for a, low, rest in zip(acc, lows[:3], lows[3:]):
        a[...] = rest[...] + dot(normed_ref[: low.shape[0], :], low[...], TN)
    norm = norm_ref[...]
    for a, w in zip(acc, (value_w, state_w, step_w)):
        norm = norm + row_sums(a[...], w[...])
    norm = norm / gain_ref[...].astype(f32)
    if fast:
        pack_vectors(acc[2], vec_ref, svec_ref, head_ref, ggain_ref, norm)
        emit(at_ref, acc, outs)
        return
    for o, a in zip(outs, acc):
        o[...] = a[...]
    outs[3][...] = norm


VEC_AT = 16
SVEC_AT = 24
HEAD_AT = 32


def pack_vectors(block, vec_ref, svec_ref, head_ref, ggain_ref, norm):
    model = block.shape[0]
    row = lax.broadcasted_iota(jnp.int32, (8, model), 0)
    vec = jnp.where(row == 5, ggain_ref[0:1, :], jnp.where(row == 6, norm[0:1, :], vec_ref[...]))

    def tall(v):
        return jnp.concatenate([v, jnp.zeros((8, model - v.shape[1]), f32)], axis=1)

    rows = jnp.concatenate(
        [
            jnp.zeros((VEC_AT, model), f32),
            vec,
            tall(svec_ref[...]),
            tall(head_ref[...]),
            jnp.zeros((LANES - HEAD_AT - 8, model), f32),
        ],
        axis=0,
    )
    lane = lax.broadcasted_iota(jnp.int32, (1, LANES), 1)
    full = jnp.where(lane < VEC_AT, block[...], rows.T)
    block[...] = carry_rest(jnp.where(lane < HALF, full, 0.0))


def carry_rest(full):
    high = full.astype(bf16).astype(f32)
    return high + pltpu.roll(full - high, HALF, 1)


def join_rest(block):
    lane = lax.broadcasted_iota(jnp.int32, (1, LANES), 1)
    return jnp.where(lane < HALF, block + pltpu.roll(block, HALF, 1), 0.0)


def fold_step(me, ins, outs, buf, vectors):
    width = buf.shape[1] - (LANES if vectors else 0)
    total = ins[0][:, :width].astype(f32)
    for r in ins[1:]:
        total = total + r[:, :width].astype(f32)
    buf[:, :width] = total.astype(bf16)
    if vectors:
        last = ins[0][:, width:].astype(f32)
        for r in ins[1:]:
            last = last + r[:, width:].astype(f32)
        buf[:, width:] = carry_rest(join_rest(last)).astype(bf16)
    rows = outs[0].shape[0]
    if rows == buf.shape[0]:
        left = 0
        for o in outs:
            o[...] = buf[:, left : left + o.shape[1]]
            left += o.shape[1]
        return
    for j, o in enumerate(outs):
        o[...] = buf[pl.ds(pl.multiple_of((me ^ j) * rows, 16), rows), :]


def join_step(me, ins, out):
    rows = ins[0].shape[0]
    count = out.shape[0] // rows
    if count == 1:
        out[...] = ins[0][...]
        return
    left = 0
    for first in range(0, len(ins), count):
        right = left + ins[first].shape[1]
        for j, r in enumerate(ins[first : first + count]):
            out[pl.ds(pl.multiple_of((me ^ j) * rows, 16), rows), left:right] = r[...]
        left = right


def stage_kernel(plan, extra, at_ref, *refs):
    n_in = sum(count for _, _, count, _, _ in plan)
    ins, refs = refs[:n_in], refs[n_in + extra :]
    n_out = sum(count for _, _, _, count, _ in plan)
    outs, bufs = refs[:n_out], list(refs[n_out:])
    for kind, axis, take, give, vectors in plan:
        if kind != "join":
            fold_step(at_ref[axis if kind == "fold" else 0], ins[:take], outs[:give], bufs.pop(0), vectors)
        else:
            join_step(at_ref[axis], ins[:take], outs[0])
        ins, outs = ins[take:], outs[give:]


def stage(at, steps, after=()):
    plan, arrays, shapes, scratch = [], [], [], []
    for kind, axis, ins, *rest in steps:
        rows, width = ins[0].shape
        count, vectors = rest if rest else (1, False)
        if kind == "fold":
            shapes += [(rows // count, width)] * count
        elif kind == "part":
            shapes += [(rows, axis), (rows, width - axis)]
        else:
            widths = {a.shape[1] for a in ins}
            shapes.append((rows * len(ins) // len(widths), sum(widths)))
        if kind != "join":
            scratch.append(pltpu.VMEM((rows, width), bf16))
        plan.append((kind, axis, len(ins), count, vectors))
        arrays += ins
    out = call(
        functools.partial(stage_kernel, tuple(plan), len(after)),
        1,
        at,
        [(a, None) for a in arrays] + [(a, pl.BlockSpec(memory_space=pl.ANY)) for a in after],
        [(shape, bf16, pl.BlockSpec(shape, lambda i, a: (0, 0))) for shape in shapes],
        scratch,
    )
    out, results = list(out), []
    for _, _, _, give, _ in plan:
        results.append(out[:give])
        out = out[give:]
    return results


def heads_kernel(at_ref, done_ref, own_ref, other_ref, out_ref):
    start = done_ref.shape[1]
    state = own_ref.shape[1] - LANES
    out_ref[:, :start] = done_ref[...]
    sums = own_ref[:, :state].astype(f32) + other_ref[:, :state].astype(f32)
    out_ref[:, start : start + state] = sums.astype(bf16)
    lane = lax.broadcasted_iota(jnp.int32, (1, LANES), 1)
    shared = (lane == VEC_AT + 6) | ((lane >= SVEC_AT) & (lane < HEAD_AT))
    mine = join_rest(own_ref[:, state:].astype(f32))
    theirs = join_rest(other_ref[:, state:].astype(f32))
    out_ref[:, start + state :] = carry_rest(mine + jnp.where(shared, theirs, 0.0)).astype(bf16)


def halves_of(at_ref, own_ref, other_ref, left, right):
    rows = own_ref.shape[0]
    for j, ref in enumerate((own_ref, other_ref)):
        yield pl.ds(pl.multiple_of((at_ref[1] ^ j) * rows, LANES), rows), ref[:, left:right].astype(f32)


def early_kernel(at_ref, own_ref, other_ref, *outs):
    outs[-1][...] = jnp.zeros_like(outs[-1])
    left = 0
    for o in outs[:-1]:
        right = left + o.shape[1]
        for at, v in halves_of(at_ref, own_ref, other_ref, left, right):
            o[at, :] = v
        left = right


def widen(piece, outs):
    left = 0
    for o in outs:
        right = left + o.shape[1]
        o[...] = piece[:, left:right].astype(f32)
        left = right


def place_kernel(at_ref, piece_ref, *refs):
    widen(piece_ref, refs[-3:-1])
    refs[-1][...] = jnp.zeros_like(refs[-1])


def late_kernel(at_ref, *refs):
    pieces, outs, block = refs[:4], refs[6:-1], refs[-1]
    widen(pieces[3], outs[:2])
    rows, right = pieces[0].shape
    for n, piece in enumerate(pieces):
        start = (at_ref[1] ^ (n // 2)) * 2 + (at_ref[2] ^ (n % 2))
        at = pl.ds(pl.multiple_of(start * rows, 16), rows)
        block[at, :] = piece[:, right - LANES :].astype(f32)
    full = join_rest(block[...])
    rows = full.T
    outs[2][...] = rows[: outs[2].shape[0]]
    vec, svec = rows[VEC_AT : VEC_AT + 8], rows[SVEC_AT : SVEC_AT + 8]
    head = rows[HEAD_AT : HEAD_AT + 8]
    vconv, vshift, ggain, norm, sconv, sshift, bias, rate, skip = outs[3:]
    vconv[...] = vec[:4]
    for o, row in ((vshift, vec[4:5]), (ggain, vec[5:6]), (norm, vec[6:7]), (sshift, svec[4:5])):
        o[...] = row[:, : o.shape[0]].reshape(o.shape)
    sconv[...] = svec[:4, : sconv.shape[1]]
    for j, o in enumerate((bias, rate, skip)):
        o[...] = head[j : j + 1, : o.shape[0]].reshape(o.shape)


def backward_kernel(
    size,
    from_row,
    carried_in,
    extra,
    at_ref,
    dy_ref,
    low_ref,
    slope_ref,
    vp_ref,
    as_ref,
    sp_ref,
    z_ref,
    step_ref,
    running_ref,
    shifted_ref,
    grownx,
    tailx,
    sin_ref,
    vconv_ref,
    sconv_ref,
    rate_ref,
    skip_ref,
    gather_ref,
    *refs,
):
    carries, refs = (refs[:6], refs[6:]) if carried_in else ((), refs)
    refs = refs[extra:]
    dvalue, dstates, dstep, dstate_out, dahalo, dshalo, grad_vconv_ref, grad_sconv_ref, grad_head_ref = refs[:9]
    dabuf, dsbuf, dstate, carried, pulled, ubuf, vtail, inner, outer = refs[9:]
    step_at = pl.program_id(0)
    nstate, width = dstate.shape
    pairs = width // LANES

    def row_at(start, count=CHUNK):
        return slice(from_row + start, from_row + start + count)


    @pl.when(step_at == 0)
    def _():
        if carried_in:
            dstate[...] = carries[0][...]
            dabuf[:, size:, :] = carries[1][...]
            dsbuf[:, size:, :] = carries[2][...]
            grad_vconv_ref[...] = carries[3][...]
            grad_sconv_ref[...] = carries[4][...]
            grad_head_ref[...] = carries[5][...]
        else:
            dstate[...] = jnp.zeros_like(dstate)
            for buf in (dabuf, dsbuf):
                buf[:, size:, :] = jnp.zeros((buf.shape[0], 8, LANES), f32)
            for ref in (grad_vconv_ref, grad_sconv_ref, grad_head_ref):
                ref[...] = jnp.zeros_like(ref)

    @pl.when(step_at > 0)
    def _():
        for buf in (dabuf, dsbuf):
            buf[:, size:, :] = buf[:, 0:8, :]

    chunks = [slice(r, r + CHUNK) for r in range(0, size, CHUNK)]
    zero_row = jnp.zeros((1, LANES), f32)
    rate = -jnp.exp(rate_ref[...])
    states, slopes = [], []
    for slab in range(2):
        out, slope = silu_slope(as_ref[row_at(0, size), slab * LANES : (slab + 1) * LANES])
        states.append(out)
        slopes.append(slope)
    for pair in range(pairs):
        lanes = slice(pair * LANES, (pair + 1) * LANES)
        there = (row_at(0, size), lanes)
        ubuf[:, lanes] = (dy_ref[there].astype(f32) * grownx[there]).astype(bf16)
    two = [chunk_scores(*(v[here] for v in states)) for here in chunks]
    helds, afters = [None] * len(chunks), [None] * len(chunks)
    for chunk in reversed(range(len(chunks))):
        here = chunks[chunk]
        b_two, c_two, _ = two[chunk]
        before = sin_ref[from_row // CHUNK + chunk, :, :]
        last = grownx[row_at(here.stop - 1, 1), :]
        grad = dstate[...]
        afters[chunk] = grad.astype(bf16)
        carried[here, :] = dot(c_two[:, :nstate], before)
        pulled[here, :] = dot(b_two[:, :nstate], afters[chunk])
        overlap = jnp.sum(before.astype(f32) * grad, axis=0, keepdims=True) * last
        overlap = jnp.broadcast_to(overlap, (8, width))
        tall = [split(overlap[:, p * LANES : (p + 1) * LANES]) for p in range(pairs)]
        held = dot(jnp.concatenate(tall, axis=1), gather_ref[...])[0:1]
        helds[chunk] = held[:, :LANES] + held[:, LANES:]
        dstate[...] = last * grad + dot(c_two[:, :nstate], ubuf[here, :], TN)

    mask = lower_mask(CHUNK)
    for chunk in reversed(range(len(chunks))):
        here = chunks[chunk]
        b_two, c_two, scores = two[chunk]
        rows_in = row_at(here.start)
        run = running_ref[rows_in, :]
        run_t = shifted_ref[rows_in, :].T
        dscores = jnp.zeros((CHUNK, CHUNK), f32)
        for quad in range(pairs // 2):
            factors, mixes = quad_mixing(scores, run, run_t, quad, mask)
            both = [slice((2 * quad + k) * LANES, (2 * quad + k + 1) * LANES) for k in range(2)]
            low = [low_ref[rows_in, lanes] for lanes in both]
            dy_low = [dy_ref[rows_in, lanes] for lanes in both]
            apart = heads_apart(*low)
            scanned = dot(jnp.concatenate(mixes, axis=1), apart)
            dsteps = dot(jnp.concatenate(mixes, axis=0), heads_apart(*dy_low), TN)
            for k, lanes in enumerate(both):
                pair = 2 * quad + k
                own = slice(k * LANES, (k + 1) * LANES)
                dmixing = dot(dy_low[k], apart[2 * k * CHUNK : 2 * (k + 1) * CHUNK, own], NT)
                dscores = dscores + dmixing[:, :CHUNK] * factors[2 * k]
                dscores = dscores + dmixing[:, CHUNK:] * factors[2 * k + 1]
                wide = slice(2 * pair * LANES, (2 * pair + 1) * LANES)
                wide_b = slice((2 * pair + 1) * LANES, (2 * pair + 2) * LANES)
                dy, values = dy_low[k].astype(f32), low[k].astype(f32)
                dvalues = dsteps[:, own]
                pulls = values * dvalues
                inside = dy * scanned[:, own] - pulls + ubuf[here, lanes].astype(f32) * carried[here, lanes]
                high = inside.astype(bf16)
                inner[here, wide] = high
                inner[here, wide_b] = (inside - high.astype(f32)).astype(bf16)
                tails, pull = tailx[rows_in, lanes], pulled[here, lanes]
                v = (values * tails).astype(bf16)
                vtail[here, lanes] = v
                outer[here, wide] = pulls.astype(bf16)
                outer[here, wide_b] = (v.astype(f32) * pull).astype(bf16)
                da = (dvalues + tails * pull + skip_ref[:, lanes] * dy) * slope_ref[rows_in, lanes].astype(f32)
                skips = jnp.sum(values * dy, axis=0, keepdims=True)
                dv, rows = causal_back(dabuf, pair, here.start, da, vp_ref[rows_in, lanes], vconv_ref, skips)
                grad_vconv_ref[:, lanes] += rows
                dvalue[here, lanes] = dv.astype(bf16)
        dlow = dscores.astype(bf16)
        drest = (dscores - dlow.astype(f32)).astype(bf16)
        b_rows, c_rows = b_two[:, :nstate], c_two[:, :nstate]
        cross = dot(
            jnp.concatenate([vtail[here, :], ubuf[here, :]], axis=0),
            jnp.concatenate([afters[chunk], sin_ref[from_row // CHUNK + chunk, :, :]], axis=0),
            NT,
        )
        db = cross[:CHUNK, :nstate] + dot(
            jnp.concatenate([dlow, dlow, drest], axis=0),
            jnp.concatenate([c_rows, c_two[:, nstate:], c_rows], axis=0),
            TN,
        )
        dc = cross[CHUNK:, nstate:] + dot(
            jnp.concatenate([dlow, dlow, drest], axis=1),
            jnp.concatenate([b_rows, b_two[:, nstate:], b_rows], axis=0),
        )
        for slab, d in enumerate((db, dc)):
            lanes = slice(slab * LANES, (slab + 1) * LANES)
            d = d * slopes[slab][here]
            dpre, rows = causal_back(dsbuf, slab, here.start, d, sp_ref[rows_in, lanes], sconv_ref, zero_row)
            grad_sconv_ref[:, lanes] += rows
            dstates[here, lanes] = dpre.astype(bf16)

    gathered = dot(jnp.concatenate([inner[...], outer[...]], axis=0), gather_ref[...])
    heads = [jnp.zeros((1, LANES), f32)] * 2
    for r in range(0, size, BLOCK):
        here = slice(r, r + BLOCK)
        sums, outs = gathered[here], gathered[size + r : size + r + BLOCK]
        ddecay = dot(chunk_mask(), split(sums[:, :LANES] + sums[:, LANES:]), TN)
        ddecay = ddecay[:, :LANES] + ddecay[:, LANES:]
        ddecay = ddecay + dot(chunk_mask(True), outs[:, LANES:].astype(bf16))
        held = [jnp.broadcast_to(helds[k // CHUNK], (CHUNK, LANES)) for k in range(r, r + BLOCK, CHUNK)]
        ddecay = ddecay + jnp.concatenate(held, axis=0)
        rows_in = row_at(r, BLOCK)
        step = step_ref[rows_in, :]
        direct = (outs[:, :LANES] + outs[:, LANES:]) / jnp.maximum(step, 1e-37)
        dz = (direct + ddecay * rate) * sigmoid(z_ref[rows_in, :])
        dstep[here, :] = dz.astype(bf16)
        heads[0] = heads[0] + jnp.sum(dz, axis=0, keepdims=True)
        heads[1] = heads[1] + jnp.sum(ddecay * step, axis=0, keepdims=True) * rate
    grad_head_ref[...] += jnp.concatenate([*heads, jnp.zeros((6, LANES), f32)], axis=0)

    @pl.when(step_at == pl.num_programs(0) - 1)
    def _():
        dstate_out[...] = dstate[...]
        vectors = grad_vconv_ref[...]
        tall = [split(vectors[:, p * LANES : (p + 1) * LANES]) for p in range(pairs)]
        skips = dot(jnp.concatenate(tall, axis=1), gather_ref[...])
        grad_head_ref[2:3, :] = skips[5:6, :LANES] + skips[5:6, LANES:]
        dahalo[...] = dabuf[:, 0:8, :]
        dshalo[...] = dsbuf[:, 0:8, :]


MIB = dict(
    forward_kernel=11,
    stats_kernel=6,
    branch_kernel=6,
    gate_kernel=10,
    backward_kernel=17,
    weights_kernel=11,
    normed_grad_kernel=12,
    mixed_kernel=8,
    input_kernel=8,
    early_kernel=10,
    late_kernel=10,
    place_kernel=8,
    partial_kernel=8,
)
COST = dict(forward_kernel=4.5, backward_kernel=7, stats_kernel=1, branch_kernel=.6, gate_kernel=2.4, weights_kernel=1.2, normed_grad_kernel=1.2, mixed_kernel=1, input_kernel=1, early_kernel=3, late_kernel=3, place_kernel=1, partial_kernel=2)


def whole(array):
    return pl.BlockSpec(array.shape, lambda i, at: (0,) * array.ndim)


def call(kernel, blocks, at, ins, outs, scratch, small=True, aliases=()):
    title = getattr(kernel, "func", kernel).__name__
    return pl.pallas_call(
        kernel,
        name=title,
        grid_spec=pltpu.PrefetchScalarGridSpec(
            num_scalar_prefetch=1,
            grid=(blocks,),
            in_specs=[whole(a) if s is None else s for a, s in ins],
            out_specs=[out[2] for out in outs],
            scratch_shapes=scratch,
        ),
        out_shape=[
            pltpu.VMEM(shape, dtype) if rest and rest[0] else jax.ShapeDtypeStruct(shape, dtype)
            for shape, dtype, _, *rest in outs
        ],
        cost_estimate=pl.CostEstimate(flops=int(COST.get(title, 1)*blocks * 10**9), bytes_accessed=0, transcendentals=0),
        input_output_aliases=dict(aliases),
        compiler_params=pltpu.CompilerParams(
            dimension_semantics=("arbitrary",), vmem_limit_bytes=(MIB.get(title, 16) if small else 48) * 2**20
        ),
    )(at, *[a for a, _ in ins])


def per_device(
    residual_in,
    norm_gain,
    gate_proj,
    value_proj,
    state_proj,
    step_proj,
    value_conv,
    value_shift,
    state_conv,
    state_shift,
    step_bias,
    log_rate,
    skip_gain,
    gated_gain,
    out_proj,
    grad_out,
):
    parts = lax.axis_size("heads")
    two = parts == 2
    rows_here, model = residual_in.shape[1:]
    length = rows_here * parts
    inner = value_conv.shape[1]
    inner_all = inner * parts
    heads = step_bias.shape[0]
    head_width = inner // heads
    pad_heads = -heads % 4
    nheads = heads + pad_heads
    width = nheads * head_width
    nstate2 = state_conv.shape[1]
    blocks = length // BLOCK
    chunks = BLOCK // CHUNK
    half_blocks = rows_here // BLOCK if two else blocks

    def wide(a, axis):
        pads = [(0, 0)] * a.ndim
        pads[axis] = (0, width - inner)
        return jnp.pad(a, pads) if width > inner else a

    def lanes_of(a):
        return jnp.pad(a, [(0, 0)] * (a.ndim - 1) + [(0, LANES - a.shape[-1])])

    residual = residual_in[0]
    cot = grad_out[0]
    batch = lax.axis_size("batch")
    fast = two and batch == 16 and width == model and model % BLOCK == 0
    nstate = nstate2 // 2
    run = functools.partial(call, small=fast)
    place = lax.axis_index("batch").astype(jnp.int32)
    across = lax.axis_index("heads").astype(jnp.int32) if two else jnp.int32(0)
    own_from = lax.axis_index("heads").astype(jnp.int32) * rows_here
    at = jnp.stack([across, place & 1, (place >> 1) & 1, place >> 2, own_from])
    if two:
        swap = [(0, 1), (1, 0)]
        pair_of = lambda a: (a, lax.ppermute(a, "heads", swap))
        add_other = lambda a: lax.ppermute(a, "heads", swap)
    else:

        def pair_of(a):
            full = lax.all_gather(a, "heads", axis=0, tiled=True)
            return (full, full)

        add_other = lambda a: lax.psum(a, "heads") - a

    def hop(a, way):
        mask = {"core": 1, "line": 2}.get(way) or 4 * way
        return lax.ppermute(a, "batch", [(i, i ^ mask) for i in range(batch)])

    def bring(*arrays):
        if not fast:
            return arrays
        return run(
            bring_kernel,
            1,
            at,
            [(a, None) for a in arrays],
            [(a.shape, a.dtype, pl.BlockSpec(a.shape, lambda i, at: (0, 0)), True) for a in arrays],
            [],
        )

    own_rows, other_rows = pair_of(residual)
    own_cot, other_cot = pair_of(cot)

    gate_w, value_w = wide(gate_proj, 1), wide(value_proj, 1)
    out_w = wide(out_proj, 0)
    step_w = lanes_of(step_proj)
    gain_in = norm_gain[None, :]
    vconv, vshift = wide(value_conv, 1), wide(value_shift[None, :], 1)
    sshift = state_shift[None, :]
    sbias, rate = lanes_of(step_bias[None, :]), lanes_of(log_rate[None, :])
    skipx = wide(jnp.repeat(skip_gain, head_width)[None, :], 1)
    ggain = wide(gated_gain[None, :], 1)
    head_of = jnp.arange(width) // head_width
    spread = (jnp.arange(LANES)[:, None] == head_of[None, :]).astype(bf16)
    spread = jnp.concatenate([spread, spread], axis=0)
    first = head_of.reshape(-1, 1, LANES, 1) + jnp.arange(2).reshape(1, 2, 1, 1) * LANES
    gather = (jnp.arange(2 * LANES) == first).reshape(-1, 2 * LANES).astype(bf16)

    gate_w, value_w, state_proj, step_w, out_w, spread, gather = bring(
        gate_w, value_w, state_proj, step_w, out_w, spread, gather
    )
    gain_in, vconv, vshift, state_conv, sshift, sbias, rate, skipx, ggain = bring(
        gain_in, vconv, vshift, state_conv, sshift, sbias, rate, skipx, ggain
    )

    def own_block(i, a):
        return (jnp.clip(i - a[0] * half_blocks, 0, half_blocks - 1), 0)

    def other_block(i, a):
        return (jnp.clip(i - (1 - a[0]) * half_blocks, 0, half_blocks - 1), 0) if two else (0, 0)

    other_read = other_block if two else own_block

    def rows(n, index=lambda i, a: (i, 0)):
        return pl.BlockSpec((BLOCK, n), index)

    along = pl.BlockSpec((8, BLOCK), lambda i, a: (0, i))
    fixed = lambda *shape: pl.BlockSpec(shape, lambda i, a: (0,) * len(shape))
    states_spec = lambda index: pl.BlockSpec((chunks, nstate, width), index)
    big = lambda *shape: pltpu.VMEM(shape, f32)
    low = lambda *shape: pltpu.VMEM(shape, bf16)
    halves = [
        ((rows_here if two else length, model), bf16, rows(model, own_block)),
        ((rows_here if two else BLOCK, model), bf16, rows(model, other_block)),
    ]

    normed, g, y, gg, values, slope, vp, conv_s, sp, z, sin, sq, step, running, shifted, grownx, tailx = run(
        functools.partial(forward_kernel, half_blocks),
        blocks,
        at,
        [
            (own_rows, rows(model, own_block)),
            (other_rows, rows(model, other_read)),
            (gain_in, None),
            (gate_w, None),
            (value_w, None),
            (state_proj, None),
            (step_w, None),
            (vconv, None),
            (vshift, None),
            (state_conv, None),
            (sshift, None),
            (sbias, None),
            (rate, None),
            (skipx, None),
            (ggain, None),
            (spread, None),
        ],
        [
            *[
                (shape, dtype, spec, fast)
                for shape, dtype, spec in (
                    ((length, model), bf16, rows(model)),
                    ((length, width), f32, rows(width)),
                    ((length, width), f32, rows(width)),
                    ((length, width), bf16, rows(width)),
                    ((length, width), bf16, rows(width)),
                    ((length, width), bf16, rows(width)),
                    ((length, width), bf16, rows(width)),
                    ((length, nstate2), f32, rows(nstate2)),
                    ((length, nstate2), bf16, rows(nstate2)),
                    ((length, LANES), f32, rows(LANES)),
                    ((blocks * chunks, nstate, width), bf16, states_spec(lambda i, a: (i, 0, 0))),
                    ((8, length), f32, along),
                    ((length, LANES), f32, rows(LANES)),
                    ((length, LANES), f32, rows(LANES)),
                    ((length, LANES), f32, rows(LANES)),
                    ((length, width), f32, rows(width)),
                    ((length, width), f32, rows(width)),
                )
            ]
        ],
        [
            big(width // LANES, BLOCK + 8, LANES),
            big(nstate2 // LANES, BLOCK + 8, LANES),
            big(nstate, width),
            big(BLOCK, width),
            big(BLOCK, width),
            low(BLOCK, width),
        ],
    )
    def stats_of(cot_rows, theirs, *before):
        first = (lambda a: (1 - a[0]) * half_blocks) if theirs else (lambda a: a[0] * half_blocks)
        count = cot_rows.shape[0]
        return run(
            stats_kernel,
            count // BLOCK,
            at,
            [
                (cot_rows, rows(model)),
                (gg, rows(width, lambda i, a: (first(a) + i, 0))),
                (sq, pl.BlockSpec((8, BLOCK), lambda i, a: (0, first(a) + i))),
                (out_w, None),
                *[(b, along) for b in before],
            ],
            [
                ((count, width), f32, rows(width), fast),
                (
                    (8 + 8 * len(before), count),
                    f32,
                    pl.BlockSpec((8 + 8 * len(before), BLOCK), lambda i, a: (0, i)),
                ),
            ],
            [],
        )

    og, stats = stats_of(own_cot, False)
    if two:
        og_b, stats = stats_of(other_cot, True, stats)
    else:
        og_b = og
    got = add_other(stats)
    above = 1 if two else 0

    def stats_at(row, block):
        return pl.BlockSpec((8, BLOCK), lambda i, a: (row, block(i, a)[0]))

    branch, branch_sent = run(
        functools.partial(branch_kernel, half_blocks),
        blocks,
        at,
        [(gg, rows(width)), (out_w, None)],
        halves,
        [],
    )

    def other_half(own, sent):
        if two:
            return lax.ppermute(sent, "heads", swap)
        total = lax.psum_scatter(own.astype(f32), "heads", scatter_dimension=0, tiled=True)
        mine = lax.dynamic_slice_in_dim(own, own_from, rows_here, 0).astype(f32)
        return total - mine

    branch_got = other_half(branch, branch_sent)
    if not two:
        branch = lax.dynamic_slice_in_dim(branch, own_from, rows_here, 0)
    if fast:
        pieces = [((model // 2, 2 * model), bf16, fixed(model // 2, 2 * model))] * 2
    else:
        pieces = [
            ((model, width), f32, fixed(model, width)),
            ((width, model), f32, fixed(width, model)),
        ]
    dg, dy, early_a, early_b, grad_gain, norm = run(
        functools.partial(gate_kernel, half_blocks, inner_all, fast),
        blocks,
        at,
        [
            (own_cot, rows(model, own_block)),
            (other_cot, rows(model, other_read)),
            (stats, stats_at(above, own_block)),
            (got, stats_at(0, own_block)),
            (stats, stats_at(0, other_read)),
            (got, stats_at(above, other_read)),
            (normed, None),
            (og, rows(width, own_block)),
            (og_b, rows(width, other_read)),
            (y, rows(width)),
            (g, rows(width)),
            (gg, None),
            (ggain, None),
            (gate_w, None),
            (branch, pl.BlockSpec(memory_space=pl.ANY)),
        ],
        [
            ((length, width), bf16, fixed(length, width), fast),
            ((length, width), bf16, rows(width), fast),
            *pieces,
            ((8, width), f32, fixed(8, width)),
            ((8, model), f32, fixed(8, model)),
        ],
        [low(length, model)] + ([big(model, width), big(width, model)] if fast else []),
    )

    def backward(start, count, carry, after=()):
        size = 2 * BLOCK if start % 2 == 0 and count % 2 == 0 else BLOCK
        size = count * BLOCK if fast else size
        steps, base = count * BLOCK // size, start * BLOCK // size

        def local(n):
            return pl.BlockSpec((size, n), lambda i, a: (steps - 1 - i, 0))

        def taken(array):
            if fast:
                return (array, None)
            shape = (size // CHUNK if array.ndim == 3 else size, *array.shape[1:])
            rest = (0,) * (array.ndim - 1)
            return (array, pl.BlockSpec(shape, lambda i, a: (base + steps - 1 - i, *rest)))

        slabs = [(width // LANES, 8, LANES), (nstate2 // LANES, 8, LANES)]
        vectors = [(nstate, width), *slabs, (8, width), (8, nstate2), (8, LANES)]
        out = run(
            functools.partial(
                backward_kernel, size, start * BLOCK if fast else 0, bool(carry), len(after)
            ),
            steps,
            at,
            [
                *[
                    taken(a)
                    for a in (dy, values, slope, vp, conv_s, sp, z, step, running, shifted, grownx, tailx, sin)
                ],
                (vconv, None),
                (state_conv, None),
                (rate, None),
                (skipx, None),
                (gather, None),
                *[(c, None) for c in carry],
                *[(a, pl.BlockSpec(memory_space=pl.ANY)) for a in after],
            ],
            [
                ((count * BLOCK, width), bf16, local(width)),
                ((count * BLOCK, nstate2), bf16, local(nstate2)),
                ((count * BLOCK, LANES), bf16, local(LANES)),
                *[(shape, f32, fixed(*shape)) for shape in vectors],
            ],
            [
                big(width // LANES, size + 8, LANES),
                big(nstate2 // LANES, size + 8, LANES),
                big(nstate, width),
                big(size, width),
                big(size, width),
                low(size, width),
                low(size, width),
                low(size, 2 * width),
                low(size, 2 * width),
            ],
        )
        return out[:3], out[3:]

    if two:
        own_stats, their_stats = stats_at(1, lambda i, a: (i, 0)), along
    else:
        own_stats = their_stats = stats_at(0, lambda i, a: (i + a[4] // BLOCK, 0))
    mixed, token = run(
        functools.partial(mixed_kernel, inner_all),
        rows_here // BLOCK,
        at,
        [
            (residual, rows(model)),
            (branch, rows(model)),
            (branch_got, rows(model)),
            (stats, own_stats),
            (got, their_stats),
        ],
        [((rows_here, model), f32, rows(model)), ((8, LANES), f32, fixed(8, LANES))],
        [],
    )
    from_gate = run(
        gate_back_kernel,
        blocks,
        at,
        [(dg, rows(width)), (gate_w, None)],
        [((length, model), f32, rows(model), fast)],
        [],
    )[0]
    cut = blocks // 2
    behind = ()
    if fast:
        steps = [("fold", 2, [early_a, hop(early_b, "core")], 2, False)]
        ((kept, sent),) = stage(at, steps, (from_gate,))
        early = [kept, hop(sent, "line")]
        behind = (kept,)
    low_b, carry = backward(cut, blocks - cut, (), behind)
    partial = run(
        functools.partial(partial_kernel, cut * BLOCK),
        1,
        at,
        [(normed, None), *[(a, None) for a in low_b]],
        [
            ((model, a.shape[1]), f32, fixed(model, a.shape[1])) for a in low_b
        ],
        [],
    )
    if fast:
        ((kept, *sent),) = stage(at, [("fold", 3, early, 4, False)])
        early = [kept] + [hop(a, k + 1) for k, a in enumerate(sent)]
        behind = (kept, branch_got, partial[2])
    low_a, carry = backward(0, cut, carry, behind)
    vec, svec, head = carry[3:]
    early = early if fast else ()
    lows = [(a, rows(a.shape[1], lambda i, at: (jnp.minimum(i, cut - 1), 0))) for a in low_a]
    lows += [(a, rows(a.shape[1], lambda i, at: (jnp.maximum(i - cut, 0), 0))) for a in low_b]

    if fast:
        shape = (model // 2, width + nstate2 + LANES)
        pieces = [(shape, bf16, fixed(*shape))] * 2
        pieces.append((early[0].shape, bf16, fixed(*early[0].shape)))
    else:
        shapes = [(model, width), (model, nstate2), (model, LANES), (8, model)]
        pieces = [(shape, f32, fixed(*shape)) for shape in shapes]
    late = run(
        functools.partial(weights_kernel, fast),
        1,
        at,
        [
            (normed, None),
            *[(a, None) for a in low_a],
            *[(a, None) for a in partial],
            (value_w, None),
            (state_proj, None),
            (step_w, None),
            (gain_in, None),
            (vec, None),
            (svec, None),
            (head, None),
            (grad_gain, None),
            (norm, None),
            *[(a, None) for a in early],
        ],
        pieces,
        [big(model, width), big(model, nstate2), big(model, LANES)],
    )
    ng, ng_sent = run(
        functools.partial(normed_grad_kernel, half_blocks, cut),
        blocks,
        at,
        [
            (from_gate, rows(model)),
            *lows,
            (value_w, None),
            (state_proj, None),
            (step_w, None),
        ],
        halves,
        [],
    )

    ng_got = other_half(ng, ng_sent)
    if not two:
        ng = lax.dynamic_slice_in_dim(ng, own_from, rows_here, 0)
    grad_input, token_b = run(
        input_kernel,
        rows_here // BLOCK,
        at,
        [
            (residual, rows(model)),
            (cot, rows(model)),
            (ng, rows(model)),
            (ng_got, rows(model)),
            (gain_in, None),
        ],
        [((rows_here, model), f32, rows(model)), ((8, LANES), f32, fixed(8, LANES))],
        [],
    )

    if fast:
        kept, sent, early = late
        ((kept, sent),) = stage(at, [("fold", 2, [kept, hop(sent, "core")], 2, True)])
        got = hop(sent, "line")
        early = [early] + [hop(early, k) for k in (1, 2, 3)]
        ((kept, *sent),) = stage(at, [("fold", 3, [kept, got], 4, True)], (ng,))
        got = [hop(a, k + 1) for k, a in enumerate(sent)]
        steps = [("part", width, [kept, *got], 2, True), ("join", 3, early)]
        (done, rest), (early,) = stage(at, steps, (token,))
        early = [early, hop(early, "line")]
        theirs = lax.ppermute(rest, "heads", swap)
        done = run(
            heads_kernel,
            1,
            at,
            [(done, None), (rest, None), (theirs, None)],
            [((rest.shape[0], width + rest.shape[1]), bf16, fixed(rest.shape[0], width + rest.shape[1]))],
            [],
        )[0]
        done = [done] + [hop(done, k) for k in (1, 2, 3)]
        (done,), (early,) = stage(at, [("join", 3, done), ("join", 2, early)], (token_b,))
        grad_gate, grad_out_proj, token_c = run(
            early_kernel,
            1,
            at,
            [(early, None), (hop(early, "core"), None)],
            [((model, model), f32, fixed(model, model))] * 2
            + [((8, LANES), f32, fixed(8, LANES))],
            [],
        )
        quarter = done.shape[0]

        def wide(n):
            def index(i, a):
                return ((a[1] ^ (n // 2)) * 2 + (a[2] ^ (n % 2)), 0)

            return [((model, w), f32, pl.BlockSpec((quarter, w), index)) for w in (width, nstate2)]

        def kept_in(arrays):
            return [(a, pl.BlockSpec(memory_space=pl.ANY)) for a in arrays]

        def place(n, piece, filled=()):
            aliases = ((2, 0), (3, 1)) if filled else ()
            ins = [(piece, None), *kept_in(filled)]
            outs = wide(n) + [((8, LANES), f32, fixed(8, LANES))]
            return run(place_kernel, 1, at, ins, outs, [], aliases=aliases)

        got = hop(done, "line")
        across = hop(done, "core")
        *filled, token_d = place(0, done)
        *filled, token_e = place(2, across, filled)
        ((got,),) = stage(at, [("join", 2, [got])], (token_c, token_e))
        done = [done, got, across, hop(got, "core")]
        *filled, token_d = place(1, got, filled)
        shapes = [
            (heads, model),
            (4, width),
            (width,),
            (width,),
            (model,),
            (4, nstate2),
            (nstate2,),
            (heads,),
            (heads,),
            (heads,),
        ]
        (
            grad_value,
            grad_state,
            grad_step,
            grad_vconv,
            grad_vshift,
            grad_ggain,
            grad_norm,
            grad_sconv,
            grad_sshift,
            grad_bias,
            grad_rate,
            grad_skip,
        ) = run(
            late_kernel,
            1,
            at,
            [*[(a, None) for a in done], *kept_in(filled)],
            wide(3) + [(shape, f32, fixed(*shape)) for shape in shapes],
            [big(model, LANES)],
            aliases=((5, 0), (6, 1)),
        )
        return (
            mixed[None],
            grad_input[None],
            grad_norm,
            grad_gate,
            grad_value,
            grad_state,
            grad_step.T,
            grad_vconv,
            grad_vshift,
            grad_sconv,
            grad_sshift,
            grad_bias,
            grad_rate,
            grad_skip,
            grad_ggain,
            grad_out_proj,
        )
    grad_value, grad_state, grad_step, norm = late
    grad_gate, grad_value, grad_out_proj, grad_step, vec, head, grad_gain = lax.psum(
        (early_a, grad_value, early_b, grad_step, vec, head, grad_gain), "batch"
    )
    grad_state, svec, norm = lax.psum((grad_state, svec, norm), ("batch", "heads"))
    norm, ggrad = norm[0], grad_gain[0]
    return (
        mixed[None],
        grad_input[None],
        norm,
        grad_gate[:, :inner],
        grad_value[:, :inner],
        grad_state,
        grad_step[:, :heads],
        vec[:4, :inner],
        vec[4, :inner],
        svec[:4],
        svec[4],
        head[0, :heads],
        head[1, :heads],
        head[2, :heads],
        ggrad[:inner],
        grad_out_proj[:inner],
    )


def solution(mesh):
    return jax.shard_map(
        per_device,
        mesh=mesh,
        in_specs=(
            P("batch", "heads", None),
            P(),
            P(None, "heads"),
            P(None, "heads"),
            P(),
            P(None, "heads"),
            P(None, "heads"),
            P("heads"),
            P(),
            P(),
            P("heads"),
            P("heads"),
            P("heads"),
            P("heads"),
            P("heads", None),
            P("batch", "heads", None),
        ),
        out_specs=(
            P("batch", "heads", None),
            P("batch", "heads", None),
            P(),
            P(None, "heads"),
            P(None, "heads"),
            P(),
            P(None, "heads"),
            P(None, "heads"),
            P("heads"),
            P(),
            P(),
            P("heads"),
            P("heads"),
            P("heads"),
            P("heads"),
            P("heads", None),
        ),
        check_vma=False,
    )
```

```python
import functools

import jax
import jax.numpy as jnp
from jax import lax
from jax.experimental import pallas as pl
from jax.experimental.pallas import tpu as pltpu
from jax.sharding import PartitionSpec as P

EPSILON = 1e-05
HIGHEST = lax.Precision.HIGHEST
BLOCK = 256
CHUNK = 128
LANES = 128
HALF = LANES // 2
QUAD = 2 * LANES
LOG2E = 1.4426950408889634
f32 = jnp.float32
bf16 = jnp.bfloat16


def dot(left, right, over=((1,), (0,)), precision=None):
    return lax.dot_general(
        left, right, (over, ((), ())), preferred_element_type=f32, precision=precision
    )


TN = ((0,), (0,))
NT = ((1,), (1,))


def sigmoid(v):
    return 0.5 * jnp.tanh(0.5 * v) + 0.5


def silu(v):
    half = 0.5 * v
    return half + half * jnp.tanh(half)


def silu_slope(v):
    half = 0.5 * v
    t = jnp.tanh(half)
    out = half + half * t
    sig = 0.5 + 0.5 * t
    return out, sig + out * (1.0 - sig)


def causal_back(buf, slab, r0, grad, pre, taps, extra):
    buf[slab, pl.ds(r0, CHUNK), :] = grad
    lanes = slice(slab * LANES, (slab + 1) * LANES)
    pre = pre.astype(f32)
    out, rows = 0.0, []
    for tap in range(4):
        moved = grad if tap == 3 else buf[slab, pl.ds(r0 + 3 - tap, CHUNK), :]
        out = out + taps[tap : tap + 1, lanes].astype(f32) * moved
        rows.append(jnp.sum(pre * moved, axis=0, keepdims=True))
    rows.append(jnp.sum(grad, axis=0, keepdims=True))
    rows += [extra, jnp.zeros((2, LANES), f32)]
    return out, jnp.concatenate(rows, axis=0)


def split(v):
    high = v.astype(bf16)
    return jnp.concatenate([high, (v - high.astype(f32)).astype(bf16)], axis=1)


def lower_mask(rows):
    return lax.broadcasted_iota(jnp.int32, (rows, rows), 0) >= lax.broadcasted_iota(
        jnp.int32, (rows, rows), 1
    )


def chunk_mask(strict=False):
    row = lax.broadcasted_iota(jnp.int32, (BLOCK, BLOCK), 0)
    column = lax.broadcasted_iota(jnp.int32, (BLOCK, BLOCK), 1)
    ordered = row > column if strict else row >= column
    return (ordered & (row // CHUNK == column // CHUNK)).astype(bf16)


def block_scalars(z, log_rate, spread):
    step = jnp.maximum(z, 0.0) + jnp.log1p(jnp.exp(-jnp.abs(z)))
    rate = -jnp.exp(log_rate)
    decay = jnp.where(lax.broadcasted_iota(jnp.int32, (1, LANES), 1) < 32, step * (rate * LOG2E), 0.0)
    high = decay.astype(bf16).astype(f32)
    middle = (decay - high).astype(bf16).astype(f32)
    packed = high + pltpu.roll(middle, 32, 1) + pltpu.roll(decay - high - middle, 64, 1)
    sums = dot(chunk_mask(), packed.astype(bf16))
    running = sums + pltpu.roll(sums, LANES - 32, 1) + pltpu.roll(sums, LANES - 64, 1)
    last = [running[r + CHUNK - 1 : r + CHUNK, :] for r in range(0, BLOCK, CHUNK)]
    tail = [jnp.exp2(v - running[k * CHUNK : (k + 1) * CHUNK, :]) for k, v in enumerate(last)]
    tail = step * jnp.concatenate(tail, axis=0)
    wide = dot(jnp.concatenate([split(jnp.exp2(running)), split(tail)], axis=0), spread)
    return step, running, running - jnp.log2(step), wide[:BLOCK], wide[BLOCK:]


def causal(buf, slab, taps, shift):
    lanes = slice(slab * LANES, (slab + 1) * LANES)
    conv = shift[:, lanes].astype(f32)
    for tap in range(4):
        conv = conv + taps[tap : tap + 1, lanes].astype(f32) * buf[slab, pl.ds(5 + tap, BLOCK), :]
    return conv


def chunk_scores(b_rows, c_rows):
    n = b_rows.shape[1]
    b, c = split(b_rows), split(c_rows)
    left = jnp.concatenate([c, c[:, :n]], axis=1)
    right = jnp.concatenate([b[:, :n], b[:, :n], b[:, n:]], axis=1)
    return b, c, dot(left, right, NT)


def quad_mixing(scores, running, shifted_t, quad, mask):
    factors, mixes = [], []
    for head in range(4 * quad, 4 * quad + 4):
        spread = running[:, head : head + 1] - shifted_t[head : head + 1, :]
        factors.append(jnp.exp2(jnp.where(mask, spread, -1e30)))
        mixes.append((scores * factors[-1]).astype(bf16))
    return factors, mixes


def heads_apart(left, right):
    lane = lax.broadcasted_iota(jnp.int32, (1, LANES), 1)
    first = (lane < HALF).astype(bf16)
    zero = jnp.zeros(left.shape, bf16)
    rows = [jnp.concatenate([left * m, zero], axis=1) for m in (first, 1 - first)]
    rows += [jnp.concatenate([zero, right * m], axis=1) for m in (first, 1 - first)]
    return jnp.concatenate(rows, axis=0)


def forward_kernel(
    half_blocks,
    at_ref,
    own_ref,
    other_ref,
    gain_ref,
    gate_w,
    value_w,
    state_w,
    step_w,
    vconv_ref,
    vshift_ref,
    sconv_ref,
    sshift_ref,
    sbias_ref,
    rate_ref,
    skip_ref,
    ggain_ref,
    spread_ref,
    normed_ref,
    g_ref,
    y_ref,
    gg_ref,
    low_ref,
    slope_ref,
    vp_ref,
    as_ref,
    sp_ref,
    z_ref,
    sin_ref,
    sq_ref,
    step_ref,
    running_ref,
    shifted_ref,
    grownx,
    tailx,
    vbuf,
    sbuf,
    state,
    carried,
    values,
    vtail,
):
    step_at = pl.program_id(0)
    pairs = vbuf.shape[0]
    nstate = state.shape[0]

    @pl.when(step_at == 0)
    def _():
        state[...] = jnp.zeros_like(state)
        for buf in (vbuf, sbuf):
            buf[:, 0:8, :] = jnp.zeros((buf.shape[0], 8, LANES), f32)

    mine = (step_at // half_blocks) == at_ref[0]
    rows = jnp.where(mine, own_ref[...], other_ref[...]).astype(f32)
    scale = lax.rsqrt(jnp.mean(rows * rows, axis=1, keepdims=True) + EPSILON)
    normed = (rows * scale * gain_ref[...].astype(f32)).astype(bf16)
    normed_ref[...] = normed
    z = dot(normed, step_w[...]) + sbias_ref[...]
    z_ref[...] = z
    for out, buf, w in ((sp_ref, sbuf, state_w), (vp_ref, vbuf, value_w)):
        pre = dot(normed, w[...])
        out[...] = pre.astype(bf16)
        for slab in range(buf.shape[0]):
            buf[slab, 8:, :] = pre[:, slab * LANES : (slab + 1) * LANES]
    g_ref[...] = dot(normed, gate_w[...])

    step, running, shifted, grownx[...], tailx[...] = block_scalars(z, rate_ref[...], spread_ref[...])
    step_ref[...] = step
    running_ref[...] = running
    shifted_ref[...] = shifted
    chunks = range(BLOCK // CHUNK)
    states = []
    for slab in range(sbuf.shape[0]):
        conv = causal(sbuf, slab, sconv_ref, sshift_ref)
        as_ref[:, slab * LANES : (slab + 1) * LANES] = conv
        states.append(silu(conv))
    for pair in range(pairs):
        lanes = slice(pair * LANES, (pair + 1) * LANES)
        out, slope = silu_slope(causal(vbuf, pair, vconv_ref, vshift_ref))
        slope_ref[:, lanes] = slope.astype(bf16)
        values[:, lanes] = out
        low_ref[:, lanes] = out.astype(bf16)
        vtail[:, lanes] = (out * tailx[:, lanes]).astype(bf16)
    parts = []
    for chunk in chunks:
        here = slice(chunk * CHUNK, (chunk + 1) * CHUNK)
        b_two, c_two, scores = chunk_scores(*(v[here] for v in states))
        parts.append(scores)
        before = state[...].astype(bf16)
        sin_ref[chunk, :, :] = before
        carried[here, :] = dot(c_two[:, :nstate], before)
        last = grownx[(chunk + 1) * CHUNK - 1 : (chunk + 1) * CHUNK, :]
        state[...] = last * state[...] + dot(b_two[:, :nstate], vtail[here, :], TN)
    mask = lower_mask(CHUNK)
    for chunk in chunks:
        here = slice(chunk * CHUNK, (chunk + 1) * CHUNK)
        run = running[here]
        run_t = shifted[here].T
        squares = jnp.zeros((CHUNK, LANES), f32)
        for quad in range(pairs // 2):
            _, mixes = quad_mixing(parts[chunk], run, run_t, quad, mask)
            sides = [slice((2 * quad + k) * LANES, (2 * quad + k + 1) * LANES) for k in range(2)]
            both = dot(
                jnp.concatenate(mixes, axis=1), heads_apart(*(low_ref[here, lanes] for lanes in sides))
            )
            for k, lanes in enumerate(sides):
                scanned = both[:, k * LANES : (k + 1) * LANES]
                scanned = scanned + grownx[here, lanes] * carried[here, lanes]
                scanned = scanned + skip_ref[:, lanes] * values[here, lanes]
                gate, slope = silu_slope(g_ref[here, lanes])
                y_ref[here, lanes] = scanned * slope
                g_ref[here, lanes] = gate
                gated = scanned * gate
                gg_ref[here, lanes] = (gated * ggain_ref[:, lanes].astype(f32)).astype(bf16)
                squares = squares + gated * gated
        sq_ref[:, here] = dot(jnp.ones((8, LANES), f32), squares, NT, HIGHEST)
    for buf in (vbuf, sbuf):
        buf[:, 0:8, :] = buf[:, BLOCK : BLOCK + 8, :]


def stats_kernel(at_ref, cot_ref, gg_ref, sq_ref, out_w, *refs):
    og_ref, stats_ref = refs[-2:]
    if len(refs) > 2:
        stats_ref[8:, :] = refs[0][...]
    og = dot(cot_ref[...], out_w[...], NT)
    og_ref[...] = og
    prod = (og * gg_ref[...].astype(f32)).astype(bf16)
    dots = dot(jnp.ones((8, prod.shape[1]), bf16), prod, NT)
    row = lax.broadcasted_iota(jnp.int32, dots.shape, 0)
    stats_ref[:8, :] = jnp.where(row == 0, sq_ref[...], dots)


def bring_kernel(at_ref, *refs):
    count = len(refs) // 2
    for src, dst in zip(refs[:count], refs[count:]):
        dst[...] = src[...]


def branch_kernel(half_blocks, at_ref, gg_ref, out_w, own_ref, other_ref):
    mine = (pl.program_id(0) // half_blocks) == at_ref[0]
    rows = dot(gg_ref[...], out_w[...]).astype(bf16)

    @pl.when(mine)
    def _():
        own_ref[...] = rows

    @pl.when(jnp.logical_not(mine))
    def _():
        other_ref[...] = rows


def gate_back_kernel(at_ref, dg_ref, gate_w, out_ref):
    out_ref[...] = dot(dg_ref[...], gate_w[...], NT)


def picked(cut, early, late):
    return jnp.where(pl.program_id(0) < cut, early[...], late[...])


def normed_grad_kernel(half_blocks, cut, at_ref, from_gate, *refs):
    lows, (value_w, state_w, step_w, own_ref, other_ref) = refs[:6], refs[6:]
    dv, ds, dz = (picked(cut, a, b) for a, b in zip(lows[:3], lows[3:]))
    mine = (pl.program_id(0) // half_blocks) == at_ref[0]
    rows = (
        from_gate[...]
        + dot(dv, value_w[...], NT)
        + dot(ds, state_w[...], NT)
        + dot(dz, step_w[...], NT)
    ).astype(bf16)

    @pl.when(mine)
    def _():
        own_ref[...] = rows

    @pl.when(jnp.logical_not(mine))
    def _():
        other_ref[...] = rows


def row_sums(grads, weights):
    prod = (grads * weights.astype(f32)).astype(bf16)
    return dot(jnp.ones((8, prod.shape[1]), bf16), prod, NT)


def emit(at_ref, parts, outs):
    half = outs[0].shape[0]
    for j, out in enumerate(outs):
        rows = pl.ds(pl.multiple_of((at_ref[1] ^ j) * half, LANES), half)
        left = 0
        for part in parts:
            out[:, left : left + part.shape[1]] = part[rows, :].astype(out.dtype)
            left += part.shape[1]


def row_column(rows):
    return jnp.concatenate([rows, jnp.zeros((LANES - rows.shape[0], rows.shape[1]), f32)], axis=0).T


def mixed_kernel(inner_all, at_ref, rows_ref, own_ref, other_ref, here_ref, there_ref, out_ref, token_ref):
    token_ref[...] = jnp.zeros_like(token_ref)
    sums = here_ref[...] + there_ref[...]
    scale = row_column(lax.rsqrt(sums / inner_all + EPSILON))[:, 0:1]
    branch = own_ref[...].astype(f32) + other_ref[...].astype(f32)
    out_ref[...] = rows_ref[...].astype(f32) + scale * branch


def input_kernel(at_ref, rows_ref, cot_ref, own_ref, other_ref, gain_ref, out_ref, token_ref):
    token_ref[...] = jnp.zeros_like(token_ref)
    rows = rows_ref[...].astype(f32)
    scale = lax.rsqrt(jnp.mean(rows * rows, axis=1, keepdims=True) + EPSILON)
    pulled = (own_ref[...].astype(f32) + other_ref[...].astype(f32)) * gain_ref[...].astype(f32)
    inner = jnp.mean(pulled * rows, axis=1, keepdims=True) * (scale * scale * scale)
    out_ref[...] = cot_ref[...].astype(f32) + scale * pulled - rows * inner


def gate_kernel(
    half_blocks,
    inner_all,
    fast,
    at_ref,
    own_ref,
    other_ref,
    here_a,
    there_a,
    here_b,
    there_b,
    normed_ref,
    og_a,
    og_b,
    y_ref,
    g_ref,
    gg_ref,
    ggain_ref,
    gate_w,
    _,
    dg_ref,
    dy_ref,
    first_ref,
    second_ref,
    grad_gain_ref,
    norm_ref,
    scaled_ref,
    *scratch,
):
    step_at = pl.program_id(0)
    size = own_ref.shape[0]
    here = pl.ds(pl.multiple_of(step_at * size, BLOCK), size)
    pairs = og_a.shape[1] // LANES
    grad_gate, grad_out = scratch if fast else (first_ref, second_ref)

    @pl.when(step_at == 0)
    def _():
        grad_gain_ref[...] = jnp.zeros_like(grad_gain_ref)

    mine = (step_at // half_blocks) == at_ref[0]
    sums = jnp.where(mine, here_a[...] + there_a[...], here_b[...] + there_b[...])
    scale_row = lax.rsqrt(sums[0:1, :] / inner_all + EPSILON)
    pull_row = scale_row * scale_row * scale_row * sums[1:2, :] / inner_all
    columns = row_column(jnp.concatenate([scale_row, pull_row], axis=0))
    scale, pull = columns[:, 0:1], columns[:, 1:2]
    cot = jnp.where(mine, own_ref[...], other_ref[...]).astype(f32)
    scaled_ref[here, :] = (cot * scale).astype(bf16)
    for pair in range(pairs):
        lanes = slice(pair * LANES, (pair + 1) * LANES)
        og = jnp.where(mine, og_a[:, lanes], og_b[:, lanes]) * scale
        gain = ggain_ref[:, lanes].astype(f32)
        inverse = 1.0 / gain
        low = gg_ref[here, lanes].astype(f32)
        grad_gain_ref[0:1, lanes] += jnp.sum(og * low, axis=0, keepdims=True) * inverse
        gated_grad = gain * og - (low * inverse) * pull
        dy_ref[:, lanes] = (gated_grad * g_ref[:, lanes]).astype(bf16)
        dg_ref[here, lanes] = (gated_grad * y_ref[:, lanes]).astype(bf16)

    @pl.when(step_at == pl.num_programs(0) - 1)
    def _():
        grad_out[...] = dot(gg_ref[...], scaled_ref[...], TN)
        grad_gate[...] = dot(normed_ref[...], dg_ref[...], TN)
        norm_ref[...] = row_sums(grad_gate[...], gate_w[...])
        if fast:
            emit(at_ref, (grad_gate, grad_out), (first_ref, second_ref))


def partial_kernel(from_row, at_ref, normed_ref, *refs):
    for low, out in zip(refs[:3], refs[3:]):
        out[...] = dot(normed_ref[from_row:, :], low[...], TN)


def weights_kernel(fast, at_ref, normed_ref, *refs):
    lows, refs = refs[:6], refs[6:]
    value_w, state_w, step_w, gain_ref, vec_ref, svec_ref, head_ref, ggain_ref, norm_ref = refs[:9]
    outs, acc = refs[9:-3], refs[-3:]
    if fast:
        pieces, outs, done_ref = outs[:4], outs[4:6], outs[6]
        total = pieces[0][...].astype(f32)
        for r in pieces[1:]:
            total = total + r[...].astype(f32)
        done_ref[...] = total.astype(bf16)
    for a, low, rest in zip(acc, lows[:3], lows[3:]):
        a[...] = rest[...] + dot(normed_ref[: low.shape[0], :], low[...], TN)
    norm = norm_ref[...]
    for a, w in zip(acc, (value_w, state_w, step_w)):
        norm = norm + row_sums(a[...], w[...])
    norm = norm / gain_ref[...].astype(f32)
    if fast:
        pack_vectors(acc[2], vec_ref, svec_ref, head_ref, ggain_ref, norm)
        emit(at_ref, acc, outs)
        return
    for o, a in zip(outs, acc):
        o[...] = a[...]
    outs[3][...] = norm


VEC_AT = 16
SVEC_AT = 24
HEAD_AT = 32


def pack_vectors(block, vec_ref, svec_ref, head_ref, ggain_ref, norm):
    model = block.shape[0]
    row = lax.broadcasted_iota(jnp.int32, (8, model), 0)
    vec = jnp.where(row == 5, ggain_ref[0:1, :], jnp.where(row == 6, norm[0:1, :], vec_ref[...]))

    def tall(v):
        return jnp.concatenate([v, jnp.zeros((8, model - v.shape[1]), f32)], axis=1)

    rows = jnp.concatenate(
        [
            jnp.zeros((VEC_AT, model), f32),
            vec,
            tall(svec_ref[...]),
            tall(head_ref[...]),
            jnp.zeros((LANES - HEAD_AT - 8, model), f32),
        ],
        axis=0,
    )
    lane = lax.broadcasted_iota(jnp.int32, (1, LANES), 1)
    full = jnp.where(lane < VEC_AT, block[...], rows.T)
    block[...] = carry_rest(jnp.where(lane < HALF, full, 0.0))


def carry_rest(full):
    high = full.astype(bf16).astype(f32)
    return high + pltpu.roll(full - high, HALF, 1)


def join_rest(block):
    lane = lax.broadcasted_iota(jnp.int32, (1, LANES), 1)
    return jnp.where(lane < HALF, block + pltpu.roll(block, HALF, 1), 0.0)


def fold_step(me, ins, outs, vectors):
    rows, width = outs[0].shape
    width -= LANES if vectors else 0
    for j, o in enumerate(outs):
        at = slice(0, rows)
        if len(outs) > 1:
            at = pl.ds(pl.multiple_of((me ^ j) * rows, 16), rows)
        o[:, :width] = sum(r[at, :width].astype(f32) for r in ins).astype(bf16)
        if vectors:
            last = sum(r[at, width:].astype(f32) for r in ins)
            o[:, width:] = carry_rest(join_rest(last)).astype(bf16)


def part_step(ins, outs, vectors):
    width = outs[0].shape[1]
    outs[0][...] = sum(r[:, :width].astype(f32) for r in ins).astype(bf16)
    state = outs[1].shape[1] - LANES
    outs[1][:, :state] = sum(r[:, width : width + state].astype(f32) for r in ins).astype(bf16)
    last = sum(r[:, width + state :].astype(f32) for r in ins)
    outs[1][:, state:] = carry_rest(join_rest(last)).astype(bf16)


def join_step(me, ins, out):
    rows = ins[0].shape[0]
    count = out.shape[0] // rows
    if count == 1:
        out[...] = ins[0][...]
        return
    left = 0
    for first in range(0, len(ins), count):
        right = left + ins[first].shape[1]
        for j, r in enumerate(ins[first : first + count]):
            out[pl.ds(pl.multiple_of((me ^ j) * rows, 16), rows), left:right] = r[...]
        left = right


def stage_kernel(plan, extra, at_ref, *refs):
    n_in = sum(count for _, _, count, _, _ in plan)
    ins, outs = refs[:n_in], refs[n_in + extra :]
    for kind, axis, take, give, vectors in plan:
        if kind == "fold":
            fold_step(at_ref[axis], ins[:take], outs[:give], vectors)
        elif kind == "part":
            part_step(ins[:take], outs[:give], vectors)
        else:
            join_step(at_ref[axis], ins[:take], outs[0])
        ins, outs = ins[take:], outs[give:]


def stage(at, steps, after=()):
    plan, arrays, shapes = [], [], []
    for kind, axis, ins, *rest in steps:
        rows, width = ins[0].shape
        count, vectors = rest if rest else (1, False)
        if kind == "fold":
            shapes += [(rows // count, width)] * count
        elif kind == "part":
            shapes += [(rows, axis), (rows, width - axis)]
        else:
            widths = {a.shape[1] for a in ins}
            shapes.append((rows * len(ins) // len(widths), sum(widths)))
        plan.append((kind, axis, len(ins), count, vectors))
        arrays += ins
    out = call(
        functools.partial(stage_kernel, tuple(plan), len(after)),
        1,
        at,
        [(a, None) for a in arrays] + [(a, pl.BlockSpec(memory_space=pl.ANY)) for a in after],
        [(shape, bf16, pl.BlockSpec(shape, lambda i, a: (0, 0))) for shape in shapes],
        [],
    )
    out, results = list(out), []
    for _, _, _, give, _ in plan:
        results.append(out[:give])
        out = out[give:]
    return results


def heads_kernel(at_ref, done_ref, own_ref, other_ref, out_ref):
    start = done_ref.shape[1]
    state = own_ref.shape[1] - LANES
    out_ref[:, :start] = done_ref[...]
    sums = own_ref[:, :state].astype(f32) + other_ref[:, :state].astype(f32)
    out_ref[:, start : start + state] = sums.astype(bf16)
    lane = lax.broadcasted_iota(jnp.int32, (1, LANES), 1)
    shared = (lane == VEC_AT + 6) | ((lane >= SVEC_AT) & (lane < HEAD_AT))
    mine = join_rest(own_ref[:, state:].astype(f32))
    theirs = join_rest(other_ref[:, state:].astype(f32))
    out_ref[:, start + state :] = carry_rest(mine + jnp.where(shared, theirs, 0.0)).astype(bf16)


def halves_of(at_ref, own_ref, other_ref, left, right):
    rows = own_ref.shape[0]
    for j, ref in enumerate((own_ref, other_ref)):
        yield pl.ds(pl.multiple_of((at_ref[1] ^ j) * rows, LANES), rows), ref[:, left:right].astype(f32)


def early_kernel(at_ref, own_ref, other_ref, *outs):
    outs[-1][...] = jnp.zeros_like(outs[-1])
    left = 0
    for o in outs[:-1]:
        right = left + o.shape[1]
        for at, v in halves_of(at_ref, own_ref, other_ref, left, right):
            o[at, :] = v
        left = right


def widen(piece, outs):
    left = 0
    for o in outs:
        right = left + o.shape[1]
        o[...] = piece[:, left:right].astype(f32)
        left = right


def place_kernel(at_ref, piece_ref, *refs):
    widen(piece_ref, refs[-3:-1])
    refs[-1][...] = jnp.zeros_like(refs[-1])


def late_kernel(at_ref, *refs):
    pieces, outs, block = refs[:4], refs[6:-1], refs[-1]
    widen(pieces[3], outs[:2])
    rows, right = pieces[0].shape
    for n, piece in enumerate(pieces):
        start = (at_ref[1] ^ (n // 2)) * 2 + (at_ref[2] ^ (n % 2))
        at = pl.ds(pl.multiple_of(start * rows, 16), rows)
        block[at, :] = piece[:, right - LANES :].astype(f32)
    full = join_rest(block[...])
    rows = full.T
    outs[2][...] = rows[: outs[2].shape[0]]
    vec, svec = rows[VEC_AT : VEC_AT + 8], rows[SVEC_AT : SVEC_AT + 8]
    head = rows[HEAD_AT : HEAD_AT + 8]
    vconv, vshift, ggain, norm, sconv, sshift, bias, rate, skip = outs[3:]
    vconv[...] = vec[:4]
    for o, row in ((vshift, vec[4:5]), (ggain, vec[5:6]), (norm, vec[6:7]), (sshift, svec[4:5])):
        o[...] = row[:, : o.shape[0]].reshape(o.shape)
    sconv[...] = svec[:4, : sconv.shape[1]]
    for j, o in enumerate((bias, rate, skip)):
        o[...] = head[j : j + 1, : o.shape[0]].reshape(o.shape)


def backward_kernel(
    size,
    from_row,
    carried_in,
    extra,
    at_ref,
    dy_ref,
    low_ref,
    slope_ref,
    vp_ref,
    as_ref,
    sp_ref,
    z_ref,
    step_ref,
    running_ref,
    shifted_ref,
    grownx,
    tailx,
    sin_ref,
    vconv_ref,
    sconv_ref,
    rate_ref,
    skip_ref,
    gather_ref,
    *refs,
):
    carries, refs = (refs[:6], refs[6:]) if carried_in else ((), refs)
    refs = refs[extra:]
    dvalue, dstates, dstep, dstate_out, dahalo, dshalo, grad_vconv_ref, grad_sconv_ref, grad_head_ref = refs[:9]
    dabuf, dsbuf, dstate, carried, pulled, ubuf, vtail, inner, outer = refs[9:]
    step_at = pl.program_id(0)
    nstate, width = dstate.shape
    pairs = width // LANES

    def row_at(start, count=CHUNK):
        return slice(from_row + start, from_row + start + count)


    @pl.when(step_at == 0)
    def _():
        if carried_in:
            dstate[...] = carries[0][...]
            dabuf[:, size:, :] = carries[1][...]
            dsbuf[:, size:, :] = carries[2][...]
            grad_vconv_ref[...] = carries[3][...]
            grad_sconv_ref[...] = carries[4][...]
            grad_head_ref[...] = carries[5][...]
        else:
            dstate[...] = jnp.zeros_like(dstate)
            for buf in (dabuf, dsbuf):
                buf[:, size:, :] = jnp.zeros((buf.shape[0], 8, LANES), f32)
            for ref in (grad_vconv_ref, grad_sconv_ref, grad_head_ref):
                ref[...] = jnp.zeros_like(ref)

    @pl.when(step_at > 0)
    def _():
        for buf in (dabuf, dsbuf):
            buf[:, size:, :] = buf[:, 0:8, :]

    chunks = [slice(r, r + CHUNK) for r in range(0, size, CHUNK)]
    zero_row = jnp.zeros((1, LANES), f32)
    rate = -jnp.exp(rate_ref[...])
    states, slopes = [], []
    for slab in range(2):
        out, slope = silu_slope(as_ref[row_at(0, size), slab * LANES : (slab + 1) * LANES])
        states.append(out)
        slopes.append(slope)
    for pair in range(pairs):
        lanes = slice(pair * LANES, (pair + 1) * LANES)
        there = (row_at(0, size), lanes)
        ubuf[:, lanes] = (dy_ref[there].astype(f32) * grownx[there]).astype(bf16)
    two = [chunk_scores(*(v[here] for v in states)) for here in chunks]
    helds, afters = [None] * len(chunks), [None] * len(chunks)
    for chunk in reversed(range(len(chunks))):
        here = chunks[chunk]
        b_two, c_two, _ = two[chunk]
        before = sin_ref[from_row // CHUNK + chunk, :, :]
        last = grownx[row_at(here.stop - 1, 1), :]
        grad = dstate[...]
        afters[chunk] = grad.astype(bf16)
        carried[here, :] = dot(c_two[:, :nstate], before)
        pulled[here, :] = dot(b_two[:, :nstate], afters[chunk])
        overlap = jnp.sum(before.astype(f32) * grad, axis=0, keepdims=True) * last
        overlap = jnp.broadcast_to(overlap, (8, width))
        tall = [split(overlap[:, p * LANES : (p + 1) * LANES]) for p in range(pairs)]
        held = dot(jnp.concatenate(tall, axis=1), gather_ref[...])[0:1]
        helds[chunk] = held[:, :LANES] + held[:, LANES:]
        dstate[...] = last * grad + dot(c_two[:, :nstate], ubuf[here, :], TN)

    mask = lower_mask(CHUNK)
    for chunk in reversed(range(len(chunks))):
        here = chunks[chunk]
        b_two, c_two, scores = two[chunk]
        rows_in = row_at(here.start)
        run = running_ref[rows_in, :]
        run_t = shifted_ref[rows_in, :].T
        dscores = jnp.zeros((CHUNK, CHUNK), f32)
        for quad in range(pairs // 2):
            factors, mixes = quad_mixing(scores, run, run_t, quad, mask)
            both = [slice((2 * quad + k) * LANES, (2 * quad + k + 1) * LANES) for k in range(2)]
            low = [low_ref[rows_in, lanes] for lanes in both]
            dy_low = [dy_ref[rows_in, lanes] for lanes in both]
            apart = heads_apart(*low)
            scanned = dot(jnp.concatenate(mixes, axis=1), apart)
            dsteps = dot(jnp.concatenate(mixes, axis=0), heads_apart(*dy_low), TN)
            for k, lanes in enumerate(both):
                pair = 2 * quad + k
                own = slice(k * LANES, (k + 1) * LANES)
                dmixing = dot(dy_low[k], apart[2 * k * CHUNK : 2 * (k + 1) * CHUNK, own], NT)
                dscores = dscores + dmixing[:, :CHUNK] * factors[2 * k]
                dscores = dscores + dmixing[:, CHUNK:] * factors[2 * k + 1]
                wide = slice(2 * pair * LANES, (2 * pair + 1) * LANES)
                wide_b = slice((2 * pair + 1) * LANES, (2 * pair + 2) * LANES)
                dy, values = dy_low[k].astype(f32), low[k].astype(f32)
                dvalues = dsteps[:, own]
                pulls = values * dvalues
                inside = dy * scanned[:, own] - pulls + ubuf[here, lanes].astype(f32) * carried[here, lanes]
                high = inside.astype(bf16)
                inner[here, wide] = high
                inner[here, wide_b] = (inside - high.astype(f32)).astype(bf16)
                tails, pull = tailx[rows_in, lanes], pulled[here, lanes]
                v = (values * tails).astype(bf16)
                vtail[here, lanes] = v
                outer[here, wide] = pulls.astype(bf16)
                outer[here, wide_b] = (v.astype(f32) * pull).astype(bf16)
                da = (dvalues + tails * pull + skip_ref[:, lanes] * dy) * slope_ref[rows_in, lanes].astype(f32)
                skips = jnp.sum(values * dy, axis=0, keepdims=True)
                dv, rows = causal_back(dabuf, pair, here.start, da, vp_ref[rows_in, lanes], vconv_ref, skips)
                grad_vconv_ref[:, lanes] += rows
                dvalue[here, lanes] = dv.astype(bf16)
        dlow = dscores.astype(bf16)
        drest = (dscores - dlow.astype(f32)).astype(bf16)
        b_rows, c_rows = b_two[:, :nstate], c_two[:, :nstate]
        cross = dot(
            jnp.concatenate([vtail[here, :], ubuf[here, :]], axis=0),
            jnp.concatenate([afters[chunk], sin_ref[from_row // CHUNK + chunk, :, :]], axis=0),
            NT,
        )
        db = cross[:CHUNK, :nstate] + dot(
            jnp.concatenate([dlow, dlow, drest], axis=0),
            jnp.concatenate([c_rows, c_two[:, nstate:], c_rows], axis=0),
            TN,
        )
        dc = cross[CHUNK:, nstate:] + dot(
            jnp.concatenate([dlow, dlow, drest], axis=1),
            jnp.concatenate([b_rows, b_two[:, nstate:], b_rows], axis=0),
        )
        for slab, d in enumerate((db, dc)):
            lanes = slice(slab * LANES, (slab + 1) * LANES)
            d = d * slopes[slab][here]
            dpre, rows = causal_back(dsbuf, slab, here.start, d, sp_ref[rows_in, lanes], sconv_ref, zero_row)
            grad_sconv_ref[:, lanes] += rows
            dstates[here, lanes] = dpre.astype(bf16)

    gathered = dot(jnp.concatenate([inner[...], outer[...]], axis=0), gather_ref[...])
    heads = [jnp.zeros((1, LANES), f32)] * 2
    for r in range(0, size, BLOCK):
        here = slice(r, r + BLOCK)
        sums, outs = gathered[here], gathered[size + r : size + r + BLOCK]
        ddecay = dot(chunk_mask(), split(sums[:, :LANES] + sums[:, LANES:]), TN)
        ddecay = ddecay[:, :LANES] + ddecay[:, LANES:]
        ddecay = ddecay + dot(chunk_mask(True), outs[:, LANES:].astype(bf16))
        held = [jnp.broadcast_to(helds[k // CHUNK], (CHUNK, LANES)) for k in range(r, r + BLOCK, CHUNK)]
        ddecay = ddecay + jnp.concatenate(held, axis=0)
        rows_in = row_at(r, BLOCK)
        step = step_ref[rows_in, :]
        direct = (outs[:, :LANES] + outs[:, LANES:]) / jnp.maximum(step, 1e-37)
        dz = (direct + ddecay * rate) * sigmoid(z_ref[rows_in, :])
        dstep[here, :] = dz.astype(bf16)
        heads[0] = heads[0] + jnp.sum(dz, axis=0, keepdims=True)
        heads[1] = heads[1] + jnp.sum(ddecay * step, axis=0, keepdims=True) * rate
    grad_head_ref[...] += jnp.concatenate([*heads, jnp.zeros((6, LANES), f32)], axis=0)

    @pl.when(step_at == pl.num_programs(0) - 1)
    def _():
        dstate_out[...] = dstate[...]
        vectors = grad_vconv_ref[...]
        tall = [split(vectors[:, p * LANES : (p + 1) * LANES]) for p in range(pairs)]
        skips = dot(jnp.concatenate(tall, axis=1), gather_ref[...])
        grad_head_ref[2:3, :] = skips[5:6, :LANES] + skips[5:6, LANES:]
        dahalo[...] = dabuf[:, 0:8, :]
        dshalo[...] = dsbuf[:, 0:8, :]


MIB = dict(
    forward_kernel=11,
    stats_kernel=6,
    branch_kernel=6,
    gate_kernel=10,
    backward_kernel=17,
    weights_kernel=11,
    normed_grad_kernel=12,
    mixed_kernel=8,
    input_kernel=8,
    early_kernel=10,
    late_kernel=10,
    place_kernel=8,
    partial_kernel=8,
)
COST = dict(forward_kernel=4.5, backward_kernel=7, stats_kernel=1, branch_kernel=.6, gate_kernel=2.4, weights_kernel=1.2, normed_grad_kernel=1.2, mixed_kernel=1, input_kernel=1, early_kernel=3, late_kernel=3, place_kernel=1, partial_kernel=2)


def whole(array):
    return pl.BlockSpec(array.shape, lambda i, at: (0,) * array.ndim)


def call(kernel, blocks, at, ins, outs, scratch, small=True, aliases=()):
    title = getattr(kernel, "func", kernel).__name__
    return pl.pallas_call(
        kernel,
        name=title,
        grid_spec=pltpu.PrefetchScalarGridSpec(
            num_scalar_prefetch=1,
            grid=(blocks,),
            in_specs=[whole(a) if s is None else s for a, s in ins],
            out_specs=[out[2] for out in outs],
            scratch_shapes=scratch,
        ),
        out_shape=[
            pltpu.VMEM(shape, dtype) if rest and rest[0] else jax.ShapeDtypeStruct(shape, dtype)
            for shape, dtype, _, *rest in outs
        ],
        cost_estimate=pl.CostEstimate(flops=int(COST.get(title, 1)*blocks * 10**9), bytes_accessed=0, transcendentals=0),
        input_output_aliases=dict(aliases),
        compiler_params=pltpu.CompilerParams(
            dimension_semantics=("arbitrary",), vmem_limit_bytes=(MIB.get(title, 16) if small else 48) * 2**20
        ),
    )(at, *[a for a, _ in ins])


def per_device(
    residual_in,
    norm_gain,
    gate_proj,
    value_proj,
    state_proj,
    step_proj,
    value_conv,
    value_shift,
    state_conv,
    state_shift,
    step_bias,
    log_rate,
    skip_gain,
    gated_gain,
    out_proj,
    grad_out,
):
    parts = lax.axis_size("heads")
    two = parts == 2
    rows_here, model = residual_in.shape[1:]
    length = rows_here * parts
    inner = value_conv.shape[1]
    inner_all = inner * parts
    heads = step_bias.shape[0]
    head_width = inner // heads
    pad_heads = -heads % 4
    nheads = heads + pad_heads
    width = nheads * head_width
    nstate2 = state_conv.shape[1]
    blocks = length // BLOCK
    chunks = BLOCK // CHUNK
    half_blocks = rows_here // BLOCK if two else blocks

    def wide(a, axis, fill=0):
        pads = [(0, 0)] * a.ndim
        pads[axis] = (0, width - inner)
        return jnp.pad(a, pads, constant_values=fill) if width > inner else a

    def lanes_of(a):
        return jnp.pad(a, [(0, 0)] * (a.ndim - 1) + [(0, LANES - a.shape[-1])])

    residual = residual_in[0]
    cot = grad_out[0]
    batch = lax.axis_size("batch")
    fast = two and batch == 16 and width == model and model % BLOCK == 0
    nstate = nstate2 // 2
    run = functools.partial(call, small=fast)
    place = lax.axis_index("batch").astype(jnp.int32)
    across = lax.axis_index("heads").astype(jnp.int32) if two else jnp.int32(0)
    own_from = lax.axis_index("heads").astype(jnp.int32) * rows_here
    at = jnp.stack([across, place & 1, (place >> 1) & 1, place >> 2, own_from])
    if two:
        swap = [(0, 1), (1, 0)]
        pair_of = lambda a: (a, lax.ppermute(a, "heads", swap))
        add_other = lambda a: lax.ppermute(a, "heads", swap)
    else:

        def pair_of(a):
            full = lax.all_gather(a, "heads", axis=0, tiled=True)
            return (full, full)

        add_other = lambda a: lax.psum(a, "heads") - a

    def hop(a, way):
        mask = {"core": 1, "line": 2}.get(way) or 4 * way
        return lax.ppermute(a, "batch", [(i, i ^ mask) for i in range(batch)])

    def bring(*arrays):
        if not fast:
            return arrays
        return run(
            bring_kernel,
            1,
            at,
            [(a, None) for a in arrays],
            [(a.shape, a.dtype, pl.BlockSpec(a.shape, lambda i, at: (0, 0)), True) for a in arrays],
            [],
        )

    own_rows, other_rows = pair_of(residual)
    own_cot, other_cot = pair_of(cot)

    gate_w, value_w = wide(gate_proj, 1), wide(value_proj, 1)
    out_w = wide(out_proj, 0)
    step_w = lanes_of(step_proj)
    gain_in = norm_gain[None, :]
    vconv, vshift = wide(value_conv, 1), wide(value_shift[None, :], 1)
    sshift = state_shift[None, :]
    sbias, rate = lanes_of(step_bias[None, :]), lanes_of(log_rate[None, :])
    skipx = wide(jnp.repeat(skip_gain, head_width)[None, :], 1)
    ggain = wide(gated_gain[None, :], 1, 1)
    head_of = jnp.arange(width) // head_width
    spread = (jnp.arange(LANES)[:, None] == head_of[None, :]).astype(bf16)
    spread = jnp.concatenate([spread, spread], axis=0)
    first = head_of.reshape(-1, 1, LANES, 1) + jnp.arange(2).reshape(1, 2, 1, 1) * LANES
    gather = (jnp.arange(2 * LANES) == first).reshape(-1, 2 * LANES).astype(bf16)

    gate_w, value_w, state_proj, step_w, out_w, spread, gather = bring(
        gate_w, value_w, state_proj, step_w, out_w, spread, gather
    )
    gain_in, vconv, vshift, state_conv, sshift, sbias, rate, skipx, ggain = bring(
        gain_in, vconv, vshift, state_conv, sshift, sbias, rate, skipx, ggain
    )

    def own_block(i, a):
        return (jnp.clip(i - a[0] * half_blocks, 0, half_blocks - 1), 0)

    def other_block(i, a):
        return (jnp.clip(i - (1 - a[0]) * half_blocks, 0, half_blocks - 1), 0) if two else (0, 0)

    other_read = other_block if two else own_block

    def rows(n, index=lambda i, a: (i, 0)):
        return pl.BlockSpec((BLOCK, n), index)

    along = pl.BlockSpec((8, BLOCK), lambda i, a: (0, i))
    unit = 2 * BLOCK if two and rows_here % (2 * BLOCK) == 0 else BLOCK
    units, half_units = length // unit, half_blocks * BLOCK // unit

    def own_unit(i, a):
        return (jnp.clip(i - a[0] * half_units, 0, half_units - 1), 0)

    def other_unit(i, a):
        return (jnp.clip(i - (1 - a[0]) * half_units, 0, half_units - 1), 0)

    other_taken = other_unit if two else own_unit

    def tall(n, index=lambda i, a: (i, 0)):
        return pl.BlockSpec((unit, n), index)

    fixed = lambda *shape: pl.BlockSpec(shape, lambda i, a: (0,) * len(shape))
    states_spec = lambda index: pl.BlockSpec((chunks, nstate, width), index)
    big = lambda *shape: pltpu.VMEM(shape, f32)
    low = lambda *shape: pltpu.VMEM(shape, bf16)
    halves = [
        ((rows_here if two else length, model), bf16, rows(model, own_block)),
        ((rows_here if two else BLOCK, model), bf16, rows(model, other_block)),
    ]

    normed, g, y, gg, values, slope, vp, conv_s, sp, z, sin, sq, step, running, shifted, grownx, tailx = run(
        functools.partial(forward_kernel, half_blocks),
        blocks,
        at,
        [
            (own_rows, rows(model, own_block)),
            (other_rows, rows(model, other_read)),
            (gain_in, None),
            (gate_w, None),
            (value_w, None),
            (state_proj, None),
            (step_w, None),
            (vconv, None),
            (vshift, None),
            (state_conv, None),
            (sshift, None),
            (sbias, None),
            (rate, None),
            (skipx, None),
            (ggain, None),
            (spread, None),
        ],
        [
            *[
                (shape, dtype, spec, fast)
                for shape, dtype, spec in (
                    ((length, model), bf16, rows(model)),
                    ((length, width), f32, rows(width)),
                    ((length, width), f32, rows(width)),
                    ((length, width), bf16, rows(width)),
                    ((length, width), bf16, rows(width)),
                    ((length, width), bf16, rows(width)),
                    ((length, width), bf16, rows(width)),
                    ((length, nstate2), f32, rows(nstate2)),
                    ((length, nstate2), bf16, rows(nstate2)),
                    ((length, LANES), f32, rows(LANES)),
                    ((blocks * chunks, nstate, width), bf16, states_spec(lambda i, a: (i, 0, 0))),
                    ((8, length), f32, along),
                    ((length, LANES), f32, rows(LANES)),
                    ((length, LANES), f32, rows(LANES)),
                    ((length, LANES), f32, rows(LANES)),
                    ((length, width), f32, rows(width)),
                    ((length, width), f32, rows(width)),
                )
            ]
        ],
        [
            big(width // LANES, BLOCK + 8, LANES),
            big(nstate2 // LANES, BLOCK + 8, LANES),
            big(nstate, width),
            big(BLOCK, width),
            big(BLOCK, width),
            low(BLOCK, width),
        ],
    )
    def stats_of(cot_rows, theirs, *before):
        first = (lambda a: (1 - a[0]) * half_units) if theirs else (lambda a: a[0] * half_units)
        count = cot_rows.shape[0]
        return run(
            stats_kernel,
            count // unit,
            at,
            [
                (cot_rows, tall(model)),
                (gg, tall(width, lambda i, a: (first(a) + i, 0))),
                (sq, pl.BlockSpec((8, unit), lambda i, a: (0, first(a) + i))),
                (out_w, None),
                *[(b, pl.BlockSpec((8, unit), lambda i, a: (0, i))) for b in before],
            ],
            [
                ((count, width), f32, tall(width), fast),
                (
                    (8 + 8 * len(before), count),
                    f32,
                    pl.BlockSpec((8 + 8 * len(before), unit), lambda i, a: (0, i)),
                ),
            ],
            [],
        )

    og, stats = stats_of(own_cot, False)
    if two:
        og_b, stats = stats_of(other_cot, True, stats)
    else:
        og_b = og
    got = add_other(stats)
    above = 1 if two else 0

    def stats_at(row, block, size=BLOCK):
        return pl.BlockSpec((8, size), lambda i, a: (row, block(i, a)[0]))

    branch, branch_sent = run(
        functools.partial(branch_kernel, half_units),
        units,
        at,
        [(gg, tall(width)), (out_w, None)],
        [
            ((rows_here if two else length, model), bf16, tall(model, own_unit)),
            ((rows_here if two else BLOCK, model), bf16, tall(model, other_unit if two else other_block)),
        ],
        [],
    )

    def other_half(own, sent):
        if two:
            return lax.ppermute(sent, "heads", swap)
        total = lax.psum_scatter(own.astype(f32), "heads", scatter_dimension=0, tiled=True)
        mine = lax.dynamic_slice_in_dim(own, own_from, rows_here, 0).astype(f32)
        return total - mine

    branch_got = other_half(branch, branch_sent)
    if not two:
        branch = lax.dynamic_slice_in_dim(branch, own_from, rows_here, 0)
    if fast:
        pieces = [((model // 2, 2 * model), bf16, fixed(model // 2, 2 * model))] * 2
    else:
        pieces = [
            ((model, width), f32, fixed(model, width)),
            ((width, model), f32, fixed(width, model)),
        ]
    dg, dy, early_a, early_b, grad_gain, norm = run(
        functools.partial(gate_kernel, half_units, inner_all, fast),
        units,
        at,
        [
            (own_cot, tall(model, own_unit)),
            (other_cot, tall(model, other_taken)),
            (stats, stats_at(above, own_unit, unit)),
            (got, stats_at(0, own_unit, unit)),
            (stats, stats_at(0, other_taken, unit)),
            (got, stats_at(above, other_taken, unit)),
            (normed, None),
            (og, tall(width, own_unit)),
            (og_b, tall(width, other_taken)),
            (y, tall(width)),
            (g, tall(width)),
            (gg, None),
            (ggain, None),
            (gate_w, None),
            (branch, pl.BlockSpec(memory_space=pl.ANY)),
        ],
        [
            ((length, width), bf16, fixed(length, width), fast),
            ((length, width), bf16, tall(width), fast),
            *pieces,
            ((8, width), f32, fixed(8, width)),
            ((8, model), f32, fixed(8, model)),
        ],
        [low(length, model)] + ([big(model, width), big(width, model)] if fast else []),
    )

    def backward(start, count, carry, after=()):
        size = 2 * BLOCK if start % 2 == 0 and count % 2 == 0 else BLOCK
        size = count * BLOCK if fast else size
        steps, base = count * BLOCK // size, start * BLOCK // size

        def local(n):
            return pl.BlockSpec((size, n), lambda i, a: (steps - 1 - i, 0))

        def taken(array):
            if fast:
                return (array, None)
            shape = (size // CHUNK if array.ndim == 3 else size, *array.shape[1:])
            rest = (0,) * (array.ndim - 1)
            return (array, pl.BlockSpec(shape, lambda i, a: (base + steps - 1 - i, *rest)))

        slabs = [(width // LANES, 8, LANES), (nstate2 // LANES, 8, LANES)]
        vectors = [(nstate, width), *slabs, (8, width), (8, nstate2), (8, LANES)]
        out = run(
            functools.partial(
                backward_kernel, size, start * BLOCK if fast else 0, bool(carry), len(after)
            ),
            steps,
            at,
            [
                *[
                    taken(a)
                    for a in (dy, values, slope, vp, conv_s, sp, z, step, running, shifted, grownx, tailx, sin)
                ],
                (vconv, None),
                (state_conv, None),
                (rate, None),
                (skipx, None),
                (gather, None),
                *[(c, None) for c in carry],
                *[(a, pl.BlockSpec(memory_space=pl.ANY)) for a in after],
            ],
            [
                ((count * BLOCK, width), bf16, local(width)),
                ((count * BLOCK, nstate2), bf16, local(nstate2)),
                ((count * BLOCK, LANES), bf16, local(LANES)),
                *[(shape, f32, fixed(*shape)) for shape in vectors],
            ],
            [
                big(width // LANES, size + 8, LANES),
                big(nstate2 // LANES, size + 8, LANES),
                big(nstate, width),
                big(size, width),
                big(size, width),
                low(size, width),
                low(size, width),
                low(size, 2 * width),
                low(size, 2 * width),
            ],
        )
        return out[:3], out[3:]

    if two:
        own_stats, their_stats = stats_at(1, lambda i, a: (i, 0)), along
    else:
        own_stats = their_stats = stats_at(0, lambda i, a: (i + a[4] // BLOCK, 0))
    mixed, token = run(
        functools.partial(mixed_kernel, inner_all),
        rows_here // BLOCK,
        at,
        [
            (residual, rows(model)),
            (branch, rows(model)),
            (branch_got, rows(model)),
            (stats, own_stats),
            (got, their_stats),
        ],
        [((rows_here, model), f32, rows(model)), ((8, LANES), f32, fixed(8, LANES))],
        [],
    )
    from_gate = run(
        gate_back_kernel,
        blocks,
        at,
        [(dg, rows(width)), (gate_w, None)],
        [((length, model), f32, rows(model), fast)],
        [],
    )[0]
    cut = blocks // 2
    behind = ()
    if fast:
        steps = [("fold", 2, [early_a, hop(early_b, "core")], 2, False)]
        ((kept, sent),) = stage(at, steps, (from_gate,))
        early = [kept, hop(sent, "line")]
        behind = (kept,)
    low_b, carry = backward(cut, blocks - cut, (), behind)
    partial = run(
        functools.partial(partial_kernel, cut * BLOCK),
        1,
        at,
        [(normed, None), *[(a, None) for a in low_b]],
        [
            ((model, a.shape[1]), f32, fixed(model, a.shape[1])) for a in low_b
        ],
        [],
    )
    if fast:
        ((kept, *sent),) = stage(at, [("fold", 3, early, 4, False)])
        early = [kept] + [hop(a, k + 1) for k, a in enumerate(sent)]
        behind = (kept, branch_got, partial[2])
    low_a, carry = backward(0, cut, carry, behind)
    vec, svec, head = carry[3:]
    early = early if fast else ()
    lows = [(a, rows(a.shape[1], lambda i, at: (jnp.minimum(i, cut - 1), 0))) for a in low_a]
    lows += [(a, rows(a.shape[1], lambda i, at: (jnp.maximum(i - cut, 0), 0))) for a in low_b]

    if fast:
        shape = (model // 2, width + nstate2 + LANES)
        pieces = [(shape, bf16, fixed(*shape))] * 2
        pieces.append((early[0].shape, bf16, fixed(*early[0].shape)))
    else:
        shapes = [(model, width), (model, nstate2), (model, LANES), (8, model)]
        pieces = [(shape, f32, fixed(*shape)) for shape in shapes]
    late = run(
        functools.partial(weights_kernel, fast),
        1,
        at,
        [
            (normed, None),
            *[(a, None) for a in low_a],
            *[(a, None) for a in partial],
            (value_w, None),
            (state_proj, None),
            (step_w, None),
            (gain_in, None),
            (vec, None),
            (svec, None),
            (head, None),
            (grad_gain, None),
            (norm, None),
            *[(a, None) for a in early],
        ],
        pieces,
        [big(model, width), big(model, nstate2), big(model, LANES)],
    )
    ng, ng_sent = run(
        functools.partial(normed_grad_kernel, half_blocks, cut),
        blocks,
        at,
        [
            (from_gate, rows(model)),
            *lows,
            (value_w, None),
            (state_proj, None),
            (step_w, None),
        ],
        halves,
        [],
    )

    ng_got = other_half(ng, ng_sent)
    if not two:
        ng = lax.dynamic_slice_in_dim(ng, own_from, rows_here, 0)
    grad_input, token_b = run(
        input_kernel,
        rows_here // BLOCK,
        at,
        [
            (residual, rows(model)),
            (cot, rows(model)),
            (ng, rows(model)),
            (ng_got, rows(model)),
            (gain_in, None),
        ],
        [((rows_here, model), f32, rows(model)), ((8, LANES), f32, fixed(8, LANES))],
        [],
    )

    if fast:
        kept, sent, early = late
        ((kept, sent),) = stage(at, [("fold", 2, [kept, hop(sent, "core")], 2, True)])
        got = hop(sent, "line")
        early = [early] + [hop(early, k) for k in (1, 2, 3)]
        ((kept, *sent),) = stage(at, [("fold", 3, [kept, got], 4, True)], (ng,))
        got = [hop(a, k + 1) for k, a in enumerate(sent)]
        steps = [("part", width, [kept, *got], 2, True), ("join", 3, early)]
        (done, rest), (early,) = stage(at, steps, (token,))
        early = [early, hop(early, "line")]
        theirs = lax.ppermute(rest, "heads", swap)
        done = run(
            heads_kernel,
            1,
            at,
            [(done, None), (rest, None), (theirs, None)],
            [((rest.shape[0], width + rest.shape[1]), bf16, fixed(rest.shape[0], width + rest.shape[1]))],
            [],
        )[0]
        done = [done] + [hop(done, k) for k in (1, 2, 3)]
        (done,), (early,) = stage(at, [("join", 3, done), ("join", 2, early)], (token_b,))
        grad_gate, grad_out_proj, token_c = run(
            early_kernel,
            1,
            at,
            [(early, None), (hop(early, "core"), None)],
            [((model, model), f32, fixed(model, model))] * 2
            + [((8, LANES), f32, fixed(8, LANES))],
            [],
        )
        quarter = done.shape[0]

        def wide(n):
            def index(i, a):
                return ((a[1] ^ (n // 2)) * 2 + (a[2] ^ (n % 2)), 0)

            return [((model, w), f32, pl.BlockSpec((quarter, w), index)) for w in (width, nstate2)]

        def kept_in(arrays):
            return [(a, pl.BlockSpec(memory_space=pl.ANY)) for a in arrays]

        def place(n, piece, filled=()):
            aliases = ((2, 0), (3, 1)) if filled else ()
            ins = [(piece, None), *kept_in(filled)]
            outs = wide(n) + [((8, LANES), f32, fixed(8, LANES))]
            return run(place_kernel, 1, at, ins, outs, [], aliases=aliases)

        got = hop(done, "line")
        across = hop(done, "core")
        *filled, token_d = place(0, done)
        *filled, token_e = place(2, across, filled)
        ((got,),) = stage(at, [("join", 2, [got])], (token_c, token_e))
        done = [done, got, across, hop(got, "core")]
        *filled, token_d = place(1, got, filled)
        shapes = [
            (heads, model),
            (4, width),
            (width,),
            (width,),
            (model,),
            (4, nstate2),
            (nstate2,),
            (heads,),
            (heads,),
            (heads,),
        ]
        (
            grad_value,
            grad_state,
            grad_step,
            grad_vconv,
            grad_vshift,
            grad_ggain,
            grad_norm,
            grad_sconv,
            grad_sshift,
            grad_bias,
            grad_rate,
            grad_skip,
        ) = run(
            late_kernel,
            1,
            at,
            [*[(a, None) for a in done], *kept_in(filled)],
            wide(3) + [(shape, f32, fixed(*shape)) for shape in shapes],
            [big(model, LANES)],
            aliases=((5, 0), (6, 1)),
        )
        return (
            mixed[None],
            grad_input[None],
            grad_norm,
            grad_gate,
            grad_value,
            grad_state,
            grad_step.T,
            grad_vconv,
            grad_vshift,
            grad_sconv,
            grad_sshift,
            grad_bias,
            grad_rate,
            grad_skip,
            grad_ggain,
            grad_out_proj,
        )
    grad_value, grad_state, grad_step, norm = late
    grad_gate, grad_value, grad_out_proj, grad_step, vec, head, grad_gain = lax.psum(
        (early_a, grad_value, early_b, grad_step, vec, head, grad_gain), "batch"
    )
    grad_state, svec, norm = lax.psum((grad_state, svec, norm), ("batch", "heads"))
    norm, ggrad = norm[0], grad_gain[0]
    return (
        mixed[None],
        grad_input[None],
        norm,
        grad_gate[:, :inner],
        grad_value[:, :inner],
        grad_state,
        grad_step[:, :heads],
        vec[:4, :inner],
        vec[4, :inner],
        svec[:4],
        svec[4],
        head[0, :heads],
        head[1, :heads],
        head[2, :heads],
        ggrad[:inner],
        grad_out_proj[:inner],
    )


def solution(mesh):
    return jax.shard_map(
        per_device,
        mesh=mesh,
        in_specs=(
            P("batch", "heads", None),
            P(),
            P(None, "heads"),
            P(None, "heads"),
            P(),
            P(None, "heads"),
            P(None, "heads"),
            P("heads"),
            P(),
            P(),
            P("heads"),
            P("heads"),
            P("heads"),
            P("heads"),
            P("heads", None),
            P("batch", "heads", None),
        ),
        out_specs=(
            P("batch", "heads", None),
            P("batch", "heads", None),
            P(),
            P(None, "heads"),
            P(None, "heads"),
            P(),
            P(None, "heads"),
            P(None, "heads"),
            P("heads"),
            P(),
            P(),
            P("heads"),
            P("heads"),
            P("heads"),
            P("heads"),
            P("heads", None),
        ),
        check_vma=False,
    )
```

```python
import functools

import jax
import jax.numpy as jnp
from jax import lax
from jax.experimental import pallas as pl
from jax.experimental.pallas import tpu as pltpu
from jax.sharding import PartitionSpec as P

EPSILON = 1e-05
HIGHEST = lax.Precision.HIGHEST
BLOCK = 256
CHUNK = 128
LANES = 128
HALF = LANES // 2
QUAD = 2 * LANES
LOG2E = 1.4426950408889634
f32 = jnp.float32
bf16 = jnp.bfloat16


def dot(left, right, over=((1,), (0,)), precision=None):
    return lax.dot_general(
        left, right, (over, ((), ())), preferred_element_type=f32, precision=precision
    )


TN = ((0,), (0,))
NT = ((1,), (1,))


def sigmoid(v):
    return 1.0 / (1.0 + jnp.exp(-v))


def silu(v):
    half = 0.5 * v
    return half + half * jnp.tanh(half)


def silu_slope(v):
    half = 0.5 * v
    t = jnp.tanh(half)
    out = half + half * t
    sig = 0.5 + 0.5 * t
    return out, sig + out * (1.0 - sig)


def causal_back(buf, slab, r0, grad, pre, taps, extra):
    buf[slab, pl.ds(r0, CHUNK), :] = grad
    lanes = slice(slab * LANES, (slab + 1) * LANES)
    pre = pre.astype(f32)
    out, rows = 0.0, []
    for tap in range(4):
        moved = grad if tap == 3 else buf[slab, pl.ds(r0 + 3 - tap, CHUNK), :]
        out = out + taps[tap : tap + 1, lanes].astype(f32) * moved
        rows.append(jnp.sum(pre * moved, axis=0, keepdims=True))
    rows.append(jnp.sum(grad, axis=0, keepdims=True))
    rows += [extra, jnp.zeros((2, LANES), f32)]
    return out, jnp.concatenate(rows, axis=0)


def split(v):
    high = v.astype(bf16)
    return jnp.concatenate([high, (v - high.astype(f32)).astype(bf16)], axis=1)


def lower_mask(rows):
    return lax.broadcasted_iota(jnp.int32, (rows, rows), 0) >= lax.broadcasted_iota(
        jnp.int32, (rows, rows), 1
    )


def chunk_mask(strict=False):
    row = lax.broadcasted_iota(jnp.int32, (BLOCK, BLOCK), 0)
    column = lax.broadcasted_iota(jnp.int32, (BLOCK, BLOCK), 1)
    ordered = row > column if strict else row >= column
    return (ordered & (row // CHUNK == column // CHUNK)).astype(bf16)


def block_scalars(z, log_rate, spread):
    step = jnp.maximum(z, 0.0) + jnp.log1p(jnp.exp(-jnp.abs(z)))
    rate = -jnp.exp(log_rate)
    decay = jnp.where(lax.broadcasted_iota(jnp.int32, (1, LANES), 1) < 32, step * (rate * LOG2E), 0.0)
    high = decay.astype(bf16).astype(f32)
    middle = (decay - high).astype(bf16).astype(f32)
    packed = high + pltpu.roll(middle, 32, 1) + pltpu.roll(decay - high - middle, 64, 1)
    sums = dot(chunk_mask(), packed.astype(bf16))
    running = sums + pltpu.roll(sums, LANES - 32, 1) + pltpu.roll(sums, LANES - 64, 1)
    last = [running[r + CHUNK - 1 : r + CHUNK, :] for r in range(0, BLOCK, CHUNK)]
    tail = [jnp.exp2(v - running[k * CHUNK : (k + 1) * CHUNK, :]) for k, v in enumerate(last)]
    tail = step * jnp.concatenate(tail, axis=0)
    wide = dot(jnp.concatenate([split(jnp.exp2(running)), split(tail)], axis=0), spread)
    return step, running, running - jnp.log2(step), wide[:BLOCK], wide[BLOCK:]


def causal(buf, slab, taps, shift):
    lanes = slice(slab * LANES, (slab + 1) * LANES)
    conv = shift[:, lanes].astype(f32)
    for tap in range(4):
        conv = conv + taps[tap : tap + 1, lanes].astype(f32) * buf[slab, pl.ds(5 + tap, BLOCK), :]
    return conv


def chunk_scores(b_rows, c_rows):
    n = b_rows.shape[1]
    b, c = split(b_rows), split(c_rows)
    left = jnp.concatenate([c, c[:, :n]], axis=1)
    right = jnp.concatenate([b[:, :n], b[:, :n], b[:, n:]], axis=1)
    return b, c, dot(left, right, NT)


def quad_mixing(scores, running, shifted_t, quad, mask):
    factors, mixes = [], []
    for head in range(4 * quad, 4 * quad + 4):
        spread = running[:, head : head + 1] - shifted_t[head : head + 1, :]
        factors.append(jnp.exp2(jnp.where(mask, spread, -1e30)))
        mixes.append((scores * factors[-1]).astype(bf16))
    return factors, mixes


def heads_apart(left, right):
    lane = lax.broadcasted_iota(jnp.int32, (1, LANES), 1)
    first = (lane < HALF).astype(bf16)
    zero = jnp.zeros(left.shape, bf16)
    rows = [jnp.concatenate([left * m, zero], axis=1) for m in (first, 1 - first)]
    rows += [jnp.concatenate([zero, right * m], axis=1) for m in (first, 1 - first)]
    return jnp.concatenate(rows, axis=0)


def forward_kernel(
    half_blocks,
    at_ref,
    own_ref,
    other_ref,
    gain_ref,
    gate_w,
    value_w,
    state_w,
    step_w,
    vconv_ref,
    vshift_ref,
    sconv_ref,
    sshift_ref,
    sbias_ref,
    rate_ref,
    skip_ref,
    ggain_ref,
    spread_ref,
    normed_ref,
    g_ref,
    y_ref,
    gg_ref,
    low_ref,
    slope_ref,
    vp_ref,
    as_ref,
    sp_ref,
    z_ref,
    sin_ref,
    sq_ref,
    step_ref,
    running_ref,
    shifted_ref,
    grownx,
    tailx,
    vbuf,
    sbuf,
    state,
    carried,
    values,
    vtail,
):
    step_at = pl.program_id(0)
    pairs = vbuf.shape[0]
    nstate = state.shape[0]

    @pl.when(step_at == 0)
    def _():
        state[...] = jnp.zeros_like(state)
        for buf in (vbuf, sbuf):
            buf[:, 0:8, :] = jnp.zeros((buf.shape[0], 8, LANES), f32)

    mine = (step_at // half_blocks) == at_ref[0]
    rows = jnp.where(mine, own_ref[...], other_ref[...]).astype(f32)
    scale = lax.rsqrt(jnp.mean(rows * rows, axis=1, keepdims=True) + EPSILON)
    normed = (rows * scale * gain_ref[...].astype(f32)).astype(bf16)
    normed_ref[...] = normed
    z = dot(normed, step_w[...]) + sbias_ref[...]
    z_ref[...] = z
    for out, buf, w in ((sp_ref, sbuf, state_w), (vp_ref, vbuf, value_w)):
        pre = dot(normed, w[...])
        out[...] = pre.astype(bf16)
        for slab in range(buf.shape[0]):
            buf[slab, 8:, :] = pre[:, slab * LANES : (slab + 1) * LANES]
    g_ref[...] = dot(normed, gate_w[...])

    step, running, shifted, grownx[...], tailx[...] = block_scalars(z, rate_ref[...], spread_ref[...])
    step_ref[...] = step
    running_ref[...] = running
    shifted_ref[...] = shifted
    chunks = range(BLOCK // CHUNK)
    states = []
    for slab in range(sbuf.shape[0]):
        conv = causal(sbuf, slab, sconv_ref, sshift_ref)
        as_ref[:, slab * LANES : (slab + 1) * LANES] = conv
        states.append(silu(conv))
    for pair in range(pairs):
        lanes = slice(pair * LANES, (pair + 1) * LANES)
        out, slope = silu_slope(causal(vbuf, pair, vconv_ref, vshift_ref))
        slope_ref[:, lanes] = slope.astype(bf16)
        values[:, lanes] = out
        low_ref[:, lanes] = out.astype(bf16)
        vtail[:, lanes] = (out * tailx[:, lanes]).astype(bf16)
    parts = []
    for chunk in chunks:
        here = slice(chunk * CHUNK, (chunk + 1) * CHUNK)
        b_two, c_two, scores = chunk_scores(*(v[here] for v in states))
        parts.append(scores)
        before = state[...].astype(bf16)
        sin_ref[chunk, :, :] = before
        carried[here, :] = dot(c_two[:, :nstate], before)
        last = grownx[(chunk + 1) * CHUNK - 1 : (chunk + 1) * CHUNK, :]
        state[...] = last * state[...] + dot(b_two[:, :nstate], vtail[here, :], TN)
    mask = lower_mask(CHUNK)
    for chunk in chunks:
        here = slice(chunk * CHUNK, (chunk + 1) * CHUNK)
        run = running[here]
        run_t = shifted[here].T
        squares = jnp.zeros((CHUNK, LANES), f32)
        for quad in range(pairs // 2):
            _, mixes = quad_mixing(parts[chunk], run, run_t, quad, mask)
            sides = [slice((2 * quad + k) * LANES, (2 * quad + k + 1) * LANES) for k in range(2)]
            both = dot(
                jnp.concatenate(mixes, axis=1), heads_apart(*(low_ref[here, lanes] for lanes in sides))
            )
            for k, lanes in enumerate(sides):
                scanned = both[:, k * LANES : (k + 1) * LANES]
                scanned = scanned + grownx[here, lanes] * carried[here, lanes]
                scanned = scanned + skip_ref[:, lanes] * values[here, lanes]
                gate, slope = silu_slope(g_ref[here, lanes])
                y_ref[here, lanes] = scanned * slope
                g_ref[here, lanes] = gate
                gated = scanned * gate
                gg_ref[here, lanes] = (gated * ggain_ref[:, lanes].astype(f32)).astype(bf16)
                squares = squares + gated * gated
        sq_ref[:, here] = dot(jnp.ones((8, LANES), f32), squares, NT, HIGHEST)
    for buf in (vbuf, sbuf):
        buf[:, 0:8, :] = buf[:, BLOCK : BLOCK + 8, :]


def stats_kernel(at_ref, cot_ref, gg_ref, sq_ref, out_w, *refs):
    og_ref, stats_ref = refs[-2:]
    if len(refs) > 2:
        stats_ref[8:, :] = refs[0][...]
    og = dot(cot_ref[...], out_w[...], NT)
    og_ref[...] = og
    prod = (og * gg_ref[...].astype(f32)).astype(bf16)
    dots = dot(jnp.ones((8, prod.shape[1]), bf16), prod, NT)
    row = lax.broadcasted_iota(jnp.int32, dots.shape, 0)
    stats_ref[:8, :] = jnp.where(row == 0, sq_ref[...], dots)


def bring_kernel(at_ref, *refs):
    count = len(refs) // 2
    for src, dst in zip(refs[:count], refs[count:]):
        dst[...] = src[...]


def branch_kernel(half_blocks, at_ref, gg_ref, out_w, own_ref, other_ref):
    mine = (pl.program_id(0) // half_blocks) == at_ref[0]
    rows = dot(gg_ref[...], out_w[...]).astype(bf16)

    @pl.when(mine)
    def _():
        own_ref[...] = rows

    @pl.when(jnp.logical_not(mine))
    def _():
        other_ref[...] = rows


def gate_back_kernel(at_ref, dg_ref, gate_w, out_ref):
    out_ref[...] = dot(dg_ref[...], gate_w[...], NT)


def picked(cut, early, late):
    return jnp.where(pl.program_id(0) < cut, early[...], late[...])


def normed_grad_kernel(half_blocks, cut, at_ref, from_gate, *refs):
    lows, (value_w, state_w, step_w, own_ref, other_ref) = refs[:6], refs[6:]
    dv, ds, dz = (picked(cut, a, b) for a, b in zip(lows[:3], lows[3:]))
    mine = (pl.program_id(0) // half_blocks) == at_ref[0]
    rows = (
        from_gate[...]
        + dot(dv, value_w[...], NT)
        + dot(ds, state_w[...], NT)
        + dot(dz, step_w[...], NT)
    ).astype(bf16)

    @pl.when(mine)
    def _():
        own_ref[...] = rows

    @pl.when(jnp.logical_not(mine))
    def _():
        other_ref[...] = rows


def row_sums(grads, weights):
    prod = (grads * weights.astype(f32)).astype(bf16)
    return dot(jnp.ones((8, prod.shape[1]), bf16), prod, NT)


def emit(at_ref, parts, outs):
    half = outs[0].shape[0]
    for j, out in enumerate(outs):
        rows = pl.ds(pl.multiple_of((at_ref[1] ^ j) * half, LANES), half)
        left = 0
        for part in parts:
            out[:, left : left + part.shape[1]] = part[rows, :].astype(out.dtype)
            left += part.shape[1]


def row_column(rows):
    return jnp.concatenate([rows, jnp.zeros((LANES - rows.shape[0], rows.shape[1]), f32)], axis=0).T


def mixed_kernel(inner_all, at_ref, rows_ref, own_ref, other_ref, here_ref, there_ref, out_ref, token_ref):
    token_ref[...] = jnp.zeros_like(token_ref)
    sums = here_ref[...] + there_ref[...]
    scale = row_column(lax.rsqrt(sums / inner_all + EPSILON))[:, 0:1]
    branch = own_ref[...].astype(f32) + other_ref[...].astype(f32)
    out_ref[...] = rows_ref[...].astype(f32) + scale * branch


def input_kernel(at_ref, rows_ref, cot_ref, own_ref, other_ref, gain_ref, out_ref, token_ref):
    token_ref[...] = jnp.zeros_like(token_ref)
    rows = rows_ref[...].astype(f32)
    scale = lax.rsqrt(jnp.mean(rows * rows, axis=1, keepdims=True) + EPSILON)
    pulled = (own_ref[...].astype(f32) + other_ref[...].astype(f32)) * gain_ref[...].astype(f32)
    inner = jnp.mean(pulled * rows, axis=1, keepdims=True) * (scale * scale * scale)
    out_ref[...] = cot_ref[...].astype(f32) + scale * pulled - rows * inner


def gate_kernel(
    half_blocks,
    inner_all,
    fast,
    at_ref,
    own_ref,
    other_ref,
    here_a,
    there_a,
    here_b,
    there_b,
    normed_ref,
    og_a,
    og_b,
    y_ref,
    g_ref,
    gg_ref,
    ggain_ref,
    gate_w,
    _,
    dg_ref,
    dy_ref,
    first_ref,
    second_ref,
    grad_gain_ref,
    norm_ref,
    scaled_ref,
    *scratch,
):
    step_at = pl.program_id(0)
    size = own_ref.shape[0]
    here = pl.ds(pl.multiple_of(step_at * size, BLOCK), size)
    pairs = og_a.shape[1] // LANES
    grad_gate, grad_out = scratch if fast else (first_ref, second_ref)

    @pl.when(step_at == 0)
    def _():
        grad_gain_ref[...] = jnp.zeros_like(grad_gain_ref)

    mine = (step_at // half_blocks) == at_ref[0]
    sums = jnp.where(mine, here_a[...] + there_a[...], here_b[...] + there_b[...])
    scale_row = lax.rsqrt(sums[0:1, :] / inner_all + EPSILON)
    pull_row = scale_row * scale_row * scale_row * sums[1:2, :] / inner_all
    columns = row_column(jnp.concatenate([scale_row, pull_row], axis=0))
    scale, pull = columns[:, 0:1], columns[:, 1:2]
    cot = jnp.where(mine, own_ref[...], other_ref[...]).astype(f32)
    scaled_ref[here, :] = (cot * scale).astype(bf16)
    for pair in range(pairs):
        lanes = slice(pair * LANES, (pair + 1) * LANES)
        og = jnp.where(mine, og_a[:, lanes], og_b[:, lanes]) * scale
        gain = ggain_ref[:, lanes].astype(f32)
        inverse = 1.0 / gain
        low = gg_ref[here, lanes].astype(f32)
        grad_gain_ref[0:1, lanes] += jnp.sum(og * low, axis=0, keepdims=True) * inverse
        gated_grad = gain * og - (low * inverse) * pull
        dy_ref[:, lanes] = (gated_grad * g_ref[:, lanes]).astype(bf16)
        dg_ref[here, lanes] = (gated_grad * y_ref[:, lanes]).astype(bf16)

    @pl.when(step_at == pl.num_programs(0) - 1)
    def _():
        grad_out[...] = dot(gg_ref[...], scaled_ref[...], TN)
        grad_gate[...] = dot(normed_ref[...], dg_ref[...], TN)
        norm_ref[...] = row_sums(grad_gate[...], gate_w[...])
        if fast:
            emit(at_ref, (grad_gate, grad_out), (first_ref, second_ref))


def partial_kernel(from_row, at_ref, normed_ref, *refs):
    for low, out in zip(refs[:3], refs[3:]):
        out[...] = dot(normed_ref[from_row:, :], low[...], TN)


def weights_kernel(fast, at_ref, normed_ref, *refs):
    lows, refs = refs[:6], refs[6:]
    value_w, state_w, step_w, gain_ref, vec_ref, svec_ref, head_ref, ggain_ref, norm_ref = refs[:9]
    outs, acc = refs[9:-3], refs[-3:]
    if fast:
        pieces, outs, done_ref = outs[:4], outs[4:6], outs[6]
        total = pieces[0][...].astype(f32)
        for r in pieces[1:]:
            total = total + r[...].astype(f32)
        done_ref[...] = total.astype(bf16)
    for a, low, rest in zip(acc, lows[:3], lows[3:]):
        a[...] = rest[...] + dot(normed_ref[: low.shape[0], :], low[...], TN)
    norm = norm_ref[...]
    for a, w in zip(acc, (value_w, state_w, step_w)):
        norm = norm + row_sums(a[...], w[...])
    norm = norm / gain_ref[...].astype(f32)
    if fast:
        pack_vectors(acc[2], vec_ref, svec_ref, head_ref, ggain_ref, norm)
        emit(at_ref, acc, outs)
        return
    for o, a in zip(outs, acc):
        o[...] = a[...]
    outs[3][...] = norm


VEC_AT = 16
SVEC_AT = 24
HEAD_AT = 32


def pack_vectors(block, vec_ref, svec_ref, head_ref, ggain_ref, norm):
    model = block.shape[0]
    row = lax.broadcasted_iota(jnp.int32, (8, model), 0)
    vec = jnp.where(row == 5, ggain_ref[0:1, :], jnp.where(row == 6, norm[0:1, :], vec_ref[...]))

    def tall(v):
        return jnp.concatenate([v, jnp.zeros((8, model - v.shape[1]), f32)], axis=1)

    rows = jnp.concatenate(
        [
            jnp.zeros((VEC_AT, model), f32),
            vec,
            tall(svec_ref[...]),
            tall(head_ref[...]),
            jnp.zeros((LANES - HEAD_AT - 8, model), f32),
        ],
        axis=0,
    )
    lane = lax.broadcasted_iota(jnp.int32, (1, LANES), 1)
    full = jnp.where(lane < VEC_AT, block[...], rows.T)
    block[...] = carry_rest(jnp.where(lane < HALF, full, 0.0))


def carry_rest(full):
    high = full.astype(bf16).astype(f32)
    return high + pltpu.roll(full - high, HALF, 1)


def join_rest(block):
    lane = lax.broadcasted_iota(jnp.int32, (1, LANES), 1)
    return jnp.where(lane < HALF, block + pltpu.roll(block, HALF, 1), 0.0)


def fold_step(me, ins, outs, vectors):
    rows, width = outs[0].shape
    width -= LANES if vectors else 0
    for j, o in enumerate(outs):
        at = slice(0, rows)
        if len(outs) > 1:
            at = pl.ds(pl.multiple_of((me ^ j) * rows, 16), rows)
        o[:, :width] = sum(r[at, :width].astype(f32) for r in ins).astype(bf16)
        if vectors:
            last = sum(r[at, width:].astype(f32) for r in ins)
            o[:, width:] = carry_rest(join_rest(last)).astype(bf16)


def part_step(ins, outs, vectors):
    width = outs[0].shape[1]
    outs[0][...] = sum(r[:, :width].astype(f32) for r in ins).astype(bf16)
    state = outs[1].shape[1] - LANES
    outs[1][:, :state] = sum(r[:, width : width + state].astype(f32) for r in ins).astype(bf16)
    last = sum(r[:, width + state :].astype(f32) for r in ins)
    outs[1][:, state:] = carry_rest(join_rest(last)).astype(bf16)


def join_step(me, ins, out):
    rows = ins[0].shape[0]
    count = out.shape[0] // rows
    if count == 1:
        out[...] = ins[0][...]
        return
    left = 0
    for first in range(0, len(ins), count):
        right = left + ins[first].shape[1]
        for j, r in enumerate(ins[first : first + count]):
            out[pl.ds(pl.multiple_of((me ^ j) * rows, 16), rows), left:right] = r[...]
        left = right


def stage_kernel(plan, extra, at_ref, *refs):
    n_in = sum(count for _, _, count, _, _ in plan)
    ins, outs = refs[:n_in], refs[n_in + extra :]
    for kind, axis, take, give, vectors in plan:
        if kind == "fold":
            fold_step(at_ref[axis], ins[:take], outs[:give], vectors)
        elif kind == "part":
            part_step(ins[:take], outs[:give], vectors)
        else:
            join_step(at_ref[axis], ins[:take], outs[0])
        ins, outs = ins[take:], outs[give:]


def stage(at, steps, after=()):
    plan, arrays, shapes = [], [], []
    for kind, axis, ins, *rest in steps:
        rows, width = ins[0].shape
        count, vectors = rest if rest else (1, False)
        if kind == "fold":
            shapes += [(rows // count, width)] * count
        elif kind == "part":
            shapes += [(rows, axis), (rows, width - axis)]
        else:
            widths = {a.shape[1] for a in ins}
            shapes.append((rows * len(ins) // len(widths), sum(widths)))
        plan.append((kind, axis, len(ins), count, vectors))
        arrays += ins
    out = call(
        functools.partial(stage_kernel, tuple(plan), len(after)),
        1,
        at,
        [(a, None) for a in arrays] + [(a, pl.BlockSpec(memory_space=pl.ANY)) for a in after],
        [(shape, bf16, pl.BlockSpec(shape, lambda i, a: (0, 0))) for shape in shapes],
        [],
    )
    out, results = list(out), []
    for _, _, _, give, _ in plan:
        results.append(out[:give])
        out = out[give:]
    return results


def heads_kernel(at_ref, done_ref, own_ref, other_ref, out_ref):
    start = done_ref.shape[1]
    state = own_ref.shape[1] - LANES
    out_ref[:, :start] = done_ref[...]
    sums = own_ref[:, :state].astype(f32) + other_ref[:, :state].astype(f32)
    out_ref[:, start : start + state] = sums.astype(bf16)
    lane = lax.broadcasted_iota(jnp.int32, (1, LANES), 1)
    shared = (lane == VEC_AT + 6) | ((lane >= SVEC_AT) & (lane < HEAD_AT))
    mine = join_rest(own_ref[:, state:].astype(f32))
    theirs = join_rest(other_ref[:, state:].astype(f32))
    out_ref[:, start + state :] = carry_rest(mine + jnp.where(shared, theirs, 0.0)).astype(bf16)


def halves_of(at_ref, own_ref, other_ref, left, right):
    rows = own_ref.shape[0]
    for j, ref in enumerate((own_ref, other_ref)):
        yield pl.ds(pl.multiple_of((at_ref[1] ^ j) * rows, LANES), rows), ref[:, left:right].astype(f32)


def early_kernel(at_ref, own_ref, other_ref, *outs):
    outs[-1][...] = jnp.zeros_like(outs[-1])
    left = 0
    for o in outs[:-1]:
        right = left + o.shape[1]
        for at, v in halves_of(at_ref, own_ref, other_ref, left, right):
            o[at, :] = v
        left = right


def widen(piece, outs):
    left = 0
    for o in outs:
        right = left + o.shape[1]
        o[...] = piece[:, left:right].astype(f32)
        left = right


def place_kernel(at_ref, piece_ref, *refs):
    widen(piece_ref, refs[-3:-1])
    refs[-1][...] = jnp.zeros_like(refs[-1])


def late_kernel(at_ref, *refs):
    pieces, outs, block = refs[:4], refs[6:-1], refs[-1]
    widen(pieces[3], outs[:2])
    rows, right = pieces[0].shape
    for n, piece in enumerate(pieces):
        start = (at_ref[1] ^ (n // 2)) * 2 + (at_ref[2] ^ (n % 2))
        at = pl.ds(pl.multiple_of(start * rows, 16), rows)
        block[at, :] = piece[:, right - LANES :].astype(f32)
    full = join_rest(block[...])
    rows = full.T
    outs[2][...] = rows[: outs[2].shape[0]]
    vec, svec = rows[VEC_AT : VEC_AT + 8], rows[SVEC_AT : SVEC_AT + 8]
    head = rows[HEAD_AT : HEAD_AT + 8]
    vconv, vshift, ggain, norm, sconv, sshift, bias, rate, skip = outs[3:]
    vconv[...] = vec[:4]
    for o, row in ((vshift, vec[4:5]), (ggain, vec[5:6]), (norm, vec[6:7]), (sshift, svec[4:5])):
        o[...] = row[:, : o.shape[0]].reshape(o.shape)
    sconv[...] = svec[:4, : sconv.shape[1]]
    for j, o in enumerate((bias, rate, skip)):
        o[...] = head[j : j + 1, : o.shape[0]].reshape(o.shape)


def backward_kernel(
    size,
    from_row,
    carried_in,
    extra,
    at_ref,
    dy_ref,
    low_ref,
    slope_ref,
    vp_ref,
    as_ref,
    sp_ref,
    z_ref,
    step_ref,
    running_ref,
    shifted_ref,
    grownx,
    tailx,
    sin_ref,
    vconv_ref,
    sconv_ref,
    rate_ref,
    skip_ref,
    gather_ref,
    *refs,
):
    carries, refs = (refs[:6], refs[6:]) if carried_in else ((), refs)
    refs = refs[extra:]
    dvalue, dstates, dstep, dstate_out, dahalo, dshalo, grad_vconv_ref, grad_sconv_ref, grad_head_ref = refs[:9]
    dabuf, dsbuf, dstate, carried, pulled, ubuf, vtail, inner, outer = refs[9:]
    step_at = pl.program_id(0)
    nstate, width = dstate.shape
    pairs = width // LANES

    def row_at(start, count=CHUNK):
        return slice(from_row + start, from_row + start + count)


    @pl.when(step_at == 0)
    def _():
        if carried_in:
            dstate[...] = carries[0][...]
            dabuf[:, size:, :] = carries[1][...]
            dsbuf[:, size:, :] = carries[2][...]
            grad_vconv_ref[...] = carries[3][...]
            grad_sconv_ref[...] = carries[4][...]
            grad_head_ref[...] = carries[5][...]
        else:
            dstate[...] = jnp.zeros_like(dstate)
            for buf in (dabuf, dsbuf):
                buf[:, size:, :] = jnp.zeros((buf.shape[0], 8, LANES), f32)
            for ref in (grad_vconv_ref, grad_sconv_ref, grad_head_ref):
                ref[...] = jnp.zeros_like(ref)

    @pl.when(step_at > 0)
    def _():
        for buf in (dabuf, dsbuf):
            buf[:, size:, :] = buf[:, 0:8, :]

    chunks = [slice(r, r + CHUNK) for r in range(0, size, CHUNK)]
    zero_row = jnp.zeros((1, LANES), f32)
    rate = -jnp.exp(rate_ref[...])
    states, slopes = [], []
    for slab in range(2):
        out, slope = silu_slope(as_ref[row_at(0, size), slab * LANES : (slab + 1) * LANES])
        states.append(out)
        slopes.append(slope)
    for pair in range(pairs):
        lanes = slice(pair * LANES, (pair + 1) * LANES)
        there = (row_at(0, size), lanes)
        ubuf[:, lanes] = (dy_ref[there].astype(f32) * grownx[there]).astype(bf16)
    two = [chunk_scores(*(v[here] for v in states)) for here in chunks]
    helds, afters = [None] * len(chunks), [None] * len(chunks)
    for chunk in reversed(range(len(chunks))):
        here = chunks[chunk]
        b_two, c_two, _ = two[chunk]
        before = sin_ref[from_row // CHUNK + chunk, :, :]
        last = grownx[row_at(here.stop - 1, 1), :]
        grad = dstate[...]
        afters[chunk] = grad.astype(bf16)
        carried[here, :] = dot(c_two[:, :nstate], before)
        pulled[here, :] = dot(b_two[:, :nstate], afters[chunk])
        overlap = jnp.sum(before.astype(f32) * grad, axis=0, keepdims=True) * last
        overlap = jnp.broadcast_to(overlap, (8, width))
        tall = [split(overlap[:, p * LANES : (p + 1) * LANES]) for p in range(pairs)]
        held = dot(jnp.concatenate(tall, axis=1), gather_ref[...])[0:1]
        helds[chunk] = held[:, :LANES] + held[:, LANES:]
        dstate[...] = last * grad + dot(c_two[:, :nstate], ubuf[here, :], TN)

    mask = lower_mask(CHUNK)
    for chunk in reversed(range(len(chunks))):
        here = chunks[chunk]
        b_two, c_two, scores = two[chunk]
        rows_in = row_at(here.start)
        run = running_ref[rows_in, :]
        run_t = shifted_ref[rows_in, :].T
        dscores = jnp.zeros((CHUNK, CHUNK), f32)
        for quad in range(pairs // 2):
            factors, mixes = quad_mixing(scores, run, run_t, quad, mask)
            both = [slice((2 * quad + k) * LANES, (2 * quad + k + 1) * LANES) for k in range(2)]
            low = [low_ref[rows_in, lanes] for lanes in both]
            dy_low = [dy_ref[rows_in, lanes] for lanes in both]
            apart = heads_apart(*low)
            scanned = dot(jnp.concatenate(mixes, axis=1), apart)
            dsteps = dot(jnp.concatenate(mixes, axis=0), heads_apart(*dy_low), TN)
            for k, lanes in enumerate(both):
                pair = 2 * quad + k
                own = slice(k * LANES, (k + 1) * LANES)
                dmixing = dot(dy_low[k], apart[2 * k * CHUNK : 2 * (k + 1) * CHUNK, own], NT)
                dscores = dscores + dmixing[:, :CHUNK] * factors[2 * k]
                dscores = dscores + dmixing[:, CHUNK:] * factors[2 * k + 1]
                wide = slice(2 * pair * LANES, (2 * pair + 1) * LANES)
                wide_b = slice((2 * pair + 1) * LANES, (2 * pair + 2) * LANES)
                dy, values = dy_low[k].astype(f32), low[k].astype(f32)
                dvalues = dsteps[:, own]
                pulls = values * dvalues
                inside = dy * scanned[:, own] - pulls + ubuf[here, lanes].astype(f32) * carried[here, lanes]
                high = inside.astype(bf16)
                inner[here, wide] = high
                inner[here, wide_b] = (inside - high.astype(f32)).astype(bf16)
                tails, pull = tailx[rows_in, lanes], pulled[here, lanes]
                v = (values * tails).astype(bf16)
                vtail[here, lanes] = v
                outer[here, wide] = pulls.astype(bf16)
                outer[here, wide_b] = (v.astype(f32) * pull).astype(bf16)
                da = (dvalues + tails * pull + skip_ref[:, lanes] * dy) * slope_ref[rows_in, lanes].astype(f32)
                skips = jnp.sum(values * dy, axis=0, keepdims=True)
                dv, rows = causal_back(dabuf, pair, here.start, da, vp_ref[rows_in, lanes], vconv_ref, skips)
                grad_vconv_ref[:, lanes] += rows
                dvalue[here, lanes] = dv.astype(bf16)
        dlow = dscores.astype(bf16)
        drest = (dscores - dlow.astype(f32)).astype(bf16)
        b_rows, c_rows = b_two[:, :nstate], c_two[:, :nstate]
        cross = dot(
            jnp.concatenate([vtail[here, :], ubuf[here, :]], axis=0),
            jnp.concatenate([afters[chunk], sin_ref[from_row // CHUNK + chunk, :, :]], axis=0),
            NT,
        )
        db = cross[:CHUNK, :nstate] + dot(
            jnp.concatenate([dlow, dlow, drest], axis=0),
            jnp.concatenate([c_rows, c_two[:, nstate:], c_rows], axis=0),
            TN,
        )
        dc = cross[CHUNK:, nstate:] + dot(
            jnp.concatenate([dlow, dlow, drest], axis=1),
            jnp.concatenate([b_rows, b_two[:, nstate:], b_rows], axis=0),
        )
        for slab, d in enumerate((db, dc)):
            lanes = slice(slab * LANES, (slab + 1) * LANES)
            d = d * slopes[slab][here]
            dpre, rows = causal_back(dsbuf, slab, here.start, d, sp_ref[rows_in, lanes], sconv_ref, zero_row)
            grad_sconv_ref[:, lanes] += rows
            dstates[here, lanes] = dpre.astype(bf16)

    gathered = dot(jnp.concatenate([inner[...], outer[...]], axis=0), gather_ref[...])
    heads = [jnp.zeros((1, LANES), f32)] * 2
    for r in range(0, size, BLOCK):
        here = slice(r, r + BLOCK)
        sums, outs = gathered[here], gathered[size + r : size + r + BLOCK]
        ddecay = dot(chunk_mask(), split(sums[:, :LANES] + sums[:, LANES:]), TN)
        ddecay = ddecay[:, :LANES] + ddecay[:, LANES:]
        ddecay = ddecay + dot(chunk_mask(True), outs[:, LANES:].astype(bf16))
        held = [jnp.broadcast_to(helds[k // CHUNK], (CHUNK, LANES)) for k in range(r, r + BLOCK, CHUNK)]
        ddecay = ddecay + jnp.concatenate(held, axis=0)
        rows_in = row_at(r, BLOCK)
        step = step_ref[rows_in, :]
        direct = (outs[:, :LANES] + outs[:, LANES:]) / jnp.maximum(step, 1e-37)
        dz = (direct + ddecay * rate) * sigmoid(z_ref[rows_in, :])
        dstep[here, :] = dz.astype(bf16)
        heads[0] = heads[0] + jnp.sum(dz, axis=0, keepdims=True)
        heads[1] = heads[1] + jnp.sum(ddecay * step, axis=0, keepdims=True) * rate
    grad_head_ref[...] += jnp.concatenate([*heads, jnp.zeros((6, LANES), f32)], axis=0)

    @pl.when(step_at == pl.num_programs(0) - 1)
    def _():
        dstate_out[...] = dstate[...]
        vectors = grad_vconv_ref[...]
        tall = [split(vectors[:, p * LANES : (p + 1) * LANES]) for p in range(pairs)]
        skips = dot(jnp.concatenate(tall, axis=1), gather_ref[...])
        grad_head_ref[2:3, :] = skips[5:6, :LANES] + skips[5:6, LANES:]
        dahalo[...] = dabuf[:, 0:8, :]
        dshalo[...] = dsbuf[:, 0:8, :]


MIB = dict(
    forward_kernel=11,
    stats_kernel=6,
    branch_kernel=6,
    gate_kernel=10,
    backward_kernel=17,
    weights_kernel=11,
    normed_grad_kernel=12,
    mixed_kernel=8,
    input_kernel=8,
    early_kernel=10,
    late_kernel=10,
    place_kernel=8,
    partial_kernel=8,
)
COST = dict(forward_kernel=4.5, backward_kernel=7, stats_kernel=1, branch_kernel=.6, gate_kernel=2.4, weights_kernel=1.2, normed_grad_kernel=1.2, mixed_kernel=1, input_kernel=1, early_kernel=3, late_kernel=3, place_kernel=1, partial_kernel=2)


def whole(array):
    return pl.BlockSpec(array.shape, lambda i, at: (0,) * array.ndim)


def call(kernel, blocks, at, ins, outs, scratch, small=True, aliases=()):
    title = getattr(kernel, "func", kernel).__name__
    return pl.pallas_call(
        kernel,
        name=title,
        grid_spec=pltpu.PrefetchScalarGridSpec(
            num_scalar_prefetch=1,
            grid=(blocks,),
            in_specs=[whole(a) if s is None else s for a, s in ins],
            out_specs=[out[2] for out in outs],
            scratch_shapes=scratch,
        ),
        out_shape=[
            pltpu.VMEM(shape, dtype) if rest and rest[0] else jax.ShapeDtypeStruct(shape, dtype)
            for shape, dtype, _, *rest in outs
        ],
        cost_estimate=pl.CostEstimate(flops=int(COST.get(title, 1)*blocks * 10**9), bytes_accessed=0, transcendentals=0),
        input_output_aliases=dict(aliases),
        compiler_params=pltpu.CompilerParams(
            dimension_semantics=("arbitrary",), vmem_limit_bytes=(MIB.get(title, 16) if small else 48) * 2**20
        ),
    )(at, *[a for a, _ in ins])


def per_device(
    residual_in,
    norm_gain,
    gate_proj,
    value_proj,
    state_proj,
    step_proj,
    value_conv,
    value_shift,
    state_conv,
    state_shift,
    step_bias,
    log_rate,
    skip_gain,
    gated_gain,
    out_proj,
    grad_out,
):
    parts = lax.axis_size("heads")
    two = parts == 2
    rows_here, model = residual_in.shape[1:]
    length = rows_here * parts
    inner = value_conv.shape[1]
    inner_all = inner * parts
    heads = step_bias.shape[0]
    head_width = inner // heads
    pad_heads = -heads % 4
    nheads = heads + pad_heads
    width = nheads * head_width
    nstate2 = state_conv.shape[1]
    blocks = length // BLOCK
    chunks = BLOCK // CHUNK
    half_blocks = rows_here // BLOCK if two else blocks

    def wide(a, axis, fill=0):
        pads = [(0, 0)] * a.ndim
        pads[axis] = (0, width - inner)
        return jnp.pad(a, pads, constant_values=fill) if width > inner else a

    def lanes_of(a):
        return jnp.pad(a, [(0, 0)] * (a.ndim - 1) + [(0, LANES - a.shape[-1])])

    residual = residual_in[0]
    cot = grad_out[0]
    batch = lax.axis_size("batch")
    fast = two and batch == 16 and width == model and model % BLOCK == 0
    nstate = nstate2 // 2
    run = functools.partial(call, small=fast)
    place = lax.axis_index("batch").astype(jnp.int32)
    across = lax.axis_index("heads").astype(jnp.int32) if two else jnp.int32(0)
    own_from = lax.axis_index("heads").astype(jnp.int32) * rows_here
    at = jnp.stack([across, place & 1, (place >> 1) & 1, place >> 2, own_from])
    if two:
        swap = [(0, 1), (1, 0)]
        pair_of = lambda a: (a, lax.ppermute(a, "heads", swap))
        add_other = lambda a: lax.ppermute(a, "heads", swap)
    else:

        def pair_of(a):
            full = lax.all_gather(a, "heads", axis=0, tiled=True)
            return (full, full)

        add_other = lambda a: lax.psum(a, "heads") - a

    def hop(a, way):
        mask = {"core": 1, "line": 2}.get(way) or 4 * way
        return lax.ppermute(a, "batch", [(i, i ^ mask) for i in range(batch)])

    def bring(*arrays):
        if not fast:
            return arrays
        return run(
            bring_kernel,
            1,
            at,
            [(a, None) for a in arrays],
            [(a.shape, a.dtype, pl.BlockSpec(a.shape, lambda i, at: (0, 0)), True) for a in arrays],
            [],
        )

    own_rows, other_rows = pair_of(residual)
    own_cot, other_cot = pair_of(cot)

    gate_w, value_w = wide(gate_proj, 1), wide(value_proj, 1)
    out_w = wide(out_proj, 0)
    step_w = lanes_of(step_proj)
    gain_in = norm_gain[None, :]
    vconv, vshift = wide(value_conv, 1), wide(value_shift[None, :], 1)
    sshift = state_shift[None, :]
    sbias, rate = lanes_of(step_bias[None, :]), lanes_of(log_rate[None, :])
    skipx = wide(jnp.repeat(skip_gain, head_width)[None, :], 1)
    ggain = wide(gated_gain[None, :], 1, 1)
    head_of = jnp.arange(width) // head_width
    spread = (jnp.arange(LANES)[:, None] == head_of[None, :]).astype(bf16)
    spread = jnp.concatenate([spread, spread], axis=0)
    first = head_of.reshape(-1, 1, LANES, 1) + jnp.arange(2).reshape(1, 2, 1, 1) * LANES
    gather = (jnp.arange(2 * LANES) == first).reshape(-1, 2 * LANES).astype(bf16)

    gate_w, value_w, state_proj, step_w, out_w, spread, gather = bring(
        gate_w, value_w, state_proj, step_w, out_w, spread, gather
    )
    gain_in, vconv, vshift, state_conv, sshift, sbias, rate, skipx, ggain = bring(
        gain_in, vconv, vshift, state_conv, sshift, sbias, rate, skipx, ggain
    )

    def own_block(i, a):
        return (jnp.clip(i - a[0] * half_blocks, 0, half_blocks - 1), 0)

    def other_block(i, a):
        return (jnp.clip(i - (1 - a[0]) * half_blocks, 0, half_blocks - 1), 0) if two else (0, 0)

    other_read = other_block if two else own_block

    def rows(n, index=lambda i, a: (i, 0)):
        return pl.BlockSpec((BLOCK, n), index)

    along = pl.BlockSpec((8, BLOCK), lambda i, a: (0, i))
    unit = 2 * BLOCK if two and rows_here % (2 * BLOCK) == 0 else BLOCK
    units, half_units = length // unit, half_blocks * BLOCK // unit

    def own_unit(i, a):
        return (jnp.clip(i - a[0] * half_units, 0, half_units - 1), 0)

    def other_unit(i, a):
        return (jnp.clip(i - (1 - a[0]) * half_units, 0, half_units - 1), 0)

    other_taken = other_unit if two else own_unit

    def tall(n, index=lambda i, a: (i, 0)):
        return pl.BlockSpec((unit, n), index)

    fixed = lambda *shape: pl.BlockSpec(shape, lambda i, a: (0,) * len(shape))
    states_spec = lambda index: pl.BlockSpec((chunks, nstate, width), index)
    big = lambda *shape: pltpu.VMEM(shape, f32)
    low = lambda *shape: pltpu.VMEM(shape, bf16)
    halves = [
        ((rows_here if two else length, model), bf16, rows(model, own_block)),
        ((rows_here if two else BLOCK, model), bf16, rows(model, other_block)),
    ]

    normed, g, y, gg, values, slope, vp, conv_s, sp, z, sin, sq, step, running, shifted, grownx, tailx = run(
        functools.partial(forward_kernel, half_blocks),
        blocks,
        at,
        [
            (own_rows, rows(model, own_block)),
            (other_rows, rows(model, other_read)),
            (gain_in, None),
            (gate_w, None),
            (value_w, None),
            (state_proj, None),
            (step_w, None),
            (vconv, None),
            (vshift, None),
            (state_conv, None),
            (sshift, None),
            (sbias, None),
            (rate, None),
            (skipx, None),
            (ggain, None),
            (spread, None),
        ],
        [
            *[
                (shape, dtype, spec, fast)
                for shape, dtype, spec in (
                    ((length, model), bf16, rows(model)),
                    ((length, width), f32, rows(width)),
                    ((length, width), f32, rows(width)),
                    ((length, width), bf16, rows(width)),
                    ((length, width), bf16, rows(width)),
                    ((length, width), bf16, rows(width)),
                    ((length, width), bf16, rows(width)),
                    ((length, nstate2), f32, rows(nstate2)),
                    ((length, nstate2), bf16, rows(nstate2)),
                    ((length, LANES), f32, rows(LANES)),
                    ((blocks * chunks, nstate, width), bf16, states_spec(lambda i, a: (i, 0, 0))),
                    ((8, length), f32, along),
                    ((length, LANES), f32, rows(LANES)),
                    ((length, LANES), f32, rows(LANES)),
                    ((length, LANES), f32, rows(LANES)),
                    ((length, width), f32, rows(width)),
                    ((length, width), f32, rows(width)),
                )
            ]
        ],
        [
            big(width // LANES, BLOCK + 8, LANES),
            big(nstate2 // LANES, BLOCK + 8, LANES),
            big(nstate, width),
            big(BLOCK, width),
            big(BLOCK, width),
            low(BLOCK, width),
        ],
    )
    def stats_of(cot_rows, theirs, *before):
        first = (lambda a: (1 - a[0]) * half_units) if theirs else (lambda a: a[0] * half_units)
        count = cot_rows.shape[0]
        return run(
            stats_kernel,
            count // unit,
            at,
            [
                (cot_rows, tall(model)),
                (gg, tall(width, lambda i, a: (first(a) + i, 0))),
                (sq, pl.BlockSpec((8, unit), lambda i, a: (0, first(a) + i))),
                (out_w, None),
                *[(b, pl.BlockSpec((8, unit), lambda i, a: (0, i))) for b in before],
            ],
            [
                ((count, width), f32, tall(width), fast),
                (
                    (8 + 8 * len(before), count),
                    f32,
                    pl.BlockSpec((8 + 8 * len(before), unit), lambda i, a: (0, i)),
                ),
            ],
            [],
        )

    og, stats = stats_of(own_cot, False)
    if two:
        og_b, stats = stats_of(other_cot, True, stats)
    else:
        og_b = og
    got = add_other(stats)
    above = 1 if two else 0

    def stats_at(row, block, size=BLOCK):
        return pl.BlockSpec((8, size), lambda i, a: (row, block(i, a)[0]))

    branch, branch_sent = run(
        functools.partial(branch_kernel, half_units),
        units,
        at,
        [(gg, tall(width)), (out_w, None)],
        [
            ((rows_here if two else length, model), bf16, tall(model, own_unit)),
            ((rows_here if two else BLOCK, model), bf16, tall(model, other_unit if two else other_block)),
        ],
        [],
    )

    def other_half(own, sent):
        if two:
            return lax.ppermute(sent, "heads", swap)
        total = lax.psum_scatter(own.astype(f32), "heads", scatter_dimension=0, tiled=True)
        mine = lax.dynamic_slice_in_dim(own, own_from, rows_here, 0).astype(f32)
        return total - mine

    branch_got = other_half(branch, branch_sent)
    if not two:
        branch = lax.dynamic_slice_in_dim(branch, own_from, rows_here, 0)
    if fast:
        pieces = [((model // 2, 2 * model), bf16, fixed(model // 2, 2 * model))] * 2
    else:
        pieces = [
            ((model, width), f32, fixed(model, width)),
            ((width, model), f32, fixed(width, model)),
        ]
    dg, dy, early_a, early_b, grad_gain, norm = run(
        functools.partial(gate_kernel, half_units, inner_all, fast),
        units,
        at,
        [
            (own_cot, tall(model, own_unit)),
            (other_cot, tall(model, other_taken)),
            (stats, stats_at(above, own_unit, unit)),
            (got, stats_at(0, own_unit, unit)),
            (stats, stats_at(0, other_taken, unit)),
            (got, stats_at(above, other_taken, unit)),
            (normed, None),
            (og, tall(width, own_unit)),
            (og_b, tall(width, other_taken)),
            (y, tall(width)),
            (g, tall(width)),
            (gg, None),
            (ggain, None),
            (gate_w, None),
            (branch, pl.BlockSpec(memory_space=pl.ANY)),
        ],
        [
            ((length, width), bf16, fixed(length, width), fast),
            ((length, width), bf16, tall(width), fast),
            *pieces,
            ((8, width), f32, fixed(8, width)),
            ((8, model), f32, fixed(8, model)),
        ],
        [low(length, model)] + ([big(model, width), big(width, model)] if fast else []),
    )

    def backward(start, count, carry, after=()):
        size = 2 * BLOCK if start % 2 == 0 and count % 2 == 0 else BLOCK
        size = count * BLOCK if fast else size
        steps, base = count * BLOCK // size, start * BLOCK // size

        def local(n):
            return pl.BlockSpec((size, n), lambda i, a: (steps - 1 - i, 0))

        def taken(array):
            if fast:
                return (array, None)
            shape = (size // CHUNK if array.ndim == 3 else size, *array.shape[1:])
            rest = (0,) * (array.ndim - 1)
            return (array, pl.BlockSpec(shape, lambda i, a: (base + steps - 1 - i, *rest)))

        slabs = [(width // LANES, 8, LANES), (nstate2 // LANES, 8, LANES)]
        vectors = [(nstate, width), *slabs, (8, width), (8, nstate2), (8, LANES)]
        out = run(
            functools.partial(
                backward_kernel, size, start * BLOCK if fast else 0, bool(carry), len(after)
            ),
            steps,
            at,
            [
                *[
                    taken(a)
                    for a in (dy, values, slope, vp, conv_s, sp, z, step, running, shifted, grownx, tailx, sin)
                ],
                (vconv, None),
                (state_conv, None),
                (rate, None),
                (skipx, None),
                (gather, None),
                *[(c, None) for c in carry],
                *[(a, pl.BlockSpec(memory_space=pl.ANY)) for a in after],
            ],
            [
                ((count * BLOCK, width), bf16, local(width)),
                ((count * BLOCK, nstate2), bf16, local(nstate2)),
                ((count * BLOCK, LANES), bf16, local(LANES)),
                *[(shape, f32, fixed(*shape)) for shape in vectors],
            ],
            [
                big(width // LANES, size + 8, LANES),
                big(nstate2 // LANES, size + 8, LANES),
                big(nstate, width),
                big(size, width),
                big(size, width),
                low(size, width),
                low(size, width),
                low(size, 2 * width),
                low(size, 2 * width),
            ],
        )
        return out[:3], out[3:]

    if two:
        own_stats, their_stats = stats_at(1, lambda i, a: (i, 0)), along
    else:
        own_stats = their_stats = stats_at(0, lambda i, a: (i + a[4] // BLOCK, 0))
    mixed, token = run(
        functools.partial(mixed_kernel, inner_all),
        rows_here // BLOCK,
        at,
        [
            (residual, rows(model)),
            (branch, rows(model)),
            (branch_got, rows(model)),
            (stats, own_stats),
            (got, their_stats),
        ],
        [((rows_here, model), f32, rows(model)), ((8, LANES), f32, fixed(8, LANES))],
        [],
    )
    from_gate = run(
        gate_back_kernel,
        blocks,
        at,
        [(dg, rows(width)), (gate_w, None)],
        [((length, model), f32, rows(model), fast)],
        [],
    )[0]
    cut = blocks // 2
    behind = ()
    if fast:
        steps = [("fold", 2, [early_a, hop(early_b, "core")], 2, False)]
        ((kept, sent),) = stage(at, steps, (from_gate,))
        early = [kept, hop(sent, "line")]
        behind = (kept,)
    low_b, carry = backward(cut, blocks - cut, (), behind)
    partial = run(
        functools.partial(partial_kernel, cut * BLOCK),
        1,
        at,
        [(normed, None), *[(a, None) for a in low_b]],
        [
            ((model, a.shape[1]), f32, fixed(model, a.shape[1])) for a in low_b
        ],
        [],
    )
    if fast:
        ((kept, *sent),) = stage(at, [("fold", 3, early, 4, False)])
        early = [kept] + [hop(a, k + 1) for k, a in enumerate(sent)]
        behind = (kept, branch_got, partial[2])
    low_a, carry = backward(0, cut, carry, behind)
    vec, svec, head = carry[3:]
    early = early if fast else ()
    lows = [(a, rows(a.shape[1], lambda i, at: (jnp.minimum(i, cut - 1), 0))) for a in low_a]
    lows += [(a, rows(a.shape[1], lambda i, at: (jnp.maximum(i - cut, 0), 0))) for a in low_b]

    if fast:
        shape = (model // 2, width + nstate2 + LANES)
        pieces = [(shape, bf16, fixed(*shape))] * 2
        pieces.append((early[0].shape, bf16, fixed(*early[0].shape)))
    else:
        shapes = [(model, width), (model, nstate2), (model, LANES), (8, model)]
        pieces = [(shape, f32, fixed(*shape)) for shape in shapes]
    late = run(
        functools.partial(weights_kernel, fast),
        1,
        at,
        [
            (normed, None),
            *[(a, None) for a in low_a],
            *[(a, None) for a in partial],
            (value_w, None),
            (state_proj, None),
            (step_w, None),
            (gain_in, None),
            (vec, None),
            (svec, None),
            (head, None),
            (grad_gain, None),
            (norm, None),
            *[(a, None) for a in early],
        ],
        pieces,
        [big(model, width), big(model, nstate2), big(model, LANES)],
    )
    ng, ng_sent = run(
        functools.partial(normed_grad_kernel, half_blocks, cut),
        blocks,
        at,
        [
            (from_gate, rows(model)),
            *lows,
            (value_w, None),
            (state_proj, None),
            (step_w, None),
        ],
        halves,
        [],
    )

    ng_got = other_half(ng, ng_sent)
    if not two:
        ng = lax.dynamic_slice_in_dim(ng, own_from, rows_here, 0)
    grad_input, token_b = run(
        input_kernel,
        rows_here // BLOCK,
        at,
        [
            (residual, rows(model)),
            (cot, rows(model)),
            (ng, rows(model)),
            (ng_got, rows(model)),
            (gain_in, None),
        ],
        [((rows_here, model), f32, rows(model)), ((8, LANES), f32, fixed(8, LANES))],
        [],
    )

    if fast:
        kept, sent, early = late
        ((kept, sent),) = stage(at, [("fold", 2, [kept, hop(sent, "core")], 2, True)])
        got = hop(sent, "line")
        early = [early] + [hop(early, k) for k in (1, 2, 3)]
        ((kept, *sent),) = stage(at, [("fold", 3, [kept, got], 4, True)], (ng,))
        got = [hop(a, k + 1) for k, a in enumerate(sent)]
        steps = [("part", width, [kept, *got], 2, True), ("join", 3, early)]
        (done, rest), (early,) = stage(at, steps, (token,))
        early = [early, hop(early, "line")]
        theirs = lax.ppermute(rest, "heads", swap)
        done = run(
            heads_kernel,
            1,
            at,
            [(done, None), (rest, None), (theirs, None)],
            [((rest.shape[0], width + rest.shape[1]), bf16, fixed(rest.shape[0], width + rest.shape[1]))],
            [],
        )[0]
        done = [done] + [hop(done, k) for k in (1, 2, 3)]
        (done,), (early,) = stage(at, [("join", 3, done), ("join", 2, early)], (token_b,))
        grad_gate, grad_out_proj, token_c = run(
            early_kernel,
            1,
            at,
            [(early, None), (hop(early, "core"), None)],
            [((model, model), f32, fixed(model, model))] * 2
            + [((8, LANES), f32, fixed(8, LANES))],
            [],
        )
        quarter = done.shape[0]

        def wide(n):
            def index(i, a):
                return ((a[1] ^ (n // 2)) * 2 + (a[2] ^ (n % 2)), 0)

            return [((model, w), f32, pl.BlockSpec((quarter, w), index)) for w in (width, nstate2)]

        def kept_in(arrays):
            return [(a, pl.BlockSpec(memory_space=pl.ANY)) for a in arrays]

        def place(n, piece, filled=()):
            aliases = ((2, 0), (3, 1)) if filled else ()
            ins = [(piece, None), *kept_in(filled)]
            outs = wide(n) + [((8, LANES), f32, fixed(8, LANES))]
            return run(place_kernel, 1, at, ins, outs, [], aliases=aliases)

        got = hop(done, "line")
        across = hop(done, "core")
        *filled, token_d = place(0, done)
        *filled, token_e = place(2, across, filled)
        ((got,),) = stage(at, [("join", 2, [got])], (token_c, token_e))
        done = [done, got, across, hop(got, "core")]
        *filled, token_d = place(1, got, filled)
        shapes = [
            (heads, model),
            (4, width),
            (width,),
            (width,),
            (model,),
            (4, nstate2),
            (nstate2,),
            (heads,),
            (heads,),
            (heads,),
        ]
        (
            grad_value,
            grad_state,
            grad_step,
            grad_vconv,
            grad_vshift,
            grad_ggain,
            grad_norm,
            grad_sconv,
            grad_sshift,
            grad_bias,
            grad_rate,
            grad_skip,
        ) = run(
            late_kernel,
            1,
            at,
            [*[(a, None) for a in done], *kept_in(filled)],
            wide(3) + [(shape, f32, fixed(*shape)) for shape in shapes],
            [big(model, LANES)],
            aliases=((5, 0), (6, 1)),
        )
        return (
            mixed[None],
            grad_input[None],
            grad_norm,
            grad_gate,
            grad_value,
            grad_state,
            grad_step.T,
            grad_vconv,
            grad_vshift,
            grad_sconv,
            grad_sshift,
            grad_bias,
            grad_rate,
            grad_skip,
            grad_ggain,
            grad_out_proj,
        )
    grad_value, grad_state, grad_step, norm = late
    grad_gate, grad_value, grad_out_proj, grad_step, vec, head, grad_gain = lax.psum(
        (early_a, grad_value, early_b, grad_step, vec, head, grad_gain), "batch"
    )
    grad_state, svec, norm = lax.psum((grad_state, svec, norm), ("batch", "heads"))
    norm, ggrad = norm[0], grad_gain[0]
    return (
        mixed[None],
        grad_input[None],
        norm,
        grad_gate[:, :inner],
        grad_value[:, :inner],
        grad_state,
        grad_step[:, :heads],
        vec[:4, :inner],
        vec[4, :inner],
        svec[:4],
        svec[4],
        head[0, :heads],
        head[1, :heads],
        head[2, :heads],
        ggrad[:inner],
        grad_out_proj[:inner],
    )


def solution(mesh):
    return jax.shard_map(
        per_device,
        mesh=mesh,
        in_specs=(
            P("batch", "heads", None),
            P(),
            P(None, "heads"),
            P(None, "heads"),
            P(),
            P(None, "heads"),
            P(None, "heads"),
            P("heads"),
            P(),
            P(),
            P("heads"),
            P("heads"),
            P("heads"),
            P("heads"),
            P("heads", None),
            P("batch", "heads", None),
        ),
        out_specs=(
            P("batch", "heads", None),
            P("batch", "heads", None),
            P(),
            P(None, "heads"),
            P(None, "heads"),
            P(),
            P(None, "heads"),
            P(None, "heads"),
            P("heads"),
            P(),
            P(),
            P("heads"),
            P("heads"),
            P("heads"),
            P("heads"),
            P("heads", None),
        ),
        check_vma=False,
    )
```

```python
import functools

import jax
import jax.numpy as jnp
from jax import lax
from jax.experimental import pallas as pl
from jax.experimental.pallas import tpu as pltpu
from jax.sharding import PartitionSpec as P

EPSILON = 1e-05
HIGHEST = lax.Precision.HIGHEST
BLOCK = 256
CHUNK = 128
LANES = 128
HALF = LANES // 2
QUAD = 2 * LANES
LOG2E = 1.4426950408889634
f32 = jnp.float32
bf16 = jnp.bfloat16


def dot(left, right, over=((1,), (0,)), precision=None):
    return lax.dot_general(
        left, right, (over, ((), ())), preferred_element_type=f32, precision=precision
    )


TN = ((0,), (0,))
NT = ((1,), (1,))


def sigmoid(v):
    return 1.0 / (1.0 + jnp.exp(-v))


def silu(v):
    half = 0.5 * v
    return half + half * jnp.tanh(half)


def silu_slope(v):
    half = 0.5 * v
    t = jnp.tanh(half)
    out = half + half * t
    sig = 0.5 + 0.5 * t
    return out, sig + out * (1.0 - sig)


def causal_back(buf, slab, r0, grad, pre, taps, extra):
    buf[slab, pl.ds(r0, CHUNK), :] = grad
    lanes = slice(slab * LANES, (slab + 1) * LANES)
    pre = pre.astype(f32)
    out, rows = 0.0, []
    for tap in range(4):
        moved = grad if tap == 3 else buf[slab, pl.ds(r0 + 3 - tap, CHUNK), :]
        out = out + taps[tap : tap + 1, lanes].astype(f32) * moved
        rows.append(jnp.sum(pre * moved, axis=0, keepdims=True))
    rows.append(jnp.sum(grad, axis=0, keepdims=True))
    rows += [extra, jnp.zeros((2, LANES), f32)]
    return out, jnp.concatenate(rows, axis=0)


def split(v):
    high = v.astype(bf16)
    return jnp.concatenate([high, (v - high.astype(f32)).astype(bf16)], axis=1)


def lower_mask(rows):
    return lax.broadcasted_iota(jnp.int32, (rows, rows), 0) >= lax.broadcasted_iota(
        jnp.int32, (rows, rows), 1
    )


def chunk_mask(strict=False):
    row = lax.broadcasted_iota(jnp.int32, (BLOCK, BLOCK), 0)
    column = lax.broadcasted_iota(jnp.int32, (BLOCK, BLOCK), 1)
    ordered = row > column if strict else row >= column
    return (ordered & (row // CHUNK == column // CHUNK)).astype(bf16)


def block_scalars(z, log_rate, spread):
    step = jnp.maximum(z, 0.0) + jnp.log1p(jnp.exp(-jnp.abs(z)))
    rate = -jnp.exp(log_rate)
    decay = jnp.where(lax.broadcasted_iota(jnp.int32, (1, LANES), 1) < 32, step * (rate * LOG2E), 0.0)
    high = decay.astype(bf16).astype(f32)
    middle = (decay - high).astype(bf16).astype(f32)
    packed = high + pltpu.roll(middle, 32, 1) + pltpu.roll(decay - high - middle, 64, 1)
    sums = dot(chunk_mask(), packed.astype(bf16))
    running = sums + pltpu.roll(sums, LANES - 32, 1) + pltpu.roll(sums, LANES - 64, 1)
    last = [running[r + CHUNK - 1 : r + CHUNK, :] for r in range(0, BLOCK, CHUNK)]
    tail = [jnp.exp2(v - running[k * CHUNK : (k + 1) * CHUNK, :]) for k, v in enumerate(last)]
    tail = step * jnp.concatenate(tail, axis=0)
    wide = dot(jnp.concatenate([split(jnp.exp2(running)), split(tail)], axis=0), spread)
    return step, running, running - jnp.log2(step), wide[:BLOCK], wide[BLOCK:]


def causal(buf, slab, taps, shift):
    lanes = slice(slab * LANES, (slab + 1) * LANES)
    conv = shift[:, lanes].astype(f32)
    for tap in range(4):
        conv = conv + taps[tap : tap + 1, lanes].astype(f32) * buf[slab, pl.ds(5 + tap, BLOCK), :]
    return conv


def chunk_scores(b_rows, c_rows):
    n = b_rows.shape[1]
    b, c = split(b_rows), split(c_rows)
    left = jnp.concatenate([c, c[:, :n]], axis=1)
    right = jnp.concatenate([b[:, :n], b[:, :n], b[:, n:]], axis=1)
    return b, c, dot(left, right, NT)


def quad_mixing(scores, running, shifted_t, quad, mask):
    factors, mixes = [], []
    for head in range(4 * quad, 4 * quad + 4):
        spread = running[:, head : head + 1] - shifted_t[head : head + 1, :]
        factors.append(jnp.exp2(jnp.where(mask, spread, -1e30)))
        mixes.append((scores * factors[-1]).astype(bf16))
    return factors, mixes


def heads_apart(left, right):
    lane = lax.broadcasted_iota(jnp.int32, (1, LANES), 1)
    first = (lane < HALF).astype(bf16)
    zero = jnp.zeros(left.shape, bf16)
    rows = [jnp.concatenate([left * m, zero], axis=1) for m in (first, 1 - first)]
    rows += [jnp.concatenate([zero, right * m], axis=1) for m in (first, 1 - first)]
    return jnp.concatenate(rows, axis=0)


def forward_kernel(
    half_blocks,
    at_ref,
    own_ref,
    other_ref,
    gain_ref,
    gate_w,
    value_w,
    state_w,
    step_w,
    vconv_ref,
    vshift_ref,
    sconv_ref,
    sshift_ref,
    sbias_ref,
    rate_ref,
    skip_ref,
    ggain_ref,
    spread_ref,
    normed_ref,
    g_ref,
    y_ref,
    gg_ref,
    low_ref,
    slope_ref,
    vp_ref,
    as_ref,
    sp_ref,
    z_ref,
    sin_ref,
    sq_ref,
    step_ref,
    running_ref,
    shifted_ref,
    grownx,
    tailx,
    vbuf,
    sbuf,
    state,
    carried,
    values,
    vtail,
):
    step_at = pl.program_id(0)
    pairs = vbuf.shape[0]
    nstate = state.shape[0]

    @pl.when(step_at == 0)
    def _():
        state[...] = jnp.zeros_like(state)
        for buf in (vbuf, sbuf):
            buf[:, 0:8, :] = jnp.zeros((buf.shape[0], 8, LANES), f32)

    mine = (step_at // half_blocks) == at_ref[0]
    rows = jnp.where(mine, own_ref[...], other_ref[...]).astype(f32)
    scale = lax.rsqrt(jnp.mean(rows * rows, axis=1, keepdims=True) + EPSILON)
    normed = (rows * scale * gain_ref[...].astype(f32)).astype(bf16)
    normed_ref[...] = normed
    z = dot(normed, step_w[...]) + sbias_ref[...]
    z_ref[...] = z
    for out, buf, w in ((sp_ref, sbuf, state_w), (vp_ref, vbuf, value_w)):
        pre = dot(normed, w[...])
        out[...] = pre.astype(bf16)
        for slab in range(buf.shape[0]):
            buf[slab, 8:, :] = pre[:, slab * LANES : (slab + 1) * LANES]
    g_ref[...] = dot(normed, gate_w[...])

    step, running, shifted, grownx[...], tailx[...] = block_scalars(z, rate_ref[...], spread_ref[...])
    step_ref[...] = step
    running_ref[...] = running
    shifted_ref[...] = shifted
    chunks = range(BLOCK // CHUNK)
    states = []
    for slab in range(sbuf.shape[0]):
        conv = causal(sbuf, slab, sconv_ref, sshift_ref)
        as_ref[:, slab * LANES : (slab + 1) * LANES] = conv
        states.append(silu(conv))
    for pair in range(pairs):
        lanes = slice(pair * LANES, (pair + 1) * LANES)
        out, slope = silu_slope(causal(vbuf, pair, vconv_ref, vshift_ref))
        slope_ref[:, lanes] = slope.astype(bf16)
        values[:, lanes] = out
        low_ref[:, lanes] = out.astype(bf16)
        vtail[:, lanes] = (out * tailx[:, lanes]).astype(bf16)
    parts = []
    for chunk in chunks:
        here = slice(chunk * CHUNK, (chunk + 1) * CHUNK)
        b_two, c_two, scores = chunk_scores(*(v[here] for v in states))
        parts.append(scores)
        before = state[...].astype(bf16)
        sin_ref[chunk, :, :] = before
        carried[here, :] = dot(c_two[:, :nstate], before)
        last = grownx[(chunk + 1) * CHUNK - 1 : (chunk + 1) * CHUNK, :]
        state[...] = last * state[...] + dot(b_two[:, :nstate], vtail[here, :], TN)
    mask = lower_mask(CHUNK)
    for chunk in chunks:
        here = slice(chunk * CHUNK, (chunk + 1) * CHUNK)
        run = running[here]
        run_t = shifted[here].T
        squares = jnp.zeros((CHUNK, LANES), f32)
        for quad in range(pairs // 2):
            _, mixes = quad_mixing(parts[chunk], run, run_t, quad, mask)
            sides = [slice((2 * quad + k) * LANES, (2 * quad + k + 1) * LANES) for k in range(2)]
            both = dot(
                jnp.concatenate(mixes, axis=1), heads_apart(*(low_ref[here, lanes] for lanes in sides))
            )
            for k, lanes in enumerate(sides):
                scanned = both[:, k * LANES : (k + 1) * LANES]
                scanned = scanned + grownx[here, lanes] * carried[here, lanes]
                scanned = scanned + skip_ref[:, lanes] * values[here, lanes]
                gate, slope = silu_slope(g_ref[here, lanes])
                y_ref[here, lanes] = scanned * slope
                g_ref[here, lanes] = gate
                gated = scanned * gate
                gg_ref[here, lanes] = (gated * ggain_ref[:, lanes].astype(f32)).astype(bf16)
                squares = squares + gated * gated
        sq_ref[:, here] = dot(jnp.ones((8, LANES), f32), squares, NT, HIGHEST)
    for buf in (vbuf, sbuf):
        buf[:, 0:8, :] = buf[:, BLOCK : BLOCK + 8, :]


def stats_kernel(at_ref, cot_ref, gg_ref, sq_ref, out_w, *refs):
    og_ref, stats_ref = refs[-2:]
    if len(refs) > 2:
        stats_ref[8:, :] = refs[0][...]
    og = dot(cot_ref[...], out_w[...], NT)
    og_ref[...] = og
    prod = (og * gg_ref[...].astype(f32)).astype(bf16)
    dots = dot(jnp.ones((8, prod.shape[1]), bf16), prod, NT)
    row = lax.broadcasted_iota(jnp.int32, dots.shape, 0)
    stats_ref[:8, :] = jnp.where(row == 0, sq_ref[...], dots)


def bring_kernel(at_ref, *refs):
    count = len(refs) // 2
    for src, dst in zip(refs[:count], refs[count:]):
        dst[...] = src[...]


def branch_kernel(half_blocks, at_ref, gg_ref, out_w, own_ref, other_ref):
    mine = (pl.program_id(0) // half_blocks) == at_ref[0]
    rows = dot(gg_ref[...], out_w[...]).astype(bf16)

    @pl.when(mine)
    def _():
        own_ref[...] = rows

    @pl.when(jnp.logical_not(mine))
    def _():
        other_ref[...] = rows


def gate_back_kernel(at_ref, dg_ref, gate_w, out_ref):
    out_ref[...] = dot(dg_ref[...], gate_w[...], NT)


def picked(cut, early, late):
    return jnp.where(pl.program_id(0) < cut, early[...], late[...])


def normed_grad_kernel(half_blocks, cut, at_ref, from_gate, *refs):
    lows, (value_w, state_w, step_w, own_ref, other_ref) = refs[:6], refs[6:]
    dv, ds, dz = (picked(cut, a, b) for a, b in zip(lows[:3], lows[3:]))
    mine = (pl.program_id(0) // half_blocks) == at_ref[0]
    rows = (
        from_gate[...]
        + dot(dv, value_w[...], NT)
        + dot(ds, state_w[...], NT)
        + dot(dz, step_w[...], NT)
    ).astype(bf16)

    @pl.when(mine)
    def _():
        own_ref[...] = rows

    @pl.when(jnp.logical_not(mine))
    def _():
        other_ref[...] = rows


def row_sums(grads, weights):
    prod = (grads * weights.astype(f32)).astype(bf16)
    return dot(jnp.ones((8, prod.shape[1]), bf16), prod, NT)


def emit(at_ref, parts, outs):
    half = outs[0].shape[0]
    for j, out in enumerate(outs):
        rows = pl.ds(pl.multiple_of((at_ref[1] ^ j) * half, LANES), half)
        left = 0
        for part in parts:
            out[:, left : left + part.shape[1]] = part[rows, :].astype(out.dtype)
            left += part.shape[1]


def row_column(rows):
    return jnp.concatenate([rows, jnp.zeros((LANES - rows.shape[0], rows.shape[1]), f32)], axis=0).T


def mixed_kernel(inner_all, at_ref, rows_ref, own_ref, other_ref, here_ref, there_ref, out_ref, token_ref):
    token_ref[...] = jnp.zeros_like(token_ref)
    sums = here_ref[...] + there_ref[...]
    scale = row_column(lax.rsqrt(sums / inner_all + EPSILON))[:, 0:1]
    branch = own_ref[...].astype(f32) + other_ref[...].astype(f32)
    out_ref[...] = rows_ref[...].astype(f32) + scale * branch


def input_kernel(at_ref, rows_ref, cot_ref, own_ref, other_ref, gain_ref, out_ref, token_ref):
    token_ref[...] = jnp.zeros_like(token_ref)
    rows = rows_ref[...].astype(f32)
    scale = lax.rsqrt(jnp.mean(rows * rows, axis=1, keepdims=True) + EPSILON)
    pulled = (own_ref[...].astype(f32) + other_ref[...].astype(f32)) * gain_ref[...].astype(f32)
    inner = jnp.mean(pulled * rows, axis=1, keepdims=True) * (scale * scale * scale)
    out_ref[...] = cot_ref[...].astype(f32) + scale * pulled - rows * inner


def gate_kernel(
    half_blocks,
    inner_all,
    fast,
    at_ref,
    own_ref,
    other_ref,
    here_a,
    there_a,
    here_b,
    there_b,
    normed_ref,
    og_a,
    og_b,
    y_ref,
    g_ref,
    gg_ref,
    ggain_ref,
    _,
    dg_ref,
    dy_ref,
    first_ref,
    second_ref,
    grad_gain_ref,
    scaled_ref,
    *scratch,
):
    step_at = pl.program_id(0)
    size = own_ref.shape[0]
    here = pl.ds(pl.multiple_of(step_at * size, BLOCK), size)
    pairs = og_a.shape[1] // LANES
    grad_gate, grad_out = scratch if fast else (first_ref, second_ref)

    @pl.when(step_at == 0)
    def _():
        grad_gain_ref[...] = jnp.zeros_like(grad_gain_ref)

    mine = (step_at // half_blocks) == at_ref[0]
    sums = jnp.where(mine, here_a[...] + there_a[...], here_b[...] + there_b[...])
    scale_row = lax.rsqrt(sums[0:1, :] / inner_all + EPSILON)
    pull_row = scale_row * scale_row * scale_row * sums[1:2, :] / inner_all
    columns = row_column(jnp.concatenate([scale_row, pull_row], axis=0))
    scale, pull = columns[:, 0:1], columns[:, 1:2]
    cot = jnp.where(mine, own_ref[...], other_ref[...]).astype(f32)
    scaled_ref[here, :] = (cot * scale).astype(bf16)
    for pair in range(pairs):
        lanes = slice(pair * LANES, (pair + 1) * LANES)
        og = jnp.where(mine, og_a[:, lanes], og_b[:, lanes]) * scale
        gain = ggain_ref[:, lanes].astype(f32)
        inverse = 1.0 / gain
        low = gg_ref[here, lanes].astype(f32)
        grad_gain_ref[0:1, lanes] += jnp.sum(og * low, axis=0, keepdims=True) * inverse
        gated_grad = gain * og - (low * inverse) * pull
        dy_ref[:, lanes] = (gated_grad * g_ref[:, lanes]).astype(bf16)
        dg_ref[here, lanes] = (gated_grad * y_ref[:, lanes]).astype(bf16)

    @pl.when(step_at == pl.num_programs(0) - 1)
    def _():
        grad_out[...] = dot(gg_ref[...], scaled_ref[...], TN)
        grad_gate[...] = dot(normed_ref[...], dg_ref[...], TN)
        if fast:
            emit(at_ref, (grad_gate, grad_out), (first_ref, second_ref))


def partial_kernel(from_row, fast, at_ref, normed_ref, *refs):
    lows, (gate_w, first_ref, second_ref), outs, norm_ref = refs[:3], refs[3:6], refs[6:9], refs[9]
    for low, out in zip(lows, outs):
        out[...] = dot(normed_ref[from_row:, :], low[...], TN)
    if not fast:
        norm_ref[...] = row_sums(first_ref[...], gate_w[...])
        return
    half, width = first_ref.shape[0], gate_w.shape[1]
    for j, ref in enumerate((first_ref, second_ref)):
        at = pl.ds(pl.multiple_of((at_ref[1] ^ j) * half, LANES), half)
        norm_ref[:, at] = row_sums(ref[:, :width].astype(f32), gate_w[at, :])


def weights_kernel(fast, at_ref, normed_ref, *refs):
    lows, refs = refs[:6], refs[6:]
    value_w, state_w, step_w, gain_ref, vec_ref, svec_ref, head_ref, ggain_ref, norm_ref = refs[:9]
    outs, acc = refs[9:-3], refs[-3:]
    if fast:
        pieces, outs, done_ref = outs[:4], outs[4:6], outs[6]
        total = pieces[0][...].astype(f32)
        for r in pieces[1:]:
            total = total + r[...].astype(f32)
        done_ref[...] = total.astype(bf16)
    for a, low, rest in zip(acc, lows[:3], lows[3:]):
        a[...] = rest[...] + dot(normed_ref[: low.shape[0], :], low[...], TN)
    norm = norm_ref[...]
    for a, w in zip(acc, (value_w, state_w, step_w)):
        norm = norm + row_sums(a[...], w[...])
    norm = norm / gain_ref[...].astype(f32)
    if fast:
        pack_vectors(acc[2], vec_ref, svec_ref, head_ref, ggain_ref, norm)
        emit(at_ref, acc, outs)
        return
    for o, a in zip(outs, acc):
        o[...] = a[...]
    outs[3][...] = norm


VEC_AT = 16
SVEC_AT = 24
HEAD_AT = 32


def pack_vectors(block, vec_ref, svec_ref, head_ref, ggain_ref, norm):
    model = block.shape[0]
    row = lax.broadcasted_iota(jnp.int32, (8, model), 0)
    vec = jnp.where(row == 5, ggain_ref[0:1, :], jnp.where(row == 6, norm[0:1, :], vec_ref[...]))

    def tall(v):
        return jnp.concatenate([v, jnp.zeros((8, model - v.shape[1]), f32)], axis=1)

    rows = jnp.concatenate(
        [
            jnp.zeros((VEC_AT, model), f32),
            vec,
            tall(svec_ref[...]),
            tall(head_ref[...]),
            jnp.zeros((LANES - HEAD_AT - 8, model), f32),
        ],
        axis=0,
    )
    lane = lax.broadcasted_iota(jnp.int32, (1, LANES), 1)
    full = jnp.where(lane < VEC_AT, block[...], rows.T)
    block[...] = carry_rest(jnp.where(lane < HALF, full, 0.0))


def carry_rest(full):
    high = full.astype(bf16).astype(f32)
    return high + pltpu.roll(full - high, HALF, 1)


def join_rest(block):
    lane = lax.broadcasted_iota(jnp.int32, (1, LANES), 1)
    return jnp.where(lane < HALF, block + pltpu.roll(block, HALF, 1), 0.0)


def fold_step(me, ins, outs, vectors):
    rows, width = outs[0].shape
    width -= LANES if vectors else 0
    for j, o in enumerate(outs):
        at = slice(0, rows)
        if len(outs) > 1:
            at = pl.ds(pl.multiple_of((me ^ j) * rows, 16), rows)
        o[:, :width] = sum(r[at, :width].astype(f32) for r in ins).astype(bf16)
        if vectors:
            last = sum(r[at, width:].astype(f32) for r in ins)
            o[:, width:] = carry_rest(join_rest(last)).astype(bf16)


def part_step(ins, outs, vectors):
    width = outs[0].shape[1]
    outs[0][...] = sum(r[:, :width].astype(f32) for r in ins).astype(bf16)
    state = outs[1].shape[1] - LANES
    outs[1][:, :state] = sum(r[:, width : width + state].astype(f32) for r in ins).astype(bf16)
    last = sum(r[:, width + state :].astype(f32) for r in ins)
    outs[1][:, state:] = carry_rest(join_rest(last)).astype(bf16)


def join_step(me, ins, out):
    rows = ins[0].shape[0]
    count = out.shape[0] // rows
    if count == 1:
        out[...] = ins[0][...]
        return
    left = 0
    for first in range(0, len(ins), count):
        right = left + ins[first].shape[1]
        for j, r in enumerate(ins[first : first + count]):
            out[pl.ds(pl.multiple_of((me ^ j) * rows, 16), rows), left:right] = r[...]
        left = right


def stage_kernel(plan, extra, at_ref, *refs):
    n_in = sum(count for _, _, count, _, _ in plan)
    ins, outs = refs[:n_in], refs[n_in + extra :]
    for kind, axis, take, give, vectors in plan:
        if kind == "fold":
            fold_step(at_ref[axis], ins[:take], outs[:give], vectors)
        elif kind == "part":
            part_step(ins[:take], outs[:give], vectors)
        else:
            join_step(at_ref[axis], ins[:take], outs[0])
        ins, outs = ins[take:], outs[give:]


def stage(at, steps, after=()):
    plan, arrays, shapes = [], [], []
    for kind, axis, ins, *rest in steps:
        rows, width = ins[0].shape
        count, vectors = rest if rest else (1, False)
        if kind == "fold":
            shapes += [(rows // count, width)] * count
        elif kind == "part":
            shapes += [(rows, axis), (rows, width - axis)]
        else:
            widths = {a.shape[1] for a in ins}
            shapes.append((rows * len(ins) // len(widths), sum(widths)))
        plan.append((kind, axis, len(ins), count, vectors))
        arrays += ins
    out = call(
        functools.partial(stage_kernel, tuple(plan), len(after)),
        1,
        at,
        [(a, None) for a in arrays] + [(a, pl.BlockSpec(memory_space=pl.ANY)) for a in after],
        [(shape, bf16, pl.BlockSpec(shape, lambda i, a: (0, 0))) for shape in shapes],
        [],
    )
    out, results = list(out), []
    for _, _, _, give, _ in plan:
        results.append(out[:give])
        out = out[give:]
    return results


def heads_kernel(at_ref, done_ref, own_ref, other_ref, out_ref):
    start = done_ref.shape[1]
    state = own_ref.shape[1] - LANES
    out_ref[:, :start] = done_ref[...]
    sums = own_ref[:, :state].astype(f32) + other_ref[:, :state].astype(f32)
    out_ref[:, start : start + state] = sums.astype(bf16)
    lane = lax.broadcasted_iota(jnp.int32, (1, LANES), 1)
    shared = (lane == VEC_AT + 6) | ((lane >= SVEC_AT) & (lane < HEAD_AT))
    mine = join_rest(own_ref[:, state:].astype(f32))
    theirs = join_rest(other_ref[:, state:].astype(f32))
    out_ref[:, start + state :] = carry_rest(mine + jnp.where(shared, theirs, 0.0)).astype(bf16)


def halves_of(at_ref, own_ref, other_ref, left, right):
    rows = own_ref.shape[0]
    for j, ref in enumerate((own_ref, other_ref)):
        yield pl.ds(pl.multiple_of((at_ref[1] ^ j) * rows, LANES), rows), ref[:, left:right].astype(f32)


def early_kernel(at_ref, own_ref, other_ref, *outs):
    outs[-1][...] = jnp.zeros_like(outs[-1])
    left = 0
    for o in outs[:-1]:
        right = left + o.shape[1]
        for at, v in halves_of(at_ref, own_ref, other_ref, left, right):
            o[at, :] = v
        left = right


def widen(piece, outs):
    left = 0
    for o in outs:
        right = left + o.shape[1]
        o[...] = piece[:, left:right].astype(f32)
        left = right


def place_kernel(at_ref, piece_ref, *refs):
    widen(piece_ref, refs[-3:-1])
    refs[-1][...] = jnp.zeros_like(refs[-1])


def late_kernel(at_ref, *refs):
    pieces, outs, block = refs[:4], refs[6:-1], refs[-1]
    widen(pieces[3], outs[:2])
    rows, right = pieces[0].shape
    for n, piece in enumerate(pieces):
        start = (at_ref[1] ^ (n // 2)) * 2 + (at_ref[2] ^ (n % 2))
        at = pl.ds(pl.multiple_of(start * rows, 16), rows)
        block[at, :] = piece[:, right - LANES :].astype(f32)
    full = join_rest(block[...])
    rows = full.T
    outs[2][...] = rows[: outs[2].shape[0]]
    vec, svec = rows[VEC_AT : VEC_AT + 8], rows[SVEC_AT : SVEC_AT + 8]
    head = rows[HEAD_AT : HEAD_AT + 8]
    vconv, vshift, ggain, norm, sconv, sshift, bias, rate, skip = outs[3:]
    vconv[...] = vec[:4]
    for o, row in ((vshift, vec[4:5]), (ggain, vec[5:6]), (norm, vec[6:7]), (sshift, svec[4:5])):
        o[...] = row[:, : o.shape[0]].reshape(o.shape)
    sconv[...] = svec[:4, : sconv.shape[1]]
    for j, o in enumerate((bias, rate, skip)):
        o[...] = head[j : j + 1, : o.shape[0]].reshape(o.shape)


def backward_kernel(
    size,
    from_row,
    carried_in,
    extra,
    at_ref,
    dy_ref,
    low_ref,
    slope_ref,
    vp_ref,
    as_ref,
    sp_ref,
    z_ref,
    step_ref,
    running_ref,
    shifted_ref,
    grownx,
    tailx,
    sin_ref,
    vconv_ref,
    sconv_ref,
    rate_ref,
    skip_ref,
    gather_ref,
    *refs,
):
    carries, refs = (refs[:6], refs[6:]) if carried_in else ((), refs)
    refs = refs[extra:]
    dvalue, dstates, dstep, dstate_out, dahalo, dshalo, grad_vconv_ref, grad_sconv_ref, grad_head_ref = refs[:9]
    dabuf, dsbuf, dstate, carried, pulled, ubuf, vtail, inner, outer = refs[9:]
    step_at = pl.program_id(0)
    nstate, width = dstate.shape
    pairs = width // LANES

    def row_at(start, count=CHUNK):
        return slice(from_row + start, from_row + start + count)


    @pl.when(step_at == 0)
    def _():
        if carried_in:
            dstate[...] = carries[0][...]
            dabuf[:, size:, :] = carries[1][...]
            dsbuf[:, size:, :] = carries[2][...]
            grad_vconv_ref[...] = carries[3][...]
            grad_sconv_ref[...] = carries[4][...]
            grad_head_ref[...] = carries[5][...]
        else:
            dstate[...] = jnp.zeros_like(dstate)
            for buf in (dabuf, dsbuf):
                buf[:, size:, :] = jnp.zeros((buf.shape[0], 8, LANES), f32)
            for ref in (grad_vconv_ref, grad_sconv_ref, grad_head_ref):
                ref[...] = jnp.zeros_like(ref)

    @pl.when(step_at > 0)
    def _():
        for buf in (dabuf, dsbuf):
            buf[:, size:, :] = buf[:, 0:8, :]

    chunks = [slice(r, r + CHUNK) for r in range(0, size, CHUNK)]
    zero_row = jnp.zeros((1, LANES), f32)
    rate = -jnp.exp(rate_ref[...])
    states, slopes = [], []
    for slab in range(2):
        out, slope = silu_slope(as_ref[row_at(0, size), slab * LANES : (slab + 1) * LANES])
        states.append(out)
        slopes.append(slope)
    for pair in range(pairs):
        lanes = slice(pair * LANES, (pair + 1) * LANES)
        there = (row_at(0, size), lanes)
        ubuf[:, lanes] = (dy_ref[there].astype(f32) * grownx[there]).astype(bf16)
    two = [chunk_scores(*(v[here] for v in states)) for here in chunks]
    helds, afters = [None] * len(chunks), [None] * len(chunks)
    for chunk in reversed(range(len(chunks))):
        here = chunks[chunk]
        b_two, c_two, _ = two[chunk]
        before = sin_ref[from_row // CHUNK + chunk, :, :]
        last = grownx[row_at(here.stop - 1, 1), :]
        grad = dstate[...]
        afters[chunk] = grad.astype(bf16)
        carried[here, :] = dot(c_two[:, :nstate], before)
        pulled[here, :] = dot(b_two[:, :nstate], afters[chunk])
        overlap = jnp.sum(before.astype(f32) * grad, axis=0, keepdims=True) * last
        overlap = jnp.broadcast_to(overlap, (8, width))
        tall = [split(overlap[:, p * LANES : (p + 1) * LANES]) for p in range(pairs)]
        held = dot(jnp.concatenate(tall, axis=1), gather_ref[...])[0:1]
        helds[chunk] = held[:, :LANES] + held[:, LANES:]
        dstate[...] = last * grad + dot(c_two[:, :nstate], ubuf[here, :], TN)

    mask = lower_mask(CHUNK)
    for chunk in reversed(range(len(chunks))):
        here = chunks[chunk]
        b_two, c_two, scores = two[chunk]
        rows_in = row_at(here.start)
        run = running_ref[rows_in, :]
        run_t = shifted_ref[rows_in, :].T
        dscores = jnp.zeros((CHUNK, CHUNK), f32)
        for quad in range(pairs // 2):
            factors, mixes = quad_mixing(scores, run, run_t, quad, mask)
            both = [slice((2 * quad + k) * LANES, (2 * quad + k + 1) * LANES) for k in range(2)]
            low = [low_ref[rows_in, lanes] for lanes in both]
            dy_low = [dy_ref[rows_in, lanes] for lanes in both]
            apart = heads_apart(*low)
            scanned = dot(jnp.concatenate(mixes, axis=1), apart)
            dsteps = dot(jnp.concatenate(mixes, axis=0), heads_apart(*dy_low), TN)
            for k, lanes in enumerate(both):
                pair = 2 * quad + k
                own = slice(k * LANES, (k + 1) * LANES)
                dmixing = dot(dy_low[k], apart[2 * k * CHUNK : 2 * (k + 1) * CHUNK, own], NT)
                dscores = dscores + dmixing[:, :CHUNK] * factors[2 * k]
                dscores = dscores + dmixing[:, CHUNK:] * factors[2 * k + 1]
                wide = slice(2 * pair * LANES, (2 * pair + 1) * LANES)
                wide_b = slice((2 * pair + 1) * LANES, (2 * pair + 2) * LANES)
                dy, values = dy_low[k].astype(f32), low[k].astype(f32)
                dvalues = dsteps[:, own]
                pulls = values * dvalues
                inside = dy * scanned[:, own] - pulls + ubuf[here, lanes].astype(f32) * carried[here, lanes]
                high = inside.astype(bf16)
                inner[here, wide] = high
                inner[here, wide_b] = (inside - high.astype(f32)).astype(bf16)
                tails, pull = tailx[rows_in, lanes], pulled[here, lanes]
                v = (values * tails).astype(bf16)
                vtail[here, lanes] = v
                outer[here, wide] = pulls.astype(bf16)
                outer[here, wide_b] = (v.astype(f32) * pull).astype(bf16)
                da = (dvalues + tails * pull + skip_ref[:, lanes] * dy) * slope_ref[rows_in, lanes].astype(f32)
                skips = jnp.sum(values * dy, axis=0, keepdims=True)
                dv, rows = causal_back(dabuf, pair, here.start, da, vp_ref[rows_in, lanes], vconv_ref, skips)
                grad_vconv_ref[:, lanes] += rows
                dvalue[here, lanes] = dv.astype(bf16)
        dlow = dscores.astype(bf16)
        drest = (dscores - dlow.astype(f32)).astype(bf16)
        b_rows, c_rows = b_two[:, :nstate], c_two[:, :nstate]
        cross = dot(
            jnp.concatenate([vtail[here, :], ubuf[here, :]], axis=0),
            jnp.concatenate([afters[chunk], sin_ref[from_row // CHUNK + chunk, :, :]], axis=0),
            NT,
        )
        db = cross[:CHUNK, :nstate] + dot(
            jnp.concatenate([dlow, dlow, drest], axis=0),
            jnp.concatenate([c_rows, c_two[:, nstate:], c_rows], axis=0),
            TN,
        )
        dc = cross[CHUNK:, nstate:] + dot(
            jnp.concatenate([dlow, dlow, drest], axis=1),
            jnp.concatenate([b_rows, b_two[:, nstate:], b_rows], axis=0),
        )
        for slab, d in enumerate((db, dc)):
            lanes = slice(slab * LANES, (slab + 1) * LANES)
            d = d * slopes[slab][here]
            dpre, rows = causal_back(dsbuf, slab, here.start, d, sp_ref[rows_in, lanes], sconv_ref, zero_row)
            grad_sconv_ref[:, lanes] += rows
            dstates[here, lanes] = dpre.astype(bf16)

    gathered = dot(jnp.concatenate([inner[...], outer[...]], axis=0), gather_ref[...])
    heads = [jnp.zeros((1, LANES), f32)] * 2
    for r in range(0, size, BLOCK):
        here = slice(r, r + BLOCK)
        sums, outs = gathered[here], gathered[size + r : size + r + BLOCK]
        ddecay = dot(chunk_mask(), split(sums[:, :LANES] + sums[:, LANES:]), TN)
        ddecay = ddecay[:, :LANES] + ddecay[:, LANES:]
        ddecay = ddecay + dot(chunk_mask(True), outs[:, LANES:].astype(bf16))
        held = [jnp.broadcast_to(helds[k // CHUNK], (CHUNK, LANES)) for k in range(r, r + BLOCK, CHUNK)]
        ddecay = ddecay + jnp.concatenate(held, axis=0)
        rows_in = row_at(r, BLOCK)
        step = step_ref[rows_in, :]
        direct = (outs[:, :LANES] + outs[:, LANES:]) / jnp.maximum(step, 1e-37)
        dz = (direct + ddecay * rate) * sigmoid(z_ref[rows_in, :])
        dstep[here, :] = dz.astype(bf16)
        heads[0] = heads[0] + jnp.sum(dz, axis=0, keepdims=True)
        heads[1] = heads[1] + jnp.sum(ddecay * step, axis=0, keepdims=True) * rate
    grad_head_ref[...] += jnp.concatenate([*heads, jnp.zeros((6, LANES), f32)], axis=0)

    @pl.when(step_at == pl.num_programs(0) - 1)
    def _():
        dstate_out[...] = dstate[...]
        vectors = grad_vconv_ref[...]
        tall = [split(vectors[:, p * LANES : (p + 1) * LANES]) for p in range(pairs)]
        skips = dot(jnp.concatenate(tall, axis=1), gather_ref[...])
        grad_head_ref[2:3, :] = skips[5:6, :LANES] + skips[5:6, LANES:]
        dahalo[...] = dabuf[:, 0:8, :]
        dshalo[...] = dsbuf[:, 0:8, :]


MIB = dict(
    forward_kernel=11,
    stats_kernel=6,
    branch_kernel=6,
    gate_kernel=10,
    backward_kernel=17,
    weights_kernel=11,
    normed_grad_kernel=12,
    mixed_kernel=8,
    input_kernel=8,
    early_kernel=10,
    late_kernel=10,
    place_kernel=8,
    partial_kernel=8,
)
COST = dict(forward_kernel=4.5, backward_kernel=7, stats_kernel=1, branch_kernel=.6, gate_kernel=2.4, weights_kernel=1.2, normed_grad_kernel=1.2, mixed_kernel=1, input_kernel=1, early_kernel=3, late_kernel=3, place_kernel=1, partial_kernel=2)


def whole(array):
    return pl.BlockSpec(array.shape, lambda i, at: (0,) * array.ndim)


def call(kernel, blocks, at, ins, outs, scratch, small=True, aliases=()):
    title = getattr(kernel, "func", kernel).__name__
    return pl.pallas_call(
        kernel,
        name=title,
        grid_spec=pltpu.PrefetchScalarGridSpec(
            num_scalar_prefetch=1,
            grid=(blocks,),
            in_specs=[whole(a) if s is None else s for a, s in ins],
            out_specs=[out[2] for out in outs],
            scratch_shapes=scratch,
        ),
        out_shape=[
            pltpu.VMEM(shape, dtype) if rest and rest[0] else jax.ShapeDtypeStruct(shape, dtype)
            for shape, dtype, _, *rest in outs
        ],
        cost_estimate=pl.CostEstimate(flops=int(COST.get(title, 1)*blocks * 10**9), bytes_accessed=0, transcendentals=0),
        input_output_aliases=dict(aliases),
        compiler_params=pltpu.CompilerParams(
            dimension_semantics=("arbitrary",), vmem_limit_bytes=(MIB.get(title, 16) if small else 48) * 2**20
        ),
    )(at, *[a for a, _ in ins])


def per_device(
    residual_in,
    norm_gain,
    gate_proj,
    value_proj,
    state_proj,
    step_proj,
    value_conv,
    value_shift,
    state_conv,
    state_shift,
    step_bias,
    log_rate,
    skip_gain,
    gated_gain,
    out_proj,
    grad_out,
):
    parts = lax.axis_size("heads")
    two = parts == 2
    rows_here, model = residual_in.shape[1:]
    length = rows_here * parts
    inner = value_conv.shape[1]
    inner_all = inner * parts
    heads = step_bias.shape[0]
    head_width = inner // heads
    pad_heads = -heads % 4
    nheads = heads + pad_heads
    width = nheads * head_width
    nstate2 = state_conv.shape[1]
    blocks = length // BLOCK
    chunks = BLOCK // CHUNK
    half_blocks = rows_here // BLOCK if two else blocks

    def wide(a, axis, fill=0):
        pads = [(0, 0)] * a.ndim
        pads[axis] = (0, width - inner)
        return jnp.pad(a, pads, constant_values=fill) if width > inner else a

    def lanes_of(a):
        return jnp.pad(a, [(0, 0)] * (a.ndim - 1) + [(0, LANES - a.shape[-1])])

    residual = residual_in[0]
    cot = grad_out[0]
    batch = lax.axis_size("batch")
    fast = two and batch == 16 and width == model and model % BLOCK == 0
    nstate = nstate2 // 2
    run = functools.partial(call, small=fast)
    place = lax.axis_index("batch").astype(jnp.int32)
    across = lax.axis_index("heads").astype(jnp.int32) if two else jnp.int32(0)
    own_from = lax.axis_index("heads").astype(jnp.int32) * rows_here
    at = jnp.stack([across, place & 1, (place >> 1) & 1, place >> 2, own_from])
    if two:
        swap = [(0, 1), (1, 0)]
        pair_of = lambda a: (a, lax.ppermute(a, "heads", swap))
        add_other = lambda a: lax.ppermute(a, "heads", swap)
    else:

        def pair_of(a):
            full = lax.all_gather(a, "heads", axis=0, tiled=True)
            return (full, full)

        add_other = lambda a: lax.psum(a, "heads") - a

    def hop(a, way):
        mask = {"core": 1, "line": 2}.get(way) or 4 * way
        return lax.ppermute(a, "batch", [(i, i ^ mask) for i in range(batch)])

    def bring(*arrays):
        if not fast:
            return arrays
        return run(
            bring_kernel,
            1,
            at,
            [(a, None) for a in arrays],
            [(a.shape, a.dtype, pl.BlockSpec(a.shape, lambda i, at: (0, 0)), True) for a in arrays],
            [],
        )

    own_rows, other_rows = pair_of(residual)
    own_cot, other_cot = pair_of(cot)

    gate_w, value_w = wide(gate_proj, 1), wide(value_proj, 1)
    out_w = wide(out_proj, 0)
    step_w = lanes_of(step_proj)
    gain_in = norm_gain[None, :]
    vconv, vshift = wide(value_conv, 1), wide(value_shift[None, :], 1)
    sshift = state_shift[None, :]
    sbias, rate = lanes_of(step_bias[None, :]), lanes_of(log_rate[None, :])
    skipx = wide(jnp.repeat(skip_gain, head_width)[None, :], 1)
    ggain = wide(gated_gain[None, :], 1, 1)
    head_of = jnp.arange(width) // head_width
    spread = (jnp.arange(LANES)[:, None] == head_of[None, :]).astype(bf16)
    spread = jnp.concatenate([spread, spread], axis=0)
    first = head_of.reshape(-1, 1, LANES, 1) + jnp.arange(2).reshape(1, 2, 1, 1) * LANES
    gather = (jnp.arange(2 * LANES) == first).reshape(-1, 2 * LANES).astype(bf16)

    gate_w, value_w, state_proj, step_w, out_w, spread, gather = bring(
        gate_w, value_w, state_proj, step_w, out_w, spread, gather
    )
    gain_in, vconv, vshift, state_conv, sshift, sbias, rate, skipx, ggain = bring(
        gain_in, vconv, vshift, state_conv, sshift, sbias, rate, skipx, ggain
    )

    def own_block(i, a):
        return (jnp.clip(i - a[0] * half_blocks, 0, half_blocks - 1), 0)

    def other_block(i, a):
        return (jnp.clip(i - (1 - a[0]) * half_blocks, 0, half_blocks - 1), 0) if two else (0, 0)

    other_read = other_block if two else own_block

    def rows(n, index=lambda i, a: (i, 0)):
        return pl.BlockSpec((BLOCK, n), index)

    along = pl.BlockSpec((8, BLOCK), lambda i, a: (0, i))
    unit = 2 * BLOCK if two and rows_here % (2 * BLOCK) == 0 else BLOCK
    units, half_units = length // unit, half_blocks * BLOCK // unit

    def own_unit(i, a):
        return (jnp.clip(i - a[0] * half_units, 0, half_units - 1), 0)

    def other_unit(i, a):
        return (jnp.clip(i - (1 - a[0]) * half_units, 0, half_units - 1), 0)

    other_taken = other_unit if two else own_unit

    def tall(n, index=lambda i, a: (i, 0)):
        return pl.BlockSpec((unit, n), index)

    fixed = lambda *shape: pl.BlockSpec(shape, lambda i, a: (0,) * len(shape))
    states_spec = lambda index: pl.BlockSpec((chunks, nstate, width), index)
    big = lambda *shape: pltpu.VMEM(shape, f32)
    low = lambda *shape: pltpu.VMEM(shape, bf16)
    halves = [
        ((rows_here if two else length, model), bf16, rows(model, own_block)),
        ((rows_here if two else BLOCK, model), bf16, rows(model, other_block)),
    ]

    normed, g, y, gg, values, slope, vp, conv_s, sp, z, sin, sq, step, running, shifted, grownx, tailx = run(
        functools.partial(forward_kernel, half_blocks),
        blocks,
        at,
        [
            (own_rows, rows(model, own_block)),
            (other_rows, rows(model, other_read)),
            (gain_in, None),
            (gate_w, None),
            (value_w, None),
            (state_proj, None),
            (step_w, None),
            (vconv, None),
            (vshift, None),
            (state_conv, None),
            (sshift, None),
            (sbias, None),
            (rate, None),
            (skipx, None),
            (ggain, None),
            (spread, None),
        ],
        [
            *[
                (shape, dtype, spec, fast)
                for shape, dtype, spec in (
                    ((length, model), bf16, rows(model)),
                    ((length, width), f32, rows(width)),
                    ((length, width), f32, rows(width)),
                    ((length, width), bf16, rows(width)),
                    ((length, width), bf16, rows(width)),
                    ((length, width), bf16, rows(width)),
                    ((length, width), bf16, rows(width)),
                    ((length, nstate2), f32, rows(nstate2)),
                    ((length, nstate2), bf16, rows(nstate2)),
                    ((length, LANES), f32, rows(LANES)),
                    ((blocks * chunks, nstate, width), bf16, states_spec(lambda i, a: (i, 0, 0))),
                    ((8, length), f32, along),
                    ((length, LANES), f32, rows(LANES)),
                    ((length, LANES), f32, rows(LANES)),
                    ((length, LANES), f32, rows(LANES)),
                    ((length, width), f32, rows(width)),
                    ((length, width), f32, rows(width)),
                )
            ]
        ],
        [
            big(width // LANES, BLOCK + 8, LANES),
            big(nstate2 // LANES, BLOCK + 8, LANES),
            big(nstate, width),
            big(BLOCK, width),
            big(BLOCK, width),
            low(BLOCK, width),
        ],
    )
    def stats_of(cot_rows, theirs, *before):
        first = (lambda a: (1 - a[0]) * half_units) if theirs else (lambda a: a[0] * half_units)
        count = cot_rows.shape[0]
        return run(
            stats_kernel,
            count // unit,
            at,
            [
                (cot_rows, tall(model)),
                (gg, tall(width, lambda i, a: (first(a) + i, 0))),
                (sq, pl.BlockSpec((8, unit), lambda i, a: (0, first(a) + i))),
                (out_w, None),
                *[(b, pl.BlockSpec((8, unit), lambda i, a: (0, i))) for b in before],
            ],
            [
                ((count, width), f32, tall(width), fast),
                (
                    (8 + 8 * len(before), count),
                    f32,
                    pl.BlockSpec((8 + 8 * len(before), unit), lambda i, a: (0, i)),
                ),
            ],
            [],
        )

    og, stats = stats_of(own_cot, False)
    if two:
        og_b, stats = stats_of(other_cot, True, stats)
    else:
        og_b = og
    got = add_other(stats)
    above = 1 if two else 0

    def stats_at(row, block, size=BLOCK):
        return pl.BlockSpec((8, size), lambda i, a: (row, block(i, a)[0]))

    branch, branch_sent = run(
        functools.partial(branch_kernel, half_units),
        units,
        at,
        [(gg, tall(width)), (out_w, None)],
        [
            ((rows_here if two else length, model), bf16, tall(model, own_unit)),
            ((rows_here if two else BLOCK, model), bf16, tall(model, other_unit if two else other_block)),
        ],
        [],
    )

    def other_half(own, sent):
        if two:
            return lax.ppermute(sent, "heads", swap)
        total = lax.psum_scatter(own.astype(f32), "heads", scatter_dimension=0, tiled=True)
        mine = lax.dynamic_slice_in_dim(own, own_from, rows_here, 0).astype(f32)
        return total - mine

    branch_got = other_half(branch, branch_sent)
    if not two:
        branch = lax.dynamic_slice_in_dim(branch, own_from, rows_here, 0)
    if fast:
        pieces = [((model // 2, 2 * model), bf16, fixed(model // 2, 2 * model))] * 2
    else:
        pieces = [
            ((model, width), f32, fixed(model, width)),
            ((width, model), f32, fixed(width, model)),
        ]
    dg, dy, early_a, early_b, grad_gain = run(
        functools.partial(gate_kernel, half_units, inner_all, fast),
        units,
        at,
        [
            (own_cot, tall(model, own_unit)),
            (other_cot, tall(model, other_taken)),
            (stats, stats_at(above, own_unit, unit)),
            (got, stats_at(0, own_unit, unit)),
            (stats, stats_at(0, other_taken, unit)),
            (got, stats_at(above, other_taken, unit)),
            (normed, None),
            (og, tall(width, own_unit)),
            (og_b, tall(width, other_taken)),
            (y, tall(width)),
            (g, tall(width)),
            (gg, None),
            (ggain, None),
            (branch, pl.BlockSpec(memory_space=pl.ANY)),
        ],
        [
            ((length, width), bf16, fixed(length, width), fast),
            ((length, width), bf16, tall(width), fast),
            *pieces,
            ((8, width), f32, fixed(8, width)),
        ],
        [low(length, model)] + ([big(model, width), big(width, model)] if fast else []),
    )

    def backward(start, count, carry, after=()):
        size = 2 * BLOCK if start % 2 == 0 and count % 2 == 0 else BLOCK
        size = count * BLOCK if fast else size
        steps, base = count * BLOCK // size, start * BLOCK // size

        def local(n):
            return pl.BlockSpec((size, n), lambda i, a: (steps - 1 - i, 0))

        def taken(array):
            if fast:
                return (array, None)
            shape = (size // CHUNK if array.ndim == 3 else size, *array.shape[1:])
            rest = (0,) * (array.ndim - 1)
            return (array, pl.BlockSpec(shape, lambda i, a: (base + steps - 1 - i, *rest)))

        slabs = [(width // LANES, 8, LANES), (nstate2 // LANES, 8, LANES)]
        vectors = [(nstate, width), *slabs, (8, width), (8, nstate2), (8, LANES)]
        out = run(
            functools.partial(
                backward_kernel, size, start * BLOCK if fast else 0, bool(carry), len(after)
            ),
            steps,
            at,
            [
                *[
                    taken(a)
                    for a in (dy, values, slope, vp, conv_s, sp, z, step, running, shifted, grownx, tailx, sin)
                ],
                (vconv, None),
                (state_conv, None),
                (rate, None),
                (skipx, None),
                (gather, None),
                *[(c, None) for c in carry],
                *[(a, pl.BlockSpec(memory_space=pl.ANY)) for a in after],
            ],
            [
                ((count * BLOCK, width), bf16, local(width)),
                ((count * BLOCK, nstate2), bf16, local(nstate2)),
                ((count * BLOCK, LANES), bf16, local(LANES)),
                *[(shape, f32, fixed(*shape)) for shape in vectors],
            ],
            [
                big(width // LANES, size + 8, LANES),
                big(nstate2 // LANES, size + 8, LANES),
                big(nstate, width),
                big(size, width),
                big(size, width),
                low(size, width),
                low(size, width),
                low(size, 2 * width),
                low(size, 2 * width),
            ],
        )
        return out[:3], out[3:]

    if two:
        own_stats, their_stats = stats_at(1, lambda i, a: (i, 0)), along
    else:
        own_stats = their_stats = stats_at(0, lambda i, a: (i + a[4] // BLOCK, 0))
    mixed, token = run(
        functools.partial(mixed_kernel, inner_all),
        rows_here // BLOCK,
        at,
        [
            (residual, rows(model)),
            (branch, rows(model)),
            (branch_got, rows(model)),
            (stats, own_stats),
            (got, their_stats),
        ],
        [((rows_here, model), f32, rows(model)), ((8, LANES), f32, fixed(8, LANES))],
        [],
    )
    from_gate = run(
        gate_back_kernel,
        blocks,
        at,
        [(dg, rows(width)), (gate_w, None)],
        [((length, model), f32, rows(model), fast)],
        [],
    )[0]
    cut = blocks // 2
    behind = ()
    if fast:
        steps = [("fold", 2, [early_a, hop(early_b, "core")], 2, False)]
        ((kept, sent),) = stage(at, steps, (from_gate,))
        early = [kept, hop(sent, "line")]
        behind = (kept,)
    low_b, carry = backward(cut, blocks - cut, (), behind)
    *partial, norm = run(
        functools.partial(partial_kernel, cut * BLOCK, fast),
        1,
        at,
        [
            (normed, None),
            *[(a, None) for a in low_b],
            (gate_w, None),
            (early_a, None),
            (early_b, None),
        ],
        [((model, a.shape[1]), f32, fixed(model, a.shape[1])) for a in low_b]
        + [((8, model), f32, fixed(8, model))],
        [],
    )
    if fast:
        ((kept, *sent),) = stage(at, [("fold", 3, early, 4, False)])
        early = [kept] + [hop(a, k + 1) for k, a in enumerate(sent)]
        behind = (kept, branch_got, partial[2])
    low_a, carry = backward(0, cut, carry, behind)
    vec, svec, head = carry[3:]
    early = early if fast else ()
    lows = [(a, rows(a.shape[1], lambda i, at: (jnp.minimum(i, cut - 1), 0))) for a in low_a]
    lows += [(a, rows(a.shape[1], lambda i, at: (jnp.maximum(i - cut, 0), 0))) for a in low_b]

    if fast:
        shape = (model // 2, width + nstate2 + LANES)
        pieces = [(shape, bf16, fixed(*shape))] * 2
        pieces.append((early[0].shape, bf16, fixed(*early[0].shape)))
    else:
        shapes = [(model, width), (model, nstate2), (model, LANES), (8, model)]
        pieces = [(shape, f32, fixed(*shape)) for shape in shapes]
    late = run(
        functools.partial(weights_kernel, fast),
        1,
        at,
        [
            (normed, None),
            *[(a, None) for a in low_a],
            *[(a, None) for a in partial],
            (value_w, None),
            (state_proj, None),
            (step_w, None),
            (gain_in, None),
            (vec, None),
            (svec, None),
            (head, None),
            (grad_gain, None),
            (norm, None),
            *[(a, None) for a in early],
        ],
        pieces,
        [big(model, width), big(model, nstate2), big(model, LANES)],
    )
    ng, ng_sent = run(
        functools.partial(normed_grad_kernel, half_blocks, cut),
        blocks,
        at,
        [
            (from_gate, rows(model)),
            *lows,
            (value_w, None),
            (state_proj, None),
            (step_w, None),
        ],
        halves,
        [],
    )

    ng_got = other_half(ng, ng_sent)
    if not two:
        ng = lax.dynamic_slice_in_dim(ng, own_from, rows_here, 0)
    grad_input, token_b = run(
        input_kernel,
        rows_here // BLOCK,
        at,
        [
            (residual, rows(model)),
            (cot, rows(model)),
            (ng, rows(model)),
            (ng_got, rows(model)),
            (gain_in, None),
        ],
        [((rows_here, model), f32, rows(model)), ((8, LANES), f32, fixed(8, LANES))],
        [],
    )

    if fast:
        kept, sent, early = late
        ((kept, sent),) = stage(at, [("fold", 2, [kept, hop(sent, "core")], 2, True)])
        got = hop(sent, "line")
        early = [early] + [hop(early, k) for k in (1, 2, 3)]
        ((kept, *sent),) = stage(at, [("fold", 3, [kept, got], 4, True)], (ng,))
        got = [hop(a, k + 1) for k, a in enumerate(sent)]
        steps = [("part", width, [kept, *got], 2, True), ("join", 3, early)]
        (done, rest), (early,) = stage(at, steps, (token,))
        early = [early, hop(early, "line")]
        theirs = lax.ppermute(rest, "heads", swap)
        done = run(
            heads_kernel,
            1,
            at,
            [(done, None), (rest, None), (theirs, None)],
            [((rest.shape[0], width + rest.shape[1]), bf16, fixed(rest.shape[0], width + rest.shape[1]))],
            [],
        )[0]
        done = [done] + [hop(done, k) for k in (1, 2, 3)]
        (done,), (early,) = stage(at, [("join", 3, done), ("join", 2, early)], (token_b,))
        grad_gate, grad_out_proj, token_c = run(
            early_kernel,
            1,
            at,
            [(early, None), (hop(early, "core"), None)],
            [((model, model), f32, fixed(model, model))] * 2
            + [((8, LANES), f32, fixed(8, LANES))],
            [],
        )
        quarter = done.shape[0]

        def wide(n):
            def index(i, a):
                return ((a[1] ^ (n // 2)) * 2 + (a[2] ^ (n % 2)), 0)

            return [((model, w), f32, pl.BlockSpec((quarter, w), index)) for w in (width, nstate2)]

        def kept_in(arrays):
            return [(a, pl.BlockSpec(memory_space=pl.ANY)) for a in arrays]

        def place(n, piece, filled=()):
            aliases = ((2, 0), (3, 1)) if filled else ()
            ins = [(piece, None), *kept_in(filled)]
            outs = wide(n) + [((8, LANES), f32, fixed(8, LANES))]
            return run(place_kernel, 1, at, ins, outs, [], aliases=aliases)

        got = hop(done, "line")
        across = hop(done, "core")
        *filled, token_d = place(0, done)
        *filled, token_e = place(2, across, filled)
        ((got,),) = stage(at, [("join", 2, [got])], (token_c, token_e))
        done = [done, got, across, hop(got, "core")]
        *filled, token_d = place(1, got, filled)
        shapes = [
            (heads, model),
            (4, width),
            (width,),
            (width,),
            (model,),
            (4, nstate2),
            (nstate2,),
            (heads,),
            (heads,),
            (heads,),
        ]
        (
            grad_value,
            grad_state,
            grad_step,
            grad_vconv,
            grad_vshift,
            grad_ggain,
            grad_norm,
            grad_sconv,
            grad_sshift,
            grad_bias,
            grad_rate,
            grad_skip,
        ) = run(
            late_kernel,
            1,
            at,
            [*[(a, None) for a in done], *kept_in(filled)],
            wide(3) + [(shape, f32, fixed(*shape)) for shape in shapes],
            [big(model, LANES)],
            aliases=((5, 0), (6, 1)),
        )
        return (
            mixed[None],
            grad_input[None],
            grad_norm,
            grad_gate,
            grad_value,
            grad_state,
            grad_step.T,
            grad_vconv,
            grad_vshift,
            grad_sconv,
            grad_sshift,
            grad_bias,
            grad_rate,
            grad_skip,
            grad_ggain,
            grad_out_proj,
        )
    grad_value, grad_state, grad_step, norm = late
    grad_gate, grad_value, grad_out_proj, grad_step, vec, head, grad_gain = lax.psum(
        (early_a, grad_value, early_b, grad_step, vec, head, grad_gain), "batch"
    )
    grad_state, svec, norm = lax.psum((grad_state, svec, norm), ("batch", "heads"))
    norm, ggrad = norm[0], grad_gain[0]
    return (
        mixed[None],
        grad_input[None],
        norm,
        grad_gate[:, :inner],
        grad_value[:, :inner],
        grad_state,
        grad_step[:, :heads],
        vec[:4, :inner],
        vec[4, :inner],
        svec[:4],
        svec[4],
        head[0, :heads],
        head[1, :heads],
        head[2, :heads],
        ggrad[:inner],
        grad_out_proj[:inner],
    )


def solution(mesh):
    return jax.shard_map(
        per_device,
        mesh=mesh,
        in_specs=(
            P("batch", "heads", None),
            P(),
            P(None, "heads"),
            P(None, "heads"),
            P(),
            P(None, "heads"),
            P(None, "heads"),
            P("heads"),
            P(),
            P(),
            P("heads"),
            P("heads"),
            P("heads"),
            P("heads"),
            P("heads", None),
            P("batch", "heads", None),
        ),
        out_specs=(
            P("batch", "heads", None),
            P("batch", "heads", None),
            P(),
            P(None, "heads"),
            P(None, "heads"),
            P(),
            P(None, "heads"),
            P(None, "heads"),
            P("heads"),
            P(),
            P(),
            P("heads"),
            P("heads"),
            P("heads"),
            P("heads"),
            P("heads", None),
        ),
        check_vma=False,
    )
```
